32 devices in a mesh: rep: 8 (over y, x, core), tp: 4 (over z).
Axes of the slice: x: 2, y: 2, z: 4, core: 2. Of those that a mesh axis runs over, the one named last changes fastest.
Arguments:
- residual: bfloat16 [16384, 8192], P(('rep', 'tp')), may hold values from -6 to 6
- norm_gain: bfloat16 [8192], P(('rep', 'tp')), may hold values from 0.5 to 1.5
- value_weight: bfloat16 [8192, 512], P(('rep', 'tp')), may hold values from -0.0625 to 0.0625
- value_cot: bfloat16 [16384, 512], P(('rep', 'tp')), may hold values from -12 to 12
- trainee_logp: float32 [16384], P(('rep', 'tp')), may hold values from -40 to -8
- ref_shard_max: float32 [4, 16384], P('tp', 'rep'), may hold values from 90 to 120
- ref_shard_sum: float32 [4, 16384], P('tp', 'rep'), may hold values from 1 to 1000
- ref_target_logit: float32 [4, 16384], P('tp', 'rep'), may hold values from 80 to 120
- target_ids: int32 [16384], P('rep'), may hold values from 0 to 128255
- lengths: int32 [8], replicated, may hold values from 1024 to 2048, as said below
Outputs:
- value_proj: bfloat16 [16384, 512], P(('rep', 'tp'))
- resid_grad: bfloat16 [16384, 8192], P(('rep', 'tp'))
- weight_grad: float32 [8192, 512], P(('rep', 'tp'))
- gain_grad: float32 [8192], P(('rep', 'tp'))
The draws below stay inside these ranges and needn't reach their ends.
Inputs may be any that keep to these rules, and one draw needn't show every extreme that they name: `lengths`: one sequence has all 2048 tokens live and one has 1024.
All inputs are finite; a program needn't handle non-finite values.
Results may differ from the reference program's by a relative error of at most 0.009.
Values may be sent and summed in bfloat16 or wider, within the bound.
No kernel may reach another device: no remote copies, remote signals or barrier semaphores. Data moves between devices by JAX's collectives and lax.ppermute only.
A program may use at most 192 MiB of HBM per device.

```python
import math
import jax
import jax.numpy as jnp
from jax import lax

D = 8192
HV = 512
VOCAB = 128256
SEQ = 2048
SEQS = 8
TOKENS = 16384
N_TP = 4


def draw_lengths(key, part):
    first_key, second_key = jax.random.split(jax.random.fold_in(key, 7))
    drawn = jax.random.randint(first_key, (SEQS,), SEQ // 2, SEQ + 1)
    order = jax.random.permutation(second_key, SEQS)
    drawn = drawn.at[order[0]].set(SEQ)
    drawn = drawn.at[order[1]].set(SEQ // 2)
    return drawn.astype(jnp.int32)


def with_ends(result, rng, low, largest):
    place = [jax.random.randint(jax.random.fold_in(rng, axis), (), 0, length) for axis, length in enumerate(result.shape)]
    longest = result.shape.index(max(result.shape))
    neighbour = place[:longest] + [(place[longest] + 1) % result.shape[longest]] + place[longest + 1:]
    return result.at[tuple(place)].set(low).at[tuple(neighbour)].set(largest)


def spiked(entries, own_key, source, target, blocks, factor):
    def block_of(dim):
        return (jnp.arange(entries.shape[dim]) // (entries.shape[dim] // blocks)).reshape((-1,) + (1,) * (entries.ndim - 1 - dim))

    first = jax.random.permutation(own_key, blocks)[block_of(target)]
    far = (block_of(target) + blocks // 2) % blocks
    return jnp.where((block_of(source) == first) | (block_of(source) == far), factor * entries, entries)


def shard_levels(own_key, shape, shards, least, top_value):
    def one(axis_at, shards_of):
        steps = jax.random.uniform(jax.random.fold_in(jax.random.fold_in(own_key, 6), axis_at), (shards_of,), jnp.float32, least / len(shards), top_value / len(shards))
        return jnp.repeat(jnp.exp(steps), shape[axis_at] // shards_of).reshape((-1,) + (1,) * (len(shape) - axis_at - 1))

    level = one(*shards[0])
    for cut in shards[1:]:
        level = level * one(*cut)
    return level


def centred(stream_key, shape, deviation, bound, shards=(), held_as=jnp.bfloat16):
    level = shard_levels(stream_key, shape, shards, -0.22, 0.18) if shards else 1.0
    array = jax.random.normal(stream_key, shape, jnp.float32) * deviation * level
    return jnp.minimum(jnp.maximum(array, -bound), bound).astype(held_as)


def gaussian_with(rng, extent, scale, reach, cuts, heavy, kind=jnp.bfloat16):
    values = scale * jax.random.normal(rng, extent, jnp.float32)
    if cuts:
        values = values * shard_levels(rng, extent, cuts, -0.22, 0.18)
    return jnp.clip(spiked(values, jax.random.fold_in(rng, 3), *heavy), -reach, reach).astype(kind)


def setup_inputs(seed: int = 0) -> dict:
    key_list = jax.random.split(jax.random.key(seed), 11)
    residual = gaussian_with(key_list[0], (TOKENS, D), 1.0, 6.0, ((0, 32),), (0, 1, 32, 2.75))
    norm_gain = jnp.clip(1.0 + 0.1 * jax.random.normal(key_list[1], (D,), jnp.float32), 0.5, 1.5).astype(jnp.bfloat16)
    value_weight = centred(key_list[2], (D, HV), D ** -0.5, 0.0625, ((0, 32),))
    value_cot = centred(key_list[3], (TOKENS, HV), 2.0, 12.0, ((0, 32),))
    trainee_logp = jnp.clip(-40.0 + 32.0 * jax.random.uniform(key_list[4], (TOKENS,), jnp.float32) ** shard_levels(key_list[4], (TOKENS,), ((0, 32),), -0.2, 0.2), -40.0, -8.0)
    ref_shard_max = jnp.clip(90.0 + 30.0 * jax.random.uniform(key_list[5], (N_TP, TOKENS), jnp.float32) ** shard_levels(key_list[5], (N_TP, TOKENS), ((0, 4), (1, 8)), -0.2, 0.2), 90.0, 120.0)
    ref_shard_sum = jnp.clip(jnp.exp(math.log(1000.0) - 6.9077553 * jax.random.uniform(key_list[6], (N_TP, TOKENS), jnp.float32) ** shard_levels(key_list[6], (N_TP, TOKENS), ((0, 4), (1, 8)), -0.2, 0.2)), 1.0, 1000.0)
    ref_target_logit = jnp.clip(80.0 + 40.0 * jax.random.uniform(key_list[7], (N_TP, TOKENS), jnp.float32) ** shard_levels(key_list[7], (N_TP, TOKENS), ((0, 4), (1, 8)), -0.2, 0.2), 80.0, 120.0)
    target_ids = with_ends(jax.random.randint(key_list[8], (TOKENS,), 0, VOCAB), jax.random.fold_in(key_list[8], 1), 0, VOCAB - 1).astype(jnp.int32)
    lengths = draw_lengths(jax.random.fold_in(key_list[10], 71), 0)
    return {"residual": residual, "norm_gain": norm_gain, "value_weight": value_weight, "value_cot": value_cot, "trainee_logp": trainee_logp, "ref_shard_max": ref_shard_max, "ref_shard_sum": ref_shard_sum, "ref_target_logit": ref_target_logit, "target_ids": target_ids, "lengths": lengths}


EPS = 1e-05
BETA = 0.5

def reference(residual, norm_gain, value_weight, value_cot, trainee_logp, ref_shard_max, ref_shard_sum, ref_target_logit, target_ids, lengths):
    top_max = lax.optimization_barrier(jnp.max(ref_shard_max, axis=0))
    sum_exp = lax.optimization_barrier(jnp.sum(ref_shard_sum * jnp.exp(ref_shard_max - top_max[None, :]), axis=0))
    owner_shard = target_ids // (VOCAB // N_TP)
    shard_ids = jnp.arange(N_TP, dtype=jnp.int32)
    picked = lax.optimization_barrier(jnp.sum(jnp.where(owner_shard[None, :] == shard_ids[:, None], ref_target_logit, jnp.zeros_like(ref_target_logit)), axis=0))
    ref_logp = picked - top_max - jnp.log(sum_exp)
    positions = jnp.arange(SEQ, dtype=jnp.int32)
    live_rows = (positions[None, :] < lengths[:, None]).astype(jnp.float32)
    token_diff = (trainee_logp - ref_logp).reshape(SEQS, SEQ) * live_rows
    seq_delta = lax.optimization_barrier(jnp.sum(token_diff, axis=1)) / lengths.astype(jnp.float32)
    seq_weight = 2.0 * jax.nn.sigmoid(BETA * seq_delta) / SEQS
    row_scale = live_rows * seq_weight[:, None]
    gain_wide = norm_gain.astype(jnp.float32)

    def one_sequence(carry, inputs):
        weight_acc, gain_acc = carry
        resid_block, cot_block, scale_block = inputs
        resid_wide = resid_block.astype(jnp.float32)
        inv_rms = lax.rsqrt(lax.optimization_barrier(jnp.mean(resid_wide * resid_wide, axis=1, keepdims=True)) + EPS)
        unit_rows = resid_wide * inv_rms
        normed = (unit_rows * gain_wide).astype(jnp.bfloat16)
        value_proj = jnp.dot(normed, value_weight, preferred_element_type=jnp.float32).astype(jnp.bfloat16)
        scaled = (scale_block[:, None] * cot_block.astype(jnp.float32)).astype(jnp.bfloat16)
        normed_grad = jnp.dot(scaled, value_weight.T, preferred_element_type=jnp.float32)
        unit_grad = normed_grad * gain_wide
        project_mean = lax.optimization_barrier(jnp.mean(unit_grad * unit_rows, axis=1, keepdims=True))
        resid_grad = (inv_rms * (unit_grad - unit_rows * project_mean)).astype(jnp.bfloat16)
        weight_acc = weight_acc + jnp.dot(normed.T, scaled, preferred_element_type=jnp.float32)
        gain_acc = gain_acc + lax.optimization_barrier(jnp.sum(normed_grad * unit_rows, axis=0))
        return ((weight_acc, gain_acc), (value_proj, resid_grad))
    start_carry = (jnp.zeros((D, HV), jnp.float32), jnp.zeros((D,), jnp.float32))
    stacked = (residual.reshape(SEQS, SEQ, D), value_cot.reshape(SEQS, SEQ, HV), row_scale)
    (weight_grad, gain_grad), (value_rows, resid_rows) = lax.scan(one_sequence, start_carry, stacked)
    return (value_rows.reshape(TOKENS, HV), resid_rows.reshape(TOKENS, D), weight_grad, gain_grad)
```

```python
import functools

import jax
import jax.numpy as jnp
from jax import lax
from jax.experimental import pallas as pl
from jax.experimental.pallas import tpu as pltpu
from jax.sharding import PartitionSpec as P

VOCAB = 128256
EPS = 1e-05
BETA = 0.5
CORES = 2
OUTER = 2


def shift_pairs(count, stride, size, step):
    pairs = []
    for place in range(count):
        digit = (place // stride) % size
        pairs.append((place, place + ((digit + step) % size - digit) * stride))
    return pairs


def swap(value, axis, stride, size, step):
    return lax.ppermute(value, axis, shift_pairs(lax.axis_size(axis), stride, size, step))


def partial_kernel(blocks_ref, places_ref, resid_ref, cot_ref, out_ref):
    product = lax.dot_general(
        resid_ref[...], cot_ref[...], (((0,), (0,)), ((), ())), preferred_element_type=jnp.float32
    )
    out_ref[0] = product.astype(out_ref.dtype)


def partial_add_kernel(blocks_ref, places_ref, resid_ref, cot_ref, other_ref, out_ref):
    product = lax.dot_general(
        resid_ref[...], cot_ref[...], (((0,), (0,)), ((), ())), preferred_element_type=jnp.float32
    )
    out_ref[0] = (product + other_ref[0].astype(jnp.float32)).astype(out_ref.dtype)


def partial_grad(resid, cot, first_col, width, blocks, places, depth, other):
    rows = resid.shape[0]
    count = blocks.shape[0]
    col = first_col // width
    in_specs = [
        pl.BlockSpec((rows, depth), lambda i, b, p: (0, b[i])),
        pl.BlockSpec((rows, width), lambda i, b, p: (0, col)),
    ]
    operands = [resid, cot]
    if other is not None:
        in_specs.append(pl.BlockSpec((1, depth, width), lambda i, b, p: (p[i], 0, col)))
        operands.append(other)
    return pl.pallas_call(
        partial_kernel if other is None else partial_add_kernel,
        out_shape=jax.ShapeDtypeStruct((count, depth, width), jnp.bfloat16),
        grid_spec=pltpu.PrefetchScalarGridSpec(
            num_scalar_prefetch=2,
            grid=(count,),
            in_specs=in_specs,
            out_specs=pl.BlockSpec((1, depth, width), lambda i, b, p: (i, 0, 0)),
        ),
        cost_estimate=pl.CostEstimate(
            flops=2 * rows * count * depth * width,
            bytes_accessed=2 * count * depth * (rows + 2 * width),
            transcendentals=0,
        ),
        compiler_params=pltpu.CompilerParams(vmem_limit_bytes=40 * 1024 * 1024),
    )(blocks, places, *operands)


def sequence_weight(trainee_logp, shard_max, shard_sum, owned, seq_length, rep_count, tp_count, tp_place):
    rows_here = trainee_logp.shape[0]
    seq = shard_max.shape[0]
    packed = jnp.concatenate([shard_max, shard_sum, owned, trainee_logp]).reshape(-1, 128)
    shares = [packed] + [swap(packed, "tp", 1, tp_count, s) for s in range(1, tp_count)]
    shares = [share.reshape(-1) for share in shares]
    top_max = functools.reduce(jnp.maximum, [share[:seq] for share in shares])
    sum_exp = sum(share[seq : 2 * seq] * jnp.exp(share[:seq] - top_max) for share in shares)
    picked = sum(share[2 * seq : 3 * seq] for share in shares)
    ref_logp = picked - top_max - jnp.log(sum_exp)
    total = jnp.zeros((), jnp.float32)
    for s, share in enumerate(shares):
        first = lax.rem(tp_place - s + tp_count, tp_count) * rows_here
        live = first + jnp.arange(rows_here, dtype=jnp.int32) < seq_length
        diff = share[3 * seq :] - lax.dynamic_slice_in_dim(ref_logp, first, rows_here)
        total = total + jnp.sum(jnp.where(live, diff, 0.0))
    seq_delta = total / seq_length.astype(jnp.float32)
    return 2.0 * jax.nn.sigmoid(BETA * seq_delta) / rep_count


def per_device(
    residual,
    norm_gain,
    value_weight,
    value_cot,
    trainee_logp,
    ref_shard_max,
    ref_shard_sum,
    ref_target_logit,
    target_ids,
    lengths,
):
    rows_here, width = residual.shape
    features = value_cot.shape[1]
    half = features // 2
    tp_count = lax.axis_size("tp")
    rep_count = lax.axis_size("rep")
    tp_place = lax.axis_index("tp")
    rep_place = lax.axis_index("rep")
    outer, inner = OUTER, rep_count // (OUTER * CORES)
    depth = width // rep_count
    own_rows = depth // tp_count
    core = lax.rem(rep_place, CORES)
    at_inner = lax.rem(rep_place // CORES, inner)
    at_outer = rep_place // (CORES * inner)

    gain_wide = norm_gain.astype(jnp.float32)[:, None]
    gained = (value_weight.astype(jnp.float32) * gain_wide).astype(jnp.bfloat16)
    weight = lax.all_gather(gained, ("rep", "tp"), axis=0, tiled=True)

    owned = jnp.where(
        target_ids // (VOCAB // tp_count) == tp_place,
        ref_target_logit[0],
        jnp.zeros_like(ref_target_logit[0]),
    )
    seq_length = lax.dynamic_index_in_dim(lengths, rep_place, keepdims=False)
    seq_weight = sequence_weight(
        trainee_logp, ref_shard_max[0], ref_shard_sum[0], owned, seq_length, rep_count, tp_count, tp_place
    )
    positions = tp_place * rows_here + jnp.arange(rows_here, dtype=jnp.int32)
    row_scale = (positions < seq_length).astype(jnp.float32) * seq_weight
    resid_wide = residual.astype(jnp.float32)
    inv_rms = lax.rsqrt(jnp.mean(resid_wide * resid_wide, axis=1, keepdims=True) + EPS)
    cot = (inv_rms * row_scale[:, None] * value_cot.astype(jnp.float32)).astype(jnp.bfloat16)

    chips = jnp.arange(outer * inner, dtype=jnp.int32)
    theirs = partial_grad(residual, cot, 0, features, chips * CORES + (1 - core), chips, depth, None)
    other = swap(theirs, "rep", 1, CORES, 1)

    def block_at(step_outer, step_inner):
        return lax.rem(at_outer + step_outer, outer) * inner + lax.rem(at_inner + step_inner, inner)

    def own_blocks(first_col, steps):
        places = jnp.stack([block_at(o, i) for o, i in steps]).astype(jnp.int32)
        return partial_grad(residual, cot, first_col, half, places * CORES + core, places, depth, other)

    def widen(parts):
        return sum(part.astype(jnp.float32) for part in parts)

    sent_a = [own_blocks(0, [(o, s) for o in range(outer)]) for s in range(1, inner)]
    got_a = [swap(x, "rep", CORES, inner, s + 1) for s, x in enumerate(sent_a)]
    sent_b = [own_blocks(half, [(s, i) for i in range(inner)]) for s in range(1, outer)]
    got_b = [swap(x, "rep", CORES * inner, outer, s + 1) for s, x in enumerate(sent_b)]
    kept_a = own_blocks(0, [(o, 0) for o in range(outer)])
    kept_b = own_blocks(half, [(0, i) for i in range(inner)])

    sent_a = [widen([kept_a[o]] + [g[o] for g in got_a]).astype(jnp.bfloat16) for o in range(1, outer)]
    next_a = [swap(x, "rep", CORES * inner, outer, s + 1) for s, x in enumerate(sent_a)]
    sent_b = [widen([kept_b[i]] + [g[i] for g in got_b]).astype(jnp.bfloat16) for i in range(1, inner)]
    next_b = [swap(x, "rep", CORES, inner, s + 1) for s, x in enumerate(sent_b)]
    chip_a = widen([kept_a[0]] + [g[0] for g in got_a] + next_a)
    chip_b = widen([kept_b[0]] + [g[0] for g in got_b] + next_b)

    def rows_for(step):
        first = lax.rem(tp_place + step, tp_count) * own_rows
        return jnp.concatenate(
            [lax.dynamic_slice_in_dim(part, first, own_rows) for part in (chip_a, chip_b)], axis=1
        )

    last = [
        swap(rows_for(s).astype(jnp.bfloat16), "tp", 1, tp_count, s) for s in range(1, tp_count)
    ]
    unit_grad_rows = rows_for(0) + widen(last)
    weight_grad = gain_wide * unit_grad_rows
    gain_grad = jnp.sum(value_weight.astype(jnp.float32) * unit_grad_rows, axis=1)

    value_acc = jnp.dot(residual, weight, preferred_element_type=jnp.float32)
    value_proj = (inv_rms * value_acc).astype(jnp.bfloat16)
    share = jnp.sum(cot.astype(jnp.float32) * value_acc, axis=1, keepdims=True)
    coefficient = inv_rms * inv_rms * share * (1.0 / width)
    normed_grad = lax.dot_general(
        cot, weight, (((1,), (1,)), ((), ())), preferred_element_type=jnp.float32
    )
    resid_grad = (normed_grad - residual.astype(jnp.float32) * coefficient).astype(jnp.bfloat16)
    return (value_proj, resid_grad, weight_grad, gain_grad)


def solution(mesh):
    placed = (
        P(("rep", "tp"), None),
        P(("rep", "tp")),
        P(("rep", "tp"), None),
        P(("rep", "tp"), None),
        P(("rep", "tp")),
        P("tp", "rep"),
        P("tp", "rep"),
        P("tp", "rep"),
        P("rep"),
        P(),
    )
    return jax.shard_map(
        per_device,
        mesh=mesh,
        in_specs=placed,
        out_specs=(
            P(("rep", "tp"), None),
            P(("rep", "tp"), None),
            P(("rep", "tp"), None),
            P(("rep", "tp")),
        ),
        check_vma=False,
    )
```

```python
import functools

import jax
import jax.numpy as jnp
from jax import lax
from jax.experimental import pallas as pl
from jax.experimental.pallas import tpu as pltpu
from jax.sharding import PartitionSpec as P

VOCAB = 128256
EPS = 1e-05
BETA = 0.5
CORES = 2
OUTER = 2


def swap(value, axis, step):
    size = lax.axis_size(axis)
    return lax.ppermute(value, axis, [(place, (place + step) % size) for place in range(size)])


def partial_kernel(blocks_ref, places_ref, resid_ref, cot_ref, out_ref):
    product = lax.dot_general(
        resid_ref[...], cot_ref[...], (((0,), (0,)), ((), ())), preferred_element_type=jnp.float32
    )
    out_ref[0] = product.astype(out_ref.dtype)


def partial_add_kernel(blocks_ref, places_ref, resid_ref, cot_ref, other_ref, out_ref):
    product = lax.dot_general(
        resid_ref[...], cot_ref[...], (((0,), (0,)), ((), ())), preferred_element_type=jnp.float32
    )
    out_ref[0] = (product + other_ref[0].astype(jnp.float32)).astype(out_ref.dtype)


def partial_grad(resid, cot, first_col, width, blocks, places, depth, other):
    rows = resid.shape[0]
    count = blocks.shape[0]
    col = first_col // width
    in_specs = [
        pl.BlockSpec((rows, depth), lambda i, b, p: (0, b[i])),
        pl.BlockSpec((rows, width), lambda i, b, p: (0, col)),
    ]
    operands = [resid, cot]
    if other is not None:
        in_specs.append(pl.BlockSpec((1, depth, width), lambda i, b, p: (p[i], 0, col)))
        operands.append(other)
    return pl.pallas_call(
        partial_kernel if other is None else partial_add_kernel,
        out_shape=jax.ShapeDtypeStruct((count, depth, width), jnp.bfloat16),
        grid_spec=pltpu.PrefetchScalarGridSpec(
            num_scalar_prefetch=2,
            grid=(count,),
            in_specs=in_specs,
            out_specs=pl.BlockSpec((1, depth, width), lambda i, b, p: (i, 0, 0)),
        ),
        cost_estimate=pl.CostEstimate(
            flops=2 * rows * count * depth * width,
            bytes_accessed=2 * count * depth * (rows + 2 * width),
            transcendentals=0,
        ),
        compiler_params=pltpu.CompilerParams(vmem_limit_bytes=40 * 1024 * 1024),
    )(blocks, places, *operands)


def value_kernel(core_ref, resid_ref, own_ref, other_ref, cot_ref, inv_ref, value_ref, coef_ref, total_ref):
    step = pl.program_id(0)
    count = pl.num_programs(0)

    @pl.when(step == 0)
    def _():
        total_ref[...] = jnp.zeros_like(total_ref)

    @pl.when(step < count // 2)
    def _():
        total_ref[...] += jnp.dot(resid_ref[...], own_ref[0], preferred_element_type=jnp.float32)

    @pl.when(step >= count // 2)
    def _():
        total_ref[...] += jnp.dot(resid_ref[...], other_ref[0], preferred_element_type=jnp.float32)

    @pl.when(step == count - 1)
    def _():
        total = total_ref[...]
        inv = inv_ref[...]
        value_ref[...] = (total * inv).astype(value_ref.dtype)
        share = jnp.sum(total * cot_ref[...].astype(jnp.float32), axis=1, keepdims=True)
        width = resid_ref.shape[1] * count
        coef_ref[...] = share * (inv * inv) * (1.0 / width)


def weight_specs(chips, depth, features):
    return [
        pl.BlockSpec((1, depth, features), lambda i, c: (jnp.minimum(i, chips - 1), 0, 0)),
        pl.BlockSpec((1, depth, features), lambda i, c: (jnp.maximum(i - chips, 0), 0, 0)),
    ]


def feature_block(chips):
    return lambda i, c: (0, lax.rem(i, chips) * CORES + jnp.where(i < chips, c[0], 1 - c[0]))


def value_product(core, residual, own, other, cot, inv_rms):
    rows, width = residual.shape
    chips, depth, features = own.shape
    whole = lambda i, c: (0, 0)
    return pl.pallas_call(
        value_kernel,
        out_shape=(
            jax.ShapeDtypeStruct((rows, features), jnp.bfloat16),
            jax.ShapeDtypeStruct((rows, 1), jnp.float32),
        ),
        grid_spec=pltpu.PrefetchScalarGridSpec(
            num_scalar_prefetch=1,
            grid=(CORES * chips,),
            in_specs=[pl.BlockSpec((rows, depth), feature_block(chips))]
            + weight_specs(chips, depth, features)
            + [pl.BlockSpec((rows, features), whole), pl.BlockSpec((rows, 1), whole)],
            out_specs=(pl.BlockSpec((rows, features), whole), pl.BlockSpec((rows, 1), whole)),
            scratch_shapes=[pltpu.VMEM((rows, features), jnp.float32)],
        ),
        cost_estimate=pl.CostEstimate(
            flops=2 * rows * width * features,
            bytes_accessed=2 * width * (rows + features),
            transcendentals=0,
        ),
        compiler_params=pltpu.CompilerParams(vmem_limit_bytes=40 * 1024 * 1024),
    )(core, residual, own, other, cot, inv_rms)


def grad_kernel(core_ref, cot_ref, coef_ref, resid_ref, own_ref, other_ref, out_ref):
    step = pl.program_id(0)
    count = pl.num_programs(0)

    def write(weight):
        grad = lax.dot_general(
            cot_ref[...], weight, (((1,), (1,)), ((), ())), preferred_element_type=jnp.float32
        )
        out_ref[...] = (grad - resid_ref[...].astype(jnp.float32) * coef_ref[...]).astype(out_ref.dtype)

    @pl.when(step < count // 2)
    def _():
        write(own_ref[0])

    @pl.when(step >= count // 2)
    def _():
        write(other_ref[0])


def residual_grad(core, cot, coefficient, residual, own, other):
    rows, width = residual.shape
    chips, depth, features = own.shape
    whole = lambda i, c: (0, 0)
    return pl.pallas_call(
        grad_kernel,
        out_shape=jax.ShapeDtypeStruct((rows, width), jnp.bfloat16),
        grid_spec=pltpu.PrefetchScalarGridSpec(
            num_scalar_prefetch=1,
            grid=(CORES * chips,),
            in_specs=[
                pl.BlockSpec((rows, features), whole),
                pl.BlockSpec((rows, 1), whole),
                pl.BlockSpec((rows, depth), feature_block(chips)),
            ]
            + weight_specs(chips, depth, features),
            out_specs=pl.BlockSpec((rows, depth), feature_block(chips)),
        ),
        cost_estimate=pl.CostEstimate(
            flops=2 * rows * width * features,
            bytes_accessed=2 * width * (2 * rows + features),
            transcendentals=0,
        ),
        compiler_params=pltpu.CompilerParams(vmem_limit_bytes=40 * 1024 * 1024),
    )(core, cot, coefficient, residual, own, other)


def sequence_weight(trainee_logp, shard_max, shard_sum, owned, seq_length, rep_count, tp_count, tp_place):
    rows_here = trainee_logp.shape[0]
    seq = shard_max.shape[0]
    packed = jnp.concatenate([shard_max, shard_sum, owned, trainee_logp]).reshape(-1, 128)
    shares = [packed] + [swap(packed, "tp", s) for s in range(1, tp_count)]
    shares = [share.reshape(-1) for share in shares]
    top_max = functools.reduce(jnp.maximum, [share[:seq] for share in shares])
    sum_exp = sum(share[seq : 2 * seq] * jnp.exp(share[:seq] - top_max) for share in shares)
    picked = sum(share[2 * seq : 3 * seq] for share in shares)
    ref_logp = picked - top_max - jnp.log(sum_exp)
    total = jnp.zeros((), jnp.float32)
    for s, share in enumerate(shares):
        first = lax.rem(tp_place - s + tp_count, tp_count) * rows_here
        live = first + jnp.arange(rows_here, dtype=jnp.int32) < seq_length
        diff = share[3 * seq :] - lax.dynamic_slice_in_dim(ref_logp, first, rows_here)
        total = total + jnp.sum(jnp.where(live, diff, 0.0))
    seq_delta = total / seq_length.astype(jnp.float32)
    return 2.0 * jax.nn.sigmoid(BETA * seq_delta) / rep_count


def per_device(
    residual,
    norm_gain,
    value_weight,
    value_cot,
    trainee_logp,
    ref_shard_max,
    ref_shard_sum,
    ref_target_logit,
    target_ids,
    lengths,
):
    rows_here, width = residual.shape
    features = value_cot.shape[1]
    half = features // 2
    tp_count = lax.axis_size("tp")
    outer, inner = lax.axis_size("outer"), lax.axis_size("inner")
    rep_count = outer * inner * CORES
    tp_place = lax.axis_index("tp")
    core = lax.axis_index("core")
    at_inner = lax.axis_index("inner")
    at_outer = lax.axis_index("outer")
    rep_place = (at_outer * inner + at_inner) * CORES + core
    depth = width // rep_count
    own_rows = depth // tp_count

    gain_wide = norm_gain.astype(jnp.float32)[:, None]
    gained = (value_weight.astype(jnp.float32) * gain_wide).astype(jnp.bfloat16)
    residual, gained = lax.optimization_barrier((residual, gained))
    own_weight = lax.all_gather(gained, ("outer", "inner", "tp"), axis=0, tiled=True)
    own_weight = own_weight.reshape(outer * inner, depth, features)

    owned = jnp.where(
        target_ids // (VOCAB // tp_count) == tp_place,
        ref_target_logit[0],
        jnp.zeros_like(ref_target_logit[0]),
    )
    seq_length = lax.dynamic_index_in_dim(lengths, rep_place, keepdims=False)
    seq_weight = sequence_weight(
        trainee_logp, ref_shard_max[0], ref_shard_sum[0], owned, seq_length, rep_count, tp_count, tp_place
    )
    positions = tp_place * rows_here + jnp.arange(rows_here, dtype=jnp.int32)
    row_scale = (positions < seq_length).astype(jnp.float32) * seq_weight
    resid_wide = residual.astype(jnp.float32)
    inv_rms = lax.rsqrt(jnp.mean(resid_wide * resid_wide, axis=1, keepdims=True) + EPS)
    cot = (inv_rms * row_scale[:, None] * value_cot.astype(jnp.float32)).astype(jnp.bfloat16)

    chips = jnp.arange(outer * inner, dtype=jnp.int32)
    theirs = partial_grad(residual, cot, 0, features, chips * CORES + (1 - core), chips, depth, None)
    other = swap(theirs, "core", 1)

    def block_at(step_outer, step_inner):
        return lax.rem(at_outer + step_outer, outer) * inner + lax.rem(at_inner + step_inner, inner)

    def own_blocks(first_col, steps):
        places = jnp.stack([block_at(o, i) for o, i in steps]).astype(jnp.int32)
        return partial_grad(residual, cot, first_col, half, places * CORES + core, places, depth, other)

    def widen(parts):
        return sum(part.astype(jnp.float32) for part in parts)

    sent_a = [own_blocks(0, [(o, s) for o in range(outer)]) for s in range(1, inner)]
    got_a = [swap(x, "inner", s + 1) for s, x in enumerate(sent_a)]
    sent_b = [own_blocks(half, [(s, i) for i in range(inner)]) for s in range(1, outer)]
    got_b = [swap(x, "outer", s + 1) for s, x in enumerate(sent_b)]
    kept_a = own_blocks(0, [(o, 0) for o in range(outer)])
    kept_b = own_blocks(half, [(0, i) for i in range(inner)])

    sent_a = [widen([kept_a[o]] + [g[o] for g in got_a]).astype(jnp.bfloat16) for o in range(1, outer)]
    next_a = [swap(x, "outer", s + 1) for s, x in enumerate(sent_a)]
    sent_b = [widen([kept_b[i]] + [g[i] for g in got_b]).astype(jnp.bfloat16) for i in range(1, inner)]
    next_b = [swap(x, "inner", s + 1) for s, x in enumerate(sent_b)]
    chip_a = widen([kept_a[0]] + [g[0] for g in got_a] + next_a)
    chip_b = widen([kept_b[0]] + [g[0] for g in got_b] + next_b)

    def rows_for(step):
        first = lax.rem(tp_place + step, tp_count) * own_rows
        return jnp.concatenate(
            [lax.dynamic_slice_in_dim(part, first, own_rows) for part in (chip_a, chip_b)], axis=1
        )

    last = [
        swap(rows_for(s).astype(jnp.bfloat16), "tp", s) for s in range(1, tp_count)
    ]
    unit_grad_rows = rows_for(0) + widen(last)
    norm_gain, value_weight, unit_grad_rows = lax.optimization_barrier(
        (norm_gain, value_weight, unit_grad_rows)
    )
    weight_grad = norm_gain.astype(jnp.float32)[:, None] * unit_grad_rows
    gain_grad = jnp.sum(value_weight.astype(jnp.float32) * unit_grad_rows, axis=1)

    own_weight, _ = lax.optimization_barrier((own_weight, (sent_a, sent_b)))
    other_weight = swap(own_weight, "core", 1)
    core_arg = core.astype(jnp.int32).reshape(1)
    value_proj, coefficient = value_product(core_arg, residual, own_weight, other_weight, cot, inv_rms)
    resid_grad = residual_grad(core_arg, cot, coefficient, residual, own_weight, other_weight)
    return (value_proj, resid_grad, weight_grad, gain_grad)


def solution(mesh):
    rep_count, tp_count = mesh.shape["rep"], mesh.shape["tp"]
    split = jax.sharding.Mesh(
        mesh.devices.reshape(OUTER, rep_count // (OUTER * CORES), CORES, tp_count),
        ("outer", "inner", "core", "tp"),
    )
    rep = ("outer", "inner", "core")
    rows = rep + ("tp",)
    return jax.shard_map(
        per_device,
        mesh=split,
        in_specs=(
            P(rows, None),
            P(rows),
            P(rows, None),
            P(rows, None),
            P(rows),
            P("tp", rep),
            P("tp", rep),
            P("tp", rep),
            P(rep),
            P(),
        ),
        out_specs=(P(rows, None), P(rows, None), P(rows, None), P(rows)),
        check_vma=False,
    )
```

```python
import functools

import jax
import jax.numpy as jnp
from jax import lax
from jax.experimental import pallas as pl
from jax.experimental.pallas import tpu as pltpu
from jax.sharding import PartitionSpec as P

VOCAB = 128256
EPS = 1e-05
BETA = 0.5
CORES = 2
OUTER = 2
VMEM_BYTES = 48 * 1024 * 1024
BF16 = jnp.bfloat16
F32 = jnp.float32


def swap(value, axis, step):
    size = lax.axis_size(axis)
    return lax.ppermute(value, axis, [(place, (place + step) % size) for place in range(size)])


def after(value, *earlier):
    return lax.optimization_barrier((value, earlier))[0]


def widen(parts):
    return functools.reduce(jnp.add, [part.astype(F32) for part in parts])


def chunk_order(tp_count):
    order = [0]
    for step in range(1, tp_count // 2 + 1):
        order += [step] if 2 * step == tp_count else [step, tp_count - step]
    return order


def inner_first(order, chunk):
    return order.index(chunk) % 2 == 0


def theirs_kernel(places_ref, cot_ref, first_ref, second_ref, out_ref):
    for slot, resid_ref in enumerate((first_ref, second_ref)):
        product = lax.dot_general(
            resid_ref[...], cot_ref[...], (((0,), (0,)), ((), ())), preferred_element_type=F32
        )
        out_ref[slot, 0] = product.astype(BF16)


def ours_kernel(places_ref, cot_ref, first_ref, second_ref, other_ref, *outs):
    step = pl.program_id(0)
    at_outer, at_inner = step // 2, lax.rem(step, 2)
    for slot, resid_ref in enumerate((first_ref, second_ref)):
        send_ref, keep_ref = outs[2 * slot : 2 * slot + 2]
        product = lax.dot_general(
            resid_ref[...], cot_ref[...], (((0,), (0,)), ((), ())), preferred_element_type=F32
        )
        total = (product + other_ref[slot, 0].astype(F32)).astype(BF16)
        way, place = (at_inner, at_outer) if slot == 0 else (at_outer, at_inner)

        @pl.when(way == 1)
        def _():
            send_ref[place] = total

        @pl.when(way == 0)
        def _():
            keep_ref[place] = total


def pair_product(residual, cot, places, rows, other):
    tokens, features = cot.shape
    steps = places.shape[0] // 2
    whole = lambda i, p: (0, 0)
    in_specs = [
        pl.BlockSpec((tokens, features), whole),
        pl.BlockSpec((tokens, rows), lambda i, p: (0, p[i])),
        pl.BlockSpec((tokens, rows), lambda i, p: (0, p[steps + i])),
    ]
    operands = [cot, residual, residual]
    block = pl.BlockSpec((2, 1, rows, features), lambda i, p: (0, i, 0, 0))
    if other is None:
        kernel, out_specs = theirs_kernel, block
        out_shape = jax.ShapeDtypeStruct((2, steps, rows, features), BF16)
    else:
        kernel = ours_kernel
        in_specs.append(block)
        operands.append(other)
        out_specs = [pl.BlockSpec((2, rows, features), lambda i, p: (0, 0, 0))] * 4
        out_shape = [jax.ShapeDtypeStruct((2, rows, features), BF16)] * 4
    return pl.pallas_call(
        kernel,
        out_shape=out_shape,
        grid_spec=pltpu.PrefetchScalarGridSpec(
            num_scalar_prefetch=1, grid=(steps,), in_specs=in_specs, out_specs=out_specs
        ),
        cost_estimate=pl.CostEstimate(
            flops=4 * tokens * steps * rows * features,
            bytes_accessed=4 * steps * rows * (tokens + 2 * features),
            transcendentals=0,
        ),
        compiler_params=pltpu.CompilerParams(vmem_limit_bytes=VMEM_BYTES),
    )(places, *operands)


def place_weight(step, inner_flags, offsets_ref, pieces, weight_ref):
    at_outer, at_inner = lax.rem(step // 2, 2), lax.rem(step, 2)
    rows = pieces[0].shape[1]
    chunks = len(inner_flags)
    for core in range(CORES):
        for chunk, flag in enumerate(inner_flags):
            way = at_outer if flag else at_inner
            where = pl.ds(pl.multiple_of(offsets_ref[chunk], rows), rows)
            for late in range(2):
                piece = pieces[(core * chunks + chunk) * 2 + late]

                @pl.when(jnp.logical_and(step // 4 == core, way == late))
                def _():
                    weight_ref[where, :] = piece[0]


def piece_specs(inner_flags, rows, features):
    specs = []
    for core in range(CORES):
        for flag in inner_flags:
            for late in range(2):
                if flag:
                    index = lambda i, *_, first=4 * core + 2 * late: (jnp.clip(i - first, 0, 1), 0, 0)
                else:
                    index = lambda i, *_, first=4 * core: (jnp.clip(i - first, 0, 3) // 2, 0, 0)
                specs.append(pl.BlockSpec((1, rows, features), index))
    return specs


def value_kernel(inner_flags, places_ref, offsets_ref, resid_ref, cot_ref, inv_ref, *rest):
    pieces, (value_ref, coef_ref, weight_ref, total_ref) = rest[:-4], rest[-4:]
    step = pl.program_id(0)
    count = pl.num_programs(0)
    place_weight(step, inner_flags, offsets_ref, pieces, weight_ref)

    @pl.when(step == 0)
    def _():
        total_ref[...] = jnp.zeros_like(total_ref)

    total_ref[...] += jnp.dot(resid_ref[...], weight_ref[...], preferred_element_type=F32)

    @pl.when(step == count - 1)
    def _():
        total = total_ref[...]
        inv = inv_ref[...]
        value_ref[...] = (total * inv).astype(BF16)
        share = jnp.sum(total * cot_ref[...].astype(F32), axis=1, keepdims=True)
        width = resid_ref.shape[1] * count
        coef_ref[...] = share * (inv * inv) * (1.0 / width)


def grad_kernel(inner_flags, places_ref, offsets_ref, resid_ref, cot_ref, coef_ref, *rest):
    pieces, (out_ref, weight_ref) = rest[:-2], rest[-2:]
    place_weight(pl.program_id(0), inner_flags, offsets_ref, pieces, weight_ref)
    grad = lax.dot_general(
        cot_ref[...], weight_ref[...], (((1,), (1,)), ((), ())), preferred_element_type=F32
    )
    out_ref[...] = (grad - resid_ref[...].astype(F32) * coef_ref[...]).astype(BF16)


def weight_call(kernel, inner_flags, places, offsets, residual, cot, column, pieces, whole_out):
    tokens, width = residual.shape
    rows, features = pieces[0].shape[1:]
    steps = places.shape[0]
    depth = width // steps
    whole = lambda i, *_: (0, 0)
    block = pl.BlockSpec((tokens, depth), lambda i, p, o: (0, p[i]))
    scratch = [pltpu.VMEM((depth, features), BF16)]
    if whole_out:
        out_shape = [
            jax.ShapeDtypeStruct((tokens, features), BF16),
            jax.ShapeDtypeStruct((tokens, 1), F32),
        ]
        out_specs = [pl.BlockSpec((tokens, features), whole), pl.BlockSpec((tokens, 1), whole)]
        scratch.append(pltpu.VMEM((tokens, features), F32))
    else:
        out_shape, out_specs = jax.ShapeDtypeStruct((tokens, width), BF16), block
    return pl.pallas_call(
        functools.partial(kernel, inner_flags),
        out_shape=out_shape,
        grid_spec=pltpu.PrefetchScalarGridSpec(
            num_scalar_prefetch=2,
            grid=(steps,),
            in_specs=[block, pl.BlockSpec((tokens, features), whole), pl.BlockSpec((tokens, 1), whole)]
            + piece_specs(inner_flags, rows, features),
            out_specs=out_specs,
            scratch_shapes=scratch,
        ),
        cost_estimate=pl.CostEstimate(
            flops=2 * tokens * width * features,
            bytes_accessed=2 * width * (2 * tokens + features),
            transcendentals=0,
        ),
        compiler_params=pltpu.CompilerParams(vmem_limit_bytes=VMEM_BYTES),
    )(places, offsets, residual, cot, column, *pieces)


def sequence_weight(trainee_logp, shard_max, shard_sum, owned, seq_length, rep_count, tp_count, tp_place):
    rows_here = trainee_logp.shape[0]
    seq = shard_max.shape[0]
    packed = jnp.concatenate([shard_max, shard_sum, owned, trainee_logp]).reshape(-1, 128)
    shares = [packed] + [swap(packed, "tp", s) for s in range(1, tp_count)]
    shares = [share.reshape(-1) for share in shares]
    top_max = functools.reduce(jnp.maximum, [share[:seq] for share in shares])
    sum_exp = sum(share[seq : 2 * seq] * jnp.exp(share[:seq] - top_max) for share in shares)
    picked = sum(share[2 * seq : 3 * seq] for share in shares)
    ref_logp = picked - top_max - jnp.log(sum_exp)
    total = jnp.zeros((), F32)
    for s, share in enumerate(shares):
        first = lax.rem(tp_place - s + tp_count, tp_count) * rows_here
        live = first + jnp.arange(rows_here, dtype=jnp.int32) < seq_length
        diff = share[3 * seq :] - lax.dynamic_slice_in_dim(ref_logp, first, rows_here)
        total = total + jnp.sum(jnp.where(live, diff, 0.0))
    seq_delta = total / seq_length.astype(F32)
    return 2.0 * jax.nn.sigmoid(BETA * seq_delta) / rep_count


def per_device(
    residual,
    norm_gain,
    value_weight,
    value_cot,
    trainee_logp,
    ref_shard_max,
    ref_shard_sum,
    ref_target_logit,
    target_ids,
    lengths,
):
    rows_here, width = residual.shape
    features = value_cot.shape[1]
    tp_count = lax.axis_size("tp")
    outer, inner = lax.axis_size("outer"), lax.axis_size("inner")
    rep_count = outer * inner * CORES
    tp_place = lax.axis_index("tp")
    core = lax.axis_index("core")
    at_inner = lax.axis_index("inner")
    at_outer = lax.axis_index("outer")
    rep_place = (at_outer * inner + at_inner) * CORES + core
    depth = width // rep_count
    rows = depth // tp_count
    order = chunk_order(tp_count)
    in_place = rows % 128 == 0 and outer == 2 and inner == 2

    gained = (value_weight.astype(F32) * norm_gain.astype(F32)[:, None]).astype(BF16)
    residual, gained = lax.optimization_barrier((residual, gained))
    arrived = [gained]
    for k in order[1:]:
        arrived.append(swap(gained if k == order[1] else after(gained, arrived[-1]), "tp", k))
    own_pieces, nears = [], []
    for k, block in zip(order, arrived):
        first, second = ("inner", "outer") if inner_first(order, k) else ("outer", "inner")
        nears.append([swap(block, first, s) for s in range(1, lax.axis_size(first))])
        near = jnp.stack([block] + nears[-1])
        far = [swap(near, second, s) for s in range(1, lax.axis_size(second))]
        own_pieces.append([near] + far)
    other_pieces = [[swap(piece, "core", 1) for piece in pieces] for pieces in own_pieces]

    owned = jnp.where(
        target_ids // (VOCAB // tp_count) == tp_place,
        ref_target_logit[0],
        jnp.zeros_like(ref_target_logit[0]),
    )
    seq_length = lax.dynamic_index_in_dim(lengths, rep_place, keepdims=False)
    seq_weight = sequence_weight(
        trainee_logp, ref_shard_max[0], ref_shard_sum[0], owned, seq_length, rep_count, tp_count, tp_place
    )
    positions = tp_place * rows_here + jnp.arange(rows_here, dtype=jnp.int32)
    row_scale = (positions < seq_length).astype(F32) * seq_weight
    resid_wide = residual.astype(F32)
    inv_rms = lax.rsqrt(jnp.mean(resid_wide * resid_wide, axis=1, keepdims=True) + EPS)
    cot = (inv_rms * row_scale[:, None] * value_cot.astype(F32)).astype(BF16)
    cot = after(cot, arrived[1], nears[0])

    def place_of(o, i, c, k):
        chip = lax.rem(at_outer + o, outer) * inner + lax.rem(at_inner + i, inner)
        return (chip * CORES + c) * tp_count + lax.rem(tp_place + k, tp_count)

    chips = [(o, i) for o in range(outer) for i in range(inner)]
    if not in_place:
        product = lax.dot_general(residual, cot, (((0,), (0,)), ((), ())), preferred_element_type=F32)
        product = product.astype(BF16).reshape(-1, rows, features)

    def places_of(pair, c):
        return jnp.stack([place_of(o, i, c, k) for k in pair for o, i in chips]).astype(jnp.int32)

    def for_other(pair, cot):
        places = places_of(pair, 1 - core)
        if in_place:
            return pair_product(residual, cot, places, rows, None)
        return product[places].reshape(2, len(chips), rows, features)

    def for_us(pair, other):
        places = places_of(pair, core)
        if in_place:
            send_a, keep_a, send_b, keep_b = pair_product(residual, cot, places, rows, other)
            return ([send_a], keep_a), ([send_b], keep_b)
        total = widen([product[places], other.reshape(-1, rows, features)]).astype(BF16)
        total = total.reshape(2, outer, inner, rows, features)
        first = ([total[0, :, s] for s in range(1, inner)], total[0, :, 0])
        second = ([total[1, s] for s in range(1, outer)], total[1, 0])
        return first, second

    backward = order[::-1]
    pairs = [backward[i : i + 2] for i in range(0, tp_count, 2)]
    theirs = []
    for n, pair in enumerate(pairs):
        theirs.append(for_other(pair, after(cot, theirs, arrived[2], nears[1]) if n else cot))
    others = [swap(part, "core", 1) for part in theirs]
    others[0] = after(others[0], theirs, nears[2])
    chunk_sums = {}
    sent = []
    for pair, other in zip(pairs, others):
        if sent:
            other = after(other, sent, arrived[3])
        for k, axes, (sends, keep) in zip(
            pair, (("inner", "outer"), ("outer", "inner")), for_us(pair, other)
        ):
            sent += sends
            got = [swap(send, axes[0], s + 1) for s, send in enumerate(sends)]
            later = [
                swap(widen([part[s] for part in [keep] + got]).astype(BF16), axes[1], s)
                for s in range(1, lax.axis_size(axes[1]))
            ]
            chunk_sums[k] = widen([part[0] for part in [keep] + got] + later)
    last = [swap(chunk_sums[k].astype(BF16), "tp", k) for k in backward[:-1]]
    grad_rows = widen([chunk_sums[0]] + last)
    late_gain, late_weight, grad_rows = lax.optimization_barrier((norm_gain, value_weight, grad_rows))
    weight_grad = late_gain.astype(F32)[:, None] * grad_rows
    gain_grad = jnp.sum(late_weight.astype(F32) * grad_rows, axis=1)

    if in_place:
        pieces = [piece for side in (own_pieces, other_pieces) for both in side for piece in both]
        flags = tuple(inner_first(order, k) for k in order)
        places = jnp.stack([place_of(o, i, c, 0) // tp_count for c in (core, 1 - core) for o, i in chips])
        offsets = jnp.stack([lax.rem(tp_place - k + tp_count, tp_count) * rows for k in order])
        places, offsets = places.astype(jnp.int32), offsets.astype(jnp.int32)
        value_proj, coefficient = weight_call(
            value_kernel, flags, places, offsets, residual, cot, after(inv_rms, sent), pieces, True
        )
        resid_grad = weight_call(
            grad_kernel, flags, places, offsets, residual, cot, coefficient, pieces, False
        )
    else:
        weight = []
        for side in (own_pieces, other_pieces):
            for k, pieces in zip(order, side):
                both = jnp.stack(pieces)
                weight.append(both if inner_first(order, k) else jnp.swapaxes(both, 0, 1))
        weight = jnp.stack(weight).reshape(CORES, tp_count, outer, inner, rows, features)
        by_place = [order.index(k) for k in range(tp_count)]
        weight = weight[:, jnp.array(by_place)]
        weight = weight[jnp.array([core, 1 - core])]
        weight = weight[:, (tp_place - jnp.arange(tp_count)) % tp_count]
        weight = weight[:, :, (at_outer - jnp.arange(outer)) % outer]
        weight = weight[:, :, :, (at_inner - jnp.arange(inner)) % inner]
        weight = weight.transpose(2, 3, 0, 1, 4, 5).reshape(width, features)
        value_acc = jnp.dot(residual, weight, preferred_element_type=F32)
        value_proj = (inv_rms * value_acc).astype(BF16)
        share = jnp.sum(cot.astype(F32) * value_acc, axis=1, keepdims=True)
        coefficient = inv_rms * inv_rms * share * (1.0 / width)
        normed_grad = lax.dot_general(
            cot, weight, (((1,), (1,)), ((), ())), preferred_element_type=F32
        )
        resid_grad = (normed_grad - residual.astype(F32) * coefficient).astype(BF16)
    return (value_proj, resid_grad, weight_grad, gain_grad)


def solution(mesh):
    rep_count, tp_count = mesh.shape["rep"], mesh.shape["tp"]
    split = jax.sharding.Mesh(
        mesh.devices.reshape(OUTER, rep_count // (OUTER * CORES), CORES, tp_count),
        ("outer", "inner", "core", "tp"),
    )
    rep = ("outer", "inner", "core")
    rows = rep + ("tp",)
    return jax.shard_map(
        per_device,
        mesh=split,
        in_specs=(
            P(rows, None),
            P(rows),
            P(rows, None),
            P(rows, None),
            P(rows),
            P("tp", rep),
            P("tp", rep),
            P("tp", rep),
            P(rep),
            P(),
        ),
        out_specs=(P(rows, None), P(rows, None), P(rows, None), P(rows)),
        check_vma=False,
    )
```

```python
import functools

import jax
import jax.numpy as jnp
from jax import lax
from jax.experimental import pallas as pl
from jax.experimental.pallas import tpu as pltpu
from jax.sharding import PartitionSpec as P

VOCAB = 128256
EPS = 1e-05
BETA = 0.5
CORES = 2
OUTER = 2
PAIR_VMEM = 14 * 1024 * 1024
WEIGHT_VMEM = 22 * 1024 * 1024
NOMINAL = pl.CostEstimate(flops=1024, bytes_accessed=1024, transcendentals=0)
BF16 = jnp.bfloat16
F32 = jnp.float32


def swap(value, axis, step):
    size = lax.axis_size(axis)
    return lax.ppermute(value, axis, [(place, (place + step) % size) for place in range(size)])


def after(value, *earlier):
    return lax.optimization_barrier((value, earlier))[0]


def widen(parts):
    return functools.reduce(jnp.add, [part.astype(F32) for part in parts])


def chunk_order(tp_count):
    order = [0]
    for step in range(1, tp_count // 2 + 1):
        order += [step] if 2 * step == tp_count else [step, tp_count - step]
    return order


def inner_first(order, chunk):
    return order.index(chunk) % 2 == 0


def theirs_kernel(places_ref, cot_ref, first_ref, second_ref, out_ref):
    for slot, resid_ref in enumerate((first_ref, second_ref)):
        product = jnp.dot(cot_ref[...], resid_ref[...], preferred_element_type=F32)
        out_ref[slot, 0] = product.astype(BF16)


def ours_kernel(places_ref, cot_ref, first_ref, second_ref, other_ref, *outs):
    step = pl.program_id(0)
    at_outer, at_inner = step // 2, lax.rem(step, 2)
    for slot, resid_ref in enumerate((first_ref, second_ref)):
        send_ref, keep_ref = outs[2 * slot : 2 * slot + 2]
        product = jnp.dot(cot_ref[...], resid_ref[...], preferred_element_type=F32)
        total = (product + other_ref[slot, 0].astype(F32)).astype(BF16)
        way, place = (at_inner, at_outer) if slot == 0 else (at_outer, at_inner)

        @pl.when(way == 1)
        def _():
            send_ref[place] = total

        @pl.when(way == 0)
        def _():
            keep_ref[place] = total


def pair_product(residual, cot_t, places, rows, other):
    features, tokens = cot_t.shape
    steps = places.shape[0] // 2
    in_specs = [
        pl.BlockSpec((features, tokens), lambda i, p: (0, 0)),
        pl.BlockSpec((tokens, rows), lambda i, p: (0, p[i])),
        pl.BlockSpec((tokens, rows), lambda i, p: (0, p[steps + i])),
    ]
    operands = [cot_t, residual, residual]
    block = pl.BlockSpec((2, 1, features, rows), lambda i, p: (0, i, 0, 0))
    if other is None:
        kernel, out_specs = theirs_kernel, block
        out_shape = jax.ShapeDtypeStruct((2, steps, features, rows), BF16)
    else:
        kernel = ours_kernel
        in_specs.append(block)
        operands.append(other)
        out_specs = [pl.BlockSpec((2, features, rows), lambda i, p: (0, 0, 0))] * 4
        out_shape = [jax.ShapeDtypeStruct((2, features, rows), BF16)] * 4
    return pl.pallas_call(
        kernel,
        out_shape=out_shape,
        grid_spec=pltpu.PrefetchScalarGridSpec(
            num_scalar_prefetch=1, grid=(steps,), in_specs=in_specs, out_specs=out_specs
        ),
        cost_estimate=NOMINAL,
        compiler_params=pltpu.CompilerParams(vmem_limit_bytes=PAIR_VMEM),
    )(places, *operands)


def place_weight(inner_flags, offsets_ref, pieces, weight_ref):
    step = pl.program_id(0)
    at_outer, at_inner = step // 2, lax.rem(step, 2)
    rows = pieces[0].shape[1]
    for chunk, flag in enumerate(inner_flags):
        way = at_outer if flag else at_inner
        where = pl.ds(pl.multiple_of(offsets_ref[chunk], rows), rows)
        for late in range(2):
            piece = pieces[chunk * 2 + late]

            @pl.when(way == late)
            def _():
                weight_ref[where, :] = piece[0]


def piece_specs(inner_flags, rows, features):
    specs = []
    for flag in inner_flags:
        for late in range(2):
            if flag:
                index = lambda i, *_, first=2 * late: (jnp.clip(i - first, 0, 1), 0, 0)
            else:
                index = lambda i, *_: (i // 2, 0, 0)
            specs.append(pl.BlockSpec((1, rows, features), index))
    return specs


def value_kernel(inner_flags, places_ref, offsets_ref, resid_ref, *rest):
    pieces, (total_ref, weight_ref) = rest[:-2], rest[-2:]
    place_weight(inner_flags, offsets_ref, pieces, weight_ref)
    product = jnp.dot(resid_ref[...], weight_ref[...], preferred_element_type=F32)

    @pl.when(pl.program_id(0) == 0)
    def _():
        total_ref[...] = product

    @pl.when(pl.program_id(0) > 0)
    def _():
        total_ref[...] += product


def value_end_kernel(
    width, inner_flags, places_ref, offsets_ref, resid_ref, first_ref, cot_ref, inv_ref, *rest
):
    pieces, (value_ref, coef_ref, weight_ref, total_ref) = rest[:-4], rest[-4:]
    step = pl.program_id(0)
    place_weight(inner_flags, offsets_ref, pieces, weight_ref)
    product = jnp.dot(resid_ref[...], weight_ref[...], preferred_element_type=F32)

    @pl.when(step == 0)
    def _():
        total_ref[...] = first_ref[...] + product

    @pl.when(step > 0)
    def _():
        total_ref[...] += product

    @pl.when(step == pl.num_programs(0) - 1)
    def _():
        total = total_ref[...]
        inv = inv_ref[...]
        value_ref[...] = (total * inv).astype(BF16)
        share = jnp.sum(total * cot_ref[...].astype(F32), axis=1, keepdims=True)
        coef_ref[...] = share * (inv * inv) * (1.0 / width)


def grad_kernel(inner_flags, places_ref, offsets_ref, resid_ref, cot_ref, coef_ref, *rest):
    pieces, (out_ref, weight_ref) = rest[: 2 * len(inner_flags)], rest[-2:]
    place_weight(inner_flags, offsets_ref, pieces, weight_ref)
    grad = lax.dot_general(
        cot_ref[...], weight_ref[...], (((1,), (1,)), ((), ())), preferred_element_type=F32
    )
    out_ref[...] = (grad - resid_ref[...].astype(F32) * coef_ref[...]).astype(BF16)


def weight_call(kernel, inner_flags, places, offsets, residual, wholes, pieces, out_shape, out_blocks, earlier=None):
    tokens, width = residual.shape
    rows, features = pieces[0].shape[1:]
    steps = places.shape[0]
    depth = width // (CORES * steps)
    block = pl.BlockSpec((tokens, depth), lambda i, p, o: (0, p[i]))

    def whole(array):
        return pl.BlockSpec(array.shape, lambda i, *_: (0, 0))

    scratch = [pltpu.VMEM((depth, features), BF16)]
    if out_blocks:
        out_specs = block
    else:
        out_specs = jax.tree.map(whole, out_shape)
        if isinstance(out_shape, list):
            scratch.append(pltpu.VMEM((tokens, features), F32))
    in_specs = [block] + [whole(array) for array in wholes] + piece_specs(inner_flags, rows, features)
    operands = [places, offsets, residual, *wholes, *pieces]
    aliases = {}
    if earlier is not None:
        aliases = {len(operands): 0}
        in_specs.append(pl.BlockSpec(memory_space=pl.ANY))
        operands.append(earlier)
    return pl.pallas_call(
        functools.partial(kernel, inner_flags),
        out_shape=out_shape,
        grid_spec=pltpu.PrefetchScalarGridSpec(
            num_scalar_prefetch=2,
            grid=(steps,),
            in_specs=in_specs,
            out_specs=out_specs,
            scratch_shapes=scratch,
        ),
        input_output_aliases=aliases,
        cost_estimate=NOMINAL,
        compiler_params=pltpu.CompilerParams(vmem_limit_bytes=WEIGHT_VMEM),
    )(*operands)


def sequence_weight(trainee_logp, shard_max, shard_sum, owned, seq_length, rep_count, tp_count, tp_place):
    rows_here = trainee_logp.shape[0]
    seq = shard_max.shape[0]
    packed = jnp.concatenate([shard_max, shard_sum, owned, trainee_logp]).reshape(-1, 128)
    shares = [packed] + [swap(packed, "tp", s) for s in range(1, tp_count)]
    shares = [share.reshape(-1) for share in shares]
    top_max = functools.reduce(jnp.maximum, [share[:seq] for share in shares])
    sum_exp = sum(share[seq : 2 * seq] * jnp.exp(share[:seq] - top_max) for share in shares)
    picked = sum(share[2 * seq : 3 * seq] for share in shares)
    ref_logp = picked - top_max - jnp.log(sum_exp)
    total = jnp.zeros((), F32)
    for s, share in enumerate(shares):
        first = lax.rem(tp_place - s + tp_count, tp_count) * rows_here
        live = first + jnp.arange(rows_here, dtype=jnp.int32) < seq_length
        diff = share[3 * seq :] - lax.dynamic_slice_in_dim(ref_logp, first, rows_here)
        total = total + jnp.sum(jnp.where(live, diff, 0.0))
    seq_delta = total / seq_length.astype(F32)
    return 2.0 * jax.nn.sigmoid(BETA * seq_delta) / rep_count


def per_device(
    residual,
    norm_gain,
    value_weight,
    value_cot,
    trainee_logp,
    ref_shard_max,
    ref_shard_sum,
    ref_target_logit,
    target_ids,
    lengths,
):
    rows_here, width = residual.shape
    features = value_cot.shape[1]
    tp_count = lax.axis_size("tp")
    outer, inner = lax.axis_size("outer"), lax.axis_size("inner")
    rep_count = outer * inner * CORES
    tp_place = lax.axis_index("tp")
    core = lax.axis_index("core")
    at_inner = lax.axis_index("inner")
    at_outer = lax.axis_index("outer")
    rep_place = (at_outer * inner + at_inner) * CORES + core
    depth = width // rep_count
    rows = depth // tp_count
    order = chunk_order(tp_count)
    in_place = rows % 128 == 0 and outer == 2 and inner == 2

    gained = (value_weight.astype(F32) * norm_gain.astype(F32)[:, None]).astype(BF16)
    residual, gained = lax.optimization_barrier((residual, gained))
    resid_wide = residual.astype(F32)
    squares = jnp.sum(resid_wide * resid_wide, axis=1, keepdims=True)

    owned = jnp.where(
        target_ids // (VOCAB // tp_count) == tp_place,
        ref_target_logit[0],
        jnp.zeros_like(ref_target_logit[0]),
    )
    owned = after(owned, squares)
    seq_length = lax.dynamic_index_in_dim(lengths, rep_place, keepdims=False)
    seq_weight = sequence_weight(
        trainee_logp, ref_shard_max[0], ref_shard_sum[0], owned, seq_length, rep_count, tp_count, tp_place
    )
    positions = tp_place * rows_here + jnp.arange(rows_here, dtype=jnp.int32)
    row_scale = (positions < seq_length).astype(F32) * seq_weight
    inv_rms = lax.rsqrt(squares * (1.0 / width) + EPS)
    cot = (inv_rms * row_scale[:, None] * value_cot.astype(F32)).astype(BF16)
    cot_t = cot.T

    def near_of(k, block):
        first = "inner" if inner_first(order, k) else "outer"
        return [swap(block, first, s) for s in range(1, lax.axis_size(first))]

    def far_of(k, block, nears):
        second = "outer" if inner_first(order, k) else "inner"
        near = jnp.stack([block] + nears)
        return [near] + [swap(near, second, s) for s in range(1, lax.axis_size(second))]

    def place_of(o, i, c, k):
        chip = lax.rem(at_outer + o, outer) * inner + lax.rem(at_inner + i, inner)
        return (chip * CORES + c) * tp_count + lax.rem(tp_place + k, tp_count)

    chips = [(o, i) for o in range(outer) for i in range(inner)]
    if not in_place:
        product = jnp.dot(cot_t, residual, preferred_element_type=F32).astype(BF16)
        product = product.reshape(features, -1, rows).transpose(1, 0, 2)

    def places_of(pair, c):
        return jnp.stack([place_of(o, i, c, k) for k in pair for o, i in chips]).astype(jnp.int32)

    def for_other(pair, cot_t):
        places = places_of(pair, 1 - core)
        if in_place:
            return pair_product(residual, cot_t, places, rows, None)
        return after(product, cot_t)[places].reshape(2, len(chips), features, rows)

    def for_us(pair, other):
        places = places_of(pair, core)
        if in_place:
            send_a, keep_a, send_b, keep_b = pair_product(residual, cot_t, places, rows, other)
            return ([send_a], keep_a), ([send_b], keep_b)
        total = widen([product[places], other.reshape(-1, features, rows)]).astype(BF16)
        total = total.reshape(2, outer, inner, features, rows)
        first = ([total[0, :, s] for s in range(1, inner)], total[0, :, 0])
        second = ([total[1, s] for s in range(1, outer)], total[1, 0])
        return first, second

    def first_round(sides):
        return [
            [swap(send, axis, s + 1) for s, send in enumerate(sends)]
            for axis, (sends, _) in zip(("inner", "outer"), sides)
        ]

    def second_round(sides, got):
        later = []
        for axis, (_, keep), parts in zip(("outer", "inner"), sides, got):
            later.append(
                [
                    swap(widen([part[s] for part in [keep] + parts]).astype(BF16), axis, s)
                    for s in range(1, lax.axis_size(axis))
                ]
            )
        return later

    def summed(sides, got, later):
        return [
            widen([part[0] for part in [keep] + parts] + last)
            for (_, keep), parts, last in zip(sides, got, later)
        ]

    backward = order[::-1]
    pairs = [backward[i : i + 2] for i in range(0, tp_count, 2)]
    own_pieces = {}
    arrived = {0: gained, order[1]: swap(gained, "tp", order[1])}
    near = {0: near_of(0, gained)}
    (arrived[order[1]], near[0], squares_done) = lax.optimization_barrier(
        (arrived[order[1]], near[0], squares)
    )
    near[order[1]] = near_of(order[1], arrived[order[1]])
    own_pieces[0] = far_of(0, gained, near[0])
    arrived[order[2]] = swap(after(gained, squares_done), "tp", order[2])
    near[order[1]], arrived[order[2]], cot_t = lax.optimization_barrier(
        (near[order[1]], arrived[order[2]], cot_t)
    )
    own_pieces[order[1]] = far_of(order[1], arrived[order[1]], near[order[1]])
    near[order[2]] = near_of(order[2], arrived[order[2]])
    for k in order[3:]:
        arrived[k] = swap(after(gained, arrived[order[2]]), "tp", k)
    theirs = [for_other(pairs[0], cot_t)]
    theirs.append(for_other(pairs[1], after(cot_t, theirs[0])))
    near[order[2]], arrived[order[3]], theirs, own_pieces[0] = lax.optimization_barrier(
        (near[order[2]], arrived[order[3]], theirs, own_pieces[0])
    )
    own_pieces[order[2]] = far_of(order[2], arrived[order[2]], near[order[2]])
    near[order[3]] = near_of(order[3], arrived[order[3]])
    others = [swap(part, "core", 1) for part in theirs]
    sides = [for_us(pairs[0], others[0])]
    got = [first_round(sides[0])]
    near[order[3]], side_done, own_pieces[order[1]] = lax.optimization_barrier(
        (near[order[3]], sides[0], own_pieces[order[1]])
    )
    own_pieces[order[3]] = far_of(order[3], arrived[order[3]], near[order[3]])
    sides.append(for_us(pairs[1], after(others[1], side_done)))
    for n in range(2, len(pairs)):
        for k in order[2 * n : 2 * n + 2]:
            own_pieces[k] = far_of(k, arrived[k], near_of(k, arrived[k]))
        others.append(swap(for_other(pairs[n], after(cot_t, sides[-1])), "core", 1))
        sides.append(for_us(pairs[n], others[-1]))
    got[0], side_done = lax.optimization_barrier((got[0], sides[1:]))
    later = [second_round(sides[0], got[0])]
    sides[1:] = after(sides[1:], got[0])
    got += [first_round(side) for side in sides[1:]]
    other_pieces = {
        k: [swap(piece, "core", 1) for piece in pieces] for k, pieces in own_pieces.items()
    }
    value_inv, own_pieces = lax.optimization_barrier((inv_rms, own_pieces))

    if in_place:
        pieces = [
            [piece for k in order for piece in side[k]] for side in (own_pieces, other_pieces)
        ]
        flags = tuple(inner_first(order, k) for k in order)
        places = [
            jnp.stack([place_of(o, i, c, 0) // tp_count for o, i in chips]).astype(jnp.int32)
            for c in (core, 1 - core)
        ]
        offsets = jnp.stack([lax.rem(tp_place - k + tp_count, tp_count) * rows for k in order])
        offsets = offsets.astype(jnp.int32)
        wide = jax.ShapeDtypeStruct((rows_here, features), F32)
        first_total = weight_call(
            value_kernel, flags, places[0], offsets, after(residual, value_inv), [], pieces[0], wide, False
        )
        value_proj, coefficient = weight_call(
            functools.partial(value_end_kernel, width),
            flags,
            places[1],
            offsets,
            residual,
            [first_total, cot, inv_rms],
            pieces[1],
            [
                jax.ShapeDtypeStruct((rows_here, features), BF16),
                jax.ShapeDtypeStruct((rows_here, 1), F32),
            ],
            False,
        )
        later[0], got[1], coefficient = lax.optimization_barrier((later[0], got[1], coefficient))
        later += [second_round(side, parts) for side, parts in zip(sides[1:], got[1:])]
        sums = dict(zip(pairs[0], summed(sides[0], got[0], later[0])))
        last = [swap(sums[k].astype(BF16), "tp", k) for k in pairs[0]]
        grad_shape = jax.ShapeDtypeStruct((rows_here, width), BF16)
        resid_grad = weight_call(
            grad_kernel, flags, places[0], offsets, residual, [cot, coefficient], pieces[0], grad_shape, True
        )
        later[1], coefficient, resid_grad = lax.optimization_barrier((later[1], coefficient, resid_grad))
        sums.update(zip(pairs[1], summed(sides[1], got[1], later[1])))
        last.append(swap(sums[pairs[1][0]].astype(BF16), "tp", pairs[1][0]))
        resid_grad = weight_call(
            grad_kernel,
            flags,
            places[1],
            offsets,
            residual,
            [cot, coefficient],
            pieces[1],
            grad_shape,
            True,
            resid_grad,
        )
    else:
        weight = []
        for side in (own_pieces, other_pieces):
            for k in order:
                both = jnp.stack(side[k])
                weight.append(both if inner_first(order, k) else jnp.swapaxes(both, 0, 1))
        weight = jnp.stack(weight).reshape(CORES, tp_count, outer, inner, rows, features)
        by_place = [order.index(k) for k in range(tp_count)]
        weight = weight[:, jnp.array(by_place)]
        weight = weight[jnp.array([core, 1 - core])]
        weight = weight[:, (tp_place - jnp.arange(tp_count)) % tp_count]
        weight = weight[:, :, (at_outer - jnp.arange(outer)) % outer]
        weight = weight[:, :, :, (at_inner - jnp.arange(inner)) % inner]
        weight = weight.transpose(2, 3, 0, 1, 4, 5).reshape(width, features)
        value_acc = jnp.dot(residual, weight, preferred_element_type=F32)
        value_proj = (inv_rms * value_acc).astype(BF16)
        share = jnp.sum(cot.astype(F32) * value_acc, axis=1, keepdims=True)
        coefficient = inv_rms * inv_rms * share * (1.0 / width)
        normed_grad = lax.dot_general(
            cot, weight, (((1,), (1,)), ((), ())), preferred_element_type=F32
        )
        resid_grad = (normed_grad - residual.astype(F32) * coefficient).astype(BF16)
        later += [second_round(side, parts) for side, parts in zip(sides[1:], got[1:])]
        sums = {}
        for pair, *rounds in zip(pairs, sides, got, later):
            sums.update(zip(pair, summed(*rounds)))
        last = [swap(sums[k].astype(BF16), "tp", k) for k in backward[:-1]]
    grad_rows = widen([sums[0]] + last)
    late_gain, late_weight, grad_rows = lax.optimization_barrier((norm_gain, value_weight, grad_rows))
    weight_grad = (late_gain.astype(F32)[None, :] * grad_rows).T
    gain_grad = jnp.sum(late_weight.astype(F32).T * grad_rows, axis=0)
    return (value_proj, resid_grad, weight_grad, gain_grad)


def solution(mesh):
    rep_count, tp_count = mesh.shape["rep"], mesh.shape["tp"]
    split = jax.sharding.Mesh(
        mesh.devices.reshape(OUTER, rep_count // (OUTER * CORES), CORES, tp_count),
        ("outer", "inner", "core", "tp"),
    )
    rep = ("outer", "inner", "core")
    rows = rep + ("tp",)
    return jax.shard_map(
        per_device,
        mesh=split,
        in_specs=(
            P(rows, None),
            P(rows),
            P(rows, None),
            P(rows, None),
            P(rows),
            P("tp", rep),
            P("tp", rep),
            P("tp", rep),
            P(rep),
            P(),
        ),
        out_specs=(P(rows, None), P(rows, None), P(rows, None), P(rows)),
        check_vma=False,
    )
```

```python
import functools

import jax
import jax.numpy as jnp
from jax import lax
from jax.experimental import pallas as pl
from jax.experimental.pallas import tpu as pltpu
from jax.sharding import PartitionSpec as P

VOCAB = 128256
EPS = 1e-05
BETA = 0.5
CORES = 2
OUTER = 2
PAIR_VMEM = 14 * 1024 * 1024
WEIGHT_VMEM = 22 * 1024 * 1024
NOMINAL = pl.CostEstimate(flops=1024, bytes_accessed=1024, transcendentals=0)
BF16 = jnp.bfloat16
F32 = jnp.float32


def swap(value, axis, step):
    size = lax.axis_size(axis)
    return lax.ppermute(value, axis, [(place, (place + step) % size) for place in range(size)])


def trade(value, axis, mask):
    size = lax.axis_size(axis)
    return lax.ppermute(value, axis, [(place, place ^ mask) for place in range(size)])


def after(value, *earlier):
    return lax.optimization_barrier((value, earlier))[0]


def widen(parts):
    return functools.reduce(jnp.add, [part.astype(F32) for part in parts])


def inner_first(chunk):
    return chunk % 2 == 0


def fetch(resid_hbm, places_ref, blocks_ref, sems, count):
    width = blocks_ref.shape[2]

    def copy(n):
        where = pl.ds(pl.multiple_of(places_ref[n] * width, width), width)
        return pltpu.make_async_copy(resid_hbm.at[:, where], blocks_ref.at[n], sems.at[n])

    @pl.when(pl.program_id(0) == 0)
    def _():
        for n in range(count):
            copy(n).start()

    return copy


def theirs_kernel(places_ref, cot_ref, resid_hbm, out_ref, blocks_ref, sems):
    step = pl.program_id(0)
    steps = blocks_ref.shape[0] // 2
    copy = fetch(resid_hbm, places_ref, blocks_ref, sems, 2 * steps)
    for slot in range(2):
        copy(2 * step + slot).wait()
        product = jnp.dot(cot_ref[...], blocks_ref[2 * step + slot], preferred_element_type=F32)
        out_ref[slot, 0] = product.astype(BF16)


def ours_kernel(places_ref, cot_ref, resid_hbm, other_ref, *rest):
    outs, (blocks_ref, sems) = rest[:4], rest[4:]
    step = pl.program_id(0)
    at_outer, at_inner = step // 2, lax.rem(step, 2)
    steps = blocks_ref.shape[0] // 2
    copy = fetch(resid_hbm, places_ref, blocks_ref, sems, 2 * steps)
    for slot in range(2):
        copy(2 * step + slot).wait()
        send_ref, keep_ref = outs[2 * slot : 2 * slot + 2]
        product = jnp.dot(cot_ref[...], blocks_ref[2 * step + slot], preferred_element_type=F32)
        total = (product + other_ref[slot, 0].astype(F32)).astype(BF16)
        way, place = (at_inner, at_outer) if slot == 0 else (at_outer, at_inner)

        @pl.when(way == 1)
        def _():
            send_ref[place] = total

        @pl.when(way == 0)
        def _():
            keep_ref[place] = total


def pair_product(residual, cot_t, places, rows, other):
    features, tokens = cot_t.shape
    steps = places.shape[0] // 2
    in_specs = [
        pl.BlockSpec((features, tokens), lambda i, p: (0, 0)),
        pl.BlockSpec(memory_space=pltpu.HBM),
    ]
    operands = [cot_t, residual]
    block = pl.BlockSpec((2, 1, features, rows), lambda i, p: (0, i, 0, 0))
    if other is None:
        kernel, out_specs = theirs_kernel, block
        out_shape = jax.ShapeDtypeStruct((2, steps, features, rows), BF16)
    else:
        kernel = ours_kernel
        in_specs.append(block)
        operands.append(other)
        out_specs = [pl.BlockSpec((2, features, rows), lambda i, p: (0, 0, 0))] * 4
        out_shape = [jax.ShapeDtypeStruct((2, features, rows), BF16)] * 4
    return pl.pallas_call(
        kernel,
        out_shape=out_shape,
        grid_spec=pltpu.PrefetchScalarGridSpec(
            num_scalar_prefetch=1,
            grid=(steps,),
            in_specs=in_specs,
            out_specs=out_specs,
            scratch_shapes=[
                pltpu.VMEM((2 * steps, tokens, rows), BF16),
                pltpu.SemaphoreType.DMA((2 * steps,)),
            ],
        ),
        cost_estimate=NOMINAL,
        compiler_params=pltpu.CompilerParams(vmem_limit_bytes=PAIR_VMEM),
    )(places, *operands)


def place_weight(inner_flags, offsets_ref, pieces, weight_ref):
    step = pl.program_id(0)
    at_outer, at_inner = step // 2, lax.rem(step, 2)
    rows = pieces[0].shape[1]
    for chunk, flag in enumerate(inner_flags):
        way = at_outer if flag else at_inner
        where = pl.ds(pl.multiple_of(offsets_ref[chunk], rows), rows)
        for late in range(2):
            piece = pieces[chunk * 2 + late]

            @pl.when(way == late)
            def _():
                weight_ref[0, where, :] = piece[0]


def piece_specs(inner_flags, rows, features):
    specs = []
    for flag in inner_flags:
        for late in range(2):
            if flag:
                index = lambda i, *_, first=2 * late: (jnp.clip(i - first, 0, 1), 0, 0)
            else:
                index = lambda i, *_: (i // 2, 0, 0)
            specs.append(pl.BlockSpec((1, rows, features), index))
    return specs


def value_kernel(inner_flags, places_ref, offsets_ref, resid_hbm, *rest):
    pieces, (total_ref, weight_ref, blocks_ref, sems) = rest[:-4], rest[-4:]
    step = pl.program_id(0)
    copy = fetch(resid_hbm, places_ref, blocks_ref, sems, blocks_ref.shape[0])
    place_weight(inner_flags, offsets_ref, pieces, weight_ref)
    copy(step).wait()
    product = jnp.dot(blocks_ref[step], weight_ref[0], preferred_element_type=F32)

    @pl.when(step == 0)
    def _():
        total_ref[...] = product

    @pl.when(step > 0)
    def _():
        total_ref[...] += product


def value_end_kernel(
    width, places_ref, resid_hbm, weight_ref, first_ref, cot_ref, inv_ref,
    value_ref, coef_ref, blocks_ref, sems, total_ref,
):
    step = pl.program_id(0)
    copy = fetch(resid_hbm, places_ref, blocks_ref, sems, blocks_ref.shape[0])
    copy(step).wait()
    product = jnp.dot(blocks_ref[step], weight_ref[0], preferred_element_type=F32)

    @pl.when(step == 0)
    def _():
        total_ref[...] = first_ref[...] + product

    @pl.when(step > 0)
    def _():
        total_ref[...] += product

    @pl.when(step == pl.num_programs(0) - 1)
    def _():
        total = total_ref[...]
        inv = inv_ref[...]
        value_ref[...] = (total * inv).astype(BF16)
        share = jnp.sum(total * cot_ref[...].astype(F32), axis=1, keepdims=True)
        coef_ref[...] = share * (inv * inv) * (1.0 / width)


def grad_kernel(places_ref, resid_hbm, weight_ref, cot_ref, coef_ref, *rest):
    out_ref, blocks_ref, sems = rest[-3:]
    step = pl.program_id(0)
    copy = fetch(resid_hbm, places_ref, blocks_ref, sems, blocks_ref.shape[0])
    grad = lax.dot_general(
        cot_ref[...], weight_ref[0], (((1,), (1,)), ((), ())), preferred_element_type=F32
    )
    copy(step).wait()
    out_ref[...] = (grad - blocks_ref[step].astype(F32) * coef_ref[...]).astype(BF16)


def whole_block(array):
    return pl.BlockSpec(array.shape, lambda i, *_: (0, 0))


def weight_scratch(tokens, depth, steps):
    return [pltpu.VMEM((steps, tokens, depth), BF16), pltpu.SemaphoreType.DMA((steps,))]


def first_value(inner_flags, places, offsets, residual, pieces):
    tokens, width = residual.shape
    rows, features = pieces[0].shape[1:]
    steps = places.shape[0]
    depth = width // (CORES * steps)
    total = jax.ShapeDtypeStruct((tokens, features), F32)
    return pl.pallas_call(
        functools.partial(value_kernel, inner_flags),
        out_shape=[total, jax.ShapeDtypeStruct((steps, depth, features), BF16)],
        grid_spec=pltpu.PrefetchScalarGridSpec(
            num_scalar_prefetch=2,
            grid=(steps,),
            in_specs=[pl.BlockSpec(memory_space=pltpu.HBM)] + piece_specs(inner_flags, rows, features),
            out_specs=[
                whole_block(total),
                pl.BlockSpec((1, depth, features), lambda i, p, o: (p[i] // CORES, 0, 0)),
            ],
            scratch_shapes=weight_scratch(tokens, depth, steps),
        ),
        cost_estimate=NOMINAL,
        compiler_params=pltpu.CompilerParams(vmem_limit_bytes=WEIGHT_VMEM),
    )(places, offsets, residual, *pieces)


def weight_call(kernel, places, residual, weight, wholes, out_shape, earlier=None):
    tokens, width = residual.shape
    steps, depth, features = weight.shape
    scratch = weight_scratch(tokens, depth, steps)
    if isinstance(out_shape, list):
        out_specs = [whole_block(array) for array in out_shape]
        scratch.append(pltpu.VMEM((tokens, features), F32))
    else:
        out_specs = pl.BlockSpec((tokens, depth), lambda i, p: (0, p[i]))
    in_specs = [
        pl.BlockSpec(memory_space=pltpu.HBM),
        pl.BlockSpec((1, depth, features), lambda i, p: (p[i] // CORES, 0, 0)),
    ] + [whole_block(array) for array in wholes]
    operands = [places, residual, weight, *wholes]
    aliases = {}
    if earlier is not None:
        aliases = {len(operands): 0}
        in_specs.append(pl.BlockSpec(memory_space=pltpu.HBM))
        operands.append(earlier)
    return pl.pallas_call(
        kernel,
        out_shape=out_shape,
        grid_spec=pltpu.PrefetchScalarGridSpec(
            num_scalar_prefetch=1,
            grid=(steps,),
            in_specs=in_specs,
            out_specs=out_specs,
            scratch_shapes=scratch,
        ),
        input_output_aliases=aliases,
        cost_estimate=NOMINAL,
        compiler_params=pltpu.CompilerParams(vmem_limit_bytes=WEIGHT_VMEM),
    )(*operands)


def sequence_weight(shares, rows_here, seq_length, rep_count, tp_place):
    seq = (shares[0].shape[0] - rows_here) // 3
    top_max = functools.reduce(jnp.maximum, [share[:seq] for share in shares])
    sum_exp = sum(share[seq : 2 * seq] * jnp.exp(share[:seq] - top_max) for share in shares)
    picked = sum(share[2 * seq : 3 * seq] for share in shares)
    ref_logp = picked - top_max - jnp.log(sum_exp)
    total = jnp.zeros((), F32)
    for mask, share in enumerate(shares):
        first = jnp.bitwise_xor(tp_place, mask) * rows_here
        live = first + jnp.arange(rows_here, dtype=jnp.int32) < seq_length
        diff = share[3 * seq :] - lax.dynamic_slice_in_dim(ref_logp, first, rows_here)
        total = total + jnp.sum(jnp.where(live, diff, 0.0))
    seq_delta = total / seq_length.astype(F32)
    return 2.0 * jax.nn.sigmoid(BETA * seq_delta) / rep_count


def per_device(
    residual,
    norm_gain,
    value_weight,
    value_cot,
    trainee_logp,
    ref_shard_max,
    ref_shard_sum,
    ref_target_logit,
    target_ids,
    lengths,
):
    rows_here, width = residual.shape
    features = value_cot.shape[1]
    tp_count = lax.axis_size("tp")
    outer, inner = lax.axis_size("outer"), lax.axis_size("inner")
    rep_count = outer * inner * CORES
    tp_place = lax.axis_index("tp")
    core = lax.axis_index("core")
    at_inner = lax.axis_index("inner")
    at_outer = lax.axis_index("outer")
    rep_place = (at_outer * inner + at_inner) * CORES + core
    depth = width // rep_count
    rows = depth // tp_count
    order = list(range(tp_count))
    in_place = rows % 128 == 0 and outer == 2 and inner == 2

    gained = (value_weight.astype(F32) * norm_gain.astype(F32)[:, None]).astype(BF16)
    residual, gained = lax.optimization_barrier((residual, gained))
    resid_wide = residual.astype(F32)
    squares = jnp.sum(resid_wide * resid_wide, axis=1, keepdims=True)

    def near_of(k, block):
        first = "inner" if inner_first(k) else "outer"
        return [swap(block, first, s) for s in range(1, lax.axis_size(first))]

    def far_of(k, block, nears):
        second = "outer" if inner_first(k) else "inner"
        near = jnp.stack([block] + nears)
        return [near] + [swap(near, second, s) for s in range(1, lax.axis_size(second))]

    own_pieces, arrived, near = {}, {0: gained}, {}
    arrived[1] = trade(gained, "tp", 1)
    near[0] = near_of(0, gained)
    arrived[1], near[0], squares, late_gained = lax.optimization_barrier(
        (arrived[1], near[0], squares, gained)
    )

    owned = jnp.where(
        target_ids // (VOCAB // tp_count) == tp_place,
        ref_target_logit[0],
        jnp.zeros_like(ref_target_logit[0]),
    )
    packed = jnp.concatenate([ref_shard_max[0], ref_shard_sum[0], owned, trainee_logp])
    packed = after(packed.reshape(1, -1, 128), squares)
    near[1] = near_of(1, arrived[1])
    arrived[2] = trade(late_gained, "tp", 2)
    packed = jnp.concatenate([packed, trade(packed, "tp", 1)])
    near[1], packed, near[0] = lax.optimization_barrier((near[1], packed, near[0]))
    own_pieces[0] = far_of(0, gained, near[0])
    own_pieces[1] = far_of(1, arrived[1], near[1])
    mask = 2
    while mask < tp_count:
        packed = jnp.concatenate([packed, trade(packed, "tp", mask)])
        mask *= 2
    seq_length = lax.dynamic_index_in_dim(lengths, rep_place, keepdims=False)
    seq_weight = sequence_weight(
        list(packed.reshape(tp_count, -1)), rows_here, seq_length, rep_count, tp_place
    )
    positions = tp_place * rows_here + jnp.arange(rows_here, dtype=jnp.int32)
    row_scale = (positions < seq_length).astype(F32) * seq_weight
    inv_rms = lax.rsqrt(squares * (1.0 / width) + EPS)
    cot = (inv_rms * row_scale[:, None] * value_cot.astype(F32)).astype(BF16)
    cot_t = cot.T

    def place_of(o, i, c, k):
        chip = lax.rem(at_outer + o, outer) * inner + lax.rem(at_inner + i, inner)
        return (chip * CORES + c) * tp_count + jnp.bitwise_xor(tp_place, k)

    chips = [(o, i) for o in range(outer) for i in range(inner)]
    if not in_place:
        product = jnp.dot(cot_t, residual, preferred_element_type=F32).astype(BF16)
        product = product.reshape(features, -1, rows).transpose(1, 0, 2)

    def places_of(pair, c):
        return jnp.stack([place_of(o, i, c, k) for o, i in chips for k in pair]).astype(jnp.int32)

    def for_other(pair, cot_t):
        places = places_of(pair, 1 - core)
        if in_place:
            return pair_product(residual, cot_t, places, rows, None)
        both = after(product, cot_t)[places].reshape(len(chips), 2, features, rows)
        return both.swapaxes(0, 1)

    def for_us(pair, other):
        places = places_of(pair, core)
        if in_place:
            send_a, keep_a, send_b, keep_b = pair_product(residual, cot_t, places, rows, other)
            return ([send_a], keep_a), ([send_b], keep_b)
        both = product[places].reshape(len(chips), 2, features, rows).swapaxes(0, 1)
        total = widen([both, other]).astype(BF16).reshape(2, outer, inner, features, rows)
        first = ([total[0, :, s] for s in range(1, inner)], total[0, :, 0])
        second = ([total[1, s] for s in range(1, outer)], total[1, 0])
        return first, second

    def first_round(sides):
        return [
            [swap(send, axis, s + 1) for s, send in enumerate(sends)]
            for axis, (sends, _) in zip(("inner", "outer"), sides)
        ]

    def second_round(sides, got):
        later = []
        for axis, (_, keep), parts in zip(("outer", "inner"), sides, got):
            later.append(
                [
                    swap(widen([part[s] for part in [keep] + parts]).astype(BF16), axis, s)
                    for s in range(1, lax.axis_size(axis))
                ]
            )
        return later

    def summed(sides, got, later):
        return [
            widen([part[0] for part in [keep] + parts] + last)
            for (_, keep), parts, last in zip(sides, got, later)
        ]

    backward = order[::-1]
    pairs = [backward[i : i + 2] for i in range(0, tp_count, 2)]
    arrived[2], cot_t = lax.optimization_barrier((arrived[2], cot_t))
    for k in order[3:]:
        arrived[k] = trade(after(gained, arrived[2]), "tp", k)
    near[2] = near_of(2, arrived[2])
    theirs = [for_other(pairs[0], cot_t)]
    theirs[0], own_pieces[0], own_pieces[1] = lax.optimization_barrier(
        (theirs[0], own_pieces[0], own_pieces[1])
    )
    others = [swap(theirs[0], "core", 1)]
    theirs.append(for_other(pairs[1], after(cot_t, theirs[0])))
    near[2], arrived[3], theirs[1] = lax.optimization_barrier((near[2], arrived[3], theirs[1]))
    others.append(swap(theirs[1], "core", 1))
    near[3] = near_of(3, arrived[3])
    own_pieces[2] = far_of(2, arrived[2], near[2])
    sides = [for_us(pairs[0], after(others[0], theirs[1]))]
    near[3], sides[0] = lax.optimization_barrier((near[3], sides[0]))
    own_pieces[3] = far_of(3, arrived[3], near[3])
    got = [first_round(sides[0])]
    sides.append(for_us(pairs[1], after(others[1], sides[0])))
    for n in range(2, len(pairs)):
        for k in order[2 * n : 2 * n + 2]:
            own_pieces[k] = far_of(k, arrived[k], near_of(k, arrived[k]))
        others.append(swap(for_other(pairs[n], after(cot_t, sides[-1])), "core", 1))
        sides.append(for_us(pairs[n], others[-1]))
    sides[1:], own_pieces = lax.optimization_barrier((sides[1:], own_pieces))

    if in_place:
        pieces = [piece for k in order for piece in own_pieces[k]]
        flags = tuple(inner_first(k) for k in order)
        places = [
            jnp.stack([place_of(o, i, c, 0) // tp_count for o, i in chips]).astype(jnp.int32)
            for c in (core, 1 - core)
        ]
        offsets = jnp.stack([jnp.bitwise_xor(tp_place, k) * rows for k in order]).astype(jnp.int32)
        total, own_weight = first_value(flags, places[0], offsets, residual, pieces)
    else:
        weight = []
        for k in order:
            both = jnp.stack(own_pieces[k])
            weight.append(both if inner_first(k) else jnp.swapaxes(both, 0, 1))
        weight = jnp.stack(weight)[jnp.bitwise_xor(tp_place, jnp.arange(tp_count))]
        weight = weight[:, (at_outer - jnp.arange(outer)) % outer]
        weight = weight[:, :, (at_inner - jnp.arange(inner)) % inner]
        own_weight = weight.transpose(1, 2, 0, 3, 4).reshape(outer * inner, depth, features)
        total = jnp.zeros((), F32)
    got[0], sides[1:], total, own_weight = lax.optimization_barrier(
        (got[0], sides[1:], total, own_weight)
    )
    other_weight = swap(own_weight, "core", 1)
    later = [second_round(sides[0], got[0])]
    got += [first_round(side) for side in sides[1:]]
    if in_place:
        value_proj, coefficient = weight_call(
            functools.partial(value_end_kernel, width),
            places[1],
            residual,
            other_weight,
            [total, cot, inv_rms],
            [
                jax.ShapeDtypeStruct((rows_here, features), BF16),
                jax.ShapeDtypeStruct((rows_here, 1), F32),
            ],
        )
    else:
        both = jnp.stack([own_weight, other_weight], axis=1)
        weight = jnp.where(core == 0, both, both[:, ::-1]).reshape(width, features)
        value_acc = jnp.dot(residual, weight, preferred_element_type=F32)
        value_proj = (inv_rms * value_acc).astype(BF16)
        share = jnp.sum(cot.astype(F32) * value_acc, axis=1, keepdims=True)
        coefficient = inv_rms * inv_rms * share * (1.0 / width)
    later[0], coefficient = lax.optimization_barrier((later[0], coefficient))
    sums = dict(zip(pairs[0], summed(sides[0], got[0], later[0])))
    last = [trade(sums[k].astype(BF16), "tp", k) for k in pairs[0]]
    got[1:], coefficient, sums = lax.optimization_barrier((got[1:], coefficient, sums))
    later += [second_round(side, parts) for side, parts in zip(sides[1:], got[1:])]
    if in_place:
        grad_shape = jax.ShapeDtypeStruct((rows_here, width), BF16)
        resid_grad = weight_call(
            grad_kernel, places[0], residual, own_weight, [cot, coefficient], grad_shape
        )
        later[1], coefficient, resid_grad = lax.optimization_barrier((later[1], coefficient, resid_grad))
    else:
        normed_grad = lax.dot_general(
            cot, weight, (((1,), (1,)), ((), ())), preferred_element_type=F32
        )
        resid_grad = (normed_grad - residual.astype(F32) * coefficient).astype(BF16)
    for pair, *rounds in zip(pairs[1:], sides[1:], got[1:], later[1:]):
        sums.update(zip(pair, summed(*rounds)))
    last += [trade(sums[k].astype(BF16), "tp", k) for k in backward[2:-1]]
    if in_place:
        resid_grad = weight_call(
            grad_kernel, places[1], residual, other_weight, [cot, coefficient], grad_shape, resid_grad
        )
    grad_rows = widen([sums[0]] + last)
    late_gain, late_weight, grad_rows = lax.optimization_barrier((norm_gain, value_weight, grad_rows))
    weight_grad = (late_gain.astype(F32)[None, :] * grad_rows).T
    gain_grad = jnp.sum(late_weight.astype(F32).T * grad_rows, axis=0)
    return (value_proj, resid_grad, weight_grad, gain_grad)


def solution(mesh):
    rep_count, tp_count = mesh.shape["rep"], mesh.shape["tp"]
    split = jax.sharding.Mesh(
        mesh.devices.reshape(OUTER, rep_count // (OUTER * CORES), CORES, tp_count),
        ("outer", "inner", "core", "tp"),
    )
    rep = ("outer", "inner", "core")
    rows = rep + ("tp",)
    return jax.shard_map(
        per_device,
        mesh=split,
        in_specs=(
            P(rows, None),
            P(rows),
            P(rows, None),
            P(rows, None),
            P(rows),
            P("tp", rep),
            P("tp", rep),
            P("tp", rep),
            P(rep),
            P(),
        ),
        out_specs=(P(rows, None), P(rows, None), P(rows, None), P(rows)),
        check_vma=False,
    )
```

```python
import functools

import jax
import jax.numpy as jnp
from jax import lax
from jax.experimental import pallas as pl
from jax.experimental.pallas import tpu as pltpu
from jax.sharding import PartitionSpec as P

VOCAB = 128256
EPS = 1e-05
BETA = 0.5
CORES = 2
OUTER = 2
PAIR_VMEM = 14 * 1024 * 1024
WEIGHT_VMEM = 22 * 1024 * 1024
NOMINAL = pl.CostEstimate(flops=1024, bytes_accessed=1024, transcendentals=0)
BF16 = jnp.bfloat16
F32 = jnp.float32


def swap(value, axis, step):
    size = lax.axis_size(axis)
    return lax.ppermute(value, axis, [(place, (place + step) % size) for place in range(size)])


def trade(value, axis, mask):
    size = lax.axis_size(axis)
    return lax.ppermute(value, axis, [(place, place ^ mask) for place in range(size)])


def in_hbm(array):
    return pltpu.with_memory_space_constraint(array, pltpu.HBM)


def after(value, *earlier):
    return lax.optimization_barrier((value, earlier))[0]


def widen(parts):
    return functools.reduce(jnp.add, [part.astype(F32) for part in parts])


def inner_first(chunk):
    return chunk % 2 == 0


def theirs_kernel(places_ref, cot_ref, *rest):
    count = len(rest) * 2 // 3
    blocks, outs = rest[:count], rest[count:]
    for slot, resid_ref in enumerate(blocks):
        product = jnp.dot(cot_ref[...], resid_ref[...], preferred_element_type=F32)
        outs[slot // 2][slot % 2, 0] = product.astype(BF16)


def theirs_product(residual, cot_t, places, rows):
    features, tokens = cot_t.shape
    steps = 4
    slots = places.shape[0] // steps
    block = pl.BlockSpec((2, 1, features, rows), lambda i, p: (0, i, 0, 0))
    return pl.pallas_call(
        theirs_kernel,
        out_shape=[pltpu.HBM((2, steps, features, rows), BF16)] * (slots // 2),
        grid_spec=pltpu.PrefetchScalarGridSpec(
            num_scalar_prefetch=1,
            grid=(steps,),
            in_specs=[pl.BlockSpec((features, tokens), lambda i, p: (0, 0))]
            + [
                pl.BlockSpec((tokens, rows), lambda i, p, slot=slot: (0, p[slots * i + slot]))
                for slot in range(slots)
            ],
            out_specs=[block] * (slots // 2),
        ),
        cost_estimate=NOMINAL,
        compiler_params=pltpu.CompilerParams(vmem_limit_bytes=PAIR_VMEM),
    )(places, cot_t, *[in_hbm(residual)] * slots)


def ours_kernel(places_ref, cot_ref, first_ref, second_ref, other_ref, *outs):
    step = pl.program_id(0)
    at_outer, at_inner = step // 2, lax.rem(step, 2)
    for slot, resid_ref in enumerate((first_ref, second_ref)):
        send_ref, keep_ref = outs[2 * slot : 2 * slot + 2]
        product = jnp.dot(cot_ref[...], resid_ref[...], preferred_element_type=F32)
        total = (product + other_ref[slot, 0].astype(F32)).astype(BF16)
        way, place = (at_inner, at_outer) if slot == 0 else (at_outer, at_inner)

        @pl.when(way == 1)
        def _():
            send_ref[place] = total

        @pl.when(way == 0)
        def _():
            keep_ref[place] = total


def ours_product(residual, cot_t, places, rows, other):
    features, tokens = cot_t.shape
    steps = places.shape[0] // 2
    return pl.pallas_call(
        ours_kernel,
        out_shape=[jax.ShapeDtypeStruct((2, features, rows), BF16)] * 4,
        grid_spec=pltpu.PrefetchScalarGridSpec(
            num_scalar_prefetch=1,
            grid=(steps,),
            in_specs=[
                pl.BlockSpec((features, tokens), lambda i, p: (0, 0)),
                pl.BlockSpec((tokens, rows), lambda i, p: (0, p[2 * i])),
                pl.BlockSpec((tokens, rows), lambda i, p: (0, p[2 * i + 1])),
                pl.BlockSpec((2, 1, features, rows), lambda i, p: (0, i, 0, 0)),
            ],
            out_specs=[pl.BlockSpec((2, features, rows), lambda i, p: (0, 0, 0))] * 4,
        ),
        cost_estimate=NOMINAL,
        compiler_params=pltpu.CompilerParams(vmem_limit_bytes=PAIR_VMEM),
    )(places, cot_t, in_hbm(residual), in_hbm(residual), other)


def place_weight(inner_flags, offsets_ref, pieces, weight_ref):
    step = pl.program_id(0)
    at_outer, at_inner = step // 2, lax.rem(step, 2)
    rows = pieces[0].shape[1]
    for chunk, flag in enumerate(inner_flags):
        way = at_outer if flag else at_inner
        where = pl.ds(pl.multiple_of(offsets_ref[chunk], rows), rows)
        for late in range(2):
            piece = pieces[chunk * 2 + late]

            @pl.when(way == late)
            def _():
                weight_ref[0, where, :] = piece[0]


def piece_specs(inner_flags, rows, features):
    specs = []
    for flag in inner_flags:
        for late in range(2):
            if flag:
                index = lambda i, *_, first=2 * late: (jnp.clip(i - first, 0, 1), 0, 0)
            else:
                index = lambda i, *_: (i // 2, 0, 0)
            specs.append(pl.BlockSpec((1, rows, features), index))
    return specs


def value_kernel(inner_flags, places_ref, offsets_ref, resid_ref, *rest):
    pieces, (total_ref, weight_ref) = rest[:-2], rest[-2:]
    step = pl.program_id(0)
    place_weight(inner_flags, offsets_ref, pieces, weight_ref)
    product = jnp.dot(resid_ref[...], weight_ref[0], preferred_element_type=F32)

    @pl.when(step == 0)
    def _():
        total_ref[...] = product

    @pl.when(step > 0)
    def _():
        total_ref[...] += product


def value_end_kernel(
    width, places_ref, resid_ref, weight_ref, first_ref, cot_ref, inv_ref, value_ref, coef_ref, total_ref
):
    step = pl.program_id(0)
    product = jnp.dot(resid_ref[...], weight_ref[0], preferred_element_type=F32)

    @pl.when(step == 0)
    def _():
        total_ref[...] = first_ref[...] + product

    @pl.when(step > 0)
    def _():
        total_ref[...] += product

    @pl.when(step == pl.num_programs(0) - 1)
    def _():
        total = total_ref[...]
        inv = inv_ref[...]
        value_ref[...] = (total * inv).astype(BF16)
        share = jnp.sum(total * cot_ref[...].astype(F32), axis=1, keepdims=True)
        coef_ref[...] = share * (inv * inv) * (1.0 / width)


def grad_kernel(places_ref, resid_ref, weight_ref, cot_ref, coef_ref, *rest):
    out_ref = rest[-1]
    grad = lax.dot_general(
        cot_ref[...], weight_ref[0], (((1,), (1,)), ((), ())), preferred_element_type=F32
    )
    out_ref[...] = (grad - resid_ref[...].astype(F32) * coef_ref[...]).astype(BF16)


def whole_block(array):
    return pl.BlockSpec(array.shape, lambda i, *_: (0, 0))


def first_value(inner_flags, places, offsets, residual, pieces):
    tokens, width = residual.shape
    rows, features = pieces[0].shape[1:]
    steps = places.shape[0]
    depth = width // (CORES * steps)
    total = jax.ShapeDtypeStruct((tokens, features), F32)
    return pl.pallas_call(
        functools.partial(value_kernel, inner_flags),
        out_shape=[total, pltpu.HBM((steps, depth, features), BF16)],
        grid_spec=pltpu.PrefetchScalarGridSpec(
            num_scalar_prefetch=2,
            grid=(steps,),
            in_specs=[pl.BlockSpec((tokens, depth), lambda i, p, o: (0, p[i]))]
            + piece_specs(inner_flags, rows, features),
            out_specs=[
                whole_block(total),
                pl.BlockSpec((1, depth, features), lambda i, p, o: (p[i] // CORES, 0, 0)),
            ],
        ),
        cost_estimate=NOMINAL,
        compiler_params=pltpu.CompilerParams(vmem_limit_bytes=WEIGHT_VMEM),
    )(places, offsets, in_hbm(residual), *pieces)


def weight_call(kernel, places, residual, weight, wholes, out_shape, earlier=None):
    tokens, width = residual.shape
    steps, depth, features = weight.shape
    scratch = []
    if isinstance(out_shape, list):
        out_specs = [whole_block(array) for array in out_shape]
        scratch.append(pltpu.VMEM((tokens, features), F32))
    else:
        out_specs = pl.BlockSpec((tokens, depth), lambda i, p: (0, p[i]))
    in_specs = [
        pl.BlockSpec((tokens, depth), lambda i, p: (0, p[i])),
        pl.BlockSpec((1, depth, features), lambda i, p: (p[i] // CORES, 0, 0)),
    ] + [whole_block(array) for array in wholes]
    operands = [places, in_hbm(residual), weight, *wholes]
    aliases = {}
    if earlier is not None:
        aliases = {len(operands): 0}
        in_specs.append(pl.BlockSpec(memory_space=pltpu.HBM))
        operands.append(earlier)
    return pl.pallas_call(
        kernel,
        out_shape=out_shape,
        grid_spec=pltpu.PrefetchScalarGridSpec(
            num_scalar_prefetch=1,
            grid=(steps,),
            in_specs=in_specs,
            out_specs=out_specs,
            scratch_shapes=scratch,
        ),
        input_output_aliases=aliases,
        cost_estimate=NOMINAL,
        compiler_params=pltpu.CompilerParams(vmem_limit_bytes=WEIGHT_VMEM),
    )(*operands)


def sequence_weight(shares, rows_here, seq_length, rep_count, tp_place):
    seq = (shares[0].shape[0] - rows_here) // 3
    top_max = functools.reduce(jnp.maximum, [share[:seq] for share in shares])
    sum_exp = sum(share[seq : 2 * seq] * jnp.exp(share[:seq] - top_max) for share in shares)
    picked = sum(share[2 * seq : 3 * seq] for share in shares)
    ref_logp = picked - top_max - jnp.log(sum_exp)
    total = jnp.zeros((), F32)
    for mask, share in enumerate(shares):
        first = jnp.bitwise_xor(tp_place, mask) * rows_here
        live = first + jnp.arange(rows_here, dtype=jnp.int32) < seq_length
        diff = share[3 * seq :] - lax.dynamic_slice_in_dim(ref_logp, first, rows_here)
        total = total + jnp.sum(jnp.where(live, diff, 0.0))
    seq_delta = total / seq_length.astype(F32)
    return 2.0 * jax.nn.sigmoid(BETA * seq_delta) / rep_count


def per_device(
    residual,
    norm_gain,
    value_weight,
    value_cot,
    trainee_logp,
    ref_shard_max,
    ref_shard_sum,
    ref_target_logit,
    target_ids,
    lengths,
):
    rows_here, width = residual.shape
    features = value_cot.shape[1]
    tp_count = lax.axis_size("tp")
    outer, inner = lax.axis_size("outer"), lax.axis_size("inner")
    rep_count = outer * inner * CORES
    tp_place = lax.axis_index("tp")
    core = lax.axis_index("core")
    at_inner = lax.axis_index("inner")
    at_outer = lax.axis_index("outer")
    rep_place = (at_outer * inner + at_inner) * CORES + core
    depth = width // rep_count
    rows = depth // tp_count
    order = list(range(tp_count))
    in_place = rows % 128 == 0 and outer == 2 and inner == 2

    gained = (value_weight.astype(F32) * norm_gain.astype(F32)[:, None]).astype(BF16)
    residual, gained = lax.optimization_barrier((residual, gained))
    resid_wide = residual.astype(F32)
    squares = jnp.sum(resid_wide * resid_wide, axis=1, keepdims=True)

    def near_of(k, block):
        first = "inner" if inner_first(k) else "outer"
        return [swap(block, first, s) for s in range(1, lax.axis_size(first))]

    def far_of(k, block, nears):
        second = "outer" if inner_first(k) else "inner"
        near = jnp.stack([block] + nears)
        return [near] + [swap(near, second, s) for s in range(1, lax.axis_size(second))]

    own_pieces, arrived, near = {}, {0: gained}, {}
    arrived[1] = trade(gained, "tp", 1)
    near[0] = near_of(0, gained)
    arrived[1], near[0], squares, late_gained = lax.optimization_barrier(
        (arrived[1], near[0], squares, gained)
    )

    owned = jnp.where(
        target_ids // (VOCAB // tp_count) == tp_place,
        ref_target_logit[0],
        jnp.zeros_like(ref_target_logit[0]),
    )
    packed = jnp.concatenate([ref_shard_max[0], ref_shard_sum[0], owned, trainee_logp])
    packed = after(packed.reshape(1, -1, 128), squares)
    near[1] = near_of(1, arrived[1])
    arrived[2] = trade(late_gained, "tp", 2)
    packed = jnp.concatenate([packed, trade(packed, "tp", 1)])
    near[1], packed, near[0] = lax.optimization_barrier((near[1], packed, near[0]))
    own_pieces[0] = far_of(0, gained, near[0])
    own_pieces[1] = far_of(1, arrived[1], near[1])
    mask = 2
    while mask < tp_count:
        packed = jnp.concatenate([packed, trade(packed, "tp", mask)])
        mask *= 2
    seq_length = lax.dynamic_index_in_dim(lengths, rep_place, keepdims=False)
    seq_weight = sequence_weight(
        list(packed.reshape(tp_count, -1)), rows_here, seq_length, rep_count, tp_place
    )
    positions = tp_place * rows_here + jnp.arange(rows_here, dtype=jnp.int32)
    row_scale = (positions < seq_length).astype(F32) * seq_weight
    inv_rms = lax.rsqrt(squares * (1.0 / width) + EPS)
    cot = (inv_rms * row_scale[:, None] * value_cot.astype(F32)).astype(BF16)
    cot_t = cot.T

    def place_of(o, i, c, k):
        chip = lax.rem(at_outer + o, outer) * inner + lax.rem(at_inner + i, inner)
        return (chip * CORES + c) * tp_count + jnp.bitwise_xor(tp_place, k)

    chips = [(o, i) for o in range(outer) for i in range(inner)]
    if not in_place:
        product = jnp.dot(cot_t, residual, preferred_element_type=F32).astype(BF16)
        product = product.reshape(features, -1, rows).transpose(1, 0, 2)

    def places_of(pair, c):
        return jnp.stack([place_of(o, i, c, k) for o, i in chips for k in pair]).astype(jnp.int32)

    def for_other(pair, cot_t):
        places = places_of(pair, 1 - core)
        both = after(product, cot_t)[places].reshape(len(chips), 2, features, rows)
        return both.swapaxes(0, 1)

    def for_us(pair, other):
        places = places_of(pair, core)
        if in_place:
            send_a, keep_a, send_b, keep_b = ours_product(residual, cot_t, places, rows, other)
            return ([send_a], keep_a), ([send_b], keep_b)
        both = product[places].reshape(len(chips), 2, features, rows).swapaxes(0, 1)
        total = widen([both, other]).astype(BF16).reshape(2, outer, inner, features, rows)
        first = ([total[0, :, s] for s in range(1, inner)], total[0, :, 0])
        second = ([total[1, s] for s in range(1, outer)], total[1, 0])
        return first, second

    def first_round(sides):
        return [
            [swap(send, axis, s + 1) for s, send in enumerate(sends)]
            for axis, (sends, _) in zip(("inner", "outer"), sides)
        ]

    def second_round(sides, got):
        later = []
        for axis, (_, keep), parts in zip(("outer", "inner"), sides, got):
            later.append(
                [
                    swap(widen([part[s] for part in [keep] + parts]).astype(BF16), axis, s)
                    for s in range(1, lax.axis_size(axis))
                ]
            )
        return later

    def summed(sides, got, later):
        return [
            widen([part[0] for part in [keep] + parts] + last)
            for (_, keep), parts, last in zip(sides, got, later)
        ]

    backward = order[::-1]
    pairs = [backward[i : i + 2] for i in range(0, tp_count, 2)]
    arrived[2], cot_t = lax.optimization_barrier((arrived[2], cot_t))
    for k in order[3:]:
        arrived[k] = trade(after(gained, arrived[2]), "tp", k)
    near[2] = near_of(2, arrived[2])
    if in_place:
        theirs = theirs_product(residual, cot_t, places_of(backward, 1 - core), rows)
    else:
        theirs = [for_other(pair, cot_t) for pair in pairs]
    near[2], arrived[3], theirs, own_pieces[0], own_pieces[1] = lax.optimization_barrier(
        (near[2], arrived[3], theirs, own_pieces[0], own_pieces[1])
    )
    others = [swap(part, "core", 1) for part in theirs]
    near[3] = near_of(3, arrived[3])
    own_pieces[2] = far_of(2, arrived[2], near[2])
    sides = [for_us(pairs[0], others[0])]
    near[3], sides[0] = lax.optimization_barrier((near[3], sides[0]))
    own_pieces[3] = far_of(3, arrived[3], near[3])
    got = [first_round(sides[0])]
    sides.append(for_us(pairs[1], after(others[1], sides[0])))
    for n in range(2, len(pairs)):
        for k in order[2 * n : 2 * n + 2]:
            own_pieces[k] = far_of(k, arrived[k], near_of(k, arrived[k]))
        sides.append(for_us(pairs[n], others[n]))
    sides[1:], own_pieces = lax.optimization_barrier((sides[1:], own_pieces))

    if in_place:
        pieces = [piece for k in order for piece in own_pieces[k]]
        flags = tuple(inner_first(k) for k in order)
        places = [
            jnp.stack([place_of(o, i, c, 0) // tp_count for o, i in chips]).astype(jnp.int32)
            for c in (core, 1 - core)
        ]
        offsets = jnp.stack([jnp.bitwise_xor(tp_place, k) * rows for k in order]).astype(jnp.int32)
        total, own_weight = first_value(flags, places[0], offsets, residual, pieces)
    else:
        weight = []
        for k in order:
            both = jnp.stack(own_pieces[k])
            weight.append(both if inner_first(k) else jnp.swapaxes(both, 0, 1))
        weight = jnp.stack(weight)[jnp.bitwise_xor(tp_place, jnp.arange(tp_count))]
        weight = weight[:, (at_outer - jnp.arange(outer)) % outer]
        weight = weight[:, :, (at_inner - jnp.arange(inner)) % inner]
        own_weight = weight.transpose(1, 2, 0, 3, 4).reshape(outer * inner, depth, features)
        total = jnp.zeros((), F32)
    got[0], sides[1:], total, own_weight = lax.optimization_barrier(
        (got[0], sides[1:], total, own_weight)
    )
    other_weight = swap(own_weight, "core", 1)
    later = [second_round(sides[0], got[0])]
    got += [first_round(side) for side in sides[1:]]
    if in_place:
        value_proj, coefficient = weight_call(
            functools.partial(value_end_kernel, width),
            places[1],
            residual,
            other_weight,
            [total, cot, inv_rms],
            [
                jax.ShapeDtypeStruct((rows_here, features), BF16),
                jax.ShapeDtypeStruct((rows_here, 1), F32),
            ],
        )
    else:
        both = jnp.stack([own_weight, other_weight], axis=1)
        weight = jnp.where(core == 0, both, both[:, ::-1]).reshape(width, features)
        value_acc = jnp.dot(residual, weight, preferred_element_type=F32)
        value_proj = (inv_rms * value_acc).astype(BF16)
        share = jnp.sum(cot.astype(F32) * value_acc, axis=1, keepdims=True)
        coefficient = inv_rms * inv_rms * share * (1.0 / width)
    later[0], coefficient = lax.optimization_barrier((later[0], coefficient))
    sums = dict(zip(pairs[0], summed(sides[0], got[0], later[0])))
    last = [trade(sums[k].astype(BF16), "tp", k) for k in pairs[0]]
    got[1:], coefficient, sums = lax.optimization_barrier((got[1:], coefficient, sums))
    later += [second_round(side, parts) for side, parts in zip(sides[1:], got[1:])]
    if in_place:
        grad_shape = jax.ShapeDtypeStruct((rows_here, width), BF16)
        resid_grad = weight_call(
            grad_kernel, places[0], residual, in_hbm(own_weight), [cot, coefficient], grad_shape
        )
        later[1], coefficient, resid_grad = lax.optimization_barrier((later[1], coefficient, resid_grad))
    else:
        normed_grad = lax.dot_general(
            cot, weight, (((1,), (1,)), ((), ())), preferred_element_type=F32
        )
        resid_grad = (normed_grad - residual.astype(F32) * coefficient).astype(BF16)
    for pair, *rounds in zip(pairs[1:], sides[1:], got[1:], later[1:]):
        sums.update(zip(pair, summed(*rounds)))
    last += [trade(sums[k].astype(BF16), "tp", k) for k in backward[2:-1]]
    if in_place:
        resid_grad = weight_call(
            grad_kernel, places[1], residual, other_weight, [cot, coefficient], grad_shape, resid_grad
        )
    grad_rows = widen([sums[0]] + last)
    late_gain, late_weight, grad_rows = lax.optimization_barrier((norm_gain, value_weight, grad_rows))
    weight_grad = (late_gain.astype(F32)[None, :] * grad_rows).T
    gain_grad = jnp.sum(late_weight.astype(F32).T * grad_rows, axis=0)
    return (value_proj, resid_grad, weight_grad, gain_grad)


def solution(mesh):
    rep_count, tp_count = mesh.shape["rep"], mesh.shape["tp"]
    split = jax.sharding.Mesh(
        mesh.devices.reshape(OUTER, rep_count // (OUTER * CORES), CORES, tp_count),
        ("outer", "inner", "core", "tp"),
    )
    rep = ("outer", "inner", "core")
    rows = rep + ("tp",)
    return jax.shard_map(
        per_device,
        mesh=split,
        in_specs=(
            P(rows, None),
            P(rows),
            P(rows, None),
            P(rows, None),
            P(rows),
            P("tp", rep),
            P("tp", rep),
            P("tp", rep),
            P(rep),
            P(),
        ),
        out_specs=(P(rows, None), P(rows, None), P(rows, None), P(rows)),
        check_vma=False,
    )
```

```python
import functools

import jax
import jax.numpy as jnp
from jax import lax
from jax.experimental import pallas as pl
from jax.experimental.pallas import tpu as pltpu
from jax.sharding import PartitionSpec as P

VOCAB = 128256
EPS = 1e-05
BETA = 0.5
CORES = 2
OUTER = 2
PAIR_VMEM = 14 * 1024 * 1024
WEIGHT_VMEM = 22 * 1024 * 1024
NOMINAL = pl.CostEstimate(flops=1024, bytes_accessed=1024, transcendentals=0)
BF16 = jnp.bfloat16
F32 = jnp.float32


def swap(value, axis, step):
    size = lax.axis_size(axis)
    return lax.ppermute(value, axis, [(place, (place + step) % size) for place in range(size)])


def trade(value, axis, mask):
    size = lax.axis_size(axis)
    return lax.ppermute(value, axis, [(place, place ^ mask) for place in range(size)])


def in_hbm(array):
    return pltpu.with_memory_space_constraint(array, pltpu.HBM)


def after(value, *earlier):
    return lax.optimization_barrier((value, earlier))[0]


def widen(parts):
    return functools.reduce(jnp.add, [part.astype(F32) for part in parts])


def inner_first(chunk):
    return chunk % 2 == 0


def theirs_kernel(places_ref, cot_ref, *rest):
    count = len(rest) * 2 // 3
    blocks, outs = rest[:count], rest[count:]
    for slot, resid_ref in enumerate(blocks):
        product = jnp.dot(cot_ref[...], resid_ref[...], preferred_element_type=F32)
        outs[slot // 2][slot % 2, 0] = product.astype(BF16)


def theirs_product(residual, cot_t, places, rows):
    features, tokens = cot_t.shape
    steps = 4
    slots = places.shape[0] // steps
    block = pl.BlockSpec((2, 1, features, rows), lambda i, p: (0, i, 0, 0))
    return pl.pallas_call(
        theirs_kernel,
        out_shape=[pltpu.HBM((2, steps, features, rows), BF16)] * (slots // 2),
        grid_spec=pltpu.PrefetchScalarGridSpec(
            num_scalar_prefetch=1,
            grid=(steps,),
            in_specs=[pl.BlockSpec((features, tokens), lambda i, p: (0, 0))]
            + [
                pl.BlockSpec((tokens, rows), lambda i, p, slot=slot: (0, p[slots * i + slot]))
                for slot in range(slots)
            ],
            out_specs=[block] * (slots // 2),
        ),
        cost_estimate=NOMINAL,
        compiler_params=pltpu.CompilerParams(vmem_limit_bytes=PAIR_VMEM),
    )(places, cot_t, *[in_hbm(residual)] * slots)


def ours_kernel(places_ref, cot_ref, first_ref, second_ref, other_ref, *outs):
    step = pl.program_id(0)
    at_outer, at_inner = step // 2, lax.rem(step, 2)
    totals = [
        (
            jnp.dot(cot_ref[...], resid_ref[...], preferred_element_type=F32)
            + other_ref[slot, 0].astype(F32)
        ).astype(BF16)
        for slot, resid_ref in enumerate((first_ref, second_ref))
    ]
    for slot, way in enumerate((at_inner, at_outer)):
        send_ref, keep_ref = outs[2 * slot : 2 * slot + 2]

        @pl.when(way == 1)
        def _():
            send_ref[0] = totals[slot]

        @pl.when(way == 0)
        def _():
            keep_ref[0] = totals[slot]


def ours_product(residual, cot_t, places, rows, other):
    features, tokens = cot_t.shape
    steps = places.shape[0] // 2
    indices = [lambda i: i // 2, lambda i: i // 2, lambda i: jnp.maximum(i - 2, 0), lambda i: jnp.minimum(i, 1)]
    return pl.pallas_call(
        ours_kernel,
        out_shape=[pltpu.HBM((2, features, rows), BF16)] * 4,
        grid_spec=pltpu.PrefetchScalarGridSpec(
            num_scalar_prefetch=1,
            grid=(steps,),
            in_specs=[
                pl.BlockSpec((features, tokens), lambda i, p: (0, 0)),
                pl.BlockSpec((tokens, rows), lambda i, p: (0, p[2 * i])),
                pl.BlockSpec((tokens, rows), lambda i, p: (0, p[2 * i + 1])),
                pl.BlockSpec((2, 1, features, rows), lambda i, p: (0, i, 0, 0)),
            ],
            out_specs=[
                pl.BlockSpec((1, features, rows), lambda i, p, index=index: (index(i), 0, 0))
                for index in indices
            ],
        ),
        cost_estimate=NOMINAL,
        compiler_params=pltpu.CompilerParams(vmem_limit_bytes=PAIR_VMEM),
    )(places, cot_t, in_hbm(residual), in_hbm(residual), other)


def place_weight(inner_flags, offsets_ref, pieces, weight_ref):
    step = pl.program_id(0)
    at_outer, at_inner = step // 2, lax.rem(step, 2)
    rows = pieces[0].shape[1]
    for chunk, flag in enumerate(inner_flags):
        way = at_outer if flag else at_inner
        where = pl.ds(pl.multiple_of(offsets_ref[chunk], rows), rows)
        for late in range(2):
            piece = pieces[chunk * 2 + late]

            @pl.when(way == late)
            def _():
                weight_ref[0, where, :] = piece[0]


def piece_specs(inner_flags, rows, features):
    specs = []
    for flag in inner_flags:
        for late in range(2):
            if flag:
                index = lambda i, *_, first=2 * late: (jnp.clip(i - first, 0, 1), 0, 0)
            else:
                index = lambda i, *_: (i // 2, 0, 0)
            specs.append(pl.BlockSpec((1, rows, features), index))
    return specs


def value_kernel(inner_flags, places_ref, offsets_ref, resid_ref, *rest):
    pieces, (total_ref, weight_ref) = rest[:-2], rest[-2:]
    step = pl.program_id(0)
    place_weight(inner_flags, offsets_ref, pieces, weight_ref)
    product = jnp.dot(resid_ref[...], weight_ref[0], preferred_element_type=F32)

    @pl.when(step == 0)
    def _():
        total_ref[...] = product

    @pl.when(step > 0)
    def _():
        total_ref[...] += product


def value_end_kernel(
    width, places_ref, resid_ref, weight_ref, first_ref, cot_ref, inv_ref, value_ref, coef_ref, total_ref
):
    step = pl.program_id(0)
    product = jnp.dot(resid_ref[...], weight_ref[0], preferred_element_type=F32)

    @pl.when(step == 0)
    def _():
        total_ref[...] = first_ref[...] + product

    @pl.when(step > 0)
    def _():
        total_ref[...] += product

    @pl.when(step == pl.num_programs(0) - 1)
    def _():
        total = total_ref[...]
        inv = inv_ref[...]
        value_ref[...] = (total * inv).astype(BF16)
        share = jnp.sum(total * cot_ref[...].astype(F32), axis=1, keepdims=True)
        coef_ref[...] = share * (inv * inv) * (1.0 / width)


def grad_kernel(places_ref, resid_ref, weight_ref, cot_ref, coef_ref, *rest):
    out_ref = rest[-1]
    grad = lax.dot_general(
        cot_ref[...], weight_ref[0], (((1,), (1,)), ((), ())), preferred_element_type=F32
    )
    out_ref[...] = (grad - resid_ref[...].astype(F32) * coef_ref[...]).astype(BF16)


def whole_block(array):
    return pl.BlockSpec(array.shape, lambda i, *_: (0, 0))


def first_value(inner_flags, places, offsets, residual, pieces):
    tokens, width = residual.shape
    rows, features = pieces[0].shape[1:]
    steps = places.shape[0]
    depth = width // (CORES * steps)
    total = pltpu.HBM((tokens, features), F32)
    return pl.pallas_call(
        functools.partial(value_kernel, inner_flags),
        out_shape=[total, pltpu.HBM((steps, depth, features), BF16)],
        grid_spec=pltpu.PrefetchScalarGridSpec(
            num_scalar_prefetch=2,
            grid=(steps,),
            in_specs=[pl.BlockSpec((tokens, depth), lambda i, p, o: (0, p[i]))]
            + piece_specs(inner_flags, rows, features),
            out_specs=[
                whole_block(total),
                pl.BlockSpec((1, depth, features), lambda i, p, o: (p[i] // CORES, 0, 0)),
            ],
        ),
        cost_estimate=NOMINAL,
        compiler_params=pltpu.CompilerParams(vmem_limit_bytes=WEIGHT_VMEM),
    )(places, offsets, in_hbm(residual), *pieces)


def weight_call(kernel, places, residual, weight, wholes, out_shape, earlier=None):
    tokens, width = residual.shape
    steps, depth, features = weight.shape
    scratch = []
    if isinstance(out_shape, list):
        out_specs = [whole_block(array) for array in out_shape]
        scratch.append(pltpu.VMEM((tokens, features), F32))
    else:
        out_specs = pl.BlockSpec((tokens, depth), lambda i, p: (0, p[i]))
    in_specs = [
        pl.BlockSpec((tokens, depth), lambda i, p: (0, p[i])),
        pl.BlockSpec((1, depth, features), lambda i, p: (p[i] // CORES, 0, 0)),
    ] + [whole_block(array) for array in wholes]
    operands = [places, in_hbm(residual), weight, *wholes]
    aliases = {}
    if earlier is not None:
        aliases = {len(operands): 0}
        in_specs.append(pl.BlockSpec(memory_space=pltpu.HBM))
        operands.append(earlier)
    return pl.pallas_call(
        kernel,
        out_shape=out_shape,
        grid_spec=pltpu.PrefetchScalarGridSpec(
            num_scalar_prefetch=1,
            grid=(steps,),
            in_specs=in_specs,
            out_specs=out_specs,
            scratch_shapes=scratch,
        ),
        input_output_aliases=aliases,
        cost_estimate=NOMINAL,
        compiler_params=pltpu.CompilerParams(vmem_limit_bytes=WEIGHT_VMEM),
    )(*operands)


def squares_kernel(resid_ref, out_ref):
    wide = resid_ref[...].astype(F32)
    out_ref[...] = jnp.sum(wide * wide, axis=1, keepdims=True)


def row_squares(residual):
    tokens, width = residual.shape
    rows = 64
    return pl.pallas_call(
        squares_kernel,
        out_shape=jax.ShapeDtypeStruct((tokens, 1), F32),
        grid=(tokens // rows,),
        in_specs=[pl.BlockSpec((rows, width), lambda i: (i, 0))],
        out_specs=pl.BlockSpec((rows, 1), lambda i: (i, 0)),
        cost_estimate=NOMINAL,
        compiler_params=pltpu.CompilerParams(vmem_limit_bytes=PAIR_VMEM),
    )(in_hbm(residual))


def cot_kernel(width, rep_count, info_ref, shares_ref, squares_ref, value_cot_ref, cot_ref, cot_t_ref, inv_ref):
    place, length = info_ref[0], info_ref[1]
    rows = value_cot_ref.shape[0]
    own = rows // 128
    seq = (shares_ref.shape[1] - own) // 3
    shares = range(shares_ref.shape[0])

    def below(first, shape):
        at = lax.broadcasted_iota(jnp.int32, shape, 0) * 128 + lax.broadcasted_iota(jnp.int32, shape, 1)
        return first + at < length

    def summed(mask, value):
        return jnp.sum(jnp.where(mask, value, 0.0), axis=(0, 1), keepdims=True)

    maxes = [shares_ref[m, 0:seq] for m in shares]
    top_max = functools.reduce(jnp.maximum, maxes)
    sum_exp = functools.reduce(
        jnp.add, [shares_ref[m, seq : 2 * seq] * jnp.exp(maxes[m] - top_max) for m in shares]
    )
    picked = functools.reduce(jnp.add, [shares_ref[m, 2 * seq : 3 * seq] for m in shares])
    ref_logp = picked - top_max - jnp.log(sum_exp)
    total = -summed(below(0, (seq, 128)), ref_logp)
    for m in shares:
        first = jnp.bitwise_xor(place, m) * rows
        total += summed(below(first, (own, 128)), shares_ref[m, 3 * seq :])
    seq_delta = total / jnp.full((1, 1), length, jnp.int32).astype(F32)
    weight = (2.0 / rep_count) * jax.nn.sigmoid(BETA * seq_delta)
    inv = lax.rsqrt(squares_ref[...] * (1.0 / width) + EPS)
    live = place * rows + lax.broadcasted_iota(jnp.int32, (rows, 1), 0) < length
    scaled = jnp.where(live, inv * weight, 0.0) * value_cot_ref[...].astype(F32)
    cot_ref[...] = scaled.astype(BF16)
    cot_t_ref[...] = scaled.T.astype(BF16)
    inv_ref[...] = inv


def scaled_cot(width, rep_count, info, shares, squares, value_cot):
    rows, features = value_cot.shape

    def whole(array):
        return pl.BlockSpec(array.shape, lambda i, p: (0,) * array.ndim)

    out_shape = [
        jax.ShapeDtypeStruct((rows, features), BF16),
        jax.ShapeDtypeStruct((features, rows), BF16),
        jax.ShapeDtypeStruct((rows, 1), F32),
    ]
    return pl.pallas_call(
        functools.partial(cot_kernel, width, rep_count),
        out_shape=out_shape,
        grid_spec=pltpu.PrefetchScalarGridSpec(
            num_scalar_prefetch=1,
            grid=(1,),
            in_specs=[whole(shares), whole(squares), whole(value_cot)],
            out_specs=[pl.BlockSpec(array.shape, lambda i, p: (0, 0)) for array in out_shape],
        ),
        cost_estimate=NOMINAL,
        compiler_params=pltpu.CompilerParams(vmem_limit_bytes=PAIR_VMEM),
    )(info, shares, squares, value_cot)


def per_device(
    residual,
    norm_gain,
    value_weight,
    value_cot,
    trainee_logp,
    ref_shard_max,
    ref_shard_sum,
    ref_target_logit,
    target_ids,
    lengths,
):
    rows_here, width = residual.shape
    features = value_cot.shape[1]
    tp_count = lax.axis_size("tp")
    outer, inner = lax.axis_size("outer"), lax.axis_size("inner")
    rep_count = outer * inner * CORES
    tp_place = lax.axis_index("tp")
    core = lax.axis_index("core")
    at_inner = lax.axis_index("inner")
    at_outer = lax.axis_index("outer")
    rep_place = (at_outer * inner + at_inner) * CORES + core
    depth = width // rep_count
    rows = depth // tp_count
    order = list(range(tp_count))
    in_place = rows % 128 == 0 and outer == 2 and inner == 2

    gained = (value_weight.astype(F32) * norm_gain.astype(F32)[:, None]).astype(BF16)
    residual, gained = lax.optimization_barrier((residual, gained))
    squares = row_squares(residual)

    def near_of(k, block):
        first = "inner" if inner_first(k) else "outer"
        return [swap(block, first, s) for s in range(1, lax.axis_size(first))]

    def far_of(k, block, nears):
        second = "outer" if inner_first(k) else "inner"
        near = jnp.stack([block] + nears)
        return [near] + [swap(near, second, s) for s in range(1, lax.axis_size(second))]

    owned = jnp.where(
        target_ids // (VOCAB // tp_count) == tp_place,
        ref_target_logit[0],
        jnp.zeros_like(ref_target_logit[0]),
    )
    packed = jnp.concatenate([ref_shard_max[0], ref_shard_sum[0], owned, trainee_logp])
    packed = packed.reshape(1, -1, 128)
    own_pieces, near = {}, {}
    arrived = {0: gained, 1: trade(gained, "tp", 1), 2: trade(gained, "tp", 2)}
    near[0] = near_of(0, gained)
    packed = jnp.concatenate([packed, trade(packed, "tp", 1)])
    arrived[1], near[0], packed, squares, late_gained = lax.optimization_barrier(
        (arrived[1], near[0], packed, squares, gained)
    )
    near[1] = near_of(1, arrived[1])
    for k in order[3:]:
        arrived[k] = trade(late_gained, "tp", k)
    mask = 2
    while mask < tp_count:
        packed = jnp.concatenate([packed, trade(packed, "tp", mask)])
        mask *= 2
    near[1], arrived[2], packed = lax.optimization_barrier((near[1], arrived[2], packed))
    own_pieces[1] = far_of(1, arrived[1], near[1])
    near[2] = near_of(2, arrived[2])
    own_pieces[0] = far_of(0, gained, near[0])
    seq_length = lax.dynamic_index_in_dim(lengths, rep_place, keepdims=False)
    info = jnp.stack([tp_place, seq_length]).astype(jnp.int32)
    cot, cot_t, inv_rms = scaled_cot(width, rep_count, info, packed, squares, value_cot)

    def place_of(o, i, c, k):
        chip = lax.rem(at_outer + o, outer) * inner + lax.rem(at_inner + i, inner)
        return (chip * CORES + c) * tp_count + lax.rem(tp_place + k, tp_count)

    chips = [(o, i) for o in range(outer) for i in range(inner)]
    if not in_place:
        product = jnp.dot(cot_t, residual, preferred_element_type=F32).astype(BF16)
        product = product.reshape(features, -1, rows).transpose(1, 0, 2)

    def places_of(pair, c):
        return jnp.stack([place_of(o, i, c, k) for o, i in chips for k in pair]).astype(jnp.int32)

    def for_other(pair, cot_t):
        places = places_of(pair, 1 - core)
        both = after(product, cot_t)[places].reshape(len(chips), 2, features, rows)
        return both.swapaxes(0, 1)

    def for_us(pair, other):
        places = places_of(pair, core)
        if in_place:
            send_a, keep_a, send_b, keep_b = ours_product(residual, cot_t, places, rows, other)
            return ([send_a], keep_a), ([send_b], keep_b)
        both = product[places].reshape(len(chips), 2, features, rows).swapaxes(0, 1)
        total = widen([both, other]).astype(BF16).reshape(2, outer, inner, features, rows)
        first = ([total[0, :, s] for s in range(1, inner)], total[0, :, 0])
        second = ([total[1, s] for s in range(1, outer)], total[1, 0])
        return first, second

    def first_round(sides):
        return [
            [swap(send, axis, s + 1) for s, send in enumerate(sends)]
            for axis, (sends, _) in zip(("inner", "outer"), sides)
        ]

    def second_round(sides, got):
        later = []
        for axis, (_, keep), parts in zip(("outer", "inner"), sides, got):
            later.append(
                [
                    swap(widen([part[s] for part in [keep] + parts]).astype(BF16), axis, s)
                    for s in range(1, lax.axis_size(axis))
                ]
            )
        return later

    def summed(sides, got, later):
        return [
            widen([part[0] for part in [keep] + parts] + last)
            for (_, keep), parts, last in zip(sides, got, later)
        ]

    backward = order[::-1]
    pairs = [backward[i : i + 2] for i in range(0, tp_count, 2)]
    def for_others(part, cot_t):
        if in_place:
            return theirs_product(residual, cot_t, places_of(part, 1 - core), rows)
        return [for_other(part, cot_t)]

    theirs = for_others(pairs[0], cot_t)
    theirs, arrived[3] = lax.optimization_barrier((theirs, arrived[3]))
    near[3] = near_of(3, arrived[3])
    for pair in pairs[1:]:
        theirs += for_others(pair, after(cot_t, theirs))
    near[2], near[3], theirs, own_pieces[0], own_pieces[1] = lax.optimization_barrier(
        (near[2], near[3], theirs, own_pieces[0], own_pieces[1])
    )
    others = [swap(part, "core", 1) for part in theirs]
    own_pieces[2] = far_of(2, arrived[2], near[2])
    sides = [for_us(pairs[0], others[0])]
    near[3], sides[0] = lax.optimization_barrier((near[3], sides[0]))
    own_pieces[3] = far_of(3, arrived[3], near[3])
    got = [first_round(sides[0])]
    sides.append(for_us(pairs[1], after(others[1], sides[0])))
    for n in range(2, len(pairs)):
        for k in order[2 * n : 2 * n + 2]:
            own_pieces[k] = far_of(k, arrived[k], near_of(k, arrived[k]))
        sides.append(for_us(pairs[n], others[n]))
    sides[1:], own_pieces = lax.optimization_barrier((sides[1:], own_pieces))

    if in_place:
        pieces = [piece for k in order for piece in own_pieces[k]]
        flags = tuple(inner_first(k) for k in order)
        places = [
            jnp.stack([place_of(o, i, c, 0) // tp_count for o, i in chips]).astype(jnp.int32)
            for c in (core, 1 - core)
        ]
        offsets = jnp.stack([jnp.bitwise_xor(tp_place, k) * rows for k in order]).astype(jnp.int32)
        total, own_weight = first_value(flags, places[0], offsets, residual, pieces)
    else:
        weight = []
        for k in order:
            both = jnp.stack(own_pieces[k])
            weight.append(both if inner_first(k) else jnp.swapaxes(both, 0, 1))
        weight = jnp.stack(weight)[jnp.bitwise_xor(tp_place, jnp.arange(tp_count))]
        weight = weight[:, (at_outer - jnp.arange(outer)) % outer]
        weight = weight[:, :, (at_inner - jnp.arange(inner)) % inner]
        own_weight = weight.transpose(1, 2, 0, 3, 4).reshape(outer * inner, depth, features)
        total = jnp.zeros((), F32)
    got[0], sides[1:], total, own_weight = lax.optimization_barrier(
        (got[0], sides[1:], total, own_weight)
    )
    other_weight = swap(own_weight, "core", 1)
    later = [second_round(sides[0], got[0])]
    got += [first_round(side) for side in sides[1:]]
    if in_place:
        value_proj, coefficient = weight_call(
            functools.partial(value_end_kernel, width),
            places[1],
            residual,
            other_weight,
            [total, cot, inv_rms],
            [
                jax.ShapeDtypeStruct((rows_here, features), BF16),
                jax.ShapeDtypeStruct((rows_here, 1), F32),
            ],
        )
    else:
        both = jnp.stack([own_weight, other_weight], axis=1)
        weight = jnp.where(core == 0, both, both[:, ::-1]).reshape(width, features)
        value_acc = jnp.dot(residual, weight, preferred_element_type=F32)
        value_proj = (inv_rms * value_acc).astype(BF16)
        share = jnp.sum(cot.astype(F32) * value_acc, axis=1, keepdims=True)
        coefficient = inv_rms * inv_rms * share * (1.0 / width)
    later[0], coefficient = lax.optimization_barrier((later[0], coefficient))
    sums = dict(zip(pairs[0], summed(sides[0], got[0], later[0])))
    last = [swap(sums[k].astype(BF16), "tp", k) for k in pairs[0]]
    got[1:], coefficient, sums = lax.optimization_barrier((got[1:], coefficient, sums))
    later += [second_round(side, parts) for side, parts in zip(sides[1:], got[1:])]
    if in_place:
        grad_shape = jax.ShapeDtypeStruct((rows_here, width), BF16)
        resid_grad = weight_call(
            grad_kernel, places[0], residual, in_hbm(own_weight), [cot, coefficient], grad_shape
        )
        later[1], coefficient, resid_grad = lax.optimization_barrier((later[1], coefficient, resid_grad))
    else:
        normed_grad = lax.dot_general(
            cot, weight, (((1,), (1,)), ((), ())), preferred_element_type=F32
        )
        resid_grad = (normed_grad - residual.astype(F32) * coefficient).astype(BF16)
    for pair, *rounds in zip(pairs[1:], sides[1:], got[1:], later[1:]):
        sums.update(zip(pair, summed(*rounds)))
    last += [swap(sums[k].astype(BF16), "tp", k) for k in backward[2:-1]]
    if in_place:
        resid_grad = weight_call(
            grad_kernel, places[1], residual, other_weight, [cot, coefficient], grad_shape, resid_grad
        )
    grad_rows = widen([sums[0]] + last)
    late_gain, late_weight, grad_rows = lax.optimization_barrier((norm_gain, value_weight, grad_rows))
    weight_grad = (late_gain.astype(F32)[None, :] * grad_rows).T
    gain_grad = jnp.sum(late_weight.astype(F32).T * grad_rows, axis=0)
    return (value_proj, resid_grad, weight_grad, gain_grad)


def solution(mesh):
    rep_count, tp_count = mesh.shape["rep"], mesh.shape["tp"]
    split = jax.sharding.Mesh(
        mesh.devices.reshape(OUTER, rep_count // (OUTER * CORES), CORES, tp_count),
        ("outer", "inner", "core", "tp"),
    )
    rep = ("outer", "inner", "core")
    rows = rep + ("tp",)
    return jax.shard_map(
        per_device,
        mesh=split,
        in_specs=(
            P(rows, None),
            P(rows),
            P(rows, None),
            P(rows, None),
            P(rows),
            P("tp", rep),
            P("tp", rep),
            P("tp", rep),
            P(rep),
            P(),
        ),
        out_specs=(P(rows, None), P(rows, None), P(rows, None), P(rows)),
        check_vma=False,
    )
```

```python
import functools

import jax
import jax.numpy as jnp
from jax import lax
from jax.experimental import pallas as pl
from jax.experimental.pallas import tpu as pltpu
from jax.sharding import PartitionSpec as P

VOCAB = 128256
EPS = 1e-05
BETA = 0.5
CORES = 2
OUTER = 2
PAIR_VMEM = 14 * 1024 * 1024
WEIGHT_VMEM = 22 * 1024 * 1024
NOMINAL = pl.CostEstimate(flops=1024, bytes_accessed=1024, transcendentals=0)
BF16 = jnp.bfloat16
F32 = jnp.float32


def swap(value, axis, step):
    size = lax.axis_size(axis)
    return lax.ppermute(value, axis, [(place, (place + step) % size) for place in range(size)])


def trade(value, axis, mask):
    size = lax.axis_size(axis)
    return lax.ppermute(value, axis, [(place, place ^ mask) for place in range(size)])


def in_hbm(array):
    return pltpu.with_memory_space_constraint(array, pltpu.HBM)


def in_vmem(array):
    return pltpu.with_memory_space_constraint(array, pltpu.VMEM)


def after(value, *earlier):
    return lax.optimization_barrier((value, earlier))[0]


def widen(parts):
    return functools.reduce(jnp.add, [part.astype(F32) for part in parts])


def chunk_shifts(tp_count):
    shifts = [0]
    for step in range(1, tp_count // 2 + 1):
        shifts += [step] if 2 * step == tp_count else [step, tp_count - step]
    return shifts


def inner_first(chunk):
    return chunk % 2 == 0


def theirs_kernel(places_ref, cot_ref, *rest):
    count = len(rest) * 2 // 3
    blocks, outs = rest[:count], rest[count:]
    for slot, resid_ref in enumerate(blocks):
        product = jnp.dot(cot_ref[...], resid_ref[...], preferred_element_type=F32)
        outs[slot // 2][slot % 2, 0] = product.astype(BF16)


def theirs_product(residual, cot_t, places, rows):
    features, tokens = cot_t.shape
    steps = 4
    slots = places.shape[0] // steps
    block = pl.BlockSpec((2, 1, features, rows), lambda i, p: (0, i, 0, 0))
    return pl.pallas_call(
        theirs_kernel,
        out_shape=[pltpu.HBM((2, steps, features, rows), BF16)] * (slots // 2),
        grid_spec=pltpu.PrefetchScalarGridSpec(
            num_scalar_prefetch=1,
            grid=(steps,),
            in_specs=[pl.BlockSpec((features, tokens), lambda i, p: (0, 0))]
            + [
                pl.BlockSpec((tokens, rows), lambda i, p, slot=slot: (0, p[slots * i + slot]))
                for slot in range(slots)
            ],
            out_specs=[block] * (slots // 2),
        ),
        cost_estimate=NOMINAL,
        compiler_params=pltpu.CompilerParams(vmem_limit_bytes=PAIR_VMEM),
    )(places, cot_t, *[in_vmem(residual)] * slots)


def ours_kernel(places_ref, cot_ref, first_ref, second_ref, other_ref, *outs):
    step = pl.program_id(0)
    at_outer, at_inner = step // 2, lax.rem(step, 2)
    totals = [
        (
            jnp.dot(cot_ref[...], resid_ref[...], preferred_element_type=F32)
            + other_ref[slot, 0].astype(F32)
        ).astype(BF16)
        for slot, resid_ref in enumerate((first_ref, second_ref))
    ]
    for slot, way in enumerate((at_inner, at_outer)):
        send_ref, keep_ref = outs[2 * slot : 2 * slot + 2]

        @pl.when(way == 1)
        def _():
            send_ref[0] = totals[slot]

        @pl.when(way == 0)
        def _():
            keep_ref[0] = totals[slot]


def ours_product(residual, cot_t, places, rows, other):
    features, tokens = cot_t.shape
    steps = places.shape[0] // 2
    indices = [lambda i: i // 2, lambda i: i // 2, lambda i: jnp.maximum(i - 2, 0), lambda i: jnp.minimum(i, 1)]
    return pl.pallas_call(
        ours_kernel,
        out_shape=[pltpu.HBM((2, features, rows), BF16)] * 4,
        grid_spec=pltpu.PrefetchScalarGridSpec(
            num_scalar_prefetch=1,
            grid=(steps,),
            in_specs=[
                pl.BlockSpec((features, tokens), lambda i, p: (0, 0)),
                pl.BlockSpec((tokens, rows), lambda i, p: (0, p[2 * i])),
                pl.BlockSpec((tokens, rows), lambda i, p: (0, p[2 * i + 1])),
                pl.BlockSpec((2, 1, features, rows), lambda i, p: (0, i, 0, 0)),
            ],
            out_specs=[
                pl.BlockSpec((1, features, rows), lambda i, p, index=index: (index(i), 0, 0))
                for index in indices
            ],
        ),
        cost_estimate=NOMINAL,
        compiler_params=pltpu.CompilerParams(vmem_limit_bytes=PAIR_VMEM),
    )(places, cot_t, in_vmem(residual), in_vmem(residual), other)


def place_weight(inner_flags, offsets_ref, pieces, weight_ref):
    step = pl.program_id(0)
    at_outer, at_inner = step // 2, lax.rem(step, 2)
    rows = pieces[0].shape[1]
    for chunk, flag in enumerate(inner_flags):
        way = at_outer if flag else at_inner
        where = pl.ds(pl.multiple_of(offsets_ref[chunk], rows), rows)
        for late in range(2):
            piece = pieces[chunk * 2 + late]

            @pl.when(way == late)
            def _():
                weight_ref[0, where, :] = piece[0]


def piece_specs(inner_flags, rows, features):
    specs = []
    for flag in inner_flags:
        for late in range(2):
            if flag:
                index = lambda i, *_, first=2 * late: (jnp.clip(i - first, 0, 1), 0, 0)
            else:
                index = lambda i, *_: (i // 2, 0, 0)
            specs.append(pl.BlockSpec((1, rows, features), index))
    return specs


def value_kernel(inner_flags, places_ref, offsets_ref, resid_ref, *rest):
    pieces, (total_ref, weight_ref) = rest[:-2], rest[-2:]
    step = pl.program_id(0)
    place_weight(inner_flags, offsets_ref, pieces, weight_ref)
    product = jnp.dot(resid_ref[...], weight_ref[0], preferred_element_type=F32)

    @pl.when(step == 0)
    def _():
        total_ref[...] = product

    @pl.when(step > 0)
    def _():
        total_ref[...] += product


def value_end_kernel(
    width, places_ref, resid_ref, weight_ref, first_ref, cot_ref, inv_ref, value_ref, coef_ref, total_ref
):
    step = pl.program_id(0)
    product = jnp.dot(resid_ref[...], weight_ref[0], preferred_element_type=F32)

    @pl.when(step == 0)
    def _():
        total_ref[...] = first_ref[...] + product

    @pl.when(step > 0)
    def _():
        total_ref[...] += product

    @pl.when(step == pl.num_programs(0) - 1)
    def _():
        total = total_ref[...]
        inv = inv_ref[...]
        value_ref[...] = (total * inv).astype(BF16)
        share = jnp.sum(total * cot_ref[...].astype(F32), axis=1, keepdims=True)
        coef_ref[...] = share * (inv * inv) * (1.0 / width)


def grad_kernel(places_ref, resid_ref, weight_ref, cot_ref, coef_ref, *rest):
    out_ref = rest[-1]
    grad = lax.dot_general(
        cot_ref[...], weight_ref[0], (((1,), (1,)), ((), ())), preferred_element_type=F32
    )
    out_ref[...] = (grad - resid_ref[...].astype(F32) * coef_ref[...]).astype(BF16)


def whole_block(array):
    return pl.BlockSpec(array.shape, lambda i, *_: (0, 0))


def first_value(inner_flags, places, offsets, residual, pieces):
    tokens, width = residual.shape
    rows, features = pieces[0].shape[1:]
    steps = places.shape[0]
    depth = width // (CORES * steps)
    total = jax.ShapeDtypeStruct((tokens, features), F32)
    return pl.pallas_call(
        functools.partial(value_kernel, inner_flags),
        out_shape=[total, pltpu.VMEM((steps, depth, features), BF16)],
        grid_spec=pltpu.PrefetchScalarGridSpec(
            num_scalar_prefetch=2,
            grid=(steps,),
            in_specs=[pl.BlockSpec((tokens, depth), lambda i, p, o: (0, p[i]))]
            + piece_specs(inner_flags, rows, features),
            out_specs=[
                whole_block(total),
                pl.BlockSpec((1, depth, features), lambda i, p, o: (p[i] // CORES, 0, 0)),
            ],
        ),
        cost_estimate=NOMINAL,
        compiler_params=pltpu.CompilerParams(vmem_limit_bytes=WEIGHT_VMEM),
    )(places, offsets, in_vmem(residual), *pieces)


def weight_call(kernel, places, residual, weight, wholes, out_shape, earlier=None):
    tokens, width = residual.shape
    steps, depth, features = weight.shape
    scratch = []
    if isinstance(out_shape, list):
        out_specs = [whole_block(array) for array in out_shape]
        scratch.append(pltpu.VMEM((tokens, features), F32))
    else:
        out_specs = pl.BlockSpec((tokens, depth), lambda i, p: (0, p[i]))
    in_specs = [
        pl.BlockSpec((tokens, depth), lambda i, p: (0, p[i])),
        pl.BlockSpec((1, depth, features), lambda i, p: (p[i] // CORES, 0, 0)),
    ] + [whole_block(array) for array in wholes]
    operands = [places, in_vmem(residual), in_vmem(weight), *wholes]
    aliases = {}
    if earlier is not None:
        aliases = {len(operands): 0}
        in_specs.append(pl.BlockSpec(memory_space=pltpu.HBM))
        operands.append(earlier)
    return pl.pallas_call(
        kernel,
        out_shape=out_shape,
        grid_spec=pltpu.PrefetchScalarGridSpec(
            num_scalar_prefetch=1,
            grid=(steps,),
            in_specs=in_specs,
            out_specs=out_specs,
            scratch_shapes=scratch,
        ),
        input_output_aliases=aliases,
        cost_estimate=NOMINAL,
        compiler_params=pltpu.CompilerParams(vmem_limit_bytes=WEIGHT_VMEM),
    )(*operands)


def squares_kernel(resid_ref, out_ref, kept_ref):
    block = resid_ref[...]
    kept_ref[...] = block
    wide = block.astype(F32)
    out_ref[...] = jnp.sum(wide * wide, axis=1, keepdims=True)


def row_squares(residual):
    tokens, width = residual.shape
    rows = 64
    block = pl.BlockSpec((rows, width), lambda i: (i, 0))
    return pl.pallas_call(
        squares_kernel,
        out_shape=[jax.ShapeDtypeStruct((tokens, 1), F32), pltpu.VMEM((tokens, width), BF16)],
        grid=(tokens // rows,),
        in_specs=[block],
        out_specs=[pl.BlockSpec((rows, 1), lambda i: (i, 0)), block],
        cost_estimate=NOMINAL,
        compiler_params=pltpu.CompilerParams(vmem_limit_bytes=PAIR_VMEM),
    )(in_hbm(residual))


def cot_kernel(width, rep_count, info_ref, shares_ref, squares_ref, value_cot_ref, cot_ref, cot_t_ref, inv_ref):
    place, length = info_ref[0], info_ref[1]
    rows = value_cot_ref.shape[0]
    own = rows // 128
    seq = (shares_ref.shape[1] - own) // 3
    shares = range(shares_ref.shape[0])

    def below(first, shape):
        at = lax.broadcasted_iota(jnp.int32, shape, 0) * 128 + lax.broadcasted_iota(jnp.int32, shape, 1)
        return first + at < length

    def summed(mask, value):
        return jnp.sum(jnp.where(mask, value, 0.0), axis=(0, 1), keepdims=True)

    maxes = [shares_ref[m, 0:seq] for m in shares]
    top_max = functools.reduce(jnp.maximum, maxes)
    sum_exp = functools.reduce(
        jnp.add, [shares_ref[m, seq : 2 * seq] * jnp.exp(maxes[m] - top_max) for m in shares]
    )
    picked = functools.reduce(jnp.add, [shares_ref[m, 2 * seq : 3 * seq] for m in shares])
    ref_logp = picked - top_max - jnp.log(sum_exp)
    total = -summed(below(0, (seq, 128)), ref_logp)
    for m in shares:
        first = jnp.bitwise_xor(place, m) * rows
        total += summed(below(first, (own, 128)), shares_ref[m, 3 * seq :])
    seq_delta = total / jnp.full((1, 1), length, jnp.int32).astype(F32)
    weight = (2.0 / rep_count) * jax.nn.sigmoid(BETA * seq_delta)
    inv = lax.rsqrt(squares_ref[...] * (1.0 / width) + EPS)
    live = place * rows + lax.broadcasted_iota(jnp.int32, (rows, 1), 0) < length
    scaled = jnp.where(live, inv * weight, 0.0) * value_cot_ref[...].astype(F32)
    cot_ref[...] = scaled.astype(BF16)
    cot_t_ref[...] = scaled.T.astype(BF16)
    inv_ref[...] = inv


def scaled_cot(width, rep_count, info, shares, squares, value_cot):
    rows, features = value_cot.shape

    def whole(array):
        return pl.BlockSpec(array.shape, lambda i, p: (0,) * array.ndim)

    out_shape = [
        jax.ShapeDtypeStruct((rows, features), BF16),
        jax.ShapeDtypeStruct((features, rows), BF16),
        jax.ShapeDtypeStruct((rows, 1), F32),
    ]
    return pl.pallas_call(
        functools.partial(cot_kernel, width, rep_count),
        out_shape=out_shape,
        grid_spec=pltpu.PrefetchScalarGridSpec(
            num_scalar_prefetch=1,
            grid=(1,),
            in_specs=[whole(shares), whole(squares), whole(value_cot)],
            out_specs=[pl.BlockSpec(array.shape, lambda i, p: (0, 0)) for array in out_shape],
        ),
        cost_estimate=NOMINAL,
        compiler_params=pltpu.CompilerParams(vmem_limit_bytes=PAIR_VMEM),
    )(info, shares, squares, value_cot)


def per_device(
    residual,
    norm_gain,
    value_weight,
    value_cot,
    trainee_logp,
    ref_shard_max,
    ref_shard_sum,
    ref_target_logit,
    target_ids,
    lengths,
):
    rows_here, width = residual.shape
    features = value_cot.shape[1]
    tp_count = lax.axis_size("tp")
    outer, inner = lax.axis_size("outer"), lax.axis_size("inner")
    rep_count = outer * inner * CORES
    tp_place = lax.axis_index("tp")
    core = lax.axis_index("core")
    at_inner = lax.axis_index("inner")
    at_outer = lax.axis_index("outer")
    rep_place = (at_outer * inner + at_inner) * CORES + core
    depth = width // rep_count
    rows = depth // tp_count
    order = list(range(tp_count))
    shifts = chunk_shifts(tp_count)
    in_place = rows % 128 == 0 and outer == 2 and inner == 2

    owned = jnp.where(
        target_ids // (VOCAB // tp_count) == tp_place,
        ref_target_logit[0],
        jnp.zeros_like(ref_target_logit[0]),
    )
    packed = jnp.concatenate([ref_shard_max[0], ref_shard_sum[0], owned, trainee_logp])
    packed = packed.reshape(1, -1, 128)
    packed = jnp.concatenate([packed, trade(packed, "tp", 1)])

    gained = (value_weight.astype(F32) * norm_gain.astype(F32)[:, None]).astype(BF16)
    residual, gained, packed = lax.optimization_barrier((residual, gained, packed))
    squares, residual = row_squares(residual)

    def near_of(k, block):
        first = "inner" if inner_first(k) else "outer"
        return [swap(block, first, s) for s in range(1, lax.axis_size(first))]

    def far_of(k, block, nears):
        second = "outer" if inner_first(k) else "inner"
        near = jnp.stack([block] + nears)
        return [near] + [swap(near, second, s) for s in range(1, lax.axis_size(second))]

    mask = 2
    while mask < tp_count:
        packed = jnp.concatenate([packed, trade(packed, "tp", mask)])
        mask *= 2
    own_pieces, near = {}, {}
    arrived = {0: gained, 1: swap(gained, "tp", shifts[1])}
    near[0] = near_of(0, gained)
    arrived[1], near[0], packed, squares, late_gained = lax.optimization_barrier(
        (arrived[1], near[0], packed, squares, gained)
    )
    near[1] = near_of(1, arrived[1])
    arrived[2] = swap(late_gained, "tp", shifts[2])
    own_pieces[0] = far_of(0, gained, near[0])
    near[1], packed, late_gained = lax.optimization_barrier((near[1], packed, late_gained))
    for k in order[3:]:
        arrived[k] = swap(late_gained, "tp", shifts[k])
    own_pieces[1] = far_of(1, arrived[1], near[1])
    seq_length = lax.dynamic_index_in_dim(lengths, rep_place, keepdims=False)
    info = jnp.stack([tp_place, seq_length]).astype(jnp.int32)
    cot, cot_t, inv_rms = scaled_cot(width, rep_count, info, packed, squares, value_cot)

    def place_of(o, i, c, k):
        chip = lax.rem(at_outer + o, outer) * inner + lax.rem(at_inner + i, inner)
        return (chip * CORES + c) * tp_count + lax.rem(tp_place + k, tp_count)

    chips = [(o, i) for o in range(outer) for i in range(inner)]
    if not in_place:
        product = jnp.dot(cot_t, residual, preferred_element_type=F32).astype(BF16)
        product = product.reshape(features, -1, rows).transpose(1, 0, 2)

    def places_of(pair, c):
        return jnp.stack([place_of(o, i, c, k) for o, i in chips for k in pair]).astype(jnp.int32)

    def for_other(pair, cot_t):
        places = places_of(pair, 1 - core)
        both = after(product, cot_t)[places].reshape(len(chips), 2, features, rows)
        return both.swapaxes(0, 1)

    def for_us(pair, other):
        places = places_of(pair, core)
        if in_place:
            send_a, keep_a, send_b, keep_b = ours_product(residual, cot_t, places, rows, other)
            return ([send_a], keep_a), ([send_b], keep_b)
        both = product[places].reshape(len(chips), 2, features, rows).swapaxes(0, 1)
        total = widen([both, other]).astype(BF16).reshape(2, outer, inner, features, rows)
        first = ([total[0, :, s] for s in range(1, inner)], total[0, :, 0])
        second = ([total[1, s] for s in range(1, outer)], total[1, 0])
        return first, second

    def first_round(sides):
        return [
            [swap(send, axis, s + 1) for s, send in enumerate(sends)]
            for axis, (sends, _) in zip(("inner", "outer"), sides)
        ]

    def second_round(sides, got):
        later = []
        for axis, (_, keep), parts in zip(("outer", "inner"), sides, got):
            later.append(
                [
                    swap(widen([part[s] for part in [keep] + parts]).astype(BF16), axis, s)
                    for s in range(1, lax.axis_size(axis))
                ]
            )
        return later

    def summed(sides, got, later):
        return [
            widen([part[0] for part in [keep] + parts] + last)
            for (_, keep), parts, last in zip(sides, got, later)
        ]

    backward = order[::-1]
    pairs = [backward[i : i + 2] for i in range(0, tp_count, 2)]
    def for_others(part, cot_t):
        if in_place:
            return theirs_product(residual, cot_t, places_of(part, 1 - core), rows)
        return [for_other(part, cot_t)]

    theirs = for_others(pairs[0], cot_t)
    theirs, arrived[2] = lax.optimization_barrier((theirs, arrived[2]))
    near[2] = near_of(2, arrived[2])
    for pair in pairs[1:]:
        theirs += for_others(pair, after(cot_t, theirs))
    theirs, arrived[3] = lax.optimization_barrier((theirs, arrived[3]))
    near[3] = near_of(3, arrived[3])
    near[2], near[3], theirs, own_pieces[0], own_pieces[1] = lax.optimization_barrier(
        (near[2], near[3], theirs, own_pieces[0], own_pieces[1])
    )
    others = [swap(part, "core", 1) for part in theirs]
    own_pieces[2] = far_of(2, arrived[2], near[2])
    own_pieces[3] = far_of(3, arrived[3], near[3])
    sides = [for_us(pairs[0], others[0])]
    got = [first_round(sides[0])]
    sides.append(for_us(pairs[1], after(others[1], sides[0])))
    for n in range(2, len(pairs)):
        for k in order[2 * n : 2 * n + 2]:
            own_pieces[k] = far_of(k, arrived[k], near_of(k, arrived[k]))
        sides.append(for_us(pairs[n], others[n]))
    sides[1:], own_pieces = lax.optimization_barrier((sides[1:], own_pieces))

    if in_place:
        pieces = [piece for k in order for piece in own_pieces[k]]
        flags = tuple(inner_first(k) for k in order)
        places = [
            jnp.stack([place_of(o, i, c, 0) // tp_count for o, i in chips]).astype(jnp.int32)
            for c in (core, 1 - core)
        ]
        offsets = jnp.stack([lax.rem(tp_place - shift + tp_count, tp_count) * rows for shift in shifts])
        offsets = offsets.astype(jnp.int32)
        total, own_weight = first_value(flags, places[0], offsets, residual, pieces)
    else:
        weight = []
        for k in order:
            both = jnp.stack(own_pieces[k])
            weight.append(both if inner_first(k) else jnp.swapaxes(both, 0, 1))
        by_shift = jnp.array([shifts.index(shift) for shift in range(tp_count)])
        weight = jnp.stack(weight)[by_shift[(tp_place - jnp.arange(tp_count)) % tp_count]]
        weight = weight[:, (at_outer - jnp.arange(outer)) % outer]
        weight = weight[:, :, (at_inner - jnp.arange(inner)) % inner]
        own_weight = weight.transpose(1, 2, 0, 3, 4).reshape(outer * inner, depth, features)
        total = jnp.zeros((), F32)
    got[0], sides[1:], total, own_weight = lax.optimization_barrier(
        (got[0], sides[1:], total, own_weight)
    )
    other_weight = swap(own_weight, "core", 1)
    later = [second_round(sides[0], got[0])]
    got += [first_round(side) for side in sides[1:]]
    if in_place:
        value_proj, coefficient = weight_call(
            functools.partial(value_end_kernel, width),
            places[1],
            residual,
            other_weight,
            [total, cot, inv_rms],
            [
                jax.ShapeDtypeStruct((rows_here, features), BF16),
                jax.ShapeDtypeStruct((rows_here, 1), F32),
            ],
        )
    else:
        both = jnp.stack([own_weight, other_weight], axis=1)
        weight = jnp.where(core == 0, both, both[:, ::-1]).reshape(width, features)
        value_acc = jnp.dot(residual, weight, preferred_element_type=F32)
        value_proj = (inv_rms * value_acc).astype(BF16)
        share = jnp.sum(cot.astype(F32) * value_acc, axis=1, keepdims=True)
        coefficient = inv_rms * inv_rms * share * (1.0 / width)
    later[0], coefficient = lax.optimization_barrier((later[0], coefficient))
    sums = dict(zip(pairs[0], summed(sides[0], got[0], later[0])))
    last = [swap(sums[k].astype(BF16), "tp", k) for k in pairs[0]]
    got[1:], coefficient, sums = lax.optimization_barrier((got[1:], coefficient, sums))
    later += [second_round(side, parts) for side, parts in zip(sides[1:], got[1:])]
    if in_place:
        grad_shape = jax.ShapeDtypeStruct((rows_here, width), BF16)
        resid_grad = weight_call(
            grad_kernel, places[0], residual, own_weight, [cot, coefficient], grad_shape
        )
        later[1], coefficient, resid_grad = lax.optimization_barrier((later[1], coefficient, resid_grad))
    else:
        normed_grad = lax.dot_general(
            cot, weight, (((1,), (1,)), ((), ())), preferred_element_type=F32
        )
        resid_grad = (normed_grad - residual.astype(F32) * coefficient).astype(BF16)
    for pair, *rounds in zip(pairs[1:], sides[1:], got[1:], later[1:]):
        sums.update(zip(pair, summed(*rounds)))
    last += [swap(sums[k].astype(BF16), "tp", k) for k in backward[2:-1]]
    if in_place:
        resid_grad = weight_call(
            grad_kernel, places[1], residual, other_weight, [cot, coefficient], grad_shape, resid_grad
        )
    grad_rows = widen([sums[0]] + last)
    late_gain, late_weight, grad_rows = lax.optimization_barrier((norm_gain, value_weight, grad_rows))
    weight_grad = (late_gain.astype(F32)[None, :] * grad_rows).T
    gain_grad = jnp.sum(late_weight.astype(F32).T * grad_rows, axis=0)
    return (value_proj, resid_grad, weight_grad, gain_grad)


def solution(mesh):
    rep_count, tp_count = mesh.shape["rep"], mesh.shape["tp"]
    split = jax.sharding.Mesh(
        mesh.devices.reshape(OUTER, rep_count // (OUTER * CORES), CORES, tp_count),
        ("outer", "inner", "core", "tp"),
    )
    rep = ("outer", "inner", "core")
    rows = rep + ("tp",)
    return jax.shard_map(
        per_device,
        mesh=split,
        in_specs=(
            P(rows, None),
            P(rows),
            P(rows, None),
            P(rows, None),
            P(rows),
            P("tp", rep),
            P("tp", rep),
            P("tp", rep),
            P(rep),
            P(),
        ),
        out_specs=(P(rows, None), P(rows, None), P(rows, None), P(rows)),
        check_vma=False,
    )
```

```python
import functools

import jax
import jax.numpy as jnp
from jax import lax
from jax.experimental import pallas as pl
from jax.experimental.pallas import tpu as pltpu
from jax.sharding import PartitionSpec as P

VOCAB = 128256
EPS = 1e-05
BETA = 0.5
CORES = 2
OUTER = 2
PAIR_VMEM = 18 * 1024 * 1024
WEIGHT_VMEM = 22 * 1024 * 1024
NOMINAL = pl.CostEstimate(flops=1024, bytes_accessed=1024, transcendentals=0)
BF16 = jnp.bfloat16
F32 = jnp.float32


def swap(value, axis, step):
    size = lax.axis_size(axis)
    return lax.ppermute(value, axis, [(place, (place + step) % size) for place in range(size)])


def trade(value, axis, mask):
    size = lax.axis_size(axis)
    return lax.ppermute(value, axis, [(place, place ^ mask) for place in range(size)])


def in_hbm(array):
    return pltpu.with_memory_space_constraint(array, pltpu.HBM)


def after(value, *earlier):
    return lax.optimization_barrier((value, earlier))[0]


def widen(parts):
    return functools.reduce(jnp.add, [part.astype(F32) for part in parts])


def chunk_shifts(tp_count):
    shifts = [0]
    for step in range(1, tp_count // 2 + 1):
        shifts += [step] if 2 * step == tp_count else [step, tp_count - step]
    return shifts


def inner_first(chunk):
    return chunk % 2 == 0


def theirs_kernel(places_ref, cot_ref, *rest):
    blocks, out_ref = rest[:-1], rest[-1]
    for slot, resid_ref in enumerate(blocks):
        product = jnp.dot(cot_ref[...], resid_ref[...], preferred_element_type=F32)
        out_ref[slot, 0] = product.astype(BF16)


def ours_kernel(places_ref, cot_ref, *rest):
    slots = len(rest) // 3
    blocks, other_ref, outs = rest[:slots], rest[slots], rest[slots + 1 :]
    step = pl.program_id(0)
    ways = (lax.rem(step, 2), step // 2)
    totals = [
        (
            jnp.dot(cot_ref[...], resid_ref[...], preferred_element_type=F32)
            + other_ref[slot, 0].astype(F32)
        ).astype(BF16)
        for slot, resid_ref in enumerate(blocks)
    ]
    for which, way in enumerate(ways):

        @pl.when(way == 1)
        def _():
            for slot in range(which, slots, 2):
                outs[2 * slot][0] = totals[slot]

        @pl.when(way == 0)
        def _():
            for slot in range(which, slots, 2):
                outs[2 * slot + 1][0] = totals[slot]


def grad_product(residual, cot_t, places, rows, other):
    features, tokens = cot_t.shape
    steps = 4
    slots = places.shape[0] // steps
    in_specs = [pl.BlockSpec((features, tokens), lambda i, p: (0, 0))] + [
        pl.BlockSpec((tokens, rows), lambda i, p, slot=slot: (0, p[slots * i + slot]))
        for slot in range(slots)
    ]
    operands = [places, cot_t] + [in_hbm(residual)] * slots
    block = pl.BlockSpec((slots, 1, features, rows), lambda i, p: (0, i, 0, 0))
    if other is None:
        kernel, out_specs = theirs_kernel, block
        out_shape = pltpu.HBM((slots, steps, features, rows), BF16)
    else:
        kernel = ours_kernel
        in_specs.append(block)
        operands.append(other)
        indices = [
            lambda i: i // 2,
            lambda i: i // 2,
            lambda i: jnp.maximum(i - 2, 0),
            lambda i: jnp.minimum(i, 1),
        ]
        out_specs = [
            pl.BlockSpec((1, features, rows), lambda i, p, index=index: (index(i), 0, 0))
            for index in indices
        ] * (slots // 2)
        out_shape = [pltpu.HBM((2, features, rows), BF16)] * (2 * slots)
    return pl.pallas_call(
        kernel,
        out_shape=out_shape,
        grid_spec=pltpu.PrefetchScalarGridSpec(
            num_scalar_prefetch=1, grid=(steps,), in_specs=in_specs, out_specs=out_specs
        ),
        cost_estimate=NOMINAL,
        compiler_params=pltpu.CompilerParams(vmem_limit_bytes=PAIR_VMEM),
    )(*operands)


def place_weight(inner_flags, offsets_ref, pieces, weight_ref):
    step = pl.program_id(0)
    at_outer, at_inner = step // 2, lax.rem(step, 2)
    rows = pieces[0].shape[1]
    for chunk, flag in enumerate(inner_flags):
        way = at_outer if flag else at_inner
        where = pl.ds(pl.multiple_of(offsets_ref[chunk], rows), rows)
        for late in range(2):
            piece = pieces[chunk * 2 + late]

            @pl.when(way == late)
            def _():
                weight_ref[0, where, :] = piece[0]


def piece_specs(inner_flags, rows, features):
    specs = []
    for flag in inner_flags:
        for late in range(2):
            if flag:
                index = lambda i, *_, first=2 * late: (jnp.clip(i - first, 0, 1), 0, 0)
            else:
                index = lambda i, *_: (i // 2, 0, 0)
            specs.append(pl.BlockSpec((1, rows, features), index))
    return specs


def value_kernel(inner_flags, places_ref, offsets_ref, resid_ref, *rest):
    pieces, (total_ref, weight_ref) = rest[:-2], rest[-2:]
    step = pl.program_id(0)
    place_weight(inner_flags, offsets_ref, pieces, weight_ref)
    product = jnp.dot(resid_ref[...], weight_ref[0], preferred_element_type=F32)

    @pl.when(step == 0)
    def _():
        total_ref[...] = product

    @pl.when(step > 0)
    def _():
        total_ref[...] += product


def value_end_kernel(
    width, places_ref, resid_ref, weight_ref, first_ref, cot_ref, inv_ref, value_ref, coef_ref, total_ref
):
    step = pl.program_id(0)
    product = jnp.dot(resid_ref[...], weight_ref[0], preferred_element_type=F32)

    @pl.when(step == 0)
    def _():
        total_ref[...] = first_ref[...] + product

    @pl.when(step > 0)
    def _():
        total_ref[...] += product

    @pl.when(step == pl.num_programs(0) - 1)
    def _():
        total = total_ref[...]
        inv = inv_ref[...]
        value_ref[...] = (total * inv).astype(BF16)
        share = jnp.sum(total * cot_ref[...].astype(F32), axis=1, keepdims=True)
        coef_ref[...] = share * (inv * inv) * (1.0 / width)


def grad_kernel(places_ref, resid_ref, weight_ref, cot_ref, coef_ref, *rest):
    out_ref = rest[-1]
    grad = lax.dot_general(
        cot_ref[...], weight_ref[0], (((1,), (1,)), ((), ())), preferred_element_type=F32
    )
    out_ref[...] = (grad - resid_ref[...].astype(F32) * coef_ref[...]).astype(BF16)


def whole_block(array):
    return pl.BlockSpec(array.shape, lambda i, *_: (0, 0))


def first_value(inner_flags, places, offsets, residual, pieces):
    tokens, width = residual.shape
    rows, features = pieces[0].shape[1:]
    steps = places.shape[0]
    depth = width // (CORES * steps)
    total = pltpu.HBM((tokens, features), F32)
    return pl.pallas_call(
        functools.partial(value_kernel, inner_flags),
        out_shape=[total, pltpu.HBM((steps, depth, features), BF16)],
        grid_spec=pltpu.PrefetchScalarGridSpec(
            num_scalar_prefetch=2,
            grid=(steps,),
            in_specs=[pl.BlockSpec((tokens, depth), lambda i, p, o: (0, p[i]))]
            + piece_specs(inner_flags, rows, features),
            out_specs=[
                whole_block(total),
                pl.BlockSpec((1, depth, features), lambda i, p, o: (p[i] // CORES, 0, 0)),
            ],
        ),
        cost_estimate=NOMINAL,
        compiler_params=pltpu.CompilerParams(vmem_limit_bytes=WEIGHT_VMEM),
    )(places, offsets, in_hbm(residual), *pieces)


def weight_call(kernel, places, residual, weight, wholes, out_shape, earlier=None):
    tokens, width = residual.shape
    steps, depth, features = weight.shape
    scratch = []
    if isinstance(out_shape, list):
        out_specs = [whole_block(array) for array in out_shape]
        scratch.append(pltpu.VMEM((tokens, features), F32))
    else:
        out_specs = pl.BlockSpec((tokens, depth), lambda i, p: (0, p[i]))
    in_specs = [
        pl.BlockSpec((tokens, depth), lambda i, p: (0, p[i])),
        pl.BlockSpec((1, depth, features), lambda i, p: (p[i] // CORES, 0, 0)),
    ] + [whole_block(array) for array in wholes]
    operands = [places, in_hbm(residual), weight, *wholes]
    aliases = {}
    if earlier is not None:
        aliases = {len(operands): 0}
        in_specs.append(pl.BlockSpec(memory_space=pltpu.HBM))
        operands.append(earlier)
    return pl.pallas_call(
        kernel,
        out_shape=out_shape,
        grid_spec=pltpu.PrefetchScalarGridSpec(
            num_scalar_prefetch=1,
            grid=(steps,),
            in_specs=in_specs,
            out_specs=out_specs,
            scratch_shapes=scratch,
        ),
        input_output_aliases=aliases,
        cost_estimate=NOMINAL,
        compiler_params=pltpu.CompilerParams(vmem_limit_bytes=WEIGHT_VMEM),
    )(*operands)


def cot_kernel(width, rep_count, info_ref, shares_ref, squares_ref, value_cot_ref, cot_ref, cot_t_ref, inv_ref):
    place, length = info_ref[0], info_ref[1]
    rows = value_cot_ref.shape[0]
    own = rows // 128
    seq = (shares_ref.shape[1] - own) // 3
    shares = range(shares_ref.shape[0])

    def below(first, shape):
        at = lax.broadcasted_iota(jnp.int32, shape, 0) * 128 + lax.broadcasted_iota(jnp.int32, shape, 1)
        return first + at < length

    def summed(mask, value):
        return jnp.sum(jnp.where(mask, value, 0.0), axis=(0, 1), keepdims=True)

    maxes = [shares_ref[m, 0:seq] for m in shares]
    top_max = functools.reduce(jnp.maximum, maxes)
    sum_exp = functools.reduce(
        jnp.add, [shares_ref[m, seq : 2 * seq] * jnp.exp(maxes[m] - top_max) for m in shares]
    )
    picked = functools.reduce(jnp.add, [shares_ref[m, 2 * seq : 3 * seq] for m in shares])
    ref_logp = picked - top_max - jnp.log(sum_exp)
    total = -summed(below(0, (seq, 128)), ref_logp)
    for m in shares:
        first = jnp.bitwise_xor(place, m) * rows
        total += summed(below(first, (own, 128)), shares_ref[m, 3 * seq :])
    seq_delta = total / jnp.full((1, 1), length, jnp.int32).astype(F32)
    weight = (2.0 / rep_count) * jax.nn.sigmoid(BETA * seq_delta)
    inv = lax.rsqrt(squares_ref[...] * (1.0 / width) + EPS)
    live = place * rows + lax.broadcasted_iota(jnp.int32, (rows, 1), 0) < length
    scaled = jnp.where(live, inv * weight, 0.0) * value_cot_ref[...].astype(F32)
    cot_ref[...] = scaled.astype(BF16)
    cot_t_ref[...] = scaled.T.astype(BF16)
    inv_ref[...] = inv


def scaled_cot(width, rep_count, info, shares, squares, value_cot):
    rows, features = value_cot.shape

    def whole(array):
        return pl.BlockSpec(array.shape, lambda i, p: (0,) * array.ndim)

    out_shape = [
        jax.ShapeDtypeStruct((rows, features), BF16),
        jax.ShapeDtypeStruct((features, rows), BF16),
        jax.ShapeDtypeStruct((rows, 1), F32),
    ]
    return pl.pallas_call(
        functools.partial(cot_kernel, width, rep_count),
        out_shape=out_shape,
        grid_spec=pltpu.PrefetchScalarGridSpec(
            num_scalar_prefetch=1,
            grid=(1,),
            in_specs=[whole(shares), whole(squares), whole(value_cot)],
            out_specs=[pl.BlockSpec(array.shape, lambda i, p: (0, 0)) for array in out_shape],
        ),
        cost_estimate=NOMINAL,
        compiler_params=pltpu.CompilerParams(vmem_limit_bytes=PAIR_VMEM),
    )(info, shares, squares, in_hbm(value_cot))


def per_device(
    residual,
    norm_gain,
    value_weight,
    value_cot,
    trainee_logp,
    ref_shard_max,
    ref_shard_sum,
    ref_target_logit,
    target_ids,
    lengths,
):
    rows_here, width = residual.shape
    features = value_cot.shape[1]
    tp_count = lax.axis_size("tp")
    outer, inner = lax.axis_size("outer"), lax.axis_size("inner")
    rep_count = outer * inner * CORES
    tp_place = lax.axis_index("tp")
    core = lax.axis_index("core")
    at_inner = lax.axis_index("inner")
    at_outer = lax.axis_index("outer")
    rep_place = (at_outer * inner + at_inner) * CORES + core
    depth = width // rep_count
    rows = depth // tp_count
    order = list(range(tp_count))
    shifts = chunk_shifts(tp_count)
    in_place = rows % 128 == 0 and outer == 2 and inner == 2

    owned = jnp.where(
        target_ids // (VOCAB // tp_count) == tp_place,
        ref_target_logit[0],
        jnp.zeros_like(ref_target_logit[0]),
    )
    packed = jnp.concatenate([ref_shard_max[0], ref_shard_sum[0], owned, trainee_logp])
    packed = packed.reshape(1, -1, 128)
    packed = jnp.concatenate([packed, trade(packed, "tp", 1)])

    gained = (value_weight.astype(F32) * norm_gain.astype(F32)[:, None]).astype(BF16)
    residual, gained, packed = lax.optimization_barrier((residual, gained, packed))
    resid_wide = residual.astype(F32)
    squares = jnp.sum(resid_wide * resid_wide, axis=1, keepdims=True)

    def near_of(k, block):
        first = "inner" if inner_first(k) else "outer"
        return [swap(block, first, s) for s in range(1, lax.axis_size(first))]

    def far_of(k, block, nears):
        second = "outer" if inner_first(k) else "inner"
        near = jnp.stack([block] + nears)
        return [near] + [swap(near, second, s) for s in range(1, lax.axis_size(second))]

    mask = 2
    while mask < tp_count:
        packed = jnp.concatenate([packed, trade(packed, "tp", mask)])
        mask *= 2
    own_pieces, near = {}, {}
    arrived = {0: gained, 1: swap(gained, "tp", shifts[1])}
    near[0] = near_of(0, gained)
    arrived[1], near[0], packed, squares, late_gained = lax.optimization_barrier(
        (arrived[1], near[0], packed, squares, gained)
    )
    near[1] = near_of(1, arrived[1])
    arrived[2] = swap(late_gained, "tp", shifts[2])
    own_pieces[0] = far_of(0, gained, near[0])
    seq_length = lax.dynamic_index_in_dim(lengths, rep_place, keepdims=False)
    info = jnp.stack([tp_place, seq_length]).astype(jnp.int32)
    near[1], arrived[2], packed, late_gained, info = lax.optimization_barrier(
        (near[1], arrived[2], packed, late_gained, info)
    )
    near[2] = near_of(2, arrived[2])
    for k in order[3:]:
        arrived[k] = swap(late_gained, "tp", shifts[k])
    own_pieces[1] = far_of(1, arrived[1], near[1])
    cot, cot_t, inv_rms = scaled_cot(width, rep_count, info, packed, squares, value_cot)

    def place_of(o, i, c, k):
        chip = lax.rem(at_outer + o, outer) * inner + lax.rem(at_inner + i, inner)
        return (chip * CORES + c) * tp_count + lax.rem(tp_place + k, tp_count)

    backward = order[::-1]
    pairs = [backward[i : i + 2] for i in range(0, tp_count, 2)]
    chips = [(o, i) for o in range(outer) for i in range(inner)]
    if not in_place:
        product = jnp.dot(cot_t, residual, preferred_element_type=F32).astype(BF16)
        product = product.reshape(features, -1, rows).transpose(1, 0, 2)

    def places_of(pair, c):
        return jnp.stack([place_of(o, i, c, k) for o, i in chips for k in pair]).astype(jnp.int32)

    def for_others(cot_t):
        places = places_of(backward, 1 - core)
        if in_place:
            return grad_product(residual, cot_t, places, rows, None)
        both = after(product, cot_t)[places].reshape(len(chips), tp_count, features, rows)
        return both.swapaxes(0, 1)

    def for_us(other):
        places = places_of(backward, core)
        if in_place:
            outs = grad_product(residual, cot_t, places, rows, other)
            sides = [([outs[2 * n]], outs[2 * n + 1]) for n in range(tp_count)]
        else:
            both = product[places].reshape(len(chips), tp_count, features, rows).swapaxes(0, 1)
            total = widen([both, other]).astype(BF16)
            total = total.reshape(tp_count, outer, inner, features, rows)
            sides = []
            for n in range(0, tp_count, 2):
                sides.append(([total[n, :, s] for s in range(1, inner)], total[n, :, 0]))
                sides.append(([total[n + 1, s] for s in range(1, outer)], total[n + 1, 0]))
        return [sides[n : n + 2] for n in range(0, tp_count, 2)]

    def first_round(sides):
        return [
            [swap(send, axis, s + 1) for s, send in enumerate(sends)]
            for axis, (sends, _) in zip(("inner", "outer"), sides)
        ]

    def second_round(sides, got):
        later = []
        for axis, (_, keep), parts in zip(("outer", "inner"), sides, got):
            later.append(
                [
                    swap(widen([part[s] for part in [keep] + parts]).astype(BF16), axis, s)
                    for s in range(1, lax.axis_size(axis))
                ]
            )
        return later

    def summed(sides, got, later):
        return [
            widen([part[0] for part in [keep] + parts] + last)
            for (_, keep), parts, last in zip(sides, got, later)
        ]

    theirs = for_others(cot_t)
    theirs, arrived, own_pieces, near = lax.optimization_barrier(
        (theirs, arrived, own_pieces, near)
    )
    other = swap(theirs, "core", 1)
    for k in order[3:]:
        near[k] = near_of(k, arrived[k])
    near, other, own_pieces = lax.optimization_barrier((near, other, own_pieces))
    for k in order[2:]:
        own_pieces[k] = far_of(k, arrived[k], near[k])
    sides = for_us(other)
    got = [first_round(sides[0])]
    sides[1:], own_pieces = lax.optimization_barrier((sides[1:], own_pieces))

    if in_place:
        pieces = [piece for k in order for piece in own_pieces[k]]
        flags = tuple(inner_first(k) for k in order)
        places = [
            jnp.stack([place_of(o, i, c, 0) // tp_count for o, i in chips]).astype(jnp.int32)
            for c in (core, 1 - core)
        ]
        offsets = jnp.stack([lax.rem(tp_place - shift + tp_count, tp_count) * rows for shift in shifts])
        offsets = offsets.astype(jnp.int32)
        total, own_weight = first_value(flags, places[0], offsets, residual, pieces)
    else:
        weight = []
        for k in order:
            both = jnp.stack(own_pieces[k])
            weight.append(both if inner_first(k) else jnp.swapaxes(both, 0, 1))
        by_shift = jnp.array([shifts.index(shift) for shift in range(tp_count)])
        weight = jnp.stack(weight)[by_shift[(tp_place - jnp.arange(tp_count)) % tp_count]]
        weight = weight[:, (at_outer - jnp.arange(outer)) % outer]
        weight = weight[:, :, (at_inner - jnp.arange(inner)) % inner]
        own_weight = weight.transpose(1, 2, 0, 3, 4).reshape(outer * inner, depth, features)
        total = jnp.zeros((), F32)
    got[0], sides[1:], total, own_weight = lax.optimization_barrier(
        (got[0], sides[1:], total, own_weight)
    )
    other_weight = swap(own_weight, "core", 1)
    later = [second_round(sides[0], got[0])]
    got += [first_round(side) for side in sides[1:]]
    if in_place:
        value_proj, coefficient = weight_call(
            functools.partial(value_end_kernel, width),
            places[1],
            residual,
            other_weight,
            [in_hbm(total), cot, inv_rms],
            [
                jax.ShapeDtypeStruct((rows_here, features), BF16),
                jax.ShapeDtypeStruct((rows_here, 1), F32),
            ],
        )
    else:
        both = jnp.stack([own_weight, other_weight], axis=1)
        weight = jnp.where(core == 0, both, both[:, ::-1]).reshape(width, features)
        value_acc = jnp.dot(residual, weight, preferred_element_type=F32)
        value_proj = (inv_rms * value_acc).astype(BF16)
        share = jnp.sum(cot.astype(F32) * value_acc, axis=1, keepdims=True)
        coefficient = inv_rms * inv_rms * share * (1.0 / width)
    later[0], coefficient = lax.optimization_barrier((later[0], coefficient))
    sums = dict(zip(pairs[0], summed(sides[0], got[0], later[0])))
    last = [swap(sums[k].astype(BF16), "tp", k) for k in pairs[0]]
    got[1:], coefficient, sums = lax.optimization_barrier((got[1:], coefficient, sums))
    later += [second_round(side, parts) for side, parts in zip(sides[1:], got[1:])]
    if in_place:
        grad_shape = jax.ShapeDtypeStruct((rows_here, width), BF16)
        resid_grad = weight_call(
            grad_kernel, places[0], residual, in_hbm(own_weight), [cot, coefficient], grad_shape
        )
        later[1], coefficient, resid_grad = lax.optimization_barrier((later[1], coefficient, resid_grad))
    else:
        normed_grad = lax.dot_general(
            cot, weight, (((1,), (1,)), ((), ())), preferred_element_type=F32
        )
        resid_grad = (normed_grad - residual.astype(F32) * coefficient).astype(BF16)
    for pair, *rounds in zip(pairs[1:], sides[1:], got[1:], later[1:]):
        sums.update(zip(pair, summed(*rounds)))
    last += [swap(sums[k].astype(BF16), "tp", k) for k in backward[2:-1]]
    if in_place:
        resid_grad = weight_call(
            grad_kernel, places[1], residual, other_weight, [cot, coefficient], grad_shape, resid_grad
        )
    grad_rows = widen([sums[0]] + last)
    late_gain, late_weight, grad_rows = lax.optimization_barrier((norm_gain, value_weight, grad_rows))
    weight_grad = (late_gain.astype(F32)[None, :] * grad_rows).T
    gain_grad = jnp.sum(late_weight.astype(F32).T * grad_rows, axis=0)
    return (value_proj, resid_grad, weight_grad, gain_grad)


def solution(mesh):
    rep_count, tp_count = mesh.shape["rep"], mesh.shape["tp"]
    split = jax.sharding.Mesh(
        mesh.devices.reshape(OUTER, rep_count // (OUTER * CORES), CORES, tp_count),
        ("outer", "inner", "core", "tp"),
    )
    rep = ("outer", "inner", "core")
    rows = rep + ("tp",)
    return jax.shard_map(
        per_device,
        mesh=split,
        in_specs=(
            P(rows, None),
            P(rows),
            P(rows, None),
            P(rows, None),
            P(rows),
            P("tp", rep),
            P("tp", rep),
            P("tp", rep),
            P(rep),
            P(),
        ),
        out_specs=(P(rows, None), P(rows, None), P(rows, None), P(rows)),
        check_vma=False,
    )
```

```python
import functools

import jax
import jax.numpy as jnp
from jax import lax
from jax.experimental import pallas as pl
from jax.experimental.pallas import tpu as pltpu
from jax.sharding import PartitionSpec as P

VOCAB = 128256
EPS = 1e-05
BETA = 0.5
CORES = 2
OUTER = 2
PAIR_VMEM = 18 * 1024 * 1024
WEIGHT_VMEM = 22 * 1024 * 1024
NOMINAL = pl.CostEstimate(flops=1024, bytes_accessed=1024, transcendentals=0)
BF16 = jnp.bfloat16
F32 = jnp.float32


def swap(value, axis, step):
    size = lax.axis_size(axis)
    return lax.ppermute(value, axis, [(place, (place + step) % size) for place in range(size)])


def trade(value, axis, mask):
    size = lax.axis_size(axis)
    return lax.ppermute(value, axis, [(place, place ^ mask) for place in range(size)])


def in_hbm(array):
    return pltpu.with_memory_space_constraint(array, pltpu.HBM)


def after(value, *earlier):
    return lax.optimization_barrier((value, earlier))[0]


def widen(parts):
    return functools.reduce(jnp.add, [part.astype(F32) for part in parts])


def chunk_shifts(tp_count):
    shifts = [0]
    for step in range(1, tp_count // 2 + 1):
        shifts += [step] if 2 * step == tp_count else [step, tp_count - step]
    return shifts


def inner_first(chunk):
    return chunk % 4 in (0, 3)


def theirs_kernel(places_ref, cot_ref, *rest):
    blocks, out_ref = rest[:-1], rest[-1]
    for slot, resid_ref in enumerate(blocks):
        product = jnp.dot(cot_ref[...], resid_ref[...], preferred_element_type=F32)
        out_ref[slot, 0] = product.astype(BF16)


def ours_kernel(places_ref, cot_ref, *rest):
    slots = len(rest) // 3
    blocks, other_ref, outs = rest[:slots], rest[slots], rest[slots + 1 :]
    step = pl.program_id(0)
    ways = (lax.rem(step, 2), step // 2)
    totals = [
        (
            jnp.dot(cot_ref[...], resid_ref[...], preferred_element_type=F32)
            + other_ref[slot, 0].astype(F32)
        ).astype(BF16)
        for slot, resid_ref in enumerate(blocks)
    ]
    for which, way in enumerate(ways):

        @pl.when(way == 1)
        def _():
            for slot in range(which, slots, 2):
                outs[2 * slot][0] = totals[slot]

        @pl.when(way == 0)
        def _():
            for slot in range(which, slots, 2):
                outs[2 * slot + 1][0] = totals[slot]


def grad_product(residual, cot_t, places, rows, other):
    features, tokens = cot_t.shape
    steps = 4
    slots = places.shape[0] // steps
    in_specs = [pl.BlockSpec((features, tokens), lambda i, p: (0, 0))] + [
        pl.BlockSpec((tokens, rows), lambda i, p, slot=slot: (0, p[slots * i + slot]))
        for slot in range(slots)
    ]
    operands = [places, cot_t] + [in_hbm(residual)] * slots
    block = pl.BlockSpec((slots, 1, features, rows), lambda i, p: (0, i, 0, 0))
    if other is None:
        kernel, out_specs = theirs_kernel, block
        out_shape = pltpu.HBM((slots, steps, features, rows), BF16)
    else:
        kernel = ours_kernel
        in_specs.append(block)
        operands.append(other)
        indices = [
            lambda i: i // 2,
            lambda i: i // 2,
            lambda i: jnp.maximum(i - 2, 0),
            lambda i: jnp.minimum(i, 1),
        ]
        out_specs = [
            pl.BlockSpec((1, features, rows), lambda i, p, index=index: (index(i), 0, 0))
            for index in indices
        ] * (slots // 2)
        out_shape = [pltpu.HBM((2, features, rows), BF16)] * (2 * slots)
    return pl.pallas_call(
        kernel,
        out_shape=out_shape,
        grid_spec=pltpu.PrefetchScalarGridSpec(
            num_scalar_prefetch=1, grid=(steps,), in_specs=in_specs, out_specs=out_specs
        ),
        cost_estimate=NOMINAL,
        compiler_params=pltpu.CompilerParams(vmem_limit_bytes=PAIR_VMEM),
    )(*operands)


def place_weight(inner_flags, offsets_ref, pieces, weight_ref):
    step = pl.program_id(0)
    at_outer, at_inner = step // 2, lax.rem(step, 2)
    rows = pieces[0].shape[1]
    for chunk, flag in enumerate(inner_flags):
        way = at_outer if flag else at_inner
        where = pl.ds(pl.multiple_of(offsets_ref[chunk], rows), rows)
        for late in range(2):
            piece = pieces[chunk * 2 + late]

            @pl.when(way == late)
            def _():
                weight_ref[0, where, :] = piece[0]


def piece_specs(inner_flags, rows, features):
    specs = []
    for flag in inner_flags:
        for late in range(2):
            if flag:
                index = lambda i, *_, first=2 * late: (jnp.clip(i - first, 0, 1), 0, 0)
            else:
                index = lambda i, *_: (i // 2, 0, 0)
            specs.append(pl.BlockSpec((1, rows, features), index))
    return specs


def value_kernel(inner_flags, places_ref, offsets_ref, resid_ref, *rest):
    pieces, (total_ref, weight_ref) = rest[:-2], rest[-2:]
    step = pl.program_id(0)
    place_weight(inner_flags, offsets_ref, pieces, weight_ref)
    product = jnp.dot(resid_ref[...], weight_ref[0], preferred_element_type=F32)

    @pl.when(step == 0)
    def _():
        total_ref[...] = product

    @pl.when(step > 0)
    def _():
        total_ref[...] += product


def value_end_kernel(
    width, places_ref, resid_ref, weight_ref, first_ref, cot_ref, inv_ref, value_ref, coef_ref, total_ref
):
    step = pl.program_id(0)
    product = jnp.dot(resid_ref[...], weight_ref[0], preferred_element_type=F32)

    @pl.when(step == 0)
    def _():
        total_ref[...] = first_ref[...] + product

    @pl.when(step > 0)
    def _():
        total_ref[...] += product

    @pl.when(step == pl.num_programs(0) - 1)
    def _():
        total = total_ref[...]
        inv = inv_ref[...]
        value_ref[...] = (total * inv).astype(BF16)
        share = jnp.sum(total * cot_ref[...].astype(F32), axis=1, keepdims=True)
        coef_ref[...] = share * (inv * inv) * (1.0 / width)


def grad_kernel(places_ref, resid_ref, weight_ref, cot_ref, coef_ref, *rest):
    out_ref = rest[-1]
    grad = lax.dot_general(
        cot_ref[...], weight_ref[0], (((1,), (1,)), ((), ())), preferred_element_type=F32
    )
    out_ref[...] = (grad - resid_ref[...].astype(F32) * coef_ref[...]).astype(BF16)


def whole_block(array):
    return pl.BlockSpec(array.shape, lambda i, *_: (0, 0))


def first_value(inner_flags, places, offsets, residual, pieces):
    tokens, width = residual.shape
    rows, features = pieces[0].shape[1:]
    steps = places.shape[0]
    depth = width // (CORES * steps)
    total = pltpu.HBM((tokens, features), F32)
    return pl.pallas_call(
        functools.partial(value_kernel, inner_flags),
        out_shape=[total, pltpu.HBM((steps, depth, features), BF16)],
        grid_spec=pltpu.PrefetchScalarGridSpec(
            num_scalar_prefetch=2,
            grid=(steps,),
            in_specs=[pl.BlockSpec((tokens, depth), lambda i, p, o: (0, p[i]))]
            + piece_specs(inner_flags, rows, features),
            out_specs=[
                whole_block(total),
                pl.BlockSpec((1, depth, features), lambda i, p, o: (p[i] // CORES, 0, 0)),
            ],
        ),
        cost_estimate=NOMINAL,
        compiler_params=pltpu.CompilerParams(vmem_limit_bytes=WEIGHT_VMEM),
    )(places, offsets, in_hbm(residual), *pieces)


def weight_call(kernel, places, residual, weight, wholes, out_shape, earlier=None):
    tokens, width = residual.shape
    _, depth, features = weight.shape
    steps = places.shape[0]
    scratch = []
    if isinstance(out_shape, list):
        out_specs = [whole_block(array) for array in out_shape]
        scratch.append(pltpu.VMEM((tokens, features), F32))
    else:
        out_specs = pl.BlockSpec((tokens, depth), lambda i, p: (0, p[i]))
    in_specs = [
        pl.BlockSpec((tokens, depth), lambda i, p: (0, p[i])),
        pl.BlockSpec((1, depth, features), lambda i, p: (p[i] // CORES, 0, 0)),
    ] + [whole_block(array) for array in wholes]
    operands = [places, in_hbm(residual), weight, *wholes]
    aliases = {}
    if earlier is not None:
        aliases = {len(operands): 0}
        in_specs.append(pl.BlockSpec(memory_space=pltpu.HBM))
        operands.append(earlier)
    return pl.pallas_call(
        kernel,
        out_shape=out_shape,
        grid_spec=pltpu.PrefetchScalarGridSpec(
            num_scalar_prefetch=1,
            grid=(steps,),
            in_specs=in_specs,
            out_specs=out_specs,
            scratch_shapes=scratch,
        ),
        input_output_aliases=aliases,
        cost_estimate=NOMINAL,
        compiler_params=pltpu.CompilerParams(vmem_limit_bytes=WEIGHT_VMEM),
    )(*operands)


def cot_kernel(width, rep_count, info_ref, shares_ref, squares_ref, value_cot_ref, cot_ref, cot_t_ref, inv_ref):
    place, length = info_ref[0], info_ref[1]
    rows = value_cot_ref.shape[0]
    own = rows // 128
    seq = (shares_ref.shape[1] - own) // 3
    shares = range(shares_ref.shape[0])

    def below(first, shape):
        at = lax.broadcasted_iota(jnp.int32, shape, 0) * 128 + lax.broadcasted_iota(jnp.int32, shape, 1)
        return first + at < length

    def summed(mask, value):
        return jnp.sum(jnp.where(mask, value, 0.0), axis=(0, 1), keepdims=True)

    maxes = [shares_ref[m, 0:seq] for m in shares]
    top_max = functools.reduce(jnp.maximum, maxes)
    sum_exp = functools.reduce(
        jnp.add, [shares_ref[m, seq : 2 * seq] * jnp.exp(maxes[m] - top_max) for m in shares]
    )
    picked = functools.reduce(jnp.add, [shares_ref[m, 2 * seq : 3 * seq] for m in shares])
    ref_logp = picked - top_max - jnp.log(sum_exp)
    total = -summed(below(0, (seq, 128)), ref_logp)
    for m in shares:
        first = jnp.bitwise_xor(place, m) * rows
        total += summed(below(first, (own, 128)), shares_ref[m, 3 * seq :])
    seq_delta = total / jnp.full((1, 1), length, jnp.int32).astype(F32)
    weight = (2.0 / rep_count) * jax.nn.sigmoid(BETA * seq_delta)
    inv = lax.rsqrt(squares_ref[...] * (1.0 / width) + EPS)
    live = place * rows + lax.broadcasted_iota(jnp.int32, (rows, 1), 0) < length
    scaled = jnp.where(live, inv * weight, 0.0) * value_cot_ref[...].astype(F32)
    cot_ref[...] = scaled.astype(BF16)
    cot_t_ref[...] = scaled.T.astype(BF16)
    inv_ref[...] = inv


def scaled_cot(width, rep_count, info, shares, squares, value_cot):
    rows, features = value_cot.shape

    def whole(array):
        return pl.BlockSpec(array.shape, lambda i, p: (0,) * array.ndim)

    out_shape = [
        jax.ShapeDtypeStruct((rows, features), BF16),
        jax.ShapeDtypeStruct((features, rows), BF16),
        jax.ShapeDtypeStruct((rows, 1), F32),
    ]
    return pl.pallas_call(
        functools.partial(cot_kernel, width, rep_count),
        out_shape=out_shape,
        grid_spec=pltpu.PrefetchScalarGridSpec(
            num_scalar_prefetch=1,
            grid=(1,),
            in_specs=[whole(shares), whole(squares), whole(value_cot)],
            out_specs=[pl.BlockSpec(array.shape, lambda i, p: (0, 0)) for array in out_shape],
        ),
        cost_estimate=NOMINAL,
        compiler_params=pltpu.CompilerParams(vmem_limit_bytes=PAIR_VMEM),
    )(info, shares, squares, in_hbm(value_cot))


def per_device(
    residual,
    norm_gain,
    value_weight,
    value_cot,
    trainee_logp,
    ref_shard_max,
    ref_shard_sum,
    ref_target_logit,
    target_ids,
    lengths,
):
    rows_here, width = residual.shape
    features = value_cot.shape[1]
    tp_count = lax.axis_size("tp")
    outer, inner = lax.axis_size("outer"), lax.axis_size("inner")
    rep_count = outer * inner * CORES
    tp_place = lax.axis_index("tp")
    core = lax.axis_index("core")
    at_inner = lax.axis_index("inner")
    at_outer = lax.axis_index("outer")
    rep_place = (at_outer * inner + at_inner) * CORES + core
    depth = width // rep_count
    rows = depth // tp_count
    order = list(range(tp_count))
    shifts = chunk_shifts(tp_count)
    in_place = rows % 128 == 0 and outer == 2 and inner == 2

    owned = jnp.where(
        target_ids // (VOCAB // tp_count) == tp_place,
        ref_target_logit[0],
        jnp.zeros_like(ref_target_logit[0]),
    )
    packed = jnp.concatenate([ref_shard_max[0], ref_shard_sum[0], owned, trainee_logp])
    packed = packed.reshape(1, -1, 128)
    packed = jnp.concatenate([packed, trade(packed, "tp", 1)])

    gained = (value_weight.astype(F32) * norm_gain.astype(F32)[:, None]).astype(BF16)
    residual, gained, packed = lax.optimization_barrier((residual, gained, packed))
    resid_wide = residual.astype(F32)
    squares = jnp.sum(resid_wide * resid_wide, axis=1, keepdims=True)

    def near_of(k, block):
        first = "inner" if inner_first(k) else "outer"
        return [swap(block, first, s) for s in range(1, lax.axis_size(first))]

    def far_of(k, block, nears):
        second = "outer" if inner_first(k) else "inner"
        near = jnp.stack([block] + nears)
        return [near] + [swap(near, second, s) for s in range(1, lax.axis_size(second))]

    mask = 2
    while mask < tp_count:
        packed = jnp.concatenate([packed, trade(packed, "tp", mask)])
        mask *= 2
    own_pieces, near = {}, {}
    arrived = {0: gained, 1: swap(gained, "tp", shifts[1])}
    near[0] = near_of(0, gained)
    arrived[1], near[0], packed, squares, late_gained = lax.optimization_barrier(
        (arrived[1], near[0], packed, squares, gained)
    )
    near[1] = near_of(1, arrived[1])
    arrived[2] = swap(late_gained, "tp", shifts[2])
    own_pieces[0] = far_of(0, gained, near[0])
    seq_length = lax.dynamic_index_in_dim(lengths, rep_place, keepdims=False)
    info = jnp.stack([tp_place, seq_length]).astype(jnp.int32)
    near[1], arrived[2], packed, late_gained, info = lax.optimization_barrier(
        (near[1], arrived[2], packed, late_gained, info)
    )
    near[2] = near_of(2, arrived[2])
    for k in order[3:]:
        arrived[k] = swap(late_gained, "tp", shifts[k])
    own_pieces[1] = far_of(1, arrived[1], near[1])
    cot, cot_t, inv_rms = scaled_cot(width, rep_count, info, packed, squares, value_cot)

    def place_of(o, i, c, k):
        chip = lax.rem(at_outer + o, outer) * inner + lax.rem(at_inner + i, inner)
        return (chip * CORES + c) * tp_count + lax.rem(tp_place + k, tp_count)

    backward = order[::-1]
    pairs = [backward[i : i + 2] for i in range(0, tp_count, 2)]
    chips = [(o, i) for o in range(outer) for i in range(inner)]
    if not in_place:
        product = jnp.dot(cot_t, residual, preferred_element_type=F32).astype(BF16)
        product = product.reshape(features, -1, rows).transpose(1, 0, 2)

    def places_of(pair, c):
        return jnp.stack([place_of(o, i, c, k) for o, i in chips for k in pair]).astype(jnp.int32)

    def for_others(cot_t):
        places = places_of(backward, 1 - core)
        if in_place:
            return grad_product(residual, cot_t, places, rows, None)
        both = after(product, cot_t)[places].reshape(len(chips), tp_count, features, rows)
        return both.swapaxes(0, 1)

    def for_us(other):
        places = places_of(backward, core)
        if in_place:
            outs = grad_product(residual, cot_t, places, rows, other)
            sides = [([outs[2 * n]], outs[2 * n + 1]) for n in range(tp_count)]
        else:
            both = product[places].reshape(len(chips), tp_count, features, rows).swapaxes(0, 1)
            total = widen([both, other]).astype(BF16)
            total = total.reshape(tp_count, outer, inner, features, rows)
            sides = []
            for n in range(0, tp_count, 2):
                sides.append(([total[n, :, s] for s in range(1, inner)], total[n, :, 0]))
                sides.append(([total[n + 1, s] for s in range(1, outer)], total[n + 1, 0]))
        return [sides[n : n + 2] for n in range(0, tp_count, 2)]

    def first_round(sides):
        return [
            [swap(send, axis, s + 1) for s, send in enumerate(sends)]
            for axis, (sends, _) in zip(("inner", "outer"), sides)
        ]

    def second_round(sides, got):
        later = []
        for axis, (_, keep), parts in zip(("outer", "inner"), sides, got):
            later.append(
                [
                    swap(widen([part[s] for part in [keep] + parts]).astype(BF16), axis, s)
                    for s in range(1, lax.axis_size(axis))
                ]
            )
        return later

    def summed(sides, got, later):
        return [
            widen([part[0] for part in [keep] + parts] + last)
            for (_, keep), parts, last in zip(sides, got, later)
        ]

    theirs = for_others(cot_t)
    theirs, arrived, own_pieces, near = lax.optimization_barrier(
        (theirs, arrived, own_pieces, near)
    )
    other = swap(theirs, "core", 1)
    for k in order[3:]:
        near[k] = near_of(k, arrived[k])
    near, other, own_pieces = lax.optimization_barrier((near, other, own_pieces))
    for k in order[2:]:
        own_pieces[k] = far_of(k, arrived[k], near[k])
    sides = for_us(other)
    got = [first_round(sides[0])]
    sides[1:], own_pieces = lax.optimization_barrier((sides[1:], own_pieces))

    if in_place:
        pieces = [piece for k in order for piece in own_pieces[k]]
        flags = tuple(inner_first(k) for k in order)
        places = [
            jnp.stack([place_of(o, i, c, 0) // tp_count for o, i in chips]).astype(jnp.int32)
            for c in (core, 1 - core)
        ]
        offsets = jnp.stack([lax.rem(tp_place - shift + tp_count, tp_count) * rows for shift in shifts])
        offsets = offsets.astype(jnp.int32)
        total, own_weight = first_value(flags, places[0], offsets, residual, pieces)
    else:
        weight = []
        for k in order:
            both = jnp.stack(own_pieces[k])
            weight.append(both if inner_first(k) else jnp.swapaxes(both, 0, 1))
        by_shift = jnp.array([shifts.index(shift) for shift in range(tp_count)])
        weight = jnp.stack(weight)[by_shift[(tp_place - jnp.arange(tp_count)) % tp_count]]
        weight = weight[:, (at_outer - jnp.arange(outer)) % outer]
        weight = weight[:, :, (at_inner - jnp.arange(inner)) % inner]
        own_weight = weight.transpose(1, 2, 0, 3, 4).reshape(outer * inner, depth, features)
        total = jnp.zeros((), F32)
    got[0], sides[1:], total, own_weight = lax.optimization_barrier(
        (got[0], sides[1:], total, own_weight)
    )
    other_weight = swap(own_weight, "core", 1)
    later = [second_round(sides[0], got[0])]
    got += [first_round(side) for side in sides[1:]]
    if in_place:
        value_proj, coefficient = weight_call(
            functools.partial(value_end_kernel, width),
            places[1],
            residual,
            other_weight,
            [in_hbm(total), cot, inv_rms],
            [
                jax.ShapeDtypeStruct((rows_here, features), BF16),
                jax.ShapeDtypeStruct((rows_here, 1), F32),
            ],
        )
    else:
        both = jnp.stack([own_weight, other_weight], axis=1)
        weight = jnp.where(core == 0, both, both[:, ::-1]).reshape(width, features)
        value_acc = jnp.dot(residual, weight, preferred_element_type=F32)
        value_proj = (inv_rms * value_acc).astype(BF16)
        share = jnp.sum(cot.astype(F32) * value_acc, axis=1, keepdims=True)
        coefficient = inv_rms * inv_rms * share * (1.0 / width)
    later[0], coefficient = lax.optimization_barrier((later[0], coefficient))
    sums = dict(zip(pairs[0], summed(sides[0], got[0], later[0])))
    last = [swap(sums[k].astype(BF16), "tp", k) for k in pairs[0]]
    if in_place:
        grad_shape = jax.ShapeDtypeStruct((rows_here, width), BF16)
        resid_grad = weight_call(
            grad_kernel, places[0], residual, in_hbm(own_weight), [cot, coefficient], grad_shape
        )
        got[1:], resid_grad = lax.optimization_barrier((got[1:], resid_grad))
    else:
        normed_grad = lax.dot_general(
            cot, weight, (((1,), (1,)), ((), ())), preferred_element_type=F32
        )
        resid_grad = (normed_grad - residual.astype(F32) * coefficient).astype(BF16)
    later += [second_round(side, parts) for side, parts in zip(sides[1:], got[1:])]
    if in_place:
        resid_grad = weight_call(
            grad_kernel, places[1][:2], residual, other_weight, [cot, coefficient], grad_shape, resid_grad
        )
        later[1], last, resid_grad = lax.optimization_barrier((later[1], last, resid_grad))
    for pair, *rounds in zip(pairs[1:], sides[1:], got[1:], later[1:]):
        sums.update(zip(pair, summed(*rounds)))
    last += [swap(sums[k].astype(BF16), "tp", k) for k in backward[2:-1]]
    if in_place:
        resid_grad = weight_call(
            grad_kernel, places[1][2:], residual, other_weight, [cot, coefficient], grad_shape, resid_grad
        )
    grad_rows = widen([sums[0]] + last)
    late_gain, late_weight, grad_rows = lax.optimization_barrier((norm_gain, value_weight, grad_rows))
    weight_grad = (late_gain.astype(F32)[None, :] * grad_rows).T
    gain_grad = jnp.sum(late_weight.astype(F32).T * grad_rows, axis=0)
    return (value_proj, resid_grad, weight_grad, gain_grad)


def solution(mesh):
    rep_count, tp_count = mesh.shape["rep"], mesh.shape["tp"]
    split = jax.sharding.Mesh(
        mesh.devices.reshape(OUTER, rep_count // (OUTER * CORES), CORES, tp_count),
        ("outer", "inner", "core", "tp"),
    )
    rep = ("outer", "inner", "core")
    rows = rep + ("tp",)
    return jax.shard_map(
        per_device,
        mesh=split,
        in_specs=(
            P(rows, None),
            P(rows),
            P(rows, None),
            P(rows, None),
            P(rows),
            P("tp", rep),
            P("tp", rep),
            P("tp", rep),
            P(rep),
            P(),
        ),
        out_specs=(P(rows, None), P(rows, None), P(rows, None), P(rows)),
        check_vma=False,
    )
```

```python
import functools

import jax
import jax.numpy as jnp
from jax import lax
from jax.experimental import pallas as pl
from jax.experimental.pallas import tpu as pltpu
from jax.sharding import PartitionSpec as P

VOCAB = 128256
EPS = 1e-05
BETA = 0.5
CORES = 2
OUTER = 2
PAIR_VMEM = 18 * 1024 * 1024
WEIGHT_VMEM = 22 * 1024 * 1024
NOMINAL = pl.CostEstimate(flops=1024, bytes_accessed=1024, transcendentals=0)
BF16 = jnp.bfloat16
F32 = jnp.float32


def swap(value, axis, step):
    size = lax.axis_size(axis)
    return lax.ppermute(value, axis, [(place, (place + step) % size) for place in range(size)])


def trade(value, axis, mask):
    size = lax.axis_size(axis)
    return lax.ppermute(value, axis, [(place, place ^ mask) for place in range(size)])


def in_hbm(array):
    return pltpu.with_memory_space_constraint(array, pltpu.HBM)


def after(value, *earlier):
    return lax.optimization_barrier((value, earlier))[0]


def widen(parts):
    return functools.reduce(jnp.add, [part.astype(F32) for part in parts])


def chunk_shifts(tp_count):
    shifts = [0]
    for step in range(1, tp_count // 2 + 1):
        shifts += [step] if 2 * step == tp_count else [step, tp_count - step]
    return shifts


def inner_first(chunk):
    return chunk % 4 in (0, 3)


def theirs_kernel(places_ref, cot_ref, *rest):
    blocks, out_ref = rest[:-1], rest[-1]
    for slot, resid_ref in enumerate(blocks):
        product = jnp.dot(cot_ref[...], resid_ref[...], preferred_element_type=F32)
        out_ref[slot, 0] = product.astype(BF16)


def ours_kernel(places_ref, cot_ref, *rest):
    slots = len(rest) // 3
    blocks, other_ref, outs = rest[:slots], rest[slots], rest[slots + 1 :]
    step = pl.program_id(0)
    ways = (lax.rem(step, 2), step // 2)
    totals = [
        (
            jnp.dot(cot_ref[...], resid_ref[...], preferred_element_type=F32)
            + other_ref[slot, 0].astype(F32)
        ).astype(BF16)
        for slot, resid_ref in enumerate(blocks)
    ]
    for which, way in enumerate(ways):

        @pl.when(way == 1)
        def _():
            for slot in range(which, slots, 2):
                outs[2 * slot][0] = totals[slot]

        @pl.when(way == 0)
        def _():
            for slot in range(which, slots, 2):
                outs[2 * slot + 1][0] = totals[slot]


def grad_product(residual, cot_t, places, rows, other):
    features, tokens = cot_t.shape
    steps = 4
    slots = places.shape[0] // steps
    in_specs = [pl.BlockSpec((features, tokens), lambda i, p: (0, 0))] + [
        pl.BlockSpec((tokens, rows), lambda i, p, slot=slot: (0, p[slots * i + slot]))
        for slot in range(slots)
    ]
    operands = [places, cot_t] + [in_hbm(residual)] * slots
    block = pl.BlockSpec((slots, 1, features, rows), lambda i, p: (0, i, 0, 0))
    if other is None:
        kernel, out_specs = theirs_kernel, block
        out_shape = pltpu.HBM((slots, steps, features, rows), BF16)
    else:
        kernel = ours_kernel
        in_specs.append(block)
        operands.append(other)
        indices = [
            lambda i: i // 2,
            lambda i: i // 2,
            lambda i: jnp.maximum(i - 2, 0),
            lambda i: jnp.minimum(i, 1),
        ]
        out_specs = [
            pl.BlockSpec((1, features, rows), lambda i, p, index=index: (index(i), 0, 0))
            for index in indices
        ] * (slots // 2)
        out_shape = [pltpu.HBM((2, features, rows), BF16)] * (2 * slots)
    return pl.pallas_call(
        kernel,
        out_shape=out_shape,
        grid_spec=pltpu.PrefetchScalarGridSpec(
            num_scalar_prefetch=1, grid=(steps,), in_specs=in_specs, out_specs=out_specs
        ),
        cost_estimate=NOMINAL,
        compiler_params=pltpu.CompilerParams(vmem_limit_bytes=PAIR_VMEM),
    )(*operands)


def sum_kernel(counts, *refs):
    ins, outs = refs[: sum(counts)], refs[sum(counts) :]
    for n, out_ref in enumerate(outs):
        first = sum(counts[:n])
        parts = [ref[...].astype(F32).reshape(out_ref.shape) for ref in ins[first : first + counts[n]]]
        out_ref[...] = functools.reduce(jnp.add, parts).astype(BF16)


def sums_of(groups, slot):
    shape = groups[0][0].shape[-2:]
    in_specs = [
        pl.BlockSpec((1,) + shape, lambda i: (slot, 0, 0))
        if part.ndim == 3
        else pl.BlockSpec(shape, lambda i: (0, 0))
        for parts in groups
        for part in parts
    ]
    return pl.pallas_call(
        functools.partial(sum_kernel, [len(parts) for parts in groups]),
        out_shape=[jax.ShapeDtypeStruct(shape, BF16)] * len(groups),
        grid=(1,),
        in_specs=in_specs,
        out_specs=[pl.BlockSpec(shape, lambda i: (0, 0))] * len(groups),
        cost_estimate=NOMINAL,
        compiler_params=pltpu.CompilerParams(vmem_limit_bytes=PAIR_VMEM),
    )(*[part for parts in groups for part in parts])


def place_weight(inner_flags, offsets_ref, pieces, weight_ref):
    step = pl.program_id(0)
    at_outer, at_inner = step // 2, lax.rem(step, 2)
    rows = pieces[0].shape[1]
    for chunk, flag in enumerate(inner_flags):
        way = at_outer if flag else at_inner
        where = pl.ds(pl.multiple_of(offsets_ref[chunk], rows), rows)
        for late in range(2):
            piece = pieces[chunk * 2 + late]

            @pl.when(way == late)
            def _():
                weight_ref[0, where, :] = piece[0]


def piece_specs(inner_flags, rows, features):
    specs = []
    for flag in inner_flags:
        for late in range(2):
            if flag:
                index = lambda i, *_, first=2 * late: (jnp.clip(i - first, 0, 1), 0, 0)
            else:
                index = lambda i, *_: (i // 2, 0, 0)
            specs.append(pl.BlockSpec((1, rows, features), index))
    return specs


def value_kernel(inner_flags, places_ref, offsets_ref, resid_ref, *rest):
    pieces, (total_ref, weight_ref) = rest[:-2], rest[-2:]
    step = pl.program_id(0)
    place_weight(inner_flags, offsets_ref, pieces, weight_ref)
    product = jnp.dot(resid_ref[...], weight_ref[0], preferred_element_type=F32)

    @pl.when(step == 0)
    def _():
        total_ref[...] = product

    @pl.when(step > 0)
    def _():
        total_ref[...] += product


def value_end_kernel(
    width, places_ref, resid_ref, weight_ref, first_ref, cot_ref, inv_ref, value_ref, coef_ref, total_ref
):
    step = pl.program_id(0)
    product = jnp.dot(resid_ref[...], weight_ref[0], preferred_element_type=F32)

    @pl.when(step == 0)
    def _():
        total_ref[...] = first_ref[...] + product

    @pl.when(step > 0)
    def _():
        total_ref[...] += product

    @pl.when(step == pl.num_programs(0) - 1)
    def _():
        total = total_ref[...]
        inv = inv_ref[...]
        value_ref[...] = (total * inv).astype(BF16)
        share = jnp.sum(total * cot_ref[...].astype(F32), axis=1, keepdims=True)
        coef_ref[...] = share * (inv * inv) * (1.0 / width)


def grad_kernel(places_ref, resid_ref, weight_ref, cot_ref, coef_ref, *rest):
    out_ref = rest[-1]
    grad = lax.dot_general(
        cot_ref[...], weight_ref[0], (((1,), (1,)), ((), ())), preferred_element_type=F32
    )
    out_ref[...] = (grad - resid_ref[...].astype(F32) * coef_ref[...]).astype(BF16)


def whole_block(array):
    return pl.BlockSpec(array.shape, lambda i, *_: (0, 0))


def first_value(inner_flags, places, offsets, residual, pieces):
    tokens, width = residual.shape
    rows, features = pieces[0].shape[1:]
    steps = places.shape[0]
    depth = width // (CORES * steps)
    total = pltpu.HBM((tokens, features), F32)
    return pl.pallas_call(
        functools.partial(value_kernel, inner_flags),
        out_shape=[total, pltpu.HBM((steps, depth, features), BF16)],
        grid_spec=pltpu.PrefetchScalarGridSpec(
            num_scalar_prefetch=2,
            grid=(steps,),
            in_specs=[pl.BlockSpec((tokens, depth), lambda i, p, o: (0, p[i]))]
            + piece_specs(inner_flags, rows, features),
            out_specs=[
                whole_block(total),
                pl.BlockSpec((1, depth, features), lambda i, p, o: (p[i] // CORES, 0, 0)),
            ],
        ),
        cost_estimate=NOMINAL,
        compiler_params=pltpu.CompilerParams(vmem_limit_bytes=WEIGHT_VMEM),
    )(places, offsets, in_hbm(residual), *pieces)


def weight_call(kernel, places, residual, weight, wholes, out_shape, earlier=None):
    tokens, width = residual.shape
    _, depth, features = weight.shape
    steps = places.shape[0]
    scratch = []
    if isinstance(out_shape, list):
        out_specs = [whole_block(array) for array in out_shape]
        scratch.append(pltpu.VMEM((tokens, features), F32))
    else:
        out_specs = pl.BlockSpec((tokens, depth), lambda i, p: (0, p[i]))
    in_specs = [
        pl.BlockSpec((tokens, depth), lambda i, p: (0, p[i])),
        pl.BlockSpec((1, depth, features), lambda i, p: (p[i] // CORES, 0, 0)),
    ] + [whole_block(array) for array in wholes]
    operands = [places, in_hbm(residual), weight, *wholes]
    aliases = {}
    if earlier is not None:
        aliases = {len(operands): 0}
        in_specs.append(pl.BlockSpec(memory_space=pltpu.HBM))
        operands.append(earlier)
    return pl.pallas_call(
        kernel,
        out_shape=out_shape,
        grid_spec=pltpu.PrefetchScalarGridSpec(
            num_scalar_prefetch=1,
            grid=(steps,),
            in_specs=in_specs,
            out_specs=out_specs,
            scratch_shapes=scratch,
        ),
        input_output_aliases=aliases,
        cost_estimate=NOMINAL,
        compiler_params=pltpu.CompilerParams(vmem_limit_bytes=WEIGHT_VMEM),
    )(*operands)


def cot_kernel(width, rep_count, info_ref, shares_ref, squares_ref, value_cot_ref, cot_ref, cot_t_ref, inv_ref):
    place, length = info_ref[0], info_ref[1]
    rows = value_cot_ref.shape[0]
    own = rows // 128
    seq = (shares_ref.shape[1] - own) // 3
    shares = range(shares_ref.shape[0])

    def below(first, shape):
        at = lax.broadcasted_iota(jnp.int32, shape, 0) * 128 + lax.broadcasted_iota(jnp.int32, shape, 1)
        return first + at < length

    def summed(mask, value):
        return jnp.sum(jnp.where(mask, value, 0.0), axis=(0, 1), keepdims=True)

    maxes = [shares_ref[m, 0:seq] for m in shares]
    top_max = functools.reduce(jnp.maximum, maxes)
    sum_exp = functools.reduce(
        jnp.add, [shares_ref[m, seq : 2 * seq] * jnp.exp(maxes[m] - top_max) for m in shares]
    )
    picked = functools.reduce(jnp.add, [shares_ref[m, 2 * seq : 3 * seq] for m in shares])
    ref_logp = picked - top_max - jnp.log(sum_exp)
    total = -summed(below(0, (seq, 128)), ref_logp)
    for m in shares:
        first = jnp.bitwise_xor(place, m) * rows
        total += summed(below(first, (own, 128)), shares_ref[m, 3 * seq :])
    seq_delta = total / jnp.full((1, 1), length, jnp.int32).astype(F32)
    weight = (2.0 / rep_count) * jax.nn.sigmoid(BETA * seq_delta)
    inv = lax.rsqrt(squares_ref[...] * (1.0 / width) + EPS)
    live = place * rows + lax.broadcasted_iota(jnp.int32, (rows, 1), 0) < length
    scaled = jnp.where(live, inv * weight, 0.0) * value_cot_ref[...].astype(F32)
    cot_ref[...] = scaled.astype(BF16)
    cot_t_ref[...] = scaled.T.astype(BF16)
    inv_ref[...] = inv


def scaled_cot(width, rep_count, info, shares, squares, value_cot):
    rows, features = value_cot.shape

    def whole(array):
        return pl.BlockSpec(array.shape, lambda i, p: (0,) * array.ndim)

    out_shape = [
        jax.ShapeDtypeStruct((rows, features), BF16),
        jax.ShapeDtypeStruct((features, rows), BF16),
        jax.ShapeDtypeStruct((rows, 1), F32),
    ]
    return pl.pallas_call(
        functools.partial(cot_kernel, width, rep_count),
        out_shape=out_shape,
        grid_spec=pltpu.PrefetchScalarGridSpec(
            num_scalar_prefetch=1,
            grid=(1,),
            in_specs=[whole(shares), whole(squares), whole(value_cot)],
            out_specs=[pl.BlockSpec(array.shape, lambda i, p: (0, 0)) for array in out_shape],
        ),
        cost_estimate=NOMINAL,
        compiler_params=pltpu.CompilerParams(vmem_limit_bytes=PAIR_VMEM),
    )(info, shares, squares, in_hbm(value_cot))


def per_device(
    residual,
    norm_gain,
    value_weight,
    value_cot,
    trainee_logp,
    ref_shard_max,
    ref_shard_sum,
    ref_target_logit,
    target_ids,
    lengths,
):
    rows_here, width = residual.shape
    features = value_cot.shape[1]
    tp_count = lax.axis_size("tp")
    outer, inner = lax.axis_size("outer"), lax.axis_size("inner")
    rep_count = outer * inner * CORES
    tp_place = lax.axis_index("tp")
    core = lax.axis_index("core")
    at_inner = lax.axis_index("inner")
    at_outer = lax.axis_index("outer")
    rep_place = (at_outer * inner + at_inner) * CORES + core
    depth = width // rep_count
    rows = depth // tp_count
    order = list(range(tp_count))
    shifts = chunk_shifts(tp_count)
    in_place = rows % 128 == 0 and outer == 2 and inner == 2

    owned = jnp.where(
        target_ids // (VOCAB // tp_count) == tp_place,
        ref_target_logit[0],
        jnp.zeros_like(ref_target_logit[0]),
    )
    packed = jnp.concatenate([ref_shard_max[0], ref_shard_sum[0], owned, trainee_logp])
    packed = packed.reshape(1, -1, 128)
    packed = jnp.concatenate([packed, trade(packed, "tp", 1)])

    gained = (value_weight.astype(F32) * norm_gain.astype(F32)[:, None]).astype(BF16)
    residual, gained, packed = lax.optimization_barrier((residual, gained, packed))
    resid_wide = residual.astype(F32)
    squares = jnp.sum(resid_wide * resid_wide, axis=1, keepdims=True)

    def near_of(k, block):
        first = "inner" if inner_first(k) else "outer"
        return [swap(block, first, s) for s in range(1, lax.axis_size(first))]

    def far_of(k, block, nears):
        second = "outer" if inner_first(k) else "inner"
        near = jnp.stack([block] + nears)
        return [near] + [swap(near, second, s) for s in range(1, lax.axis_size(second))]

    mask = 2
    while mask < tp_count:
        packed = jnp.concatenate([packed, trade(packed, "tp", mask)])
        mask *= 2
    own_pieces, near = {}, {}
    arrived = {0: gained, 1: swap(gained, "tp", shifts[1])}
    near[0] = near_of(0, gained)
    arrived[1], near[0], squares, late_gained = lax.optimization_barrier(
        (arrived[1], near[0], squares, gained)
    )
    near[1] = near_of(1, arrived[1])
    arrived[2] = swap(late_gained, "tp", shifts[2])
    own_pieces[0] = far_of(0, gained, near[0])
    seq_length = lax.dynamic_index_in_dim(lengths, rep_place, keepdims=False)
    info = jnp.stack([tp_place, seq_length]).astype(jnp.int32)
    near[1], arrived[2], packed, late_gained, info = lax.optimization_barrier(
        (near[1], arrived[2], packed, late_gained, info)
    )
    near[2] = near_of(2, arrived[2])
    for k in order[3:]:
        arrived[k] = swap(late_gained, "tp", shifts[k])
    own_pieces[1] = far_of(1, arrived[1], near[1])
    cot, cot_t, inv_rms = scaled_cot(width, rep_count, info, packed, squares, value_cot)

    def place_of(o, i, c, k):
        chip = lax.rem(at_outer + o, outer) * inner + lax.rem(at_inner + i, inner)
        return (chip * CORES + c) * tp_count + lax.rem(tp_place + k, tp_count)

    backward = order[::-1]
    pairs = [backward[i : i + 2] for i in range(0, tp_count, 2)]
    chips = [(o, i) for o in range(outer) for i in range(inner)]
    if not in_place:
        product = jnp.dot(cot_t, residual, preferred_element_type=F32).astype(BF16)
        product = product.reshape(features, -1, rows).transpose(1, 0, 2)

    def places_of(pair, c):
        return jnp.stack([place_of(o, i, c, k) for o, i in chips for k in pair]).astype(jnp.int32)

    def for_others(cot_t):
        places = places_of(backward, 1 - core)
        if in_place:
            return grad_product(residual, cot_t, places, rows, None)
        both = after(product, cot_t)[places].reshape(len(chips), tp_count, features, rows)
        return both.swapaxes(0, 1)

    def for_us(other):
        places = places_of(backward, core)
        if in_place:
            outs = grad_product(residual, cot_t, places, rows, other)
            sides = [([outs[2 * n]], outs[2 * n + 1]) for n in range(tp_count)]
        else:
            both = product[places].reshape(len(chips), tp_count, features, rows).swapaxes(0, 1)
            total = widen([both, other]).astype(BF16)
            total = total.reshape(tp_count, outer, inner, features, rows)
            sides = []
            for n in range(0, tp_count, 2):
                sides.append(([total[n, :, s] for s in range(1, inner)], total[n, :, 0]))
                sides.append(([total[n + 1, s] for s in range(1, outer)], total[n + 1, 0]))
        return [sides[n : n + 2] for n in range(0, tp_count, 2)]

    def first_round(sides):
        return [
            [swap(send, axis, s + 1) for s, send in enumerate(sends)]
            for axis, (sends, _) in zip(("inner", "outer"), sides)
        ]

    def second_round(sides, got, following=()):
        axes = ("outer", "inner")
        groups = [[keep] + parts for (_, keep), parts in zip(sides, got)]
        if in_place:
            sent, following = lax.optimization_barrier((sums_of(groups, 1), following))
            return [[swap(x, axis, 1)] for x, axis in zip(sent, axes)], following
        return [
            [
                swap(widen([part[s] for part in parts]).astype(BF16), axis, s)
                for s in range(1, lax.axis_size(axis))
            ]
            for parts, axis in zip(groups, axes)
        ], following

    def summed(sides, got, later):
        return [
            widen([part[0] for part in [keep] + parts] + last)
            for (_, keep), parts, last in zip(sides, got, later)
        ]

    theirs = for_others(cot_t)
    theirs, arrived = lax.optimization_barrier((theirs, arrived))
    near.update({k: near_of(k, arrived[k]) for k in order[3:]})
    theirs, own_pieces, near = lax.optimization_barrier((theirs, own_pieces, near))
    other = swap(theirs, "core", 1)
    near, own_pieces = lax.optimization_barrier((near, own_pieces))
    for k in order[2:]:
        own_pieces[k] = far_of(k, arrived[k], near[k])
    sides = for_us(other)
    got = [first_round(sides[0])]
    sides[1:], own_pieces = lax.optimization_barrier((sides[1:], own_pieces))

    if in_place:
        pieces = [piece for k in order for piece in own_pieces[k]]
        flags = tuple(inner_first(k) for k in order)
        places = [
            jnp.stack([place_of(o, i, c, 0) // tp_count for o, i in chips]).astype(jnp.int32)
            for c in (core, 1 - core)
        ]
        offsets = jnp.stack([lax.rem(tp_place - shift + tp_count, tp_count) * rows for shift in shifts])
        offsets = offsets.astype(jnp.int32)
        total, own_weight = first_value(flags, places[0], offsets, residual, pieces)
    else:
        weight = []
        for k in order:
            both = jnp.stack(own_pieces[k])
            weight.append(both if inner_first(k) else jnp.swapaxes(both, 0, 1))
        by_shift = jnp.array([shifts.index(shift) for shift in range(tp_count)])
        weight = jnp.stack(weight)[by_shift[(tp_place - jnp.arange(tp_count)) % tp_count]]
        weight = weight[:, (at_outer - jnp.arange(outer)) % outer]
        weight = weight[:, :, (at_inner - jnp.arange(inner)) % inner]
        own_weight = weight.transpose(1, 2, 0, 3, 4).reshape(outer * inner, depth, features)
        total = jnp.zeros((), F32)
    got[0], sides[1:], total, own_weight = lax.optimization_barrier(
        (got[0], sides[1:], total, own_weight)
    )
    other_weight = swap(own_weight, "core", 1)
    first_later, sides[1:] = second_round(sides[0], got[0], sides[1:])
    later = [first_later]
    got += [first_round(side) for side in sides[1:]]
    if in_place:
        value_proj, coefficient = weight_call(
            functools.partial(value_end_kernel, width),
            places[1],
            residual,
            other_weight,
            [in_hbm(total), cot, inv_rms],
            [
                jax.ShapeDtypeStruct((rows_here, features), BF16),
                jax.ShapeDtypeStruct((rows_here, 1), F32),
            ],
        )
    else:
        both = jnp.stack([own_weight, other_weight], axis=1)
        weight = jnp.where(core == 0, both, both[:, ::-1]).reshape(width, features)
        value_acc = jnp.dot(residual, weight, preferred_element_type=F32)
        value_proj = (inv_rms * value_acc).astype(BF16)
        share = jnp.sum(cot.astype(F32) * value_acc, axis=1, keepdims=True)
        coefficient = inv_rms * inv_rms * share * (1.0 / width)
    later[0], coefficient = lax.optimization_barrier((later[0], coefficient))
    if in_place:
        groups = [[keep] + parts + then for (_, keep), parts, then in zip(sides[0], got[0], later[0])]
        sums = dict(zip(pairs[0], sums_of(groups, 0)))
    else:
        sums = dict(zip(pairs[0], summed(sides[0], got[0], later[0])))
    last = [swap(sums[k].astype(BF16), "tp", k) for k in pairs[0]]
    if in_place:
        grad_shape = jax.ShapeDtypeStruct((rows_here, width), BF16)
        resid_grad = weight_call(
            grad_kernel, places[0], residual, in_hbm(own_weight), [cot, coefficient], grad_shape
        )
        got[1:], resid_grad = lax.optimization_barrier((got[1:], resid_grad))
    else:
        normed_grad = lax.dot_general(
            cot, weight, (((1,), (1,)), ((), ())), preferred_element_type=F32
        )
        resid_grad = (normed_grad - residual.astype(F32) * coefficient).astype(BF16)
    later += [second_round(side, parts)[0] for side, parts in zip(sides[1:], got[1:])]
    if in_place:
        resid_grad = weight_call(
            grad_kernel, places[1][:2], residual, other_weight, [cot, coefficient], grad_shape, resid_grad
        )
        later[1], last, resid_grad = lax.optimization_barrier((later[1], last, resid_grad))
    for pair, *rounds in zip(pairs[1:], sides[1:], got[1:], later[1:]):
        sums.update(zip(pair, summed(*rounds)))
    last += [swap(sums[k].astype(BF16), "tp", k) for k in backward[2:-1]]
    if in_place:
        resid_grad = weight_call(
            grad_kernel, places[1][2:], residual, other_weight, [cot, coefficient], grad_shape, resid_grad
        )
    grad_rows = widen([sums[0]] + last)
    late_gain, late_weight, grad_rows = lax.optimization_barrier((norm_gain, value_weight, grad_rows))
    weight_grad = (late_gain.astype(F32)[None, :] * grad_rows).T
    gain_grad = jnp.sum(late_weight.astype(F32).T * grad_rows, axis=0)
    return (value_proj, resid_grad, weight_grad, gain_grad)


def solution(mesh):
    rep_count, tp_count = mesh.shape["rep"], mesh.shape["tp"]
    split = jax.sharding.Mesh(
        mesh.devices.reshape(OUTER, rep_count // (OUTER * CORES), CORES, tp_count),
        ("outer", "inner", "core", "tp"),
    )
    rep = ("outer", "inner", "core")
    rows = rep + ("tp",)
    return jax.shard_map(
        per_device,
        mesh=split,
        in_specs=(
            P(rows, None),
            P(rows),
            P(rows, None),
            P(rows, None),
            P(rows),
            P("tp", rep),
            P("tp", rep),
            P("tp", rep),
            P(rep),
            P(),
        ),
        out_specs=(P(rows, None), P(rows, None), P(rows, None), P(rows)),
        check_vma=False,
    )
```

```python
import functools

import jax
import jax.numpy as jnp
from jax import lax
from jax.experimental import pallas as pl
from jax.experimental.pallas import tpu as pltpu
from jax.sharding import PartitionSpec as P

VOCAB = 128256
EPS = 1e-05
BETA = 0.5
CORES = 2
OUTER = 2
PAIR_VMEM = 18 * 1024 * 1024
WEIGHT_VMEM = 22 * 1024 * 1024
NOMINAL = pl.CostEstimate(flops=1024, bytes_accessed=1024, transcendentals=0)
BF16 = jnp.bfloat16
F32 = jnp.float32


def swap(value, axis, step):
    size = lax.axis_size(axis)
    return lax.ppermute(value, axis, [(place, (place + step) % size) for place in range(size)])


def trade(value, axis, mask):
    size = lax.axis_size(axis)
    return lax.ppermute(value, axis, [(place, place ^ mask) for place in range(size)])


def in_hbm(array):
    return pltpu.with_memory_space_constraint(array, pltpu.HBM)


def after(value, *earlier):
    return lax.optimization_barrier((value, earlier))[0]


def widen(parts):
    return functools.reduce(jnp.add, [part.astype(F32) for part in parts])


def chunk_shifts(tp_count):
    shifts = [0]
    for step in range(1, tp_count // 2 + 1):
        shifts += [step] if 2 * step == tp_count else [step, tp_count - step]
    return shifts


def inner_first(chunk):
    return chunk % 4 in (0, 3)


def theirs_kernel(places_ref, cot_ref, *rest):
    blocks, out_ref = rest[:-1], rest[-1]
    for slot, resid_ref in enumerate(blocks):
        product = jnp.dot(cot_ref[...], resid_ref[...], preferred_element_type=F32)
        out_ref[slot, 0] = product.astype(BF16)


def ours_kernel(places_ref, cot_ref, *rest):
    slots = len(rest) // 3
    blocks, other_ref, outs = rest[:slots], rest[slots], rest[slots + 1 :]
    step = pl.program_id(0)
    ways = (lax.rem(step, 2), step // 2)
    totals = [
        (
            jnp.dot(cot_ref[...], resid_ref[...], preferred_element_type=F32)
            + other_ref[slot, 0].astype(F32)
        ).astype(BF16)
        for slot, resid_ref in enumerate(blocks)
    ]
    for which, way in enumerate(ways):

        @pl.when(way == 1)
        def _():
            for slot in range(which, slots, 2):
                outs[2 * slot][0] = totals[slot]

        @pl.when(way == 0)
        def _():
            for slot in range(which, slots, 2):
                outs[2 * slot + 1][0] = totals[slot]


def grad_product(residual, cot_t, places, rows, other):
    features, tokens = cot_t.shape
    steps = 4
    slots = places.shape[0] // steps
    in_specs = [pl.BlockSpec((features, tokens), lambda i, p: (0, 0))] + [
        pl.BlockSpec((tokens, rows), lambda i, p, slot=slot: (0, p[slots * i + slot]))
        for slot in range(slots)
    ]
    operands = [places, cot_t] + [in_hbm(residual)] * slots
    block = pl.BlockSpec((slots, 1, features, rows), lambda i, p: (0, i, 0, 0))
    if other is None:
        kernel, out_specs = theirs_kernel, block
        out_shape = pltpu.HBM((slots, steps, features, rows), BF16)
    else:
        kernel = ours_kernel
        in_specs.append(block)
        operands.append(other)
        indices = [
            lambda i: i // 2,
            lambda i: i // 2,
            lambda i: jnp.maximum(i - 2, 0),
            lambda i: jnp.minimum(i, 1),
        ]
        out_specs = [
            pl.BlockSpec((1, features, rows), lambda i, p, index=index: (index(i), 0, 0))
            for index in indices
        ] * (slots // 2)
        out_shape = [pltpu.HBM((2, features, rows), BF16)] * (2 * slots)
    return pl.pallas_call(
        kernel,
        out_shape=out_shape,
        grid_spec=pltpu.PrefetchScalarGridSpec(
            num_scalar_prefetch=1, grid=(steps,), in_specs=in_specs, out_specs=out_specs
        ),
        cost_estimate=NOMINAL,
        compiler_params=pltpu.CompilerParams(vmem_limit_bytes=PAIR_VMEM),
    )(*operands)


def sum_kernel(counts, *refs):
    ins, outs = refs[: sum(counts)], refs[sum(counts) :]
    for n, out_ref in enumerate(outs):
        first = sum(counts[:n])
        parts = [ref[...].astype(F32).reshape(out_ref.shape) for ref in ins[first : first + counts[n]]]
        out_ref[...] = functools.reduce(jnp.add, parts).astype(BF16)


def sums_of(groups, slot):
    shape = groups[0][0].shape[-2:]
    in_specs = [
        pl.BlockSpec((1,) + shape, lambda i: (slot, 0, 0))
        if part.ndim == 3
        else pl.BlockSpec(shape, lambda i: (0, 0))
        for parts in groups
        for part in parts
    ]
    return pl.pallas_call(
        functools.partial(sum_kernel, [len(parts) for parts in groups]),
        out_shape=[jax.ShapeDtypeStruct(shape, BF16)] * len(groups),
        grid=(1,),
        in_specs=in_specs,
        out_specs=[pl.BlockSpec(shape, lambda i: (0, 0))] * len(groups),
        cost_estimate=NOMINAL,
        compiler_params=pltpu.CompilerParams(vmem_limit_bytes=PAIR_VMEM),
    )(*[part for parts in groups for part in parts])


def place_weight(inner_flags, offsets_ref, pieces, weight_ref):
    step = pl.program_id(0)
    at_outer, at_inner = step // 2, lax.rem(step, 2)
    rows = pieces[0].shape[1]
    for chunk, flag in enumerate(inner_flags):
        way = at_outer if flag else at_inner
        where = pl.ds(pl.multiple_of(offsets_ref[chunk], rows), rows)
        for late in range(2):
            piece = pieces[chunk * 2 + late]

            @pl.when(way == late)
            def _():
                weight_ref[0, where, :] = piece[0]


def piece_specs(inner_flags, rows, features):
    specs = []
    for flag in inner_flags:
        for late in range(2):
            if flag:
                index = lambda i, *_, first=2 * late: (jnp.clip(i - first, 0, 1), 0, 0)
            else:
                index = lambda i, *_: (i // 2, 0, 0)
            specs.append(pl.BlockSpec((1, rows, features), index))
    return specs


def value_kernel(inner_flags, places_ref, offsets_ref, resid_ref, *rest):
    pieces, (total_ref, weight_ref) = rest[:-2], rest[-2:]
    step = pl.program_id(0)
    place_weight(inner_flags, offsets_ref, pieces, weight_ref)
    product = jnp.dot(resid_ref[...], weight_ref[0], preferred_element_type=F32)

    @pl.when(step == 0)
    def _():
        total_ref[...] = product

    @pl.when(step > 0)
    def _():
        total_ref[...] += product


def value_end_kernel(
    width, places_ref, resid_ref, weight_ref, first_ref, cot_ref, inv_ref, value_ref, coef_ref, total_ref
):
    step = pl.program_id(0)
    product = jnp.dot(resid_ref[...], weight_ref[0], preferred_element_type=F32)

    @pl.when(step == 0)
    def _():
        total_ref[...] = first_ref[...] + product

    @pl.when(step > 0)
    def _():
        total_ref[...] += product

    @pl.when(step == pl.num_programs(0) - 1)
    def _():
        total = total_ref[...]
        inv = inv_ref[...]
        value_ref[...] = (total * inv).astype(BF16)
        share = jnp.sum(total * cot_ref[...].astype(F32), axis=1, keepdims=True)
        coef_ref[...] = share * (inv * inv) * (1.0 / width)


def grad_kernel(places_ref, resid_ref, weight_ref, cot_ref, coef_ref, *rest):
    out_ref = rest[-1]
    grad = lax.dot_general(
        cot_ref[...], weight_ref[0], (((1,), (1,)), ((), ())), preferred_element_type=F32
    )
    out_ref[...] = (grad - resid_ref[...].astype(F32) * coef_ref[...]).astype(BF16)


def whole_block(array):
    return pl.BlockSpec(array.shape, lambda i, *_: (0, 0))


def first_value(inner_flags, places, offsets, residual, pieces):
    tokens, width = residual.shape
    rows, features = pieces[0].shape[1:]
    steps = places.shape[0]
    depth = width // (CORES * steps)
    total = pltpu.HBM((tokens, features), F32)
    return pl.pallas_call(
        functools.partial(value_kernel, inner_flags),
        out_shape=[total, pltpu.HBM((steps, depth, features), BF16)],
        grid_spec=pltpu.PrefetchScalarGridSpec(
            num_scalar_prefetch=2,
            grid=(steps,),
            in_specs=[pl.BlockSpec((tokens, depth), lambda i, p, o: (0, p[i]))]
            + piece_specs(inner_flags, rows, features),
            out_specs=[
                whole_block(total),
                pl.BlockSpec((1, depth, features), lambda i, p, o: (p[i] // CORES, 0, 0)),
            ],
        ),
        cost_estimate=NOMINAL,
        compiler_params=pltpu.CompilerParams(vmem_limit_bytes=WEIGHT_VMEM),
    )(places, offsets, in_hbm(residual), *pieces)


def weight_call(kernel, places, residual, weight, wholes, out_shape, earlier=None):
    tokens, width = residual.shape
    _, depth, features = weight.shape
    steps = places.shape[0]
    scratch = []
    if isinstance(out_shape, list):
        out_specs = [whole_block(array) for array in out_shape]
        scratch.append(pltpu.VMEM((tokens, features), F32))
    else:
        out_specs = pl.BlockSpec((tokens, depth), lambda i, p: (0, p[i]))
    in_specs = [
        pl.BlockSpec((tokens, depth), lambda i, p: (0, p[i])),
        pl.BlockSpec((1, depth, features), lambda i, p: (p[i] // CORES, 0, 0)),
    ] + [whole_block(array) for array in wholes]
    operands = [places, in_hbm(residual), weight, *wholes]
    aliases = {}
    if earlier is not None:
        aliases = {len(operands): 0}
        in_specs.append(pl.BlockSpec(memory_space=pltpu.HBM))
        operands.append(earlier)
    return pl.pallas_call(
        kernel,
        out_shape=out_shape,
        grid_spec=pltpu.PrefetchScalarGridSpec(
            num_scalar_prefetch=1,
            grid=(steps,),
            in_specs=in_specs,
            out_specs=out_specs,
            scratch_shapes=scratch,
        ),
        input_output_aliases=aliases,
        cost_estimate=NOMINAL,
        compiler_params=pltpu.CompilerParams(vmem_limit_bytes=WEIGHT_VMEM),
    )(*operands)


def cot_kernel(width, rep_count, info_ref, shares_ref, squares_ref, value_cot_ref, cot_ref, cot_t_ref, inv_ref):
    place, length = info_ref[0], info_ref[1]
    rows = value_cot_ref.shape[0]
    own = rows // 128
    seq = (shares_ref.shape[1] - own) // 3
    shares = range(shares_ref.shape[0])

    def below(first, shape):
        at = lax.broadcasted_iota(jnp.int32, shape, 0) * 128 + lax.broadcasted_iota(jnp.int32, shape, 1)
        return first + at < length

    def summed(mask, value):
        return jnp.sum(jnp.where(mask, value, 0.0), axis=(0, 1), keepdims=True)

    maxes = [shares_ref[m, 0:seq] for m in shares]
    top_max = functools.reduce(jnp.maximum, maxes)
    sum_exp = functools.reduce(
        jnp.add, [shares_ref[m, seq : 2 * seq] * jnp.exp(maxes[m] - top_max) for m in shares]
    )
    picked = functools.reduce(jnp.add, [shares_ref[m, 2 * seq : 3 * seq] for m in shares])
    ref_logp = picked - top_max - jnp.log(sum_exp)
    total = -summed(below(0, (seq, 128)), ref_logp)
    for m in shares:
        first = jnp.bitwise_xor(place, m) * rows
        total += summed(below(first, (own, 128)), shares_ref[m, 3 * seq :])
    seq_delta = total / jnp.full((1, 1), length, jnp.int32).astype(F32)
    weight = (2.0 / rep_count) * jax.nn.sigmoid(BETA * seq_delta)
    inv = lax.rsqrt(squares_ref[...] * (1.0 / width) + EPS)
    live = place * rows + lax.broadcasted_iota(jnp.int32, (rows, 1), 0) < length
    scaled = jnp.where(live, inv * weight, 0.0) * value_cot_ref[...].astype(F32)
    cot_ref[...] = scaled.astype(BF16)
    cot_t_ref[...] = scaled.T.astype(BF16)
    inv_ref[...] = inv


def scaled_cot(width, rep_count, info, shares, squares, value_cot):
    rows, features = value_cot.shape

    def whole(array):
        return pl.BlockSpec(array.shape, lambda i, p: (0,) * array.ndim)

    out_shape = [
        jax.ShapeDtypeStruct((rows, features), BF16),
        jax.ShapeDtypeStruct((features, rows), BF16),
        jax.ShapeDtypeStruct((rows, 1), F32),
    ]
    return pl.pallas_call(
        functools.partial(cot_kernel, width, rep_count),
        out_shape=out_shape,
        grid_spec=pltpu.PrefetchScalarGridSpec(
            num_scalar_prefetch=1,
            grid=(1,),
            in_specs=[whole(shares), whole(squares), whole(value_cot)],
            out_specs=[pl.BlockSpec(array.shape, lambda i, p: (0, 0)) for array in out_shape],
        ),
        cost_estimate=NOMINAL,
        compiler_params=pltpu.CompilerParams(vmem_limit_bytes=PAIR_VMEM),
    )(info, shares, squares, in_hbm(value_cot))


def per_device(
    residual,
    norm_gain,
    value_weight,
    value_cot,
    trainee_logp,
    ref_shard_max,
    ref_shard_sum,
    ref_target_logit,
    target_ids,
    lengths,
):
    rows_here, width = residual.shape
    features = value_cot.shape[1]
    tp_count = lax.axis_size("tp")
    outer, inner = lax.axis_size("outer"), lax.axis_size("inner")
    rep_count = outer * inner * CORES
    tp_place = lax.axis_index("tp")
    core = lax.axis_index("core")
    at_inner = lax.axis_index("inner")
    at_outer = lax.axis_index("outer")
    rep_place = (at_outer * inner + at_inner) * CORES + core
    depth = width // rep_count
    rows = depth // tp_count
    order = list(range(tp_count))
    shifts = chunk_shifts(tp_count)
    in_place = rows % 128 == 0 and outer == 2 and inner == 2

    owned = jnp.where(
        target_ids // (VOCAB // tp_count) == tp_place,
        ref_target_logit[0],
        jnp.zeros_like(ref_target_logit[0]),
    )
    packed = jnp.concatenate([ref_shard_max[0], ref_shard_sum[0], owned, trainee_logp])
    packed = packed.reshape(1, -1, 128)
    packed = jnp.concatenate([packed, trade(packed, "tp", 1)])

    gained = (value_weight.astype(F32) * norm_gain.astype(F32)[:, None]).astype(BF16)
    residual, gained, packed = lax.optimization_barrier((residual, gained, packed))
    resid_wide = residual.astype(F32)
    squares = jnp.sum(resid_wide * resid_wide, axis=1, keepdims=True)

    def near_of(k, block):
        first = "inner" if inner_first(k) else "outer"
        return [swap(block, first, s) for s in range(1, lax.axis_size(first))]

    def far_of(k, block, nears):
        second = "outer" if inner_first(k) else "inner"
        near = jnp.stack([block] + nears)
        return [near] + [swap(near, second, s) for s in range(1, lax.axis_size(second))]

    mask = 2
    while mask < tp_count:
        packed = jnp.concatenate([packed, trade(packed, "tp", mask)])
        mask *= 2
    own_pieces, near = {}, {}
    arrived = {0: gained, 1: swap(gained, "tp", shifts[1])}
    near[0] = near_of(0, gained)
    arrived[1], near[0], squares, late_gained = lax.optimization_barrier(
        (arrived[1], near[0], squares, gained)
    )
    near[1] = near_of(1, arrived[1])
    arrived[2] = swap(late_gained, "tp", shifts[2])
    own_pieces[0] = far_of(0, gained, near[0])
    seq_length = lax.dynamic_index_in_dim(lengths, rep_place, keepdims=False)
    info = jnp.stack([tp_place, seq_length]).astype(jnp.int32)
    packed, squares, info = lax.optimization_barrier((packed, squares, info))
    cot, cot_t, inv_rms = scaled_cot(width, rep_count, info, packed, squares, value_cot)

    def place_of(o, i, c, k):
        chip = lax.rem(at_outer + o, outer) * inner + lax.rem(at_inner + i, inner)
        return (chip * CORES + c) * tp_count + lax.rem(tp_place + k, tp_count)

    backward = order[::-1]
    pairs = [backward[i : i + 2] for i in range(0, tp_count, 2)]
    chips = [(o, i) for o in range(outer) for i in range(inner)]
    if not in_place:
        product = jnp.dot(cot_t, residual, preferred_element_type=F32).astype(BF16)
        product = product.reshape(features, -1, rows).transpose(1, 0, 2)

    def places_of(pair, c):
        return jnp.stack([place_of(o, i, c, k) for o, i in chips for k in pair]).astype(jnp.int32)

    def for_others(cot_t):
        places = places_of(backward, 1 - core)
        if in_place:
            return grad_product(residual, cot_t, places, rows, None)
        both = after(product, cot_t)[places].reshape(len(chips), tp_count, features, rows)
        return both.swapaxes(0, 1)

    def for_us(other):
        places = places_of(backward, core)
        if in_place:
            outs = grad_product(residual, cot_t, places, rows, other)
            sides = [([outs[2 * n]], outs[2 * n + 1]) for n in range(tp_count)]
        else:
            both = product[places].reshape(len(chips), tp_count, features, rows).swapaxes(0, 1)
            total = widen([both, other]).astype(BF16)
            total = total.reshape(tp_count, outer, inner, features, rows)
            sides = []
            for n in range(0, tp_count, 2):
                sides.append(([total[n, :, s] for s in range(1, inner)], total[n, :, 0]))
                sides.append(([total[n + 1, s] for s in range(1, outer)], total[n + 1, 0]))
        return [sides[n : n + 2] for n in range(0, tp_count, 2)]

    def first_round(sides):
        return [
            [swap(send, axis, s + 1) for s, send in enumerate(sends)]
            for axis, (sends, _) in zip(("inner", "outer"), sides)
        ]

    def second_round(sides, got, following=()):
        axes = ("outer", "inner")
        groups = [[keep] + parts for (_, keep), parts in zip(sides, got)]
        if in_place:
            sent, following = lax.optimization_barrier((sums_of(groups, 1), following))
            return [[swap(x, axis, 1)] for x, axis in zip(sent, axes)], following
        return [
            [
                swap(widen([part[s] for part in parts]).astype(BF16), axis, s)
                for s in range(1, lax.axis_size(axis))
            ]
            for parts, axis in zip(groups, axes)
        ], following

    def summed(sides, got, later):
        return [
            widen([part[0] for part in [keep] + parts] + last)
            for (_, keep), parts, last in zip(sides, got, later)
        ]

    theirs = for_others(cot_t)
    theirs, near[1], arrived[2], late_gained = lax.optimization_barrier(
        (theirs, near[1], arrived[2], late_gained)
    )
    other = swap(theirs, "core", 1)
    for k in order[3:]:
        arrived[k] = swap(late_gained, "tp", shifts[k])
    own_pieces[1] = far_of(1, arrived[1], near[1])
    near[2] = near_of(2, arrived[2])
    sides = for_us(other)
    sides, arrived, own_pieces, near[2] = lax.optimization_barrier(
        (sides, arrived, own_pieces, near[2])
    )
    for k in order[3:]:
        near[k] = near_of(k, arrived[k])
    got = [first_round(sides[0])]
    near, sides[1:] = lax.optimization_barrier((near, sides[1:]))
    for k in order[2:]:
        own_pieces[k] = far_of(k, arrived[k], near[k])
    first_later, _ = second_round(sides[0], got[0])
    later = [first_later]
    sides[1:], own_pieces = lax.optimization_barrier((sides[1:], own_pieces))
    got += [first_round(side) for side in sides[1:]]

    if in_place:
        pieces = [piece for k in order for piece in own_pieces[k]]
        flags = tuple(inner_first(k) for k in order)
        places = [
            jnp.stack([place_of(o, i, c, 0) // tp_count for o, i in chips]).astype(jnp.int32)
            for c in (core, 1 - core)
        ]
        offsets = jnp.stack([lax.rem(tp_place - shift + tp_count, tp_count) * rows for shift in shifts])
        offsets = offsets.astype(jnp.int32)
        total, own_weight = first_value(flags, places[0], offsets, residual, pieces)
    else:
        weight = []
        for k in order:
            both = jnp.stack(own_pieces[k])
            weight.append(both if inner_first(k) else jnp.swapaxes(both, 0, 1))
        by_shift = jnp.array([shifts.index(shift) for shift in range(tp_count)])
        weight = jnp.stack(weight)[by_shift[(tp_place - jnp.arange(tp_count)) % tp_count]]
        weight = weight[:, (at_outer - jnp.arange(outer)) % outer]
        weight = weight[:, :, (at_inner - jnp.arange(inner)) % inner]
        own_weight = weight.transpose(1, 2, 0, 3, 4).reshape(outer * inner, depth, features)
        total = jnp.zeros((), F32)
    total, own_weight, later[0] = lax.optimization_barrier((total, own_weight, later[0]))
    other_weight = swap(own_weight, "core", 1)
    if in_place:
        groups = [[keep] + parts + then for (_, keep), parts, then in zip(sides[0], got[0], later[0])]
        sums = dict(zip(pairs[0], sums_of(groups, 0)))
    else:
        sums = dict(zip(pairs[0], summed(sides[0], got[0], later[0])))
    last = [swap(sums[k].astype(BF16), "tp", k) for k in pairs[0]]
    total = after(total, sums)
    if in_place:
        value_proj, coefficient = weight_call(
            functools.partial(value_end_kernel, width),
            places[1],
            residual,
            other_weight,
            [in_hbm(total), cot, inv_rms],
            [
                jax.ShapeDtypeStruct((rows_here, features), BF16),
                jax.ShapeDtypeStruct((rows_here, 1), F32),
            ],
        )
    else:
        both = jnp.stack([own_weight, other_weight], axis=1)
        weight = jnp.where(core == 0, both, both[:, ::-1]).reshape(width, features)
        value_acc = jnp.dot(residual, weight, preferred_element_type=F32)
        value_proj = (inv_rms * value_acc).astype(BF16)
        share = jnp.sum(cot.astype(F32) * value_acc, axis=1, keepdims=True)
        coefficient = inv_rms * inv_rms * share * (1.0 / width)
    got[1:], coefficient = lax.optimization_barrier((got[1:], coefficient))
    later += [second_round(side, parts)[0] for side, parts in zip(sides[1:], got[1:])]
    if in_place:
        grad_shape = jax.ShapeDtypeStruct((rows_here, width), BF16)
        resid_grad = weight_call(
            grad_kernel, places[0], residual, in_hbm(own_weight), [cot, coefficient], grad_shape
        )
        later[1], last, resid_grad = lax.optimization_barrier((later[1], last, resid_grad))
    else:
        normed_grad = lax.dot_general(
            cot, weight, (((1,), (1,)), ((), ())), preferred_element_type=F32
        )
        resid_grad = (normed_grad - residual.astype(F32) * coefficient).astype(BF16)
    for pair, *rounds in zip(pairs[1:], sides[1:], got[1:], later[1:]):
        sums.update(zip(pair, summed(*rounds)))
    last += [swap(sums[k].astype(BF16), "tp", k) for k in backward[2:-1]]
    if in_place:
        resid_grad = weight_call(
            grad_kernel, places[1], residual, other_weight, [cot, coefficient], grad_shape, resid_grad
        )
    grad_rows = widen([sums[0]] + last)
    late_gain, late_weight, grad_rows = lax.optimization_barrier((norm_gain, value_weight, grad_rows))
    weight_grad = (late_gain.astype(F32)[None, :] * grad_rows).T
    gain_grad = jnp.sum(late_weight.astype(F32).T * grad_rows, axis=0)
    return (value_proj, resid_grad, weight_grad, gain_grad)


def solution(mesh):
    rep_count, tp_count = mesh.shape["rep"], mesh.shape["tp"]
    split = jax.sharding.Mesh(
        mesh.devices.reshape(OUTER, rep_count // (OUTER * CORES), CORES, tp_count),
        ("outer", "inner", "core", "tp"),
    )
    rep = ("outer", "inner", "core")
    rows = rep + ("tp",)
    return jax.shard_map(
        per_device,
        mesh=split,
        in_specs=(
            P(rows, None),
            P(rows),
            P(rows, None),
            P(rows, None),
            P(rows),
            P("tp", rep),
            P("tp", rep),
            P("tp", rep),
            P(rep),
            P(),
        ),
        out_specs=(P(rows, None), P(rows, None), P(rows, None), P(rows)),
        check_vma=False,
    )
```

```python
import functools

import jax
import jax.numpy as jnp
from jax import lax
from jax.experimental import pallas as pl
from jax.experimental.pallas import tpu as pltpu
from jax.sharding import PartitionSpec as P

VOCAB = 128256
EPS = 1e-05
BETA = 0.5
CORES = 2
OUTER = 2
PAIR_VMEM = 18 * 1024 * 1024
WEIGHT_VMEM = 22 * 1024 * 1024
NOMINAL = pl.CostEstimate(flops=1024, bytes_accessed=1024, transcendentals=0)
BF16 = jnp.bfloat16
F32 = jnp.float32


def swap(value, axis, step):
    size = lax.axis_size(axis)
    return lax.ppermute(value, axis, [(place, (place + step) % size) for place in range(size)])


def trade(value, axis, mask):
    size = lax.axis_size(axis)
    return lax.ppermute(value, axis, [(place, place ^ mask) for place in range(size)])


def in_hbm(array):
    return pltpu.with_memory_space_constraint(array, pltpu.HBM)


def after(value, *earlier):
    return lax.optimization_barrier((value, earlier))[0]


def widen(parts):
    return functools.reduce(jnp.add, [part.astype(F32) for part in parts])


def chunk_shifts(tp_count):
    shifts = [0]
    for step in range(1, tp_count // 2 + 1):
        shifts += [step] if 2 * step == tp_count else [step, tp_count - step]
    return shifts


def inner_first(chunk):
    return chunk % 4 in (0, 3)


def theirs_kernel(places_ref, cot_ref, *rest):
    blocks, out_ref = rest[:-1], rest[-1]
    for slot, resid_ref in enumerate(blocks):
        product = jnp.dot(cot_ref[...], resid_ref[...], preferred_element_type=F32)
        out_ref[slot, 0] = product.astype(BF16)


def ours_kernel(places_ref, cot_ref, *rest):
    slots = len(rest) // 3
    blocks, other_ref, outs = rest[:slots], rest[slots], rest[slots + 1 :]
    step = pl.program_id(0)
    ways = (lax.rem(step, 2), step // 2)
    totals = [
        (
            jnp.dot(cot_ref[...], resid_ref[...], preferred_element_type=F32)
            + other_ref[slot, 0].astype(F32)
        ).astype(BF16)
        for slot, resid_ref in enumerate(blocks)
    ]
    for which, way in enumerate(ways):

        @pl.when(way == 1)
        def _():
            for slot in range(which, slots, 2):
                outs[2 * slot][0] = totals[slot]

        @pl.when(way == 0)
        def _():
            for slot in range(which, slots, 2):
                outs[2 * slot + 1][0] = totals[slot]


def grad_product(residual, cot_t, places, rows, other):
    features, tokens = cot_t.shape
    steps = 4
    slots = places.shape[0] // steps
    in_specs = [pl.BlockSpec((features, tokens), lambda i, p: (0, 0))] + [
        pl.BlockSpec((tokens, rows), lambda i, p, slot=slot: (0, p[slots * i + slot]))
        for slot in range(slots)
    ]
    operands = [places, cot_t] + [in_hbm(residual)] * slots
    block = pl.BlockSpec((slots, 1, features, rows), lambda i, p: (0, i, 0, 0))
    if other is None:
        kernel, out_specs = theirs_kernel, block
        out_shape = pltpu.HBM((slots, steps, features, rows), BF16)
    else:
        kernel = ours_kernel
        in_specs.append(block)
        operands.append(other)
        indices = [
            lambda i: i // 2,
            lambda i: i // 2,
            lambda i: jnp.maximum(i - 2, 0),
            lambda i: jnp.minimum(i, 1),
        ]
        out_specs = [
            pl.BlockSpec((1, features, rows), lambda i, p, index=index: (index(i), 0, 0))
            for index in indices
        ] * (slots // 2)
        out_shape = [pltpu.HBM((2, features, rows), BF16)] * (2 * slots)
    return pl.pallas_call(
        kernel,
        out_shape=out_shape,
        grid_spec=pltpu.PrefetchScalarGridSpec(
            num_scalar_prefetch=1, grid=(steps,), in_specs=in_specs, out_specs=out_specs
        ),
        cost_estimate=NOMINAL,
        compiler_params=pltpu.CompilerParams(vmem_limit_bytes=PAIR_VMEM),
    )(*operands)


def sum_kernel(counts, *refs):
    ins, outs = refs[: sum(counts)], refs[sum(counts) :]
    for n, out_ref in enumerate(outs):
        first = sum(counts[:n])
        parts = [ref[...].astype(F32).reshape(out_ref.shape) for ref in ins[first : first + counts[n]]]
        out_ref[...] = functools.reduce(jnp.add, parts).astype(BF16)


def sums_of(groups, slot):
    shape = groups[0][0].shape[-2:]
    in_specs = [
        pl.BlockSpec((1,) + shape, lambda i: (slot, 0, 0))
        if part.ndim == 3
        else pl.BlockSpec(shape, lambda i: (0, 0))
        for parts in groups
        for part in parts
    ]
    return pl.pallas_call(
        functools.partial(sum_kernel, [len(parts) for parts in groups]),
        out_shape=[jax.ShapeDtypeStruct(shape, BF16)] * len(groups),
        grid=(1,),
        in_specs=in_specs,
        out_specs=[pl.BlockSpec(shape, lambda i: (0, 0))] * len(groups),
        cost_estimate=NOMINAL,
        compiler_params=pltpu.CompilerParams(vmem_limit_bytes=PAIR_VMEM),
    )(*[part for parts in groups for part in parts])


def place_weight(inner_flags, offsets_ref, pieces, weight_ref):
    step = pl.program_id(0)
    at_outer, at_inner = step // 2, lax.rem(step, 2)
    rows = pieces[0].shape[1]
    for chunk, flag in enumerate(inner_flags):
        way = at_outer if flag else at_inner
        where = pl.ds(pl.multiple_of(offsets_ref[chunk], rows), rows)
        for late in range(2):
            piece = pieces[chunk * 2 + late]

            @pl.when(way == late)
            def _():
                weight_ref[0, where, :] = piece[0]


def piece_specs(inner_flags, rows, features):
    specs = []
    for flag in inner_flags:
        for late in range(2):
            if flag:
                index = lambda i, *_, first=2 * late: (jnp.clip(i - first, 0, 1), 0, 0)
            else:
                index = lambda i, *_: (i // 2, 0, 0)
            specs.append(pl.BlockSpec((1, rows, features), index))
    return specs


def value_kernel(inner_flags, places_ref, offsets_ref, resid_ref, *rest):
    pieces, (total_ref, weight_ref) = rest[:-2], rest[-2:]
    step = pl.program_id(0)
    place_weight(inner_flags, offsets_ref, pieces, weight_ref)
    product = jnp.dot(resid_ref[...], weight_ref[0], preferred_element_type=F32)

    @pl.when(step == 0)
    def _():
        total_ref[...] = product

    @pl.when(step > 0)
    def _():
        total_ref[...] += product


def value_end_kernel(
    width, places_ref, resid_ref, weight_ref, first_ref, cot_ref, inv_ref, value_ref, coef_ref, total_ref
):
    step = pl.program_id(0)
    product = jnp.dot(resid_ref[...], weight_ref[0], preferred_element_type=F32)

    @pl.when(step == 0)
    def _():
        total_ref[...] = first_ref[...] + product

    @pl.when(step > 0)
    def _():
        total_ref[...] += product

    @pl.when(step == pl.num_programs(0) - 1)
    def _():
        total = total_ref[...]
        inv = inv_ref[...]
        value_ref[...] = (total * inv).astype(BF16)
        share = jnp.sum(total * cot_ref[...].astype(F32), axis=1, keepdims=True)
        coef_ref[...] = share * (inv * inv) * (1.0 / width)


def grad_kernel(places_ref, resid_ref, weight_ref, cot_ref, coef_ref, *rest):
    out_ref = rest[-1]
    grad = lax.dot_general(
        cot_ref[...], weight_ref[0], (((1,), (1,)), ((), ())), preferred_element_type=F32
    )
    out_ref[...] = (grad - resid_ref[...].astype(F32) * coef_ref[...]).astype(BF16)


def whole_block(array):
    return pl.BlockSpec(array.shape, lambda i, *_: (0, 0))


def first_value(inner_flags, places, offsets, residual, pieces):
    tokens, width = residual.shape
    rows, features = pieces[0].shape[1:]
    steps = places.shape[0]
    depth = width // (CORES * steps)
    total = pltpu.HBM((tokens, features), F32)
    return pl.pallas_call(
        functools.partial(value_kernel, inner_flags),
        out_shape=[total, pltpu.HBM((steps, depth, features), BF16)],
        grid_spec=pltpu.PrefetchScalarGridSpec(
            num_scalar_prefetch=2,
            grid=(steps,),
            in_specs=[pl.BlockSpec((tokens, depth), lambda i, p, o: (0, p[i]))]
            + piece_specs(inner_flags, rows, features),
            out_specs=[
                whole_block(total),
                pl.BlockSpec((1, depth, features), lambda i, p, o: (p[i] // CORES, 0, 0)),
            ],
        ),
        cost_estimate=NOMINAL,
        compiler_params=pltpu.CompilerParams(vmem_limit_bytes=WEIGHT_VMEM),
    )(places, offsets, in_hbm(residual), *pieces)


def weight_call(kernel, places, residual, weight, wholes, out_shape, earlier=None):
    tokens, width = residual.shape
    _, depth, features = weight.shape
    steps = places.shape[0]
    scratch = []
    if isinstance(out_shape, list):
        out_specs = [whole_block(array) for array in out_shape]
        scratch.append(pltpu.VMEM((tokens, features), F32))
    else:
        out_specs = pl.BlockSpec((tokens, depth), lambda i, p: (0, p[i]))
    in_specs = [
        pl.BlockSpec((tokens, depth), lambda i, p: (0, p[i])),
        pl.BlockSpec((1, depth, features), lambda i, p: (p[i] // CORES, 0, 0)),
    ] + [whole_block(array) for array in wholes]
    operands = [places, in_hbm(residual), weight, *wholes]
    aliases = {}
    if earlier is not None:
        aliases = {len(operands): 0}
        in_specs.append(pl.BlockSpec(memory_space=pltpu.HBM))
        operands.append(earlier)
    return pl.pallas_call(
        kernel,
        out_shape=out_shape,
        grid_spec=pltpu.PrefetchScalarGridSpec(
            num_scalar_prefetch=1,
            grid=(steps,),
            in_specs=in_specs,
            out_specs=out_specs,
            scratch_shapes=scratch,
        ),
        input_output_aliases=aliases,
        cost_estimate=NOMINAL,
        compiler_params=pltpu.CompilerParams(vmem_limit_bytes=WEIGHT_VMEM),
    )(*operands)


def cot_kernel(width, rep_count, info_ref, shares_ref, squares_ref, value_cot_ref, cot_ref, cot_t_ref, inv_ref):
    place, length = info_ref[0], info_ref[1]
    rows = value_cot_ref.shape[0]
    own = rows // 128
    seq = (shares_ref.shape[1] - own) // 3
    shares = range(shares_ref.shape[0])

    def below(first, shape):
        at = lax.broadcasted_iota(jnp.int32, shape, 0) * 128 + lax.broadcasted_iota(jnp.int32, shape, 1)
        return first + at < length

    def summed(mask, value):
        return jnp.sum(jnp.where(mask, value, 0.0), axis=(0, 1), keepdims=True)

    maxes = [shares_ref[m, 0:seq] for m in shares]
    top_max = functools.reduce(jnp.maximum, maxes)
    sum_exp = functools.reduce(
        jnp.add, [shares_ref[m, seq : 2 * seq] * jnp.exp(maxes[m] - top_max) for m in shares]
    )
    picked = functools.reduce(jnp.add, [shares_ref[m, 2 * seq : 3 * seq] for m in shares])
    ref_logp = picked - top_max - jnp.log(sum_exp)
    total = -summed(below(0, (seq, 128)), ref_logp)
    for m in shares:
        first = jnp.bitwise_xor(place, m) * rows
        total += summed(below(first, (own, 128)), shares_ref[m, 3 * seq :])
    seq_delta = total / jnp.full((1, 1), length, jnp.int32).astype(F32)
    weight = (2.0 / rep_count) * jax.nn.sigmoid(BETA * seq_delta)
    inv = lax.rsqrt(squares_ref[...] * (1.0 / width) + EPS)
    live = place * rows + lax.broadcasted_iota(jnp.int32, (rows, 1), 0) < length
    scaled = jnp.where(live, inv * weight, 0.0) * value_cot_ref[...].astype(F32)
    cot_ref[...] = scaled.astype(BF16)
    cot_t_ref[...] = scaled.T.astype(BF16)
    inv_ref[...] = inv


def scaled_cot(width, rep_count, info, shares, squares, value_cot):
    rows, features = value_cot.shape

    def whole(array):
        return pl.BlockSpec(array.shape, lambda i, p: (0,) * array.ndim)

    out_shape = [
        jax.ShapeDtypeStruct((rows, features), BF16),
        jax.ShapeDtypeStruct((features, rows), BF16),
        jax.ShapeDtypeStruct((rows, 1), F32),
    ]
    return pl.pallas_call(
        functools.partial(cot_kernel, width, rep_count),
        out_shape=out_shape,
        grid_spec=pltpu.PrefetchScalarGridSpec(
            num_scalar_prefetch=1,
            grid=(1,),
            in_specs=[whole(shares), whole(squares), whole(value_cot)],
            out_specs=[pl.BlockSpec(array.shape, lambda i, p: (0, 0)) for array in out_shape],
        ),
        cost_estimate=NOMINAL,
        compiler_params=pltpu.CompilerParams(vmem_limit_bytes=PAIR_VMEM),
    )(info, shares, squares, in_hbm(value_cot))


def per_device(
    residual,
    norm_gain,
    value_weight,
    value_cot,
    trainee_logp,
    ref_shard_max,
    ref_shard_sum,
    ref_target_logit,
    target_ids,
    lengths,
):
    rows_here, width = residual.shape
    features = value_cot.shape[1]
    tp_count = lax.axis_size("tp")
    outer, inner = lax.axis_size("outer"), lax.axis_size("inner")
    rep_count = outer * inner * CORES
    tp_place = lax.axis_index("tp")
    core = lax.axis_index("core")
    at_inner = lax.axis_index("inner")
    at_outer = lax.axis_index("outer")
    rep_place = (at_outer * inner + at_inner) * CORES + core
    depth = width // rep_count
    rows = depth // tp_count
    order = list(range(tp_count))
    shifts = chunk_shifts(tp_count)
    in_place = rows % 128 == 0 and outer == 2 and inner == 2

    owned = jnp.where(
        target_ids // (VOCAB // tp_count) == tp_place,
        ref_target_logit[0],
        jnp.zeros_like(ref_target_logit[0]),
    )
    packed = jnp.concatenate([ref_shard_max[0], ref_shard_sum[0], owned, trainee_logp])
    packed = packed.reshape(1, -1, 128)
    resid_wide = residual.astype(F32)
    squares = jnp.sum(resid_wide * resid_wide, axis=1, keepdims=True)
    squares, packed, late_gain, late_weight = lax.optimization_barrier(
        (squares, packed, norm_gain, value_weight)
    )
    packed = jnp.concatenate([packed, trade(packed, "tp", 1)])

    gained = (late_weight.astype(F32) * late_gain.astype(F32)[:, None]).astype(BF16)
    gained, packed = lax.optimization_barrier((gained, packed))

    def near_of(k, block):
        first = "inner" if inner_first(k) else "outer"
        return [swap(block, first, s) for s in range(1, lax.axis_size(first))]

    def far_of(k, stacked):
        second = "outer" if inner_first(k) else "inner"
        return [stacked] + [swap(stacked, second, s) for s in range(1, lax.axis_size(second))]

    mask = 2
    while mask < tp_count:
        packed = jnp.concatenate([packed, trade(packed, "tp", mask)])
        mask *= 2
    own_pieces, near = {}, {}
    arrived = {0: gained, 1: swap(gained, "tp", shifts[1])}
    near[0] = near_of(0, gained)
    arrived[1], near[0], packed, late_gained = lax.optimization_barrier(
        (arrived[1], near[0], packed, gained)
    )
    near[1] = near_of(1, arrived[1])
    for k in order[2:]:
        arrived[k] = swap(late_gained, "tp", shifts[k])
    seq_length = lax.dynamic_index_in_dim(lengths, rep_place, keepdims=False)
    info = jnp.stack([tp_place, seq_length]).astype(jnp.int32)
    cot, cot_t, inv_rms = scaled_cot(width, rep_count, info, packed, squares, value_cot)

    def place_of(o, i, c, k):
        chip = lax.rem(at_outer + o, outer) * inner + lax.rem(at_inner + i, inner)
        return (chip * CORES + c) * tp_count + lax.rem(tp_place + k, tp_count)

    backward = order[::-1]
    pairs = [backward[i : i + 2] for i in range(0, tp_count, 2)]
    chips = [(o, i) for o in range(outer) for i in range(inner)]
    if not in_place:
        product = jnp.dot(cot_t, residual, preferred_element_type=F32).astype(BF16)
        product = product.reshape(features, -1, rows).transpose(1, 0, 2)

    def places_of(pair, c):
        return jnp.stack([place_of(o, i, c, k) for o, i in chips for k in pair]).astype(jnp.int32)

    def for_others(cot_t):
        places = places_of(backward, 1 - core)
        if in_place:
            return grad_product(residual, cot_t, places, rows, None)
        both = after(product, cot_t)[places].reshape(len(chips), tp_count, features, rows)
        return both.swapaxes(0, 1)

    def for_us(other):
        places = places_of(backward, core)
        if in_place:
            outs = grad_product(residual, cot_t, places, rows, other)
            sides = [([outs[2 * n]], outs[2 * n + 1]) for n in range(tp_count)]
        else:
            both = product[places].reshape(len(chips), tp_count, features, rows).swapaxes(0, 1)
            total = widen([both, other]).astype(BF16)
            total = total.reshape(tp_count, outer, inner, features, rows)
            sides = []
            for n in range(0, tp_count, 2):
                sides.append(([total[n, :, s] for s in range(1, inner)], total[n, :, 0]))
                sides.append(([total[n + 1, s] for s in range(1, outer)], total[n + 1, 0]))
        return [sides[n : n + 2] for n in range(0, tp_count, 2)]

    def first_round(sides):
        return [
            [swap(send, axis, s + 1) for s, send in enumerate(sends)]
            for axis, (sends, _) in zip(("inner", "outer"), sides)
        ]

    def second_round(sides, got, following=()):
        axes = ("outer", "inner")
        groups = [[keep] + parts for (_, keep), parts in zip(sides, got)]
        if in_place:
            sent, following = lax.optimization_barrier((sums_of(groups, 1), following))
            return [[swap(x, axis, 1)] for x, axis in zip(sent, axes)], following
        return [
            [
                swap(widen([part[s] for part in parts]).astype(BF16), axis, s)
                for s in range(1, lax.axis_size(axis))
            ]
            for parts, axis in zip(groups, axes)
        ], following

    def summed(sides, got, later):
        return [
            widen([part[0] for part in [keep] + parts] + last)
            for (_, keep), parts, last in zip(sides, got, later)
        ]

    theirs = for_others(cot_t)
    theirs, near[1], arrived = lax.optimization_barrier((theirs, near[1], arrived))
    other = swap(theirs, "core", 1)
    for k in order[2:]:
        near[k] = near_of(k, arrived[k])
    for k in order[:2]:
        own_pieces[k] = far_of(k, jnp.stack([arrived[k]] + near[k]))
    sides = for_us(other)
    near, own_pieces, late_sides = lax.optimization_barrier((near, own_pieces, sides))
    stacked = {k: jnp.stack([arrived[k]] + near[k]) for k in order[2:]}
    sides, stacked = lax.optimization_barrier((late_sides, stacked))
    for k in order[2:]:
        own_pieces[k] = far_of(k, stacked[k])
    got = [first_round(sides[0])]
    first_later, _ = second_round(sides[0], got[0])
    later = [first_later]
    sides[1:], own_pieces = lax.optimization_barrier((sides[1:], own_pieces))
    got += [first_round(side) for side in sides[1:]]

    if in_place:
        pieces = [piece for k in order for piece in own_pieces[k]]
        flags = tuple(inner_first(k) for k in order)
        places = [
            jnp.stack([place_of(o, i, c, 0) // tp_count for o, i in chips]).astype(jnp.int32)
            for c in (core, 1 - core)
        ]
        offsets = jnp.stack([lax.rem(tp_place - shift + tp_count, tp_count) * rows for shift in shifts])
        offsets = offsets.astype(jnp.int32)
        total, own_weight = first_value(flags, places[0], offsets, residual, pieces)
    else:
        weight = []
        for k in order:
            both = jnp.stack(own_pieces[k])
            weight.append(both if inner_first(k) else jnp.swapaxes(both, 0, 1))
        by_shift = jnp.array([shifts.index(shift) for shift in range(tp_count)])
        weight = jnp.stack(weight)[by_shift[(tp_place - jnp.arange(tp_count)) % tp_count]]
        weight = weight[:, (at_outer - jnp.arange(outer)) % outer]
        weight = weight[:, :, (at_inner - jnp.arange(inner)) % inner]
        own_weight = weight.transpose(1, 2, 0, 3, 4).reshape(outer * inner, depth, features)
        total = jnp.zeros((), F32)
    total, own_weight, later[0] = lax.optimization_barrier((total, own_weight, later[0]))
    other_weight = swap(own_weight, "core", 1)
    if in_place:
        groups = [[keep] + parts + then for (_, keep), parts, then in zip(sides[0], got[0], later[0])]
        sums = dict(zip(pairs[0], sums_of(groups, 0)))
    else:
        sums = dict(zip(pairs[0], summed(sides[0], got[0], later[0])))
    last = [swap(sums[k].astype(BF16), "tp", k) for k in pairs[0]]
    total = after(total, sums)
    if in_place:
        value_proj, coefficient = weight_call(
            functools.partial(value_end_kernel, width),
            places[1],
            residual,
            other_weight,
            [in_hbm(total), cot, inv_rms],
            [
                jax.ShapeDtypeStruct((rows_here, features), BF16),
                jax.ShapeDtypeStruct((rows_here, 1), F32),
            ],
        )
    else:
        both = jnp.stack([own_weight, other_weight], axis=1)
        weight = jnp.where(core == 0, both, both[:, ::-1]).reshape(width, features)
        value_acc = jnp.dot(residual, weight, preferred_element_type=F32)
        value_proj = (inv_rms * value_acc).astype(BF16)
        share = jnp.sum(cot.astype(F32) * value_acc, axis=1, keepdims=True)
        coefficient = inv_rms * inv_rms * share * (1.0 / width)
    got[1:], coefficient = lax.optimization_barrier((got[1:], coefficient))
    later += [second_round(side, parts)[0] for side, parts in zip(sides[1:], got[1:])]
    if in_place:
        grad_shape = jax.ShapeDtypeStruct((rows_here, width), BF16)
        resid_grad = weight_call(
            grad_kernel, places[0], residual, in_hbm(own_weight), [cot, coefficient], grad_shape
        )
        later[1], last, resid_grad = lax.optimization_barrier((later[1], last, resid_grad))
    else:
        normed_grad = lax.dot_general(
            cot, weight, (((1,), (1,)), ((), ())), preferred_element_type=F32
        )
        resid_grad = (normed_grad - residual.astype(F32) * coefficient).astype(BF16)
    for pair, *rounds in zip(pairs[1:], sides[1:], got[1:], later[1:]):
        sums.update(zip(pair, summed(*rounds)))
    last += [swap(sums[k].astype(BF16), "tp", k) for k in backward[2:-1]]
    if in_place:
        resid_grad = weight_call(
            grad_kernel, places[1], residual, other_weight, [cot, coefficient], grad_shape, resid_grad
        )
    grad_rows = widen([sums[0]] + last)
    late_gain, late_weight, grad_rows = lax.optimization_barrier((norm_gain, value_weight, grad_rows))
    weight_grad = (late_gain.astype(F32)[None, :] * grad_rows).T
    gain_grad = jnp.sum(late_weight.astype(F32).T * grad_rows, axis=0)
    return (value_proj, resid_grad, weight_grad, gain_grad)


def solution(mesh):
    rep_count, tp_count = mesh.shape["rep"], mesh.shape["tp"]
    split = jax.sharding.Mesh(
        mesh.devices.reshape(OUTER, rep_count // (OUTER * CORES), CORES, tp_count),
        ("outer", "inner", "core", "tp"),
    )
    rep = ("outer", "inner", "core")
    rows = rep + ("tp",)
    return jax.shard_map(
        per_device,
        mesh=split,
        in_specs=(
            P(rows, None),
            P(rows),
            P(rows, None),
            P(rows, None),
            P(rows),
            P("tp", rep),
            P("tp", rep),
            P("tp", rep),
            P(rep),
            P(),
        ),
        out_specs=(P(rows, None), P(rows, None), P(rows, None), P(rows)),
        check_vma=False,
    )
```

```python
import functools

import jax
import jax.numpy as jnp
from jax import lax
from jax.experimental import pallas as pl
from jax.experimental.pallas import tpu as pltpu
from jax.sharding import PartitionSpec as P

VOCAB = 128256
EPS = 1e-05
BETA = 0.5
CORES = 2
OUTER = 2
PAIR_VMEM = 18 * 1024 * 1024
WEIGHT_VMEM = 22 * 1024 * 1024
NOMINAL = pl.CostEstimate(flops=1024, bytes_accessed=1024, transcendentals=0)
BF16 = jnp.bfloat16
F32 = jnp.float32


def swap(value, axis, step):
    size = lax.axis_size(axis)
    return lax.ppermute(value, axis, [(place, (place + step) % size) for place in range(size)])


def trade(value, axis, mask):
    size = lax.axis_size(axis)
    return lax.ppermute(value, axis, [(place, place ^ mask) for place in range(size)])


def in_hbm(array):
    return pltpu.with_memory_space_constraint(array, pltpu.HBM)


def after(value, *earlier):
    return lax.optimization_barrier((value, earlier))[0]


def widen(parts):
    return functools.reduce(jnp.add, [part.astype(F32) for part in parts])


def chunk_shifts(tp_count):
    shifts = [0]
    for step in range(1, tp_count // 2 + 1):
        shifts += [step] if 2 * step == tp_count else [step, tp_count - step]
    return shifts


def inner_first(chunk):
    return chunk % 4 in (0, 3)


def theirs_kernel(places_ref, cot_ref, *rest):
    blocks, out_ref = rest[:-1], rest[-1]
    for slot, resid_ref in enumerate(blocks):
        product = jnp.dot(cot_ref[...], resid_ref[...], preferred_element_type=F32)
        out_ref[slot, 0] = product.astype(BF16)


def ours_kernel(places_ref, cot_ref, *rest):
    slots = 4
    blocks, other_ref, outs = rest[:slots], rest[slots], rest[slots + 1 :]
    step = pl.program_id(0)
    ways = (lax.rem(step, 2), step // 2)
    totals = [
        (
            jnp.dot(cot_ref[...], resid_ref[...], preferred_element_type=F32)
            + other_ref[slot, 0].astype(F32)
        ).astype(BF16)
        for slot, resid_ref in enumerate(blocks)
    ]
    for slot, way in enumerate(ways):
        send_ref, keep_ref = outs[2 * slot : 2 * slot + 2]

        @pl.when(way == 1)
        def _():
            send_ref[0] = totals[slot]

        @pl.when(way == 0)
        def _():
            keep_ref[0] = totals[slot]

    for slot in (2, 3):
        outs[slot + 2][0] = totals[slot]


def grad_product(residual, cot_t, places, rows, other):
    features, tokens = cot_t.shape
    steps = 4
    slots = places.shape[0] // steps
    in_specs = [pl.BlockSpec((features, tokens), lambda i, p: (0, 0))] + [
        pl.BlockSpec((tokens, rows), lambda i, p, slot=slot: (0, p[slots * i + slot]))
        for slot in range(slots)
    ]
    operands = [places, cot_t] + [in_hbm(residual)] * slots
    block = pl.BlockSpec((slots, 1, features, rows), lambda i, p: (0, i, 0, 0))
    if other is None:
        kernel, out_specs = theirs_kernel, block
        out_shape = pltpu.HBM((slots, steps, features, rows), BF16)
    else:
        kernel = ours_kernel
        in_specs.append(block)
        operands.append(other)
        indices = [
            lambda i: i // 2,
            lambda i: i // 2,
            lambda i: jnp.maximum(i - 2, 0),
            lambda i: jnp.minimum(i, 1),
            lambda i: i,
            lambda i: i,
        ]
        out_specs = [
            pl.BlockSpec((1, features, rows), lambda i, p, index=index: (index(i), 0, 0))
            for index in indices
        ]
        out_shape = [pltpu.HBM((n, features, rows), BF16) for n in (2, 2, 2, 2, steps, steps)]
    return pl.pallas_call(
        kernel,
        out_shape=out_shape,
        grid_spec=pltpu.PrefetchScalarGridSpec(
            num_scalar_prefetch=1, grid=(steps,), in_specs=in_specs, out_specs=out_specs
        ),
        cost_estimate=NOMINAL,
        compiler_params=pltpu.CompilerParams(vmem_limit_bytes=PAIR_VMEM),
    )(*operands)


def sum_kernel(counts, *refs):
    ins, outs = refs[: sum(counts)], refs[sum(counts) :]
    for n, out_ref in enumerate(outs):
        first = sum(counts[:n])
        parts = [ref[...].astype(F32).reshape(out_ref.shape) for ref in ins[first : first + counts[n]]]
        out_ref[...] = functools.reduce(jnp.add, parts).astype(BF16)


def sums_of(groups, slot):
    shape = groups[0][0].shape[-2:]
    in_specs = [
        pl.BlockSpec((1,) + shape, lambda i: (slot, 0, 0))
        if part.ndim == 3
        else pl.BlockSpec(shape, lambda i: (0, 0))
        for parts in groups
        for part in parts
    ]
    return pl.pallas_call(
        functools.partial(sum_kernel, [len(parts) for parts in groups]),
        out_shape=[jax.ShapeDtypeStruct(shape, BF16)] * len(groups),
        grid=(1,),
        in_specs=in_specs,
        out_specs=[pl.BlockSpec(shape, lambda i: (0, 0))] * len(groups),
        cost_estimate=NOMINAL,
        compiler_params=pltpu.CompilerParams(vmem_limit_bytes=PAIR_VMEM),
    )(*[part for parts in groups for part in parts])


def place_weight(inner_flags, offsets_ref, pieces, weight_ref):
    step = pl.program_id(0)
    at_outer, at_inner = step // 2, lax.rem(step, 2)
    rows = pieces[0].shape[1]
    for chunk, flag in enumerate(inner_flags):
        way = at_outer if flag else at_inner
        where = pl.ds(pl.multiple_of(offsets_ref[chunk], rows), rows)
        for late in range(2):
            piece = pieces[chunk * 2 + late]

            @pl.when(way == late)
            def _():
                weight_ref[0, where, :] = piece[0]


def piece_specs(inner_flags, rows, features):
    specs = []
    for flag in inner_flags:
        for late in range(2):
            if flag:
                index = lambda i, *_, first=2 * late: (jnp.clip(i - first, 0, 1), 0, 0)
            else:
                index = lambda i, *_: (i // 2, 0, 0)
            specs.append(pl.BlockSpec((1, rows, features), index))
    return specs


def value_kernel(inner_flags, places_ref, offsets_ref, resid_ref, *rest):
    pieces, (total_ref, weight_ref) = rest[:-2], rest[-2:]
    step = pl.program_id(0)
    place_weight(inner_flags, offsets_ref, pieces, weight_ref)
    product = jnp.dot(resid_ref[...], weight_ref[0], preferred_element_type=F32)

    @pl.when(step == 0)
    def _():
        total_ref[...] = product

    @pl.when(step > 0)
    def _():
        total_ref[...] += product


def value_end_kernel(
    width, places_ref, resid_ref, weight_ref, first_ref, cot_ref, inv_ref, value_ref, coef_ref, total_ref
):
    step = pl.program_id(0)
    product = jnp.dot(resid_ref[...], weight_ref[0], preferred_element_type=F32)

    @pl.when(step == 0)
    def _():
        total_ref[...] = first_ref[...] + product

    @pl.when(step > 0)
    def _():
        total_ref[...] += product

    @pl.when(step == pl.num_programs(0) - 1)
    def _():
        total = total_ref[...]
        inv = inv_ref[...]
        value_ref[...] = (total * inv).astype(BF16)
        share = jnp.sum(total * cot_ref[...].astype(F32), axis=1, keepdims=True)
        coef_ref[...] = share * (inv * inv) * (1.0 / width)


def grad_kernel(places_ref, resid_ref, weight_ref, cot_ref, coef_ref, *rest):
    out_ref = rest[-1]
    grad = lax.dot_general(
        cot_ref[...], weight_ref[0], (((1,), (1,)), ((), ())), preferred_element_type=F32
    )
    out_ref[...] = (grad - resid_ref[...].astype(F32) * coef_ref[...]).astype(BF16)


def whole_block(array):
    return pl.BlockSpec(array.shape, lambda i, *_: (0, 0))


def first_value(inner_flags, places, offsets, residual, pieces):
    tokens, width = residual.shape
    rows, features = pieces[0].shape[1:]
    steps = places.shape[0]
    depth = width // (CORES * steps)
    total = pltpu.HBM((tokens, features), F32)
    return pl.pallas_call(
        functools.partial(value_kernel, inner_flags),
        out_shape=[total, pltpu.HBM((steps, depth, features), BF16)],
        grid_spec=pltpu.PrefetchScalarGridSpec(
            num_scalar_prefetch=2,
            grid=(steps,),
            in_specs=[pl.BlockSpec((tokens, depth), lambda i, p, o: (0, p[i]))]
            + piece_specs(inner_flags, rows, features),
            out_specs=[
                whole_block(total),
                pl.BlockSpec((1, depth, features), lambda i, p, o: (p[i] // CORES, 0, 0)),
            ],
        ),
        cost_estimate=NOMINAL,
        compiler_params=pltpu.CompilerParams(vmem_limit_bytes=WEIGHT_VMEM),
    )(places, offsets, in_hbm(residual), *pieces)


def weight_call(kernel, places, residual, weight, wholes, out_shape, earlier=None):
    tokens, width = residual.shape
    _, depth, features = weight.shape
    steps = places.shape[0]
    scratch = []
    if isinstance(out_shape, list):
        out_specs = [whole_block(array) for array in out_shape]
        scratch.append(pltpu.VMEM((tokens, features), F32))
    else:
        out_specs = pl.BlockSpec((tokens, depth), lambda i, p: (0, p[i]))
    in_specs = [
        pl.BlockSpec((tokens, depth), lambda i, p: (0, p[i])),
        pl.BlockSpec((1, depth, features), lambda i, p: (p[i] // CORES, 0, 0)),
    ] + [whole_block(array) for array in wholes]
    operands = [places, in_hbm(residual), weight, *wholes]
    aliases = {}
    if earlier is not None:
        aliases = {len(operands): 0}
        in_specs.append(pl.BlockSpec(memory_space=pltpu.HBM))
        operands.append(earlier)
    return pl.pallas_call(
        kernel,
        out_shape=out_shape,
        grid_spec=pltpu.PrefetchScalarGridSpec(
            num_scalar_prefetch=1,
            grid=(steps,),
            in_specs=in_specs,
            out_specs=out_specs,
            scratch_shapes=scratch,
        ),
        input_output_aliases=aliases,
        cost_estimate=NOMINAL,
        compiler_params=pltpu.CompilerParams(vmem_limit_bytes=WEIGHT_VMEM),
    )(*operands)


def cot_kernel(width, rep_count, info_ref, shares_ref, squares_ref, value_cot_ref, cot_ref, cot_t_ref, inv_ref):
    place, length = info_ref[0], info_ref[1]
    rows = value_cot_ref.shape[0]
    own = rows // 128
    seq = (shares_ref.shape[1] - own) // 3
    shares = range(shares_ref.shape[0])

    def below(first, shape):
        at = lax.broadcasted_iota(jnp.int32, shape, 0) * 128 + lax.broadcasted_iota(jnp.int32, shape, 1)
        return first + at < length

    def summed(mask, value):
        return jnp.sum(jnp.where(mask, value, 0.0), axis=(0, 1), keepdims=True)

    maxes = [shares_ref[m, 0:seq] for m in shares]
    top_max = functools.reduce(jnp.maximum, maxes)
    sum_exp = functools.reduce(
        jnp.add, [shares_ref[m, seq : 2 * seq] * jnp.exp(maxes[m] - top_max) for m in shares]
    )
    picked = functools.reduce(jnp.add, [shares_ref[m, 2 * seq : 3 * seq] for m in shares])
    ref_logp = picked - top_max - jnp.log(sum_exp)
    total = -summed(below(0, (seq, 128)), ref_logp)
    for m in shares:
        first = jnp.bitwise_xor(place, m) * rows
        total += summed(below(first, (own, 128)), shares_ref[m, 3 * seq :])
    seq_delta = total / jnp.full((1, 1), length, jnp.int32).astype(F32)
    weight = (2.0 / rep_count) * jax.nn.sigmoid(BETA * seq_delta)
    inv = lax.rsqrt(squares_ref[...] * (1.0 / width) + EPS)
    live = place * rows + lax.broadcasted_iota(jnp.int32, (rows, 1), 0) < length
    scaled = jnp.where(live, inv * weight, 0.0) * value_cot_ref[...].astype(F32)
    cot_ref[...] = scaled.astype(BF16)
    cot_t_ref[...] = scaled.T.astype(BF16)
    inv_ref[...] = inv


def scaled_cot(width, rep_count, info, shares, squares, value_cot):
    rows, features = value_cot.shape

    def whole(array):
        return pl.BlockSpec(array.shape, lambda i, p: (0,) * array.ndim)

    out_shape = [
        jax.ShapeDtypeStruct((rows, features), BF16),
        jax.ShapeDtypeStruct((features, rows), BF16),
        jax.ShapeDtypeStruct((rows, 1), F32),
    ]
    return pl.pallas_call(
        functools.partial(cot_kernel, width, rep_count),
        out_shape=out_shape,
        grid_spec=pltpu.PrefetchScalarGridSpec(
            num_scalar_prefetch=1,
            grid=(1,),
            in_specs=[whole(shares), whole(squares), whole(value_cot)],
            out_specs=[pl.BlockSpec(array.shape, lambda i, p: (0, 0)) for array in out_shape],
        ),
        cost_estimate=NOMINAL,
        compiler_params=pltpu.CompilerParams(vmem_limit_bytes=PAIR_VMEM),
    )(info, shares, squares, in_hbm(value_cot))


def per_device(
    residual,
    norm_gain,
    value_weight,
    value_cot,
    trainee_logp,
    ref_shard_max,
    ref_shard_sum,
    ref_target_logit,
    target_ids,
    lengths,
):
    rows_here, width = residual.shape
    features = value_cot.shape[1]
    tp_count = lax.axis_size("tp")
    outer, inner = lax.axis_size("outer"), lax.axis_size("inner")
    rep_count = outer * inner * CORES
    tp_place = lax.axis_index("tp")
    core = lax.axis_index("core")
    at_inner = lax.axis_index("inner")
    at_outer = lax.axis_index("outer")
    rep_place = (at_outer * inner + at_inner) * CORES + core
    depth = width // rep_count
    rows = depth // tp_count
    order = list(range(tp_count))
    shifts = chunk_shifts(tp_count)
    in_place = rows % 128 == 0 and outer == 2 and inner == 2 and tp_count == 4

    owned = jnp.where(
        target_ids // (VOCAB // tp_count) == tp_place,
        ref_target_logit[0],
        jnp.zeros_like(ref_target_logit[0]),
    )
    packed = jnp.concatenate([ref_shard_max[0], ref_shard_sum[0], owned, trainee_logp])
    packed = packed.reshape(1, -1, 128)
    packed = jnp.concatenate([packed, trade(packed, "tp", 1)])

    gained = (value_weight.astype(F32) * norm_gain.astype(F32)[:, None]).astype(BF16)
    residual, gained, packed = lax.optimization_barrier((residual, gained, packed))
    resid_wide = residual.astype(F32)
    squares = jnp.sum(resid_wide * resid_wide, axis=1, keepdims=True)

    def near_of(k, block):
        first = "inner" if inner_first(k) else "outer"
        return [swap(block, first, s) for s in range(1, lax.axis_size(first))]

    def far_of(k, block, nears):
        second = "outer" if inner_first(k) else "inner"
        near = jnp.stack([block] + nears)
        return [near] + [swap(near, second, s) for s in range(1, lax.axis_size(second))]

    mask = 2
    while mask < tp_count:
        packed = jnp.concatenate([packed, trade(packed, "tp", mask)])
        mask *= 2
    own_pieces, near = {}, {}
    arrived = {0: gained, 1: swap(gained, "tp", shifts[1])}
    near[0] = near_of(0, gained)
    arrived[1], near[0], squares, late_gained = lax.optimization_barrier(
        (arrived[1], near[0], squares, gained)
    )
    near[1] = near_of(1, arrived[1])
    arrived[2] = swap(late_gained, "tp", shifts[2])
    own_pieces[0] = far_of(0, gained, near[0])
    seq_length = lax.dynamic_index_in_dim(lengths, rep_place, keepdims=False)
    info = jnp.stack([tp_place, seq_length]).astype(jnp.int32)
    near[1], arrived[2], packed, late_gained, info = lax.optimization_barrier(
        (near[1], arrived[2], packed, late_gained, info)
    )
    near[2] = near_of(2, arrived[2])
    for k in order[3:]:
        arrived[k] = swap(late_gained, "tp", shifts[k])
    own_pieces[1] = far_of(1, arrived[1], near[1])
    cot, cot_t, inv_rms = scaled_cot(width, rep_count, info, packed, squares, value_cot)

    def place_of(o, i, c, k):
        chip = lax.rem(at_outer + o, outer) * inner + lax.rem(at_inner + i, inner)
        return (chip * CORES + c) * tp_count + lax.rem(tp_place + k, tp_count)

    backward = order[::-1]
    pairs = [backward[i : i + 2] for i in range(0, tp_count, 2)]
    chips = [(o, i) for o in range(outer) for i in range(inner)]
    if not in_place:
        product = jnp.dot(cot_t, residual, preferred_element_type=F32).astype(BF16)
        product = product.reshape(features, -1, rows).transpose(1, 0, 2)

    def places_of(pair, c):
        return jnp.stack([place_of(o, i, c, k) for o, i in chips for k in pair]).astype(jnp.int32)

    def for_others(cot_t):
        places = places_of(backward, 1 - core)
        if in_place:
            return grad_product(residual, cot_t, places, rows, None)
        both = after(product, cot_t)[places].reshape(len(chips), tp_count, features, rows)
        return both.swapaxes(0, 1)

    def for_us(other):
        places = places_of(backward, core)
        if in_place:
            outs = grad_product(residual, cot_t, places, rows, other)
            return [[([outs[0]], outs[1]), ([outs[2]], outs[3])], outs[4], outs[5]]
        else:
            both = product[places].reshape(len(chips), tp_count, features, rows).swapaxes(0, 1)
            total = widen([both, other]).astype(BF16)
            total = total.reshape(tp_count, outer, inner, features, rows)
            sides = []
            for n in range(0, tp_count, 2):
                sides.append(([total[n, :, s] for s in range(1, inner)], total[n, :, 0]))
                sides.append(([total[n + 1, s] for s in range(1, outer)], total[n + 1, 0]))
        return [sides[n : n + 2] for n in range(0, tp_count, 2)]

    def first_round(sides):
        return [
            [swap(send, axis, s + 1) for s, send in enumerate(sends)]
            for axis, (sends, _) in zip(("inner", "outer"), sides)
        ]

    def second_round(sides, got):
        axes = ("outer", "inner")
        groups = [[keep] + parts for (_, keep), parts in zip(sides, got)]
        return [
            [
                swap(widen([part[s] for part in parts]).astype(BF16), axis, s)
                for s in range(1, lax.axis_size(axis))
            ]
            for parts, axis in zip(groups, axes)
        ]

    def summed(sides, got, later):
        return [
            widen([part[0] for part in [keep] + parts] + last)
            for (_, keep), parts, last in zip(sides, got, later)
        ]

    theirs = for_others(cot_t)
    theirs, arrived = lax.optimization_barrier((theirs, arrived))
    near.update({k: near_of(k, arrived[k]) for k in order[3:]})
    theirs, own_pieces, near = lax.optimization_barrier((theirs, own_pieces, near))
    other = swap(theirs, "core", 1)
    near, own_pieces = lax.optimization_barrier((near, own_pieces))
    for k in order[2:]:
        own_pieces[k] = far_of(k, arrived[k], near[k])
    sides = for_us(other)
    if in_place:
        sides, passed, kept = sides[:1], sides[1], sides[2]
        kept, own_pieces = lax.optimization_barrier((kept, own_pieces))
        passed = swap(passed, "tp", 1)
    got = [first_round(sides[0])]
    sides[1:], own_pieces = lax.optimization_barrier((sides[1:], own_pieces))

    if in_place:
        pieces = [piece for k in order for piece in own_pieces[k]]
        flags = tuple(inner_first(k) for k in order)
        places = [
            jnp.stack([place_of(o, i, c, 0) // tp_count for o, i in chips]).astype(jnp.int32)
            for c in (core, 1 - core)
        ]
        offsets = jnp.stack([lax.rem(tp_place - shift + tp_count, tp_count) * rows for shift in shifts])
        offsets = offsets.astype(jnp.int32)
        total, own_weight = first_value(flags, places[0], offsets, residual, pieces)
    else:
        weight = []
        for k in order:
            both = jnp.stack(own_pieces[k])
            weight.append(both if inner_first(k) else jnp.swapaxes(both, 0, 1))
        by_shift = jnp.array([shifts.index(shift) for shift in range(tp_count)])
        weight = jnp.stack(weight)[by_shift[(tp_place - jnp.arange(tp_count)) % tp_count]]
        weight = weight[:, (at_outer - jnp.arange(outer)) % outer]
        weight = weight[:, :, (at_inner - jnp.arange(inner)) % inner]
        own_weight = weight.transpose(1, 2, 0, 3, 4).reshape(outer * inner, depth, features)
        total = jnp.zeros((), F32)
    got[0], sides[1:], total, own_weight = lax.optimization_barrier(
        (got[0], sides[1:], total, own_weight)
    )
    other_weight = swap(own_weight, "core", 1)
    later = [second_round(sides[0], got[0])]
    got += [first_round(side) for side in sides[1:]]
    if in_place:
        value_proj, coefficient = weight_call(
            functools.partial(value_end_kernel, width),
            places[1],
            residual,
            other_weight,
            [in_hbm(total), cot, inv_rms],
            [
                jax.ShapeDtypeStruct((rows_here, features), BF16),
                jax.ShapeDtypeStruct((rows_here, 1), F32),
            ],
        )
    else:
        both = jnp.stack([own_weight, other_weight], axis=1)
        weight = jnp.where(core == 0, both, both[:, ::-1]).reshape(width, features)
        value_acc = jnp.dot(residual, weight, preferred_element_type=F32)
        value_proj = (inv_rms * value_acc).astype(BF16)
        share = jnp.sum(cot.astype(F32) * value_acc, axis=1, keepdims=True)
        coefficient = inv_rms * inv_rms * share * (1.0 / width)
    later[0], coefficient = lax.optimization_barrier((later[0], coefficient))
    if in_place:
        passed, coefficient = lax.optimization_barrier((passed, coefficient))
        crossed = swap(widen([kept[2:], passed[2:]]).astype(BF16), "outer", 1)
        groups = [[keep] + parts + then for (_, keep), parts, then in zip(sides[0], got[0], later[0])]
        last = [swap(x, "tp", k) for x, k in zip(sums_of(groups, 0), pairs[0])]
        grad_shape = jax.ShapeDtypeStruct((rows_here, width), BF16)
        resid_grad = weight_call(
            grad_kernel, places[0], residual, in_hbm(own_weight), [cot, coefficient], grad_shape
        )
        crossed, resid_grad = lax.optimization_barrier((crossed, resid_grad))
        beside = swap(widen([kept[1], passed[1], crossed[1]]).astype(BF16), "inner", 1)
        resid_grad = weight_call(
            grad_kernel, places[1][:3], residual, other_weight, [cot, coefficient], grad_shape, resid_grad
        )
        beside, last, resid_grad = lax.optimization_barrier((beside, last, resid_grad))
        resid_grad = weight_call(
            grad_kernel, places[1][3:], residual, other_weight, [cot, coefficient], grad_shape, resid_grad
        )
        grad_rows = widen([kept[0], passed[0], crossed[0], beside] + last)
    else:
        normed_grad = lax.dot_general(
            cot, weight, (((1,), (1,)), ((), ())), preferred_element_type=F32
        )
        resid_grad = (normed_grad - residual.astype(F32) * coefficient).astype(BF16)
        later += [second_round(side, parts) for side, parts in zip(sides[1:], got[1:])]
        sums = {}
        for pair, *rounds in zip(pairs, sides, got, later):
            sums.update(zip(pair, summed(*rounds)))
        last = [swap(sums[k].astype(BF16), "tp", k) for k in backward[:-1]]
        grad_rows = widen([sums[0]] + last)
    late_gain, late_weight, grad_rows = lax.optimization_barrier((norm_gain, value_weight, grad_rows))
    weight_grad = (late_gain.astype(F32)[None, :] * grad_rows).T
    gain_grad = jnp.sum(late_weight.astype(F32).T * grad_rows, axis=0)
    return (value_proj, resid_grad, weight_grad, gain_grad)


def solution(mesh):
    rep_count, tp_count = mesh.shape["rep"], mesh.shape["tp"]
    split = jax.sharding.Mesh(
        mesh.devices.reshape(OUTER, rep_count // (OUTER * CORES), CORES, tp_count),
        ("outer", "inner", "core", "tp"),
    )
    rep = ("outer", "inner", "core")
    rows = rep + ("tp",)
    return jax.shard_map(
        per_device,
        mesh=split,
        in_specs=(
            P(rows, None),
            P(rows),
            P(rows, None),
            P(rows, None),
            P(rows),
            P("tp", rep),
            P("tp", rep),
            P("tp", rep),
            P(rep),
            P(),
        ),
        out_specs=(P(rows, None), P(rows, None), P(rows, None), P(rows)),
        check_vma=False,
    )
```

```python
import functools

import jax
import jax.numpy as jnp
from jax import lax
from jax.experimental import pallas as pl
from jax.experimental.pallas import tpu as pltpu
from jax.sharding import PartitionSpec as P

VOCAB = 128256
EPS = 1e-05
BETA = 0.5
CORES = 2
OUTER = 2
PAIR_VMEM = 18 * 1024 * 1024
WEIGHT_VMEM = 22 * 1024 * 1024
NOMINAL = pl.CostEstimate(flops=1024, bytes_accessed=1024, transcendentals=0)
BF16 = jnp.bfloat16
F32 = jnp.float32


def swap(value, axis, step):
    size = lax.axis_size(axis)
    return lax.ppermute(value, axis, [(place, (place + step) % size) for place in range(size)])


def trade(value, axis, mask):
    size = lax.axis_size(axis)
    return lax.ppermute(value, axis, [(place, place ^ mask) for place in range(size)])


def in_hbm(array):
    return pltpu.with_memory_space_constraint(array, pltpu.HBM)


def after(value, *earlier):
    return lax.optimization_barrier((value, earlier))[0]


def widen(parts):
    return functools.reduce(jnp.add, [part.astype(F32) for part in parts])


def chunk_shifts(tp_count):
    shifts = [0]
    for step in range(1, tp_count // 2 + 1):
        shifts += [step] if 2 * step == tp_count else [step, tp_count - step]
    return shifts


def inner_first(chunk):
    return chunk % 4 in (0, 3)


def theirs_kernel(places_ref, cot_ref, *rest):
    blocks, out_ref = rest[:-1], rest[-1]
    for slot, resid_ref in enumerate(blocks):
        product = jnp.dot(cot_ref[...], resid_ref[...], preferred_element_type=F32)
        out_ref[slot, 0] = product.astype(BF16)


def ours_kernel(places_ref, cot_ref, *rest):
    slots = 4
    blocks, other_ref, outs = rest[:slots], rest[slots], rest[slots + 1 :]
    step = pl.program_id(0)
    ways = (lax.rem(step, 2), step // 2)
    totals = [
        (
            jnp.dot(cot_ref[...], resid_ref[...], preferred_element_type=F32)
            + other_ref[slot, 0].astype(F32)
        ).astype(BF16)
        for slot, resid_ref in enumerate(blocks)
    ]
    for slot, way in enumerate(ways):
        send_ref, keep_ref = outs[2 * slot : 2 * slot + 2]

        @pl.when(way == 1)
        def _():
            send_ref[0] = totals[slot]

        @pl.when(way == 0)
        def _():
            keep_ref[0] = totals[slot]

    near_ref, far_ref, kept_ref = outs[4:]
    kept_ref[0] = totals[3]

    @pl.when(ways[1] == 1)
    def _():
        far_ref[0] = totals[2]

    @pl.when(ways[1] == 0)
    def _():
        near_ref[0] = totals[2]


def grad_product(residual, cot_t, places, rows, other):
    features, tokens = cot_t.shape
    steps = 4
    slots = places.shape[0] // steps
    in_specs = [pl.BlockSpec((features, tokens), lambda i, p: (0, 0))] + [
        pl.BlockSpec((tokens, rows), lambda i, p, slot=slot: (0, p[slots * i + slot]))
        for slot in range(slots)
    ]
    operands = [places, cot_t] + [in_hbm(residual)] * slots
    block = pl.BlockSpec((slots, 1, features, rows), lambda i, p: (0, i, 0, 0))
    if other is None:
        kernel, out_specs = theirs_kernel, block
        out_shape = pltpu.HBM((slots, steps, features, rows), BF16)
    else:
        kernel = ours_kernel
        in_specs.append(block)
        operands.append(other)
        indices = [
            lambda i: i // 2,
            lambda i: i // 2,
            lambda i: jnp.maximum(i - 2, 0),
            lambda i: jnp.minimum(i, 1),
            lambda i: jnp.minimum(i, 1),
            lambda i: jnp.maximum(i - 2, 0),
            lambda i: i,
        ]
        out_specs = [
            pl.BlockSpec((1, features, rows), lambda i, p, index=index: (index(i), 0, 0))
            for index in indices
        ]
        out_shape = [pltpu.HBM((n, features, rows), BF16) for n in (2, 2, 2, 2, 2, 2, steps)]
    return pl.pallas_call(
        kernel,
        out_shape=out_shape,
        grid_spec=pltpu.PrefetchScalarGridSpec(
            num_scalar_prefetch=1, grid=(steps,), in_specs=in_specs, out_specs=out_specs
        ),
        cost_estimate=NOMINAL,
        compiler_params=pltpu.CompilerParams(vmem_limit_bytes=PAIR_VMEM),
    )(*operands)


def sum_kernel(counts, *refs):
    ins, outs = refs[: sum(counts)], refs[sum(counts) :]
    for n, out_ref in enumerate(outs):
        first = sum(counts[:n])
        parts = [ref[...].astype(F32).reshape(out_ref.shape) for ref in ins[first : first + counts[n]]]
        out_ref[...] = functools.reduce(jnp.add, parts).astype(BF16)


def sums_of(groups, slot):
    shape = groups[0][0].shape[-2:]
    in_specs = [
        pl.BlockSpec((1,) + shape, lambda i: (slot, 0, 0))
        if part.ndim == 3
        else pl.BlockSpec(shape, lambda i: (0, 0))
        for parts in groups
        for part in parts
    ]
    return pl.pallas_call(
        functools.partial(sum_kernel, [len(parts) for parts in groups]),
        out_shape=[jax.ShapeDtypeStruct(shape, BF16)] * len(groups),
        grid=(1,),
        in_specs=in_specs,
        out_specs=[pl.BlockSpec(shape, lambda i: (0, 0))] * len(groups),
        cost_estimate=NOMINAL,
        compiler_params=pltpu.CompilerParams(vmem_limit_bytes=PAIR_VMEM),
    )(*[part for parts in groups for part in parts])


def place_weight(inner_flags, offsets_ref, pieces, weight_ref):
    step = pl.program_id(0)
    at_outer, at_inner = step // 2, lax.rem(step, 2)
    rows = pieces[0].shape[1]
    for chunk, flag in enumerate(inner_flags):
        way = at_outer if flag else at_inner
        where = pl.ds(pl.multiple_of(offsets_ref[chunk], rows), rows)
        for late in range(2):
            piece = pieces[chunk * 2 + late]

            @pl.when(way == late)
            def _():
                weight_ref[0, where, :] = piece[0]


def piece_specs(inner_flags, rows, features):
    specs = []
    for flag in inner_flags:
        for late in range(2):
            if flag:
                index = lambda i, *_, first=2 * late: (jnp.clip(i - first, 0, 1), 0, 0)
            else:
                index = lambda i, *_: (i // 2, 0, 0)
            specs.append(pl.BlockSpec((1, rows, features), index))
    return specs


def value_kernel(inner_flags, places_ref, offsets_ref, resid_ref, *rest):
    pieces, (total_ref, weight_ref) = rest[:-2], rest[-2:]
    step = pl.program_id(0)
    place_weight(inner_flags, offsets_ref, pieces, weight_ref)
    product = jnp.dot(resid_ref[...], weight_ref[0], preferred_element_type=F32)

    @pl.when(step == 0)
    def _():
        total_ref[...] = product

    @pl.when(step > 0)
    def _():
        total_ref[...] += product


def value_end_kernel(
    width, places_ref, resid_ref, weight_ref, first_ref, cot_ref, inv_ref, value_ref, coef_ref, total_ref
):
    step = pl.program_id(0)
    product = jnp.dot(resid_ref[...], weight_ref[0], preferred_element_type=F32)

    @pl.when(step == 0)
    def _():
        total_ref[...] = first_ref[...] + product

    @pl.when(step > 0)
    def _():
        total_ref[...] += product

    @pl.when(step == pl.num_programs(0) - 1)
    def _():
        total = total_ref[...]
        inv = inv_ref[...]
        value_ref[...] = (total * inv).astype(BF16)
        share = jnp.sum(total * cot_ref[...].astype(F32), axis=1, keepdims=True)
        coef_ref[...] = share * (inv * inv) * (1.0 / width)


def grad_kernel(places_ref, resid_ref, weight_ref, cot_ref, coef_ref, *rest):
    out_ref = rest[-1]
    grad = lax.dot_general(
        cot_ref[...], weight_ref[0], (((1,), (1,)), ((), ())), preferred_element_type=F32
    )
    out_ref[...] = (grad - resid_ref[...].astype(F32) * coef_ref[...]).astype(BF16)


def whole_block(array):
    return pl.BlockSpec(array.shape, lambda i, *_: (0, 0))


def first_value(inner_flags, places, offsets, residual, pieces):
    tokens, width = residual.shape
    rows, features = pieces[0].shape[1:]
    steps = places.shape[0]
    depth = width // (CORES * steps)
    total = pltpu.HBM((tokens, features), F32)
    return pl.pallas_call(
        functools.partial(value_kernel, inner_flags),
        out_shape=[total, pltpu.HBM((steps, depth, features), BF16)],
        grid_spec=pltpu.PrefetchScalarGridSpec(
            num_scalar_prefetch=2,
            grid=(steps,),
            in_specs=[pl.BlockSpec((tokens, depth), lambda i, p, o: (0, p[i]))]
            + piece_specs(inner_flags, rows, features),
            out_specs=[
                whole_block(total),
                pl.BlockSpec((1, depth, features), lambda i, p, o: (p[i] // CORES, 0, 0)),
            ],
        ),
        cost_estimate=NOMINAL,
        compiler_params=pltpu.CompilerParams(vmem_limit_bytes=WEIGHT_VMEM),
    )(places, offsets, in_hbm(residual), *pieces)


def weight_call(kernel, places, residual, weight, wholes, out_shape, earlier=None):
    tokens, width = residual.shape
    _, depth, features = weight.shape
    steps = places.shape[0]
    scratch = []
    if isinstance(out_shape, list):
        out_specs = [whole_block(array) for array in out_shape]
        scratch.append(pltpu.VMEM((tokens, features), F32))
    else:
        out_specs = pl.BlockSpec((tokens, depth), lambda i, p: (0, p[i]))
    in_specs = [
        pl.BlockSpec((tokens, depth), lambda i, p: (0, p[i])),
        pl.BlockSpec((1, depth, features), lambda i, p: (p[i] // CORES, 0, 0)),
    ] + [whole_block(array) for array in wholes]
    operands = [places, in_hbm(residual), weight, *wholes]
    aliases = {}
    if earlier is not None:
        aliases = {len(operands): 0}
        in_specs.append(pl.BlockSpec(memory_space=pltpu.HBM))
        operands.append(earlier)
    return pl.pallas_call(
        kernel,
        out_shape=out_shape,
        grid_spec=pltpu.PrefetchScalarGridSpec(
            num_scalar_prefetch=1,
            grid=(steps,),
            in_specs=in_specs,
            out_specs=out_specs,
            scratch_shapes=scratch,
        ),
        input_output_aliases=aliases,
        cost_estimate=NOMINAL,
        compiler_params=pltpu.CompilerParams(vmem_limit_bytes=WEIGHT_VMEM),
    )(*operands)


def cot_kernel(width, rep_count, info_ref, shares_ref, squares_ref, value_cot_ref, cot_ref, cot_t_ref, inv_ref):
    place, length = info_ref[0], info_ref[1]
    rows = value_cot_ref.shape[0]
    own = rows // 128
    seq = (shares_ref.shape[1] - own) // 3
    shares = range(shares_ref.shape[0])

    def below(first, shape):
        at = lax.broadcasted_iota(jnp.int32, shape, 0) * 128 + lax.broadcasted_iota(jnp.int32, shape, 1)
        return first + at < length

    def summed(mask, value):
        return jnp.sum(jnp.where(mask, value, 0.0), axis=(0, 1), keepdims=True)

    maxes = [shares_ref[m, 0:seq] for m in shares]
    top_max = functools.reduce(jnp.maximum, maxes)
    sum_exp = functools.reduce(
        jnp.add, [shares_ref[m, seq : 2 * seq] * jnp.exp(maxes[m] - top_max) for m in shares]
    )
    picked = functools.reduce(jnp.add, [shares_ref[m, 2 * seq : 3 * seq] for m in shares])
    ref_logp = picked - top_max - jnp.log(sum_exp)
    total = -summed(below(0, (seq, 128)), ref_logp)
    for m in shares:
        first = jnp.bitwise_xor(place, m) * rows
        total += summed(below(first, (own, 128)), shares_ref[m, 3 * seq :])
    seq_delta = total / jnp.full((1, 1), length, jnp.int32).astype(F32)
    weight = (2.0 / rep_count) * jax.nn.sigmoid(BETA * seq_delta)
    inv = lax.rsqrt(squares_ref[...] * (1.0 / width) + EPS)
    live = place * rows + lax.broadcasted_iota(jnp.int32, (rows, 1), 0) < length
    scaled = jnp.where(live, inv * weight, 0.0) * value_cot_ref[...].astype(F32)
    cot_ref[...] = scaled.astype(BF16)
    cot_t_ref[...] = scaled.T.astype(BF16)
    inv_ref[...] = inv


def scaled_cot(width, rep_count, info, shares, squares, value_cot):
    rows, features = value_cot.shape

    def whole(array):
        return pl.BlockSpec(array.shape, lambda i, p: (0,) * array.ndim)

    out_shape = [
        jax.ShapeDtypeStruct((rows, features), BF16),
        jax.ShapeDtypeStruct((features, rows), BF16),
        jax.ShapeDtypeStruct((rows, 1), F32),
    ]
    return pl.pallas_call(
        functools.partial(cot_kernel, width, rep_count),
        out_shape=out_shape,
        grid_spec=pltpu.PrefetchScalarGridSpec(
            num_scalar_prefetch=1,
            grid=(1,),
            in_specs=[whole(shares), whole(squares), whole(value_cot)],
            out_specs=[pl.BlockSpec(array.shape, lambda i, p: (0, 0)) for array in out_shape],
        ),
        cost_estimate=NOMINAL,
        compiler_params=pltpu.CompilerParams(vmem_limit_bytes=PAIR_VMEM),
    )(info, shares, squares, in_hbm(value_cot))


def per_device(
    residual,
    norm_gain,
    value_weight,
    value_cot,
    trainee_logp,
    ref_shard_max,
    ref_shard_sum,
    ref_target_logit,
    target_ids,
    lengths,
):
    rows_here, width = residual.shape
    features = value_cot.shape[1]
    tp_count = lax.axis_size("tp")
    outer, inner = lax.axis_size("outer"), lax.axis_size("inner")
    rep_count = outer * inner * CORES
    tp_place = lax.axis_index("tp")
    core = lax.axis_index("core")
    at_inner = lax.axis_index("inner")
    at_outer = lax.axis_index("outer")
    rep_place = (at_outer * inner + at_inner) * CORES + core
    depth = width // rep_count
    rows = depth // tp_count
    order = list(range(tp_count))
    shifts = chunk_shifts(tp_count)
    in_place = rows % 128 == 0 and outer == 2 and inner == 2 and tp_count == 4

    owned = jnp.where(
        target_ids // (VOCAB // tp_count) == tp_place,
        ref_target_logit[0],
        jnp.zeros_like(ref_target_logit[0]),
    )
    packed = jnp.concatenate([ref_shard_max[0], ref_shard_sum[0], owned, trainee_logp])
    packed = packed.reshape(1, -1, 128)
    packed = jnp.concatenate([packed, trade(packed, "tp", 1)])

    gained = (value_weight.astype(F32) * norm_gain.astype(F32)[:, None]).astype(BF16)
    residual, gained, packed = lax.optimization_barrier((residual, gained, packed))
    resid_wide = residual.astype(F32)
    squares = jnp.sum(resid_wide * resid_wide, axis=1, keepdims=True)

    def near_of(k, block):
        first = "inner" if inner_first(k) else "outer"
        return [swap(block, first, s) for s in range(1, lax.axis_size(first))]

    def far_of(k, block, nears):
        second = "outer" if inner_first(k) else "inner"
        near = jnp.stack([block] + nears)
        return [near] + [swap(near, second, s) for s in range(1, lax.axis_size(second))]

    mask = 2
    while mask < tp_count:
        packed = jnp.concatenate([packed, trade(packed, "tp", mask)])
        mask *= 2
    own_pieces, near = {}, {}
    arrived = {0: gained, 1: swap(gained, "tp", shifts[1])}
    near[0] = near_of(0, gained)
    arrived[1], near[0], squares, late_gained = lax.optimization_barrier(
        (arrived[1], near[0], squares, gained)
    )
    near[1] = near_of(1, arrived[1])
    arrived[2] = swap(late_gained, "tp", shifts[2])
    own_pieces[0] = far_of(0, gained, near[0])
    seq_length = lax.dynamic_index_in_dim(lengths, rep_place, keepdims=False)
    info = jnp.stack([tp_place, seq_length]).astype(jnp.int32)
    near[1], arrived[2], packed, late_gained, info = lax.optimization_barrier(
        (near[1], arrived[2], packed, late_gained, info)
    )
    near[2] = near_of(2, arrived[2])
    for k in order[3:]:
        arrived[k] = swap(late_gained, "tp", shifts[k])
    own_pieces[1] = far_of(1, arrived[1], near[1])
    cot, cot_t, inv_rms = scaled_cot(width, rep_count, info, packed, squares, value_cot)

    def place_of(o, i, c, k):
        chip = lax.rem(at_outer + o, outer) * inner + lax.rem(at_inner + i, inner)
        return (chip * CORES + c) * tp_count + lax.rem(tp_place + k, tp_count)

    backward = order[::-1]
    pairs = [backward[i : i + 2] for i in range(0, tp_count, 2)]
    chips = [(o, i) for o in range(outer) for i in range(inner)]
    if not in_place:
        product = jnp.dot(cot_t, residual, preferred_element_type=F32).astype(BF16)
        product = product.reshape(features, -1, rows).transpose(1, 0, 2)

    def places_of(pair, c):
        return jnp.stack([place_of(o, i, c, k) for o, i in chips for k in pair]).astype(jnp.int32)

    def for_others(cot_t):
        places = places_of(backward, 1 - core)
        if in_place:
            return grad_product(residual, cot_t, places, rows, None)
        both = after(product, cot_t)[places].reshape(len(chips), tp_count, features, rows)
        return both.swapaxes(0, 1)

    def for_us(other):
        places = places_of(backward, core)
        if in_place:
            outs = grad_product(residual, cot_t, places, rows, other)
            return [[([outs[0]], outs[1]), ([outs[2]], outs[3])], outs[4], outs[5], outs[6]]
        else:
            both = product[places].reshape(len(chips), tp_count, features, rows).swapaxes(0, 1)
            total = widen([both, other]).astype(BF16)
            total = total.reshape(tp_count, outer, inner, features, rows)
            sides = []
            for n in range(0, tp_count, 2):
                sides.append(([total[n, :, s] for s in range(1, inner)], total[n, :, 0]))
                sides.append(([total[n + 1, s] for s in range(1, outer)], total[n + 1, 0]))
        return [sides[n : n + 2] for n in range(0, tp_count, 2)]

    def first_round(sides):
        return [
            [swap(send, axis, s + 1) for s, send in enumerate(sends)]
            for axis, (sends, _) in zip(("inner", "outer"), sides)
        ]

    def second_round(sides, got):
        axes = ("outer", "inner")
        groups = [[keep] + parts for (_, keep), parts in zip(sides, got)]
        return [
            [
                swap(widen([part[s] for part in parts]).astype(BF16), axis, s)
                for s in range(1, lax.axis_size(axis))
            ]
            for parts, axis in zip(groups, axes)
        ]

    def summed(sides, got, later):
        return [
            widen([part[0] for part in [keep] + parts] + last)
            for (_, keep), parts, last in zip(sides, got, later)
        ]

    theirs = for_others(cot_t)
    theirs, arrived = lax.optimization_barrier((theirs, arrived))
    near.update({k: near_of(k, arrived[k]) for k in order[3:]})
    theirs, own_pieces, near = lax.optimization_barrier((theirs, own_pieces, near))
    other = swap(theirs, "core", 1)
    near, own_pieces = lax.optimization_barrier((near, own_pieces))
    for k in order[2:]:
        own_pieces[k] = far_of(k, arrived[k], near[k])
    sides = for_us(other)
    if in_place:
        sides, passed_near, passed_far, kept = sides[:1], sides[1], sides[2], sides[3]
        kept, own_pieces = lax.optimization_barrier((kept, own_pieces))
        beyond = swap(passed_far, "tp", 1)
    else:
        beyond = ()
    got = [first_round(sides[0])]
    sides[1:], own_pieces = lax.optimization_barrier((sides[1:], own_pieces))

    if in_place:
        pieces = [piece for k in order for piece in own_pieces[k]]
        flags = tuple(inner_first(k) for k in order)
        places = [
            jnp.stack([place_of(o, i, c, 0) // tp_count for o, i in chips]).astype(jnp.int32)
            for c in (core, 1 - core)
        ]
        offsets = jnp.stack([lax.rem(tp_place - shift + tp_count, tp_count) * rows for shift in shifts])
        offsets = offsets.astype(jnp.int32)
        total, own_weight = first_value(flags, places[0], offsets, residual, pieces)
    else:
        weight = []
        for k in order:
            both = jnp.stack(own_pieces[k])
            weight.append(both if inner_first(k) else jnp.swapaxes(both, 0, 1))
        by_shift = jnp.array([shifts.index(shift) for shift in range(tp_count)])
        weight = jnp.stack(weight)[by_shift[(tp_place - jnp.arange(tp_count)) % tp_count]]
        weight = weight[:, (at_outer - jnp.arange(outer)) % outer]
        weight = weight[:, :, (at_inner - jnp.arange(inner)) % inner]
        own_weight = weight.transpose(1, 2, 0, 3, 4).reshape(outer * inner, depth, features)
        total = jnp.zeros((), F32)
    got[0], sides[1:], total, own_weight, beyond = lax.optimization_barrier(
        (got[0], sides[1:], total, own_weight, beyond)
    )
    if in_place:
        beyond, passed_near = lax.optimization_barrier((beyond, passed_near))
        passed_near = swap(passed_near, "tp", 1)
        crossed = swap(widen([kept[2:], beyond]).astype(BF16), "outer", 1)
    other_weight = swap(own_weight, "core", 1)
    later = [second_round(sides[0], got[0])]
    got += [first_round(side) for side in sides[1:]]
    if in_place:
        value_proj, coefficient = weight_call(
            functools.partial(value_end_kernel, width),
            places[1],
            residual,
            other_weight,
            [in_hbm(total), cot, inv_rms],
            [
                jax.ShapeDtypeStruct((rows_here, features), BF16),
                jax.ShapeDtypeStruct((rows_here, 1), F32),
            ],
        )
    else:
        both = jnp.stack([own_weight, other_weight], axis=1)
        weight = jnp.where(core == 0, both, both[:, ::-1]).reshape(width, features)
        value_acc = jnp.dot(residual, weight, preferred_element_type=F32)
        value_proj = (inv_rms * value_acc).astype(BF16)
        share = jnp.sum(cot.astype(F32) * value_acc, axis=1, keepdims=True)
        coefficient = inv_rms * inv_rms * share * (1.0 / width)
    later[0], coefficient = lax.optimization_barrier((later[0], coefficient))
    if in_place:
        crossed, passed_near, coefficient = lax.optimization_barrier(
            (crossed, passed_near, coefficient)
        )
        beside = swap(widen([kept[1], passed_near[1], crossed[1]]).astype(BF16), "inner", 1)
        groups = [[keep] + parts + then for (_, keep), parts, then in zip(sides[0], got[0], later[0])]
        last = [swap(x, "tp", k) for x, k in zip(sums_of(groups, 0), pairs[0])]
        grad_shape = jax.ShapeDtypeStruct((rows_here, width), BF16)
        resid_grad = weight_call(
            grad_kernel, places[0], residual, in_hbm(own_weight), [cot, coefficient], grad_shape
        )
        beside, resid_grad = lax.optimization_barrier((beside, resid_grad))
        resid_grad = weight_call(
            grad_kernel, places[1][:3], residual, other_weight, [cot, coefficient], grad_shape, resid_grad
        )
        last, resid_grad = lax.optimization_barrier((last, resid_grad))
        resid_grad = weight_call(
            grad_kernel, places[1][3:], residual, other_weight, [cot, coefficient], grad_shape, resid_grad
        )
        grad_rows = widen([kept[0], passed_near[0], crossed[0], beside] + last)
    else:
        normed_grad = lax.dot_general(
            cot, weight, (((1,), (1,)), ((), ())), preferred_element_type=F32
        )
        resid_grad = (normed_grad - residual.astype(F32) * coefficient).astype(BF16)
        later += [second_round(side, parts) for side, parts in zip(sides[1:], got[1:])]
        sums = {}
        for pair, *rounds in zip(pairs, sides, got, later):
            sums.update(zip(pair, summed(*rounds)))
        last = [swap(sums[k].astype(BF16), "tp", k) for k in backward[:-1]]
        grad_rows = widen([sums[0]] + last)
    late_gain, late_weight, grad_rows = lax.optimization_barrier((norm_gain, value_weight, grad_rows))
    weight_grad = (late_gain.astype(F32)[None, :] * grad_rows).T
    gain_grad = jnp.sum(late_weight.astype(F32).T * grad_rows, axis=0)
    return (value_proj, resid_grad, weight_grad, gain_grad)


def solution(mesh):
    rep_count, tp_count = mesh.shape["rep"], mesh.shape["tp"]
    split = jax.sharding.Mesh(
        mesh.devices.reshape(OUTER, rep_count // (OUTER * CORES), CORES, tp_count),
        ("outer", "inner", "core", "tp"),
    )
    rep = ("outer", "inner", "core")
    rows = rep + ("tp",)
    return jax.shard_map(
        per_device,
        mesh=split,
        in_specs=(
            P(rows, None),
            P(rows),
            P(rows, None),
            P(rows, None),
            P(rows),
            P("tp", rep),
            P("tp", rep),
            P("tp", rep),
            P(rep),
            P(),
        ),
        out_specs=(P(rows, None), P(rows, None), P(rows, None), P(rows)),
        check_vma=False,
    )
```

```python
import functools

import jax
import jax.numpy as jnp
from jax import lax
from jax.experimental import pallas as pl
from jax.experimental.pallas import tpu as pltpu
from jax.sharding import PartitionSpec as P

VOCAB = 128256
EPS = 1e-05
BETA = 0.5
CORES = 2
OUTER = 2
PAIR_VMEM = 18 * 1024 * 1024
WEIGHT_VMEM = 22 * 1024 * 1024
NOMINAL = pl.CostEstimate(flops=1024, bytes_accessed=1024, transcendentals=0)
BF16 = jnp.bfloat16
F32 = jnp.float32


def swap(value, axis, step):
    size = lax.axis_size(axis)
    return lax.ppermute(value, axis, [(place, (place + step) % size) for place in range(size)])


def trade(value, axis, mask):
    size = lax.axis_size(axis)
    return lax.ppermute(value, axis, [(place, place ^ mask) for place in range(size)])


def in_hbm(array):
    return pltpu.with_memory_space_constraint(array, pltpu.HBM)


def after(value, *earlier):
    return lax.optimization_barrier((value, earlier))[0]


def widen(parts):
    return functools.reduce(jnp.add, [part.astype(F32) for part in parts])


def chunk_shifts(tp_count):
    shifts = [0]
    for step in range(1, tp_count // 2 + 1):
        shifts += [step] if 2 * step == tp_count else [step, tp_count - step]
    return shifts


def inner_first(chunk):
    return chunk % 4 in (0, 3)


def theirs_kernel(places_ref, cot_ref, *rest):
    blocks, out_ref = rest[:-1], rest[-1]
    for slot, resid_ref in enumerate(blocks):
        product = jnp.dot(cot_ref[...], resid_ref[...], preferred_element_type=F32)
        out_ref[slot, 0] = product.astype(BF16)


def ours_kernel(places_ref, cot_ref, *rest):
    slots = 4
    blocks, other_ref, outs = rest[:slots], rest[slots], rest[slots + 1 :]
    step = pl.program_id(0)
    ways = (lax.rem(step, 2), step // 2)
    totals = [
        (
            jnp.dot(cot_ref[...], resid_ref[...], preferred_element_type=F32)
            + other_ref[slot, 0].astype(F32)
        ).astype(BF16)
        for slot, resid_ref in enumerate(blocks)
    ]
    for slot, way in enumerate(ways):
        send_ref, keep_ref = outs[2 * slot : 2 * slot + 2]

        @pl.when(way == 1)
        def _():
            send_ref[0] = totals[slot]

        @pl.when(way == 0)
        def _():
            keep_ref[0] = totals[slot]

    near_ref, far_ref, kept_ref = outs[4:]
    kept_ref[0] = totals[3]

    @pl.when(ways[1] == 1)
    def _():
        far_ref[0] = totals[2]

    @pl.when(ways[1] == 0)
    def _():
        near_ref[0] = totals[2]


def grad_product(residual, cot_t, places, rows, other):
    features, tokens = cot_t.shape
    steps = 4
    slots = places.shape[0] // steps
    in_specs = [pl.BlockSpec((features, tokens), lambda i, p: (0, 0))] + [
        pl.BlockSpec((tokens, rows), lambda i, p, slot=slot: (0, p[slots * i + slot]))
        for slot in range(slots)
    ]
    operands = [places, cot_t] + [in_hbm(residual)] * slots
    block = pl.BlockSpec((slots, 1, features, rows), lambda i, p: (0, i, 0, 0))
    if other is None:
        kernel, out_specs = theirs_kernel, block
        out_shape = pltpu.HBM((slots, steps, features, rows), BF16)
    else:
        kernel = ours_kernel
        in_specs.append(block)
        operands.append(other)
        indices = [
            lambda i: i // 2,
            lambda i: i // 2,
            lambda i: jnp.maximum(i - 2, 0),
            lambda i: jnp.minimum(i, 1),
            lambda i: jnp.minimum(i, 1),
            lambda i: jnp.maximum(i - 2, 0),
            lambda i: i,
        ]
        out_specs = [
            pl.BlockSpec((1, features, rows), lambda i, p, index=index: (index(i), 0, 0))
            for index in indices
        ]
        out_shape = [pltpu.HBM((n, features, rows), BF16) for n in (2, 2, 2, 2, 2, 2, steps)]
    return pl.pallas_call(
        kernel,
        out_shape=out_shape,
        grid_spec=pltpu.PrefetchScalarGridSpec(
            num_scalar_prefetch=1, grid=(steps,), in_specs=in_specs, out_specs=out_specs
        ),
        cost_estimate=NOMINAL,
        compiler_params=pltpu.CompilerParams(vmem_limit_bytes=PAIR_VMEM),
    )(*operands)


def sum_kernel(counts, *refs):
    ins, outs = refs[: sum(counts)], refs[sum(counts) :]
    for n, out_ref in enumerate(outs):
        first = sum(counts[:n])
        parts = [ref[...].astype(F32).reshape(out_ref.shape) for ref in ins[first : first + counts[n]]]
        out_ref[...] = functools.reduce(jnp.add, parts).astype(BF16)


def sums_of(groups, slot):
    shape = groups[0][0].shape[-2:]
    in_specs = [
        pl.BlockSpec((1,) + shape, lambda i: (slot, 0, 0))
        if part.ndim == 3
        else pl.BlockSpec(shape, lambda i: (0, 0))
        for parts in groups
        for part in parts
    ]
    return pl.pallas_call(
        functools.partial(sum_kernel, [len(parts) for parts in groups]),
        out_shape=[jax.ShapeDtypeStruct(shape, BF16)] * len(groups),
        grid=(1,),
        in_specs=in_specs,
        out_specs=[pl.BlockSpec(shape, lambda i: (0, 0))] * len(groups),
        cost_estimate=NOMINAL,
        compiler_params=pltpu.CompilerParams(vmem_limit_bytes=PAIR_VMEM),
    )(*[part for parts in groups for part in parts])


def place_weight(inner_flags, offsets_ref, pieces, weight_ref):
    step = pl.program_id(0)
    at_outer, at_inner = step // 2, lax.rem(step, 2)
    rows = pieces[0].shape[1]
    for chunk, flag in enumerate(inner_flags):
        way = at_outer if flag else at_inner
        where = pl.ds(pl.multiple_of(offsets_ref[chunk], rows), rows)
        for late in range(2):
            piece = pieces[chunk * 2 + late]

            @pl.when(way == late)
            def _():
                weight_ref[0, where, :] = piece[0]


def piece_specs(inner_flags, rows, features):
    specs = []
    for flag in inner_flags:
        for late in range(2):
            if flag:
                index = lambda i, *_, first=2 * late: (jnp.clip(i - first, 0, 1), 0, 0)
            else:
                index = lambda i, *_: (i // 2, 0, 0)
            specs.append(pl.BlockSpec((1, rows, features), index))
    return specs


def value_kernel(inner_flags, places_ref, offsets_ref, resid_ref, *rest):
    pieces, (total_ref, weight_ref) = rest[:-2], rest[-2:]
    step = pl.program_id(0)
    place_weight(inner_flags, offsets_ref, pieces, weight_ref)
    product = jnp.dot(resid_ref[...], weight_ref[0], preferred_element_type=F32)

    @pl.when(step == 0)
    def _():
        total_ref[...] = product

    @pl.when(step > 0)
    def _():
        total_ref[...] += product


def value_end_kernel(
    width, places_ref, resid_ref, weight_ref, first_ref, cot_ref, inv_ref, value_ref, coef_ref, total_ref
):
    step = pl.program_id(0)
    product = jnp.dot(resid_ref[...], weight_ref[0], preferred_element_type=F32)

    @pl.when(step == 0)
    def _():
        total_ref[...] = first_ref[...] + product

    @pl.when(step > 0)
    def _():
        total_ref[...] += product

    @pl.when(step == pl.num_programs(0) - 1)
    def _():
        total = total_ref[...]
        inv = inv_ref[...]
        value_ref[...] = (total * inv).astype(BF16)
        share = jnp.sum(total * cot_ref[...].astype(F32), axis=1, keepdims=True)
        coef_ref[...] = share * (inv * inv) * (1.0 / width)


def grad_kernel(places_ref, resid_ref, weight_ref, cot_ref, coef_ref, *rest):
    out_ref = rest[-1]
    grad = lax.dot_general(
        cot_ref[...], weight_ref[0], (((1,), (1,)), ((), ())), preferred_element_type=F32
    )
    out_ref[...] = (grad - resid_ref[...].astype(F32) * coef_ref[...]).astype(BF16)


def whole_block(array):
    return pl.BlockSpec(array.shape, lambda i, *_: (0, 0))


def first_value(inner_flags, places, offsets, residual, pieces):
    tokens, width = residual.shape
    rows, features = pieces[0].shape[1:]
    steps = places.shape[0]
    depth = width // (CORES * steps)
    total = pltpu.HBM((tokens, features), F32)
    return pl.pallas_call(
        functools.partial(value_kernel, inner_flags),
        out_shape=[total, pltpu.HBM((steps, depth, features), BF16)],
        grid_spec=pltpu.PrefetchScalarGridSpec(
            num_scalar_prefetch=2,
            grid=(steps,),
            in_specs=[pl.BlockSpec((tokens, depth), lambda i, p, o: (0, p[i]))]
            + piece_specs(inner_flags, rows, features),
            out_specs=[
                whole_block(total),
                pl.BlockSpec((1, depth, features), lambda i, p, o: (p[i] // CORES, 0, 0)),
            ],
        ),
        cost_estimate=NOMINAL,
        compiler_params=pltpu.CompilerParams(vmem_limit_bytes=WEIGHT_VMEM),
    )(places, offsets, in_hbm(residual), *pieces)


def weight_call(kernel, places, residual, weight, wholes, out_shape, earlier=None):
    tokens, width = residual.shape
    _, depth, features = weight.shape
    steps = places.shape[0]
    scratch = []
    if isinstance(out_shape, list):
        out_specs = [whole_block(array) for array in out_shape]
        scratch.append(pltpu.VMEM((tokens, features), F32))
    else:
        out_specs = pl.BlockSpec((tokens, depth), lambda i, p: (0, p[i]))
    in_specs = [
        pl.BlockSpec((tokens, depth), lambda i, p: (0, p[i])),
        pl.BlockSpec((1, depth, features), lambda i, p: (p[i] // CORES, 0, 0)),
    ] + [whole_block(array) for array in wholes]
    operands = [places, in_hbm(residual), weight, *wholes]
    aliases = {}
    if earlier is not None:
        aliases = {len(operands): 0}
        in_specs.append(pl.BlockSpec(memory_space=pltpu.HBM))
        operands.append(earlier)
    return pl.pallas_call(
        kernel,
        out_shape=out_shape,
        grid_spec=pltpu.PrefetchScalarGridSpec(
            num_scalar_prefetch=1,
            grid=(steps,),
            in_specs=in_specs,
            out_specs=out_specs,
            scratch_shapes=scratch,
        ),
        input_output_aliases=aliases,
        cost_estimate=NOMINAL,
        compiler_params=pltpu.CompilerParams(vmem_limit_bytes=WEIGHT_VMEM),
    )(*operands)


def cot_kernel(width, rep_count, info_ref, shares_ref, squares_ref, value_cot_ref, cot_ref, cot_t_ref, inv_ref):
    place, length = info_ref[0], info_ref[1]
    rows = value_cot_ref.shape[0]
    own = rows // 128
    seq = (shares_ref.shape[1] - own) // 3
    shares = range(shares_ref.shape[0])

    def below(first, shape):
        at = lax.broadcasted_iota(jnp.int32, shape, 0) * 128 + lax.broadcasted_iota(jnp.int32, shape, 1)
        return first + at < length

    def summed(mask, value):
        return jnp.sum(jnp.where(mask, value, 0.0), axis=(0, 1), keepdims=True)

    maxes = [shares_ref[m, 0:seq] for m in shares]
    top_max = functools.reduce(jnp.maximum, maxes)
    sum_exp = functools.reduce(
        jnp.add, [shares_ref[m, seq : 2 * seq] * jnp.exp(maxes[m] - top_max) for m in shares]
    )
    picked = functools.reduce(jnp.add, [shares_ref[m, 2 * seq : 3 * seq] for m in shares])
    ref_logp = picked - top_max - jnp.log(sum_exp)
    total = -summed(below(0, (seq, 128)), ref_logp)
    for m in shares:
        first = jnp.bitwise_xor(place, m) * rows
        total += summed(below(first, (own, 128)), shares_ref[m, 3 * seq :])
    seq_delta = total / jnp.full((1, 1), length, jnp.int32).astype(F32)
    weight = (2.0 / rep_count) * jax.nn.sigmoid(BETA * seq_delta)
    inv = lax.rsqrt(squares_ref[...] * (1.0 / width) + EPS)
    live = place * rows + lax.broadcasted_iota(jnp.int32, (rows, 1), 0) < length
    scaled = jnp.where(live, inv * weight, 0.0) * value_cot_ref[...].astype(F32)
    cot_ref[...] = scaled.astype(BF16)
    cot_t_ref[...] = scaled.T.astype(BF16)
    inv_ref[...] = inv


def scaled_cot(width, rep_count, info, shares, squares, value_cot):
    rows, features = value_cot.shape

    def whole(array):
        return pl.BlockSpec(array.shape, lambda i, p: (0,) * array.ndim)

    out_shape = [
        jax.ShapeDtypeStruct((rows, features), BF16),
        jax.ShapeDtypeStruct((features, rows), BF16),
        jax.ShapeDtypeStruct((rows, 1), F32),
    ]
    return pl.pallas_call(
        functools.partial(cot_kernel, width, rep_count),
        out_shape=out_shape,
        grid_spec=pltpu.PrefetchScalarGridSpec(
            num_scalar_prefetch=1,
            grid=(1,),
            in_specs=[whole(shares), whole(squares), whole(value_cot)],
            out_specs=[pl.BlockSpec(array.shape, lambda i, p: (0, 0)) for array in out_shape],
        ),
        cost_estimate=NOMINAL,
        compiler_params=pltpu.CompilerParams(vmem_limit_bytes=PAIR_VMEM),
    )(info, shares, squares, in_hbm(value_cot))


def per_device(
    residual,
    norm_gain,
    value_weight,
    value_cot,
    trainee_logp,
    ref_shard_max,
    ref_shard_sum,
    ref_target_logit,
    target_ids,
    lengths,
):
    rows_here, width = residual.shape
    features = value_cot.shape[1]
    tp_count = lax.axis_size("tp")
    outer, inner = lax.axis_size("outer"), lax.axis_size("inner")
    rep_count = outer * inner * CORES
    tp_place = lax.axis_index("tp")
    core = lax.axis_index("core")
    at_inner = lax.axis_index("inner")
    at_outer = lax.axis_index("outer")
    rep_place = (at_outer * inner + at_inner) * CORES + core
    depth = width // rep_count
    rows = depth // tp_count
    order = list(range(tp_count))
    shifts = chunk_shifts(tp_count)
    in_place = rows % 128 == 0 and outer == 2 and inner == 2 and tp_count == 4

    owned = jnp.where(
        target_ids // (VOCAB // tp_count) == tp_place,
        ref_target_logit[0],
        jnp.zeros_like(ref_target_logit[0]),
    )
    packed = jnp.concatenate([ref_shard_max[0], ref_shard_sum[0], owned, trainee_logp])
    packed = packed.reshape(1, -1, 128)
    packed = jnp.concatenate([packed, trade(packed, "tp", 1)])

    gained = (value_weight.astype(F32) * norm_gain.astype(F32)[:, None]).astype(BF16)
    residual, gained, packed = lax.optimization_barrier((residual, gained, packed))
    resid_wide = residual.astype(F32)
    squares = jnp.sum(resid_wide * resid_wide, axis=1, keepdims=True)

    def near_of(k, block):
        first = "inner" if inner_first(k) else "outer"
        return [swap(block, first, s) for s in range(1, lax.axis_size(first))]

    def far_of(k, block, nears):
        second = "outer" if inner_first(k) else "inner"
        near = jnp.stack([block] + nears)
        return [near] + [swap(near, second, s) for s in range(1, lax.axis_size(second))]

    mask = 2
    while mask < tp_count:
        packed = jnp.concatenate([packed, trade(packed, "tp", mask)])
        mask *= 2
    own_pieces, near = {}, {}
    arrived = {0: gained, 1: swap(gained, "tp", shifts[1])}
    near[0] = near_of(0, gained)
    arrived[1], near[0], squares, late_gained = lax.optimization_barrier(
        (arrived[1], near[0], squares, gained)
    )
    near[1] = near_of(1, arrived[1])
    arrived[2] = swap(late_gained, "tp", shifts[2])
    own_pieces[0] = far_of(0, gained, near[0])
    seq_length = lax.dynamic_index_in_dim(lengths, rep_place, keepdims=False)
    info = jnp.stack([tp_place, seq_length]).astype(jnp.int32)
    near[1], arrived[2], packed, late_gained, info = lax.optimization_barrier(
        (near[1], arrived[2], packed, late_gained, info)
    )
    near[2] = near_of(2, arrived[2])
    for k in order[3:]:
        arrived[k] = swap(late_gained, "tp", shifts[k])
    own_pieces[1] = far_of(1, arrived[1], near[1])
    cot, cot_t, inv_rms = scaled_cot(width, rep_count, info, packed, squares, value_cot)

    def place_of(o, i, c, k):
        chip = lax.rem(at_outer + o, outer) * inner + lax.rem(at_inner + i, inner)
        return (chip * CORES + c) * tp_count + lax.rem(tp_place + k, tp_count)

    backward = order[::-1]
    pairs = [backward[i : i + 2] for i in range(0, tp_count, 2)]
    chips = [(o, i) for o in range(outer) for i in range(inner)]
    if not in_place:
        product = jnp.dot(cot_t, residual, preferred_element_type=F32).astype(BF16)
        product = product.reshape(features, -1, rows).transpose(1, 0, 2)

    def places_of(pair, c):
        return jnp.stack([place_of(o, i, c, k) for o, i in chips for k in pair]).astype(jnp.int32)

    def for_others(cot_t):
        places = places_of(backward, 1 - core)
        if in_place:
            return grad_product(residual, cot_t, places, rows, None)
        both = after(product, cot_t)[places].reshape(len(chips), tp_count, features, rows)
        return both.swapaxes(0, 1)

    def for_us(other):
        places = places_of(backward, core)
        if in_place:
            outs = grad_product(residual, cot_t, places, rows, other)
            return [[([outs[0]], outs[1]), ([outs[2]], outs[3])], outs[4], outs[5], outs[6]]
        else:
            both = product[places].reshape(len(chips), tp_count, features, rows).swapaxes(0, 1)
            total = widen([both, other]).astype(BF16)
            total = total.reshape(tp_count, outer, inner, features, rows)
            sides = []
            for n in range(0, tp_count, 2):
                sides.append(([total[n, :, s] for s in range(1, inner)], total[n, :, 0]))
                sides.append(([total[n + 1, s] for s in range(1, outer)], total[n + 1, 0]))
        return [sides[n : n + 2] for n in range(0, tp_count, 2)]

    def first_round(sides):
        return [
            [swap(send, axis, s + 1) for s, send in enumerate(sends)]
            for axis, (sends, _) in zip(("inner", "outer"), sides)
        ]

    def second_round(sides, got):
        axes = ("outer", "inner")
        groups = [[keep] + parts for (_, keep), parts in zip(sides, got)]
        return [
            [
                swap(widen([part[s] for part in parts]).astype(BF16), axis, s)
                for s in range(1, lax.axis_size(axis))
            ]
            for parts, axis in zip(groups, axes)
        ]

    def summed(sides, got, later):
        return [
            widen([part[0] for part in [keep] + parts] + last)
            for (_, keep), parts, last in zip(sides, got, later)
        ]

    theirs = for_others(cot_t)
    theirs, arrived = lax.optimization_barrier((theirs, arrived))
    near.update({k: near_of(k, arrived[k]) for k in order[3:]})
    theirs, own_pieces, near = lax.optimization_barrier((theirs, own_pieces, near))
    other = swap(theirs, "core", 1)
    near, own_pieces = lax.optimization_barrier((near, own_pieces))
    for k in order[2:]:
        own_pieces[k] = far_of(k, arrived[k], near[k])
    sides = for_us(other)
    if in_place:
        sides, passed_near, passed_far, kept = sides[:1], sides[1], sides[2], sides[3]
        kept, own_pieces = lax.optimization_barrier((kept, own_pieces))
        beyond = swap(passed_far, "tp", 1)
    else:
        beyond = ()
    got = [first_round(sides[0])]
    sides[1:], own_pieces = lax.optimization_barrier((sides[1:], own_pieces))

    if in_place:
        pieces = [piece for k in order for piece in own_pieces[k]]
        flags = tuple(inner_first(k) for k in order)
        places = [
            jnp.stack([place_of(o, i, c, 0) // tp_count for o, i in chips]).astype(jnp.int32)
            for c in (core, 1 - core)
        ]
        offsets = jnp.stack([lax.rem(tp_place - shift + tp_count, tp_count) * rows for shift in shifts])
        offsets = offsets.astype(jnp.int32)
        total, own_weight = first_value(flags, places[0], offsets, residual, pieces)
    else:
        weight = []
        for k in order:
            both = jnp.stack(own_pieces[k])
            weight.append(both if inner_first(k) else jnp.swapaxes(both, 0, 1))
        by_shift = jnp.array([shifts.index(shift) for shift in range(tp_count)])
        weight = jnp.stack(weight)[by_shift[(tp_place - jnp.arange(tp_count)) % tp_count]]
        weight = weight[:, (at_outer - jnp.arange(outer)) % outer]
        weight = weight[:, :, (at_inner - jnp.arange(inner)) % inner]
        own_weight = weight.transpose(1, 2, 0, 3, 4).reshape(outer * inner, depth, features)
        total = jnp.zeros((), F32)
    got[0], sides[1:], total, own_weight, beyond = lax.optimization_barrier(
        (got[0], sides[1:], total, own_weight, beyond)
    )
    if in_place:
        sent = [
            widen([keep[1], parts[0][1]]).astype(BF16) for (_, keep), parts in zip(sides[0], got[0])
        ]
        sent, beyond, passed_near = lax.optimization_barrier((sent, beyond, passed_near))
        later = [[[swap(x, axis, 1)] for x, axis in zip(sent, ("outer", "inner"))]]
        passed_near = swap(passed_near, "tp", 1)
    else:
        later = [second_round(sides[0], got[0])]
    other_weight = swap(own_weight, "core", 1)
    got += [first_round(side) for side in sides[1:]]
    if in_place:
        value_proj, coefficient = weight_call(
            functools.partial(value_end_kernel, width),
            places[1],
            residual,
            other_weight,
            [in_hbm(total), cot, inv_rms],
            [
                jax.ShapeDtypeStruct((rows_here, features), BF16),
                jax.ShapeDtypeStruct((rows_here, 1), F32),
            ],
        )
    else:
        both = jnp.stack([own_weight, other_weight], axis=1)
        weight = jnp.where(core == 0, both, both[:, ::-1]).reshape(width, features)
        value_acc = jnp.dot(residual, weight, preferred_element_type=F32)
        value_proj = (inv_rms * value_acc).astype(BF16)
        share = jnp.sum(cot.astype(F32) * value_acc, axis=1, keepdims=True)
        coefficient = inv_rms * inv_rms * share * (1.0 / width)
    later[0], coefficient = lax.optimization_barrier((later[0], coefficient))
    if in_place:
        groups = [[keep] + parts + then for (_, keep), parts, then in zip(sides[0], got[0], later[0])]
        sent = sums_of(groups, 0)
        last = [swap(x, "tp", k) for x, k in zip(sent, pairs[0])]
        coefficient, beyond, _ = lax.optimization_barrier((coefficient, beyond, sent))
        crossed = swap(widen([kept[2:], beyond]).astype(BF16), "outer", 1)
        grad_shape = jax.ShapeDtypeStruct((rows_here, width), BF16)
        resid_grad = weight_call(
            grad_kernel, places[0], residual, in_hbm(own_weight), [cot, coefficient], grad_shape
        )
        crossed, passed_near, resid_grad = lax.optimization_barrier(
            (crossed, passed_near, resid_grad)
        )
        beside = swap(widen([kept[1], passed_near[1], crossed[1]]).astype(BF16), "inner", 1)
        resid_grad = weight_call(
            grad_kernel, places[1], residual, other_weight, [cot, coefficient], grad_shape, resid_grad
        )
        last, beside, resid_grad = lax.optimization_barrier((last, beside, resid_grad))
        grad_rows = widen([kept[0], passed_near[0], crossed[0], beside] + last)
    else:
        normed_grad = lax.dot_general(
            cot, weight, (((1,), (1,)), ((), ())), preferred_element_type=F32
        )
        resid_grad = (normed_grad - residual.astype(F32) * coefficient).astype(BF16)
        later += [second_round(side, parts) for side, parts in zip(sides[1:], got[1:])]
        sums = {}
        for pair, *rounds in zip(pairs, sides, got, later):
            sums.update(zip(pair, summed(*rounds)))
        last = [swap(sums[k].astype(BF16), "tp", k) for k in backward[:-1]]
        grad_rows = widen([sums[0]] + last)
    late_gain, late_weight, grad_rows = lax.optimization_barrier((norm_gain, value_weight, grad_rows))
    weight_grad = (late_gain.astype(F32)[None, :] * grad_rows).T
    gain_grad = jnp.sum(late_weight.astype(F32).T * grad_rows, axis=0)
    return (value_proj, resid_grad, weight_grad, gain_grad)


def solution(mesh):
    rep_count, tp_count = mesh.shape["rep"], mesh.shape["tp"]
    split = jax.sharding.Mesh(
        mesh.devices.reshape(OUTER, rep_count // (OUTER * CORES), CORES, tp_count),
        ("outer", "inner", "core", "tp"),
    )
    rep = ("outer", "inner", "core")
    rows = rep + ("tp",)
    return jax.shard_map(
        per_device,
        mesh=split,
        in_specs=(
            P(rows, None),
            P(rows),
            P(rows, None),
            P(rows, None),
            P(rows),
            P("tp", rep),
            P("tp", rep),
            P("tp", rep),
            P(rep),
            P(),
        ),
        out_specs=(P(rows, None), P(rows, None), P(rows, None), P(rows)),
        check_vma=False,
    )
```

```python
import functools

import jax
import jax.numpy as jnp
from jax import lax
from jax.experimental import pallas as pl
from jax.experimental.pallas import tpu as pltpu
from jax.sharding import PartitionSpec as P

VOCAB = 128256
EPS = 1e-05
BETA = 0.5
CORES = 2
OUTER = 2
PAIR_VMEM = 12 * 1024 * 1024
WEIGHT_VMEM = 15 * 1024 * 1024
NOMINAL = pl.CostEstimate(flops=1024, bytes_accessed=1024, transcendentals=0)
BF16 = jnp.bfloat16
F32 = jnp.float32


def swap(value, axis, step):
    size = lax.axis_size(axis)
    return lax.ppermute(value, axis, [(place, (place + step) % size) for place in range(size)])


def trade(value, axis, mask):
    size = lax.axis_size(axis)
    return lax.ppermute(value, axis, [(place, place ^ mask) for place in range(size)])


def in_hbm(array):
    return pltpu.with_memory_space_constraint(array, pltpu.HBM)


def after(value, *earlier):
    return lax.optimization_barrier((value, earlier))[0]


def widen(parts):
    return functools.reduce(jnp.add, [part.astype(F32) for part in parts])


def chunk_shifts(tp_count):
    shifts = [0]
    for step in range(1, tp_count // 2 + 1):
        shifts += [step] if 2 * step == tp_count else [step, tp_count - step]
    return shifts


def inner_first(chunk):
    return chunk % 4 in (0, 3)


def theirs_kernel(places_ref, cot_ref, *rest):
    blocks, out_ref = rest[:-1], rest[-1]
    for slot, resid_ref in enumerate(blocks):
        product = jnp.dot(cot_ref[...], resid_ref[...], preferred_element_type=F32)
        out_ref[slot, 0] = product.astype(BF16)


def ours_kernel(places_ref, cot_ref, *rest):
    slots = 4
    blocks, other_ref, outs = rest[:slots], rest[slots], rest[slots + 1 :]
    step = pl.program_id(0)
    ways = (lax.rem(step, 2), step // 2)
    totals = [
        (
            jnp.dot(cot_ref[...], resid_ref[...], preferred_element_type=F32)
            + other_ref[slot, 0].astype(F32)
        ).astype(BF16)
        for slot, resid_ref in enumerate(blocks)
    ]
    for slot, way in enumerate(ways):
        send_ref, keep_ref = outs[2 * slot : 2 * slot + 2]

        @pl.when(way == 1)
        def _():
            send_ref[0] = totals[slot]

        @pl.when(way == 0)
        def _():
            keep_ref[0] = totals[slot]

    near_ref, far_ref, kept_ref = outs[4:]
    kept_ref[0] = totals[3]

    @pl.when(ways[1] == 1)
    def _():
        far_ref[0] = totals[2]

    @pl.when(ways[1] == 0)
    def _():
        near_ref[0] = totals[2]


def grad_product(residual, cot_t, places, rows, other):
    features, tokens = cot_t.shape
    steps = 4
    slots = places.shape[0] // steps
    in_specs = [pl.BlockSpec((features, tokens), lambda i, p: (0, 0))] + [
        pl.BlockSpec((tokens, rows), lambda i, p, slot=slot: (0, p[slots * i + slot]))
        for slot in range(slots)
    ]
    operands = [places, cot_t] + [in_hbm(residual)] * slots
    block = pl.BlockSpec((slots, 1, features, rows), lambda i, p: (0, i, 0, 0))
    if other is None:
        kernel, out_specs = theirs_kernel, block
        out_shape = pltpu.HBM((slots, steps, features, rows), BF16)
    else:
        kernel = ours_kernel
        in_specs.append(block)
        operands.append(other)
        indices = [
            lambda i: i // 2,
            lambda i: i // 2,
            lambda i: jnp.maximum(i - 2, 0),
            lambda i: jnp.minimum(i, 1),
            lambda i: jnp.minimum(i, 1),
            lambda i: jnp.maximum(i - 2, 0),
            lambda i: i,
        ]
        out_specs = [
            pl.BlockSpec((1, features, rows), lambda i, p, index=index: (index(i), 0, 0))
            for index in indices
        ]
        out_shape = [pltpu.HBM((n, features, rows), BF16) for n in (2, 2, 2, 2, 2, 2, steps)]
    return pl.pallas_call(
        kernel,
        out_shape=out_shape,
        grid_spec=pltpu.PrefetchScalarGridSpec(
            num_scalar_prefetch=1, grid=(steps,), in_specs=in_specs, out_specs=out_specs
        ),
        cost_estimate=NOMINAL,
        compiler_params=pltpu.CompilerParams(vmem_limit_bytes=PAIR_VMEM),
    )(*operands)


def sum_kernel(counts, *refs):
    ins, outs = refs[: sum(counts)], refs[sum(counts) :]
    for n, out_ref in enumerate(outs):
        first = sum(counts[:n])
        parts = [ref[...].astype(F32).reshape(out_ref.shape) for ref in ins[first : first + counts[n]]]
        out_ref[...] = functools.reduce(jnp.add, parts).astype(BF16)


def sums_of(groups, slot):
    shape = groups[0][0].shape[-2:]
    in_specs = [
        pl.BlockSpec((1,) + shape, lambda i: (slot, 0, 0))
        if part.ndim == 3
        else pl.BlockSpec(shape, lambda i: (0, 0))
        for parts in groups
        for part in parts
    ]
    return pl.pallas_call(
        functools.partial(sum_kernel, [len(parts) for parts in groups]),
        out_shape=[jax.ShapeDtypeStruct(shape, BF16)] * len(groups),
        grid=(1,),
        in_specs=in_specs,
        out_specs=[pl.BlockSpec(shape, lambda i: (0, 0))] * len(groups),
        cost_estimate=NOMINAL,
        compiler_params=pltpu.CompilerParams(vmem_limit_bytes=PAIR_VMEM),
    )(*[part for parts in groups for part in parts])


def place_weight(inner_flags, offsets_ref, pieces, weight_ref):
    step = pl.program_id(0)
    at_outer, at_inner = step // 2, lax.rem(step, 2)
    rows = pieces[0].shape[1]
    for chunk, flag in enumerate(inner_flags):
        way = at_outer if flag else at_inner
        where = pl.ds(pl.multiple_of(offsets_ref[chunk], rows), rows)
        for late in range(2):
            piece = pieces[chunk * 2 + late]

            @pl.when(way == late)
            def _():
                weight_ref[0, where, :] = piece[0]


def piece_specs(inner_flags, rows, features):
    specs = []
    for flag in inner_flags:
        for late in range(2):
            if flag:
                index = lambda i, *_, first=2 * late: (jnp.clip(i - first, 0, 1), 0, 0)
            else:
                index = lambda i, *_: (i // 2, 0, 0)
            specs.append(pl.BlockSpec((1, rows, features), index))
    return specs


def value_kernel(inner_flags, places_ref, offsets_ref, resid_ref, *rest):
    pieces, (total_ref, weight_ref) = rest[:-2], rest[-2:]
    step = pl.program_id(0)
    place_weight(inner_flags, offsets_ref, pieces, weight_ref)
    product = jnp.dot(resid_ref[...], weight_ref[0], preferred_element_type=F32)

    @pl.when(step == 0)
    def _():
        total_ref[...] = product

    @pl.when(step > 0)
    def _():
        total_ref[...] += product


def value_end_kernel(
    width, places_ref, resid_ref, weight_ref, first_ref, cot_ref, inv_ref, value_ref, coef_ref, total_ref
):
    step = pl.program_id(0)
    product = jnp.dot(resid_ref[...], weight_ref[0], preferred_element_type=F32)

    @pl.when(step == 0)
    def _():
        total_ref[...] = first_ref[...] + product

    @pl.when(step > 0)
    def _():
        total_ref[...] += product

    @pl.when(step == pl.num_programs(0) - 1)
    def _():
        total = total_ref[...]
        inv = inv_ref[...]
        value_ref[...] = (total * inv).astype(BF16)
        share = jnp.sum(total * cot_ref[...].astype(F32), axis=1, keepdims=True)
        coef_ref[...] = share * (inv * inv) * (1.0 / width)


def grad_kernel(places_ref, resid_ref, weight_ref, cot_ref, coef_ref, *rest):
    out_ref = rest[-1]
    grad = lax.dot_general(
        cot_ref[...], weight_ref[0], (((1,), (1,)), ((), ())), preferred_element_type=F32
    )
    out_ref[...] = (grad - resid_ref[...].astype(F32) * coef_ref[...]).astype(BF16)


def whole_block(array):
    return pl.BlockSpec(array.shape, lambda i, *_: (0, 0))


def first_value(inner_flags, places, offsets, residual, pieces):
    tokens, width = residual.shape
    rows, features = pieces[0].shape[1:]
    steps = places.shape[0]
    depth = width // (CORES * steps)
    total = pltpu.HBM((tokens, features), F32)
    return pl.pallas_call(
        functools.partial(value_kernel, inner_flags),
        out_shape=[total, pltpu.HBM((steps, depth, features), BF16)],
        grid_spec=pltpu.PrefetchScalarGridSpec(
            num_scalar_prefetch=2,
            grid=(steps,),
            in_specs=[pl.BlockSpec((tokens, depth), lambda i, p, o: (0, p[i]))]
            + piece_specs(inner_flags, rows, features),
            out_specs=[
                whole_block(total),
                pl.BlockSpec((1, depth, features), lambda i, p, o: (p[i] // CORES, 0, 0)),
            ],
        ),
        cost_estimate=NOMINAL,
        compiler_params=pltpu.CompilerParams(vmem_limit_bytes=WEIGHT_VMEM),
    )(places, offsets, in_hbm(residual), *pieces)


def weight_call(kernel, places, residual, weight, wholes, out_shape, earlier=None):
    tokens, width = residual.shape
    _, depth, features = weight.shape
    steps = places.shape[0]
    scratch = []
    if isinstance(out_shape, list):
        out_specs = [whole_block(array) for array in out_shape]
        scratch.append(pltpu.VMEM((tokens, features), F32))
    else:
        out_specs = pl.BlockSpec((tokens, depth), lambda i, p: (0, p[i]))
    in_specs = [
        pl.BlockSpec((tokens, depth), lambda i, p: (0, p[i])),
        pl.BlockSpec((1, depth, features), lambda i, p: (p[i] // CORES, 0, 0)),
    ] + [whole_block(array) for array in wholes]
    operands = [places, in_hbm(residual), weight, *wholes]
    aliases = {}
    if earlier is not None:
        aliases = {len(operands): 0}
        in_specs.append(pl.BlockSpec(memory_space=pltpu.HBM))
        operands.append(earlier)
    return pl.pallas_call(
        kernel,
        out_shape=out_shape,
        grid_spec=pltpu.PrefetchScalarGridSpec(
            num_scalar_prefetch=1,
            grid=(steps,),
            in_specs=in_specs,
            out_specs=out_specs,
            scratch_shapes=scratch,
        ),
        input_output_aliases=aliases,
        cost_estimate=NOMINAL,
        compiler_params=pltpu.CompilerParams(vmem_limit_bytes=WEIGHT_VMEM),
    )(*operands)


def cot_kernel(width, rep_count, info_ref, shares_ref, squares_ref, value_cot_ref, cot_ref, cot_t_ref, inv_ref):
    place, length = info_ref[0], info_ref[1]
    rows = value_cot_ref.shape[0]
    own = rows // 128
    seq = (shares_ref.shape[1] - own) // 3
    shares = range(shares_ref.shape[0])

    def below(first, shape):
        at = lax.broadcasted_iota(jnp.int32, shape, 0) * 128 + lax.broadcasted_iota(jnp.int32, shape, 1)
        return first + at < length

    def summed(mask, value):
        return jnp.sum(jnp.where(mask, value, 0.0), axis=(0, 1), keepdims=True)

    maxes = [shares_ref[m, 0:seq] for m in shares]
    top_max = functools.reduce(jnp.maximum, maxes)
    sum_exp = functools.reduce(
        jnp.add, [shares_ref[m, seq : 2 * seq] * jnp.exp(maxes[m] - top_max) for m in shares]
    )
    picked = functools.reduce(jnp.add, [shares_ref[m, 2 * seq : 3 * seq] for m in shares])
    ref_logp = picked - top_max - jnp.log(sum_exp)
    total = -summed(below(0, (seq, 128)), ref_logp)
    for m in shares:
        first = jnp.bitwise_xor(place, m) * rows
        total += summed(below(first, (own, 128)), shares_ref[m, 3 * seq :])
    seq_delta = total / jnp.full((1, 1), length, jnp.int32).astype(F32)
    weight = (2.0 / rep_count) * jax.nn.sigmoid(BETA * seq_delta)
    inv = lax.rsqrt(squares_ref[...] * (1.0 / width) + EPS)
    live = place * rows + lax.broadcasted_iota(jnp.int32, (rows, 1), 0) < length
    scaled = jnp.where(live, inv * weight, 0.0) * value_cot_ref[...].astype(F32)
    cot_ref[...] = scaled.astype(BF16)
    cot_t_ref[...] = scaled.T.astype(BF16)
    inv_ref[...] = inv


def scaled_cot(width, rep_count, info, shares, squares, value_cot):
    rows, features = value_cot.shape

    def whole(array):
        return pl.BlockSpec(array.shape, lambda i, p: (0,) * array.ndim)

    out_shape = [
        jax.ShapeDtypeStruct((rows, features), BF16),
        jax.ShapeDtypeStruct((features, rows), BF16),
        jax.ShapeDtypeStruct((rows, 1), F32),
    ]
    return pl.pallas_call(
        functools.partial(cot_kernel, width, rep_count),
        out_shape=out_shape,
        grid_spec=pltpu.PrefetchScalarGridSpec(
            num_scalar_prefetch=1,
            grid=(1,),
            in_specs=[whole(shares), whole(squares), whole(value_cot)],
            out_specs=[pl.BlockSpec(array.shape, lambda i, p: (0, 0)) for array in out_shape],
        ),
        cost_estimate=NOMINAL,
        compiler_params=pltpu.CompilerParams(vmem_limit_bytes=PAIR_VMEM),
    )(info, shares, squares, in_hbm(value_cot))


def per_device(
    residual,
    norm_gain,
    value_weight,
    value_cot,
    trainee_logp,
    ref_shard_max,
    ref_shard_sum,
    ref_target_logit,
    target_ids,
    lengths,
):
    rows_here, width = residual.shape
    features = value_cot.shape[1]
    tp_count = lax.axis_size("tp")
    outer, inner = lax.axis_size("outer"), lax.axis_size("inner")
    rep_count = outer * inner * CORES
    tp_place = lax.axis_index("tp")
    core = lax.axis_index("core")
    at_inner = lax.axis_index("inner")
    at_outer = lax.axis_index("outer")
    rep_place = (at_outer * inner + at_inner) * CORES + core
    depth = width // rep_count
    rows = depth // tp_count
    order = list(range(tp_count))
    shifts = chunk_shifts(tp_count)
    in_place = rows % 128 == 0 and outer == 2 and inner == 2 and tp_count == 4

    owned = jnp.where(
        target_ids // (VOCAB // tp_count) == tp_place,
        ref_target_logit[0],
        jnp.zeros_like(ref_target_logit[0]),
    )
    packed = jnp.concatenate([ref_shard_max[0], ref_shard_sum[0], owned, trainee_logp])
    packed = packed.reshape(1, -1, 128)
    packed = jnp.concatenate([packed, trade(packed, "tp", 1)])

    gained = (value_weight.astype(F32) * norm_gain.astype(F32)[:, None]).astype(BF16)
    residual, gained, packed = lax.optimization_barrier((residual, gained, packed))
    resid_wide = residual.astype(F32)
    squares = jnp.sum(resid_wide * resid_wide, axis=1, keepdims=True)

    def near_of(k, block):
        first = "inner" if inner_first(k) else "outer"
        return [swap(block, first, s) for s in range(1, lax.axis_size(first))]

    def far_of(k, block, nears):
        second = "outer" if inner_first(k) else "inner"
        near = jnp.stack([block] + nears)
        return [near] + [swap(near, second, s) for s in range(1, lax.axis_size(second))]

    mask = 2
    while mask < tp_count:
        packed = jnp.concatenate([packed, trade(packed, "tp", mask)])
        mask *= 2
    own_pieces, near = {}, {}
    arrived = {0: gained, 1: swap(gained, "tp", shifts[1])}
    near[0] = near_of(0, gained)
    arrived[1], near[0], squares, late_gained = lax.optimization_barrier(
        (arrived[1], near[0], squares, gained)
    )
    near[1] = near_of(1, arrived[1])
    arrived[2] = swap(late_gained, "tp", shifts[2])
    own_pieces[0] = far_of(0, gained, near[0])
    seq_length = lax.dynamic_index_in_dim(lengths, rep_place, keepdims=False)
    info = jnp.stack([tp_place, seq_length]).astype(jnp.int32)
    near[1], arrived[2], packed, late_gained, info = lax.optimization_barrier(
        (near[1], arrived[2], packed, late_gained, info)
    )
    near[2] = near_of(2, arrived[2])
    for k in order[3:]:
        arrived[k] = swap(late_gained, "tp", shifts[k])
    own_pieces[1] = far_of(1, arrived[1], near[1])
    cot, cot_t, inv_rms = scaled_cot(width, rep_count, info, packed, squares, value_cot)

    def place_of(o, i, c, k):
        chip = lax.rem(at_outer + o, outer) * inner + lax.rem(at_inner + i, inner)
        return (chip * CORES + c) * tp_count + lax.rem(tp_place + k, tp_count)

    backward = order[::-1]
    pairs = [backward[i : i + 2] for i in range(0, tp_count, 2)]
    chips = [(o, i) for o in range(outer) for i in range(inner)]
    if not in_place:
        product = jnp.dot(cot_t, residual, preferred_element_type=F32).astype(BF16)
        product = product.reshape(features, -1, rows).transpose(1, 0, 2)

    def places_of(pair, c):
        return jnp.stack([place_of(o, i, c, k) for o, i in chips for k in pair]).astype(jnp.int32)

    def for_others(cot_t):
        places = places_of(backward, 1 - core)
        if in_place:
            return grad_product(residual, cot_t, places, rows, None)
        both = after(product, cot_t)[places].reshape(len(chips), tp_count, features, rows)
        return both.swapaxes(0, 1)

    def for_us(other):
        places = places_of(backward, core)
        if in_place:
            outs = grad_product(residual, cot_t, places, rows, other)
            return [[([outs[0]], outs[1]), ([outs[2]], outs[3])], outs[4], outs[5], outs[6]]
        else:
            both = product[places].reshape(len(chips), tp_count, features, rows).swapaxes(0, 1)
            total = widen([both, other]).astype(BF16)
            total = total.reshape(tp_count, outer, inner, features, rows)
            sides = []
            for n in range(0, tp_count, 2):
                sides.append(([total[n, :, s] for s in range(1, inner)], total[n, :, 0]))
                sides.append(([total[n + 1, s] for s in range(1, outer)], total[n + 1, 0]))
        return [sides[n : n + 2] for n in range(0, tp_count, 2)]

    def first_round(sides):
        return [
            [swap(send, axis, s + 1) for s, send in enumerate(sends)]
            for axis, (sends, _) in zip(("inner", "outer"), sides)
        ]

    def second_round(sides, got):
        axes = ("outer", "inner")
        groups = [[keep] + parts for (_, keep), parts in zip(sides, got)]
        return [
            [
                swap(widen([part[s] for part in parts]).astype(BF16), axis, s)
                for s in range(1, lax.axis_size(axis))
            ]
            for parts, axis in zip(groups, axes)
        ]

    def summed(sides, got, later):
        return [
            widen([part[0] for part in [keep] + parts] + last)
            for (_, keep), parts, last in zip(sides, got, later)
        ]

    theirs = for_others(cot_t)
    theirs, arrived = lax.optimization_barrier((theirs, arrived))
    near.update({k: near_of(k, arrived[k]) for k in order[3:]})
    theirs, own_pieces, near = lax.optimization_barrier((theirs, own_pieces, near))
    other = swap(theirs, "core", 1)
    near, own_pieces = lax.optimization_barrier((near, own_pieces))
    for k in order[2:]:
        own_pieces[k] = far_of(k, arrived[k], near[k])
    sides = for_us(other)
    if in_place:
        sides, passed_near, passed_far, kept = sides[:1], sides[1], sides[2], sides[3]
        kept, own_pieces = lax.optimization_barrier((kept, own_pieces))
        beyond = swap(passed_far, "tp", 1)
    else:
        beyond = ()
    got = [first_round(sides[0])]
    sides[1:], own_pieces = lax.optimization_barrier((sides[1:], own_pieces))

    if in_place:
        pieces = [piece for k in order for piece in own_pieces[k]]
        flags = tuple(inner_first(k) for k in order)
        places = [
            jnp.stack([place_of(o, i, c, 0) // tp_count for o, i in chips]).astype(jnp.int32)
            for c in (core, 1 - core)
        ]
        offsets = jnp.stack([lax.rem(tp_place - shift + tp_count, tp_count) * rows for shift in shifts])
        offsets = offsets.astype(jnp.int32)
        total, own_weight = first_value(flags, places[0], offsets, residual, pieces)
    else:
        weight = []
        for k in order:
            both = jnp.stack(own_pieces[k])
            weight.append(both if inner_first(k) else jnp.swapaxes(both, 0, 1))
        by_shift = jnp.array([shifts.index(shift) for shift in range(tp_count)])
        weight = jnp.stack(weight)[by_shift[(tp_place - jnp.arange(tp_count)) % tp_count]]
        weight = weight[:, (at_outer - jnp.arange(outer)) % outer]
        weight = weight[:, :, (at_inner - jnp.arange(inner)) % inner]
        own_weight = weight.transpose(1, 2, 0, 3, 4).reshape(outer * inner, depth, features)
        total = jnp.zeros((), F32)
    got[0], sides[1:], total, own_weight, beyond = lax.optimization_barrier(
        (got[0], sides[1:], total, own_weight, beyond)
    )
    if in_place:
        sent = [
            widen([keep[1], parts[0][1]]).astype(BF16) for (_, keep), parts in zip(sides[0], got[0])
        ]
        sent, beyond, passed_near = lax.optimization_barrier((sent, beyond, passed_near))
        later = [[[swap(x, axis, 1)] for x, axis in zip(sent, ("outer", "inner"))]]
        passed_near = swap(passed_near, "tp", 1)
    else:
        later = [second_round(sides[0], got[0])]
    other_weight = swap(own_weight, "core", 1)
    got += [first_round(side) for side in sides[1:]]
    if in_place:
        value_proj, coefficient = weight_call(
            functools.partial(value_end_kernel, width),
            places[1],
            residual,
            other_weight,
            [in_hbm(total), cot, inv_rms],
            [
                jax.ShapeDtypeStruct((rows_here, features), BF16),
                jax.ShapeDtypeStruct((rows_here, 1), F32),
            ],
        )
    else:
        both = jnp.stack([own_weight, other_weight], axis=1)
        weight = jnp.where(core == 0, both, both[:, ::-1]).reshape(width, features)
        value_acc = jnp.dot(residual, weight, preferred_element_type=F32)
        value_proj = (inv_rms * value_acc).astype(BF16)
        share = jnp.sum(cot.astype(F32) * value_acc, axis=1, keepdims=True)
        coefficient = inv_rms * inv_rms * share * (1.0 / width)
    later[0], coefficient = lax.optimization_barrier((later[0], coefficient))
    if in_place:
        groups = [[keep] + parts + then for (_, keep), parts, then in zip(sides[0], got[0], later[0])]
        sent = sums_of(groups, 0)
        last = [swap(x, "tp", k) for x, k in zip(sent, pairs[0])]
        coefficient, beyond = lax.optimization_barrier((coefficient, beyond))
        crossed = swap(widen([kept[2:], beyond]).astype(BF16), "outer", 1)
        grad_shape = jax.ShapeDtypeStruct((rows_here, width), BF16)
        resid_grad = weight_call(
            grad_kernel, places[0], residual, in_hbm(own_weight), [cot, coefficient], grad_shape
        )
        crossed, passed_near, resid_grad = lax.optimization_barrier(
            (crossed, passed_near, resid_grad)
        )
        beside = swap(widen([kept[1], passed_near[1], crossed[1]]).astype(BF16), "inner", 1)
        resid_grad = weight_call(
            grad_kernel, places[1], residual, other_weight, [cot, coefficient], grad_shape, resid_grad
        )
        last, beside, resid_grad = lax.optimization_barrier((last, beside, resid_grad))
        grad_rows = widen([kept[0], passed_near[0], crossed[0], beside] + last)
    else:
        normed_grad = lax.dot_general(
            cot, weight, (((1,), (1,)), ((), ())), preferred_element_type=F32
        )
        resid_grad = (normed_grad - residual.astype(F32) * coefficient).astype(BF16)
        later += [second_round(side, parts) for side, parts in zip(sides[1:], got[1:])]
        sums = {}
        for pair, *rounds in zip(pairs, sides, got, later):
            sums.update(zip(pair, summed(*rounds)))
        last = [swap(sums[k].astype(BF16), "tp", k) for k in backward[:-1]]
        grad_rows = widen([sums[0]] + last)
    late_gain, late_weight, grad_rows = lax.optimization_barrier((norm_gain, value_weight, grad_rows))
    weight_grad = (late_gain.astype(F32)[None, :] * grad_rows).T
    gain_grad = jnp.sum(late_weight.astype(F32).T * grad_rows, axis=0)
    return (value_proj, resid_grad, weight_grad, gain_grad)


def solution(mesh):
    rep_count, tp_count = mesh.shape["rep"], mesh.shape["tp"]
    split = jax.sharding.Mesh(
        mesh.devices.reshape(OUTER, rep_count // (OUTER * CORES), CORES, tp_count),
        ("outer", "inner", "core", "tp"),
    )
    rep = ("outer", "inner", "core")
    rows = rep + ("tp",)
    return jax.shard_map(
        per_device,
        mesh=split,
        in_specs=(
            P(rows, None),
            P(rows),
            P(rows, None),
            P(rows, None),
            P(rows),
            P("tp", rep),
            P("tp", rep),
            P("tp", rep),
            P(rep),
            P(),
        ),
        out_specs=(P(rows, None), P(rows, None), P(rows, None), P(rows)),
        check_vma=False,
    )
```

```python
import functools

import jax
import jax.numpy as jnp
from jax import lax
from jax.experimental import pallas as pl
from jax.experimental.pallas import tpu as pltpu
from jax.sharding import PartitionSpec as P

VOCAB = 128256
EPS = 1e-05
BETA = 0.5
CORES = 2
OUTER = 2
PAIR_VMEM = 12 * 1024 * 1024
WEIGHT_VMEM = 15 * 1024 * 1024
NOMINAL = pl.CostEstimate(flops=1024, bytes_accessed=1024, transcendentals=0)
BF16 = jnp.bfloat16
F32 = jnp.float32


def swap(value, axis, step):
    size = lax.axis_size(axis)
    return lax.ppermute(value, axis, [(place, (place + step) % size) for place in range(size)])


def trade(value, axis, mask):
    size = lax.axis_size(axis)
    return lax.ppermute(value, axis, [(place, place ^ mask) for place in range(size)])


def in_hbm(array):
    return pltpu.with_memory_space_constraint(array, pltpu.HBM)


def after(value, *earlier):
    return lax.optimization_barrier((value, earlier))[0]


def widen(parts):
    return functools.reduce(jnp.add, [part.astype(F32) for part in parts])


def chunk_shifts(tp_count):
    shifts = [0]
    for step in range(1, tp_count // 2 + 1):
        shifts += [step] if 2 * step == tp_count else [step, tp_count - step]
    return shifts


def inner_first(chunk):
    return chunk % 4 in (0, 3)


def theirs_kernel(places_ref, cot_ref, *rest):
    blocks, out_ref = rest[:-1], rest[-1]
    for slot, resid_ref in enumerate(blocks):
        product = jnp.dot(cot_ref[...], resid_ref[...], preferred_element_type=F32)
        out_ref[slot, 0] = product.astype(BF16)


def ours_kernel(places_ref, cot_ref, *rest):
    slots = 4
    blocks, other_ref, outs = rest[:slots], rest[slots], rest[slots + 1 :]
    step = pl.program_id(0)
    ways = (lax.rem(step, 2), step // 2)
    totals = [
        (
            jnp.dot(cot_ref[...], resid_ref[...], preferred_element_type=F32)
            + other_ref[slot, 0].astype(F32)
        ).astype(BF16)
        for slot, resid_ref in enumerate(blocks)
    ]
    for slot, way in enumerate(ways):
        send_ref, keep_ref = outs[2 * slot : 2 * slot + 2]

        @pl.when(way == 1)
        def _():
            send_ref[0] = totals[slot]

        @pl.when(way == 0)
        def _():
            keep_ref[0] = totals[slot]

    near_ref, far_ref, kept_ref = outs[4:]
    kept_ref[0] = totals[3]

    @pl.when(ways[1] == 1)
    def _():
        far_ref[0] = totals[2]

    @pl.when(ways[1] == 0)
    def _():
        near_ref[0] = totals[2]


def grad_product(residual, cot_t, places, rows, other):
    features, tokens = cot_t.shape
    steps = 4
    slots = places.shape[0] // steps
    in_specs = [pl.BlockSpec((features, tokens), lambda i, p: (0, 0))] + [
        pl.BlockSpec((tokens, rows), lambda i, p, slot=slot: (0, p[slots * i + slot]))
        for slot in range(slots)
    ]
    operands = [places, cot_t] + [in_hbm(residual)] * slots
    block = pl.BlockSpec((slots, 1, features, rows), lambda i, p: (0, i, 0, 0))
    if other is None:
        kernel, out_specs = theirs_kernel, block
        out_shape = pltpu.HBM((slots, steps, features, rows), BF16)
    else:
        kernel = ours_kernel
        in_specs.append(block)
        operands.append(other)
        indices = [
            lambda i: i // 2,
            lambda i: i // 2,
            lambda i: jnp.maximum(i - 2, 0),
            lambda i: jnp.minimum(i, 1),
            lambda i: jnp.minimum(i, 1),
            lambda i: jnp.maximum(i - 2, 0),
            lambda i: i,
        ]
        out_specs = [
            pl.BlockSpec((1, features, rows), lambda i, p, index=index: (index(i), 0, 0))
            for index in indices
        ]
        out_shape = [pltpu.HBM((n, features, rows), BF16) for n in (2, 2, 2, 2, 2, 2, steps)]
    return pl.pallas_call(
        kernel,
        out_shape=out_shape,
        grid_spec=pltpu.PrefetchScalarGridSpec(
            num_scalar_prefetch=1, grid=(steps,), in_specs=in_specs, out_specs=out_specs
        ),
        cost_estimate=NOMINAL,
        compiler_params=pltpu.CompilerParams(vmem_limit_bytes=PAIR_VMEM),
    )(*operands)


def sum_kernel(counts, *refs):
    ins, outs = refs[: sum(counts)], refs[sum(counts) :]
    for n, out_ref in enumerate(outs):
        first = sum(counts[:n])
        parts = [ref[...].astype(F32).reshape(out_ref.shape) for ref in ins[first : first + counts[n]]]
        out_ref[...] = functools.reduce(jnp.add, parts).astype(BF16)


def sums_of(groups, slot):
    shape = groups[0][0].shape[-2:]
    in_specs = [
        pl.BlockSpec((1,) + shape, lambda i: (slot, 0, 0))
        if part.ndim == 3
        else pl.BlockSpec(shape, lambda i: (0, 0))
        for parts in groups
        for part in parts
    ]
    return pl.pallas_call(
        functools.partial(sum_kernel, [len(parts) for parts in groups]),
        out_shape=[jax.ShapeDtypeStruct(shape, BF16)] * len(groups),
        grid=(1,),
        in_specs=in_specs,
        out_specs=[pl.BlockSpec(shape, lambda i: (0, 0))] * len(groups),
        cost_estimate=NOMINAL,
        compiler_params=pltpu.CompilerParams(vmem_limit_bytes=PAIR_VMEM),
    )(*[part for parts in groups for part in parts])


def place_weight(inner_flags, offsets_ref, pieces, weight_ref):
    step = pl.program_id(0)
    at_outer, at_inner = step // 2, lax.rem(step, 2)
    rows = pieces[0].shape[1]
    for chunk, flag in enumerate(inner_flags):
        way = at_outer if flag else at_inner
        where = pl.ds(pl.multiple_of(offsets_ref[chunk], rows), rows)
        for late in range(2):
            piece = pieces[chunk * 2 + late]

            @pl.when(way == late)
            def _():
                weight_ref[0, where, :] = piece[0]


def piece_specs(inner_flags, rows, features):
    specs = []
    for flag in inner_flags:
        for late in range(2):
            if flag:
                index = lambda i, *_, first=2 * late: (jnp.clip(i - first, 0, 1), 0, 0)
            else:
                index = lambda i, *_: (i // 2, 0, 0)
            specs.append(pl.BlockSpec((1, rows, features), index))
    return specs


def value_kernel(inner_flags, places_ref, offsets_ref, resid_ref, *rest):
    pieces, (total_ref, weight_ref) = rest[:-2], rest[-2:]
    step = pl.program_id(0)
    place_weight(inner_flags, offsets_ref, pieces, weight_ref)
    product = jnp.dot(resid_ref[...], weight_ref[0], preferred_element_type=F32)

    @pl.when(step == 0)
    def _():
        total_ref[...] = product

    @pl.when(step > 0)
    def _():
        total_ref[...] += product


def value_end_kernel(
    width, places_ref, resid_ref, weight_ref, first_ref, cot_ref, inv_ref, value_ref, coef_ref, total_ref
):
    step = pl.program_id(0)
    product = jnp.dot(resid_ref[...], weight_ref[0], preferred_element_type=F32)

    @pl.when(step == 0)
    def _():
        total_ref[...] = first_ref[...] + product

    @pl.when(step > 0)
    def _():
        total_ref[...] += product

    @pl.when(step == pl.num_programs(0) - 1)
    def _():
        total = total_ref[...]
        inv = inv_ref[...]
        value_ref[...] = (total * inv).astype(BF16)
        share = jnp.sum(total * cot_ref[...].astype(F32), axis=1, keepdims=True)
        coef_ref[...] = share * (inv * inv) * (1.0 / width)


def grad_kernel(places_ref, resid_ref, weight_ref, cot_ref, coef_ref, *rest):
    out_ref = rest[-1]
    grad = lax.dot_general(
        cot_ref[...], weight_ref[0], (((1,), (1,)), ((), ())), preferred_element_type=F32
    )
    out_ref[...] = (grad - resid_ref[...].astype(F32) * coef_ref[...]).astype(BF16)


def whole_block(array):
    return pl.BlockSpec(array.shape, lambda i, *_: (0, 0))


def first_value(inner_flags, places, offsets, residual, pieces):
    tokens, width = residual.shape
    rows, features = pieces[0].shape[1:]
    steps = places.shape[0]
    depth = width // (CORES * steps)
    total = pltpu.HBM((tokens, features), F32)
    return pl.pallas_call(
        functools.partial(value_kernel, inner_flags),
        out_shape=[total, pltpu.HBM((steps, depth, features), BF16)],
        grid_spec=pltpu.PrefetchScalarGridSpec(
            num_scalar_prefetch=2,
            grid=(steps,),
            in_specs=[pl.BlockSpec((tokens, depth), lambda i, p, o: (0, p[i]))]
            + piece_specs(inner_flags, rows, features),
            out_specs=[
                whole_block(total),
                pl.BlockSpec((1, depth, features), lambda i, p, o: (p[i] // CORES, 0, 0)),
            ],
        ),
        cost_estimate=NOMINAL,
        compiler_params=pltpu.CompilerParams(vmem_limit_bytes=WEIGHT_VMEM),
    )(places, offsets, in_hbm(residual), *pieces)


def weight_call(kernel, places, residual, weight, wholes, out_shape, earlier=None):
    tokens, width = residual.shape
    _, depth, features = weight.shape
    steps = places.shape[0]
    scratch = []
    if isinstance(out_shape, list):
        out_specs = [whole_block(array) for array in out_shape]
        scratch.append(pltpu.VMEM((tokens, features), F32))
    else:
        out_specs = pl.BlockSpec((tokens, depth), lambda i, p: (0, p[i]))
    in_specs = [
        pl.BlockSpec((tokens, depth), lambda i, p: (0, p[i])),
        pl.BlockSpec((1, depth, features), lambda i, p: (p[i] // CORES, 0, 0)),
    ] + [whole_block(array) for array in wholes]
    operands = [places, in_hbm(residual), weight, *wholes]
    aliases = {}
    if earlier is not None:
        aliases = {len(operands): 0}
        in_specs.append(pl.BlockSpec(memory_space=pltpu.HBM))
        operands.append(earlier)
    return pl.pallas_call(
        kernel,
        out_shape=out_shape,
        grid_spec=pltpu.PrefetchScalarGridSpec(
            num_scalar_prefetch=1,
            grid=(steps,),
            in_specs=in_specs,
            out_specs=out_specs,
            scratch_shapes=scratch,
        ),
        input_output_aliases=aliases,
        cost_estimate=NOMINAL,
        compiler_params=pltpu.CompilerParams(vmem_limit_bytes=WEIGHT_VMEM),
    )(*operands)


def cot_kernel(width, rep_count, info_ref, shares_ref, squares_ref, value_cot_ref, cot_ref, cot_t_ref, inv_ref):
    place, length = info_ref[0], info_ref[1]
    rows = value_cot_ref.shape[0]
    own = rows // 128
    seq = (shares_ref.shape[1] - own) // 3
    shares = range(shares_ref.shape[0])

    def below(first, shape):
        at = lax.broadcasted_iota(jnp.int32, shape, 0) * 128 + lax.broadcasted_iota(jnp.int32, shape, 1)
        return first + at < length

    def summed(mask, value):
        return jnp.sum(jnp.where(mask, value, 0.0), axis=(0, 1), keepdims=True)

    maxes = [shares_ref[m, 0:seq] for m in shares]
    top_max = functools.reduce(jnp.maximum, maxes)
    sum_exp = functools.reduce(
        jnp.add, [shares_ref[m, seq : 2 * seq] * jnp.exp(maxes[m] - top_max) for m in shares]
    )
    picked = functools.reduce(jnp.add, [shares_ref[m, 2 * seq : 3 * seq] for m in shares])
    ref_logp = picked - top_max - jnp.log(sum_exp)
    total = -summed(below(0, (seq, 128)), ref_logp)
    for m in shares:
        first = jnp.bitwise_xor(place, m) * rows
        total += summed(below(first, (own, 128)), shares_ref[m, 3 * seq :])
    seq_delta = total / jnp.full((1, 1), length, jnp.int32).astype(F32)
    weight = (2.0 / rep_count) * jax.nn.sigmoid(BETA * seq_delta)
    inv = lax.rsqrt(squares_ref[...] * (1.0 / width) + EPS)
    live = place * rows + lax.broadcasted_iota(jnp.int32, (rows, 1), 0) < length
    scaled = jnp.where(live, inv * weight, 0.0) * value_cot_ref[...].astype(F32)
    cot_ref[...] = scaled.astype(BF16)
    cot_t_ref[...] = scaled.T.astype(BF16)
    inv_ref[...] = inv


def scaled_cot(width, rep_count, info, shares, squares, value_cot):
    rows, features = value_cot.shape

    def whole(array):
        return pl.BlockSpec(array.shape, lambda i, p: (0,) * array.ndim)

    out_shape = [
        jax.ShapeDtypeStruct((rows, features), BF16),
        jax.ShapeDtypeStruct((features, rows), BF16),
        jax.ShapeDtypeStruct((rows, 1), F32),
    ]
    return pl.pallas_call(
        functools.partial(cot_kernel, width, rep_count),
        out_shape=out_shape,
        grid_spec=pltpu.PrefetchScalarGridSpec(
            num_scalar_prefetch=1,
            grid=(1,),
            in_specs=[whole(shares), whole(squares), whole(value_cot)],
            out_specs=[pl.BlockSpec(array.shape, lambda i, p: (0, 0)) for array in out_shape],
        ),
        cost_estimate=NOMINAL,
        compiler_params=pltpu.CompilerParams(vmem_limit_bytes=PAIR_VMEM),
    )(info, shares, squares, in_hbm(value_cot))


def per_device(
    residual,
    norm_gain,
    value_weight,
    value_cot,
    trainee_logp,
    ref_shard_max,
    ref_shard_sum,
    ref_target_logit,
    target_ids,
    lengths,
):
    rows_here, width = residual.shape
    features = value_cot.shape[1]
    tp_count = lax.axis_size("tp")
    outer, inner = lax.axis_size("outer"), lax.axis_size("inner")
    rep_count = outer * inner * CORES
    tp_place = lax.axis_index("tp")
    core = lax.axis_index("core")
    at_inner = lax.axis_index("inner")
    at_outer = lax.axis_index("outer")
    rep_place = (at_outer * inner + at_inner) * CORES + core
    depth = width // rep_count
    rows = depth // tp_count
    order = list(range(tp_count))
    shifts = chunk_shifts(tp_count)
    in_place = rows % 128 == 0 and outer == 2 and inner == 2 and tp_count == 4

    owned = jnp.where(
        target_ids // (VOCAB // tp_count) == tp_place,
        ref_target_logit[0],
        jnp.zeros_like(ref_target_logit[0]),
    )
    packed = jnp.concatenate([ref_shard_max[0], ref_shard_sum[0], owned, trainee_logp])
    packed = packed.reshape(1, -1, 128)
    packed = jnp.concatenate([packed, trade(packed, "tp", 1)])

    gained = (value_weight.astype(F32) * norm_gain.astype(F32)[:, None]).astype(BF16)
    residual, gained, packed = lax.optimization_barrier((residual, gained, packed))
    resid_wide = residual.astype(F32)
    squares = jnp.sum(resid_wide * resid_wide, axis=1, keepdims=True)

    def near_of(k, block):
        first = "inner" if inner_first(k) else "outer"
        return [swap(block, first, s) for s in range(1, lax.axis_size(first))]

    def far_of(k, block, nears):
        second = "outer" if inner_first(k) else "inner"
        near = jnp.stack([block] + nears)
        return [near] + [swap(near, second, s) for s in range(1, lax.axis_size(second))]

    mask = 2
    while mask < tp_count:
        packed = jnp.concatenate([packed, trade(packed, "tp", mask)])
        mask *= 2
    own_pieces, near = {}, {}
    arrived = {0: gained, 1: swap(gained, "tp", shifts[1])}
    near[0] = near_of(0, gained)
    arrived[1], near[0], squares, late_gained = lax.optimization_barrier(
        (arrived[1], near[0], squares, gained)
    )
    near[1] = near_of(1, arrived[1])
    arrived[2] = swap(late_gained, "tp", shifts[2])
    seq_length = lax.dynamic_index_in_dim(lengths, rep_place, keepdims=False)
    info = jnp.stack([tp_place, seq_length]).astype(jnp.int32)
    near[0], near[1], arrived[2], packed, late_gained, info = lax.optimization_barrier(
        (near[0], near[1], arrived[2], packed, late_gained, info)
    )
    near[2] = near_of(2, arrived[2])
    for k in order[3:]:
        arrived[k] = swap(late_gained, "tp", shifts[k])
    own_pieces[1] = far_of(1, arrived[1], near[1])
    own_pieces[0] = far_of(0, gained, near[0])
    cot, cot_t, inv_rms = scaled_cot(width, rep_count, info, packed, squares, value_cot)

    def place_of(o, i, c, k):
        chip = lax.rem(at_outer + o, outer) * inner + lax.rem(at_inner + i, inner)
        return (chip * CORES + c) * tp_count + lax.rem(tp_place + k, tp_count)

    backward = order[::-1]
    pairs = [backward[i : i + 2] for i in range(0, tp_count, 2)]
    chips = [(o, i) for o in range(outer) for i in range(inner)]
    if not in_place:
        product = jnp.dot(cot_t, residual, preferred_element_type=F32).astype(BF16)
        product = product.reshape(features, -1, rows).transpose(1, 0, 2)

    def places_of(pair, c):
        return jnp.stack([place_of(o, i, c, k) for o, i in chips for k in pair]).astype(jnp.int32)

    def for_others(cot_t):
        places = places_of(backward, 1 - core)
        if in_place:
            return grad_product(residual, cot_t, places, rows, None)
        both = after(product, cot_t)[places].reshape(len(chips), tp_count, features, rows)
        return both.swapaxes(0, 1)

    def for_us(other):
        places = places_of(backward, core)
        if in_place:
            outs = grad_product(residual, cot_t, places, rows, other)
            return [[([outs[0]], outs[1]), ([outs[2]], outs[3])], outs[4], outs[5], outs[6]]
        else:
            both = product[places].reshape(len(chips), tp_count, features, rows).swapaxes(0, 1)
            total = widen([both, other]).astype(BF16)
            total = total.reshape(tp_count, outer, inner, features, rows)
            sides = []
            for n in range(0, tp_count, 2):
                sides.append(([total[n, :, s] for s in range(1, inner)], total[n, :, 0]))
                sides.append(([total[n + 1, s] for s in range(1, outer)], total[n + 1, 0]))
        return [sides[n : n + 2] for n in range(0, tp_count, 2)]

    def first_round(sides):
        return [
            [swap(send, axis, s + 1) for s, send in enumerate(sends)]
            for axis, (sends, _) in zip(("inner", "outer"), sides)
        ]

    def second_round(sides, got):
        axes = ("outer", "inner")
        groups = [[keep] + parts for (_, keep), parts in zip(sides, got)]
        return [
            [
                swap(widen([part[s] for part in parts]).astype(BF16), axis, s)
                for s in range(1, lax.axis_size(axis))
            ]
            for parts, axis in zip(groups, axes)
        ]

    def summed(sides, got, later):
        return [
            widen([part[0] for part in [keep] + parts] + last)
            for (_, keep), parts, last in zip(sides, got, later)
        ]

    theirs = for_others(cot_t)
    theirs, arrived = lax.optimization_barrier((theirs, arrived))
    near.update({k: near_of(k, arrived[k]) for k in order[3:]})
    theirs, own_pieces, near = lax.optimization_barrier((theirs, own_pieces, near))
    other = swap(theirs, "core", 1)
    near, own_pieces = lax.optimization_barrier((near, own_pieces))
    for k in order[2:]:
        own_pieces[k] = far_of(k, arrived[k], near[k])
    sides = for_us(other)
    if in_place:
        sides, passed_near, passed_far, kept = sides[:1], sides[1], sides[2], sides[3]
        kept, own_pieces = lax.optimization_barrier((kept, own_pieces))
        beyond = swap(passed_far, "tp", 1)
    else:
        beyond = ()
    got = [first_round(sides[0])]
    sides[1:], own_pieces = lax.optimization_barrier((sides[1:], own_pieces))

    if in_place:
        pieces = [piece for k in order for piece in own_pieces[k]]
        flags = tuple(inner_first(k) for k in order)
        places = [
            jnp.stack([place_of(o, i, c, 0) // tp_count for o, i in chips]).astype(jnp.int32)
            for c in (core, 1 - core)
        ]
        offsets = jnp.stack([lax.rem(tp_place - shift + tp_count, tp_count) * rows for shift in shifts])
        offsets = offsets.astype(jnp.int32)
        total, own_weight = first_value(flags, places[0], offsets, residual, pieces)
    else:
        weight = []
        for k in order:
            both = jnp.stack(own_pieces[k])
            weight.append(both if inner_first(k) else jnp.swapaxes(both, 0, 1))
        by_shift = jnp.array([shifts.index(shift) for shift in range(tp_count)])
        weight = jnp.stack(weight)[by_shift[(tp_place - jnp.arange(tp_count)) % tp_count]]
        weight = weight[:, (at_outer - jnp.arange(outer)) % outer]
        weight = weight[:, :, (at_inner - jnp.arange(inner)) % inner]
        own_weight = weight.transpose(1, 2, 0, 3, 4).reshape(outer * inner, depth, features)
        total = jnp.zeros((), F32)
    got[0], sides[1:], total, own_weight, beyond = lax.optimization_barrier(
        (got[0], sides[1:], total, own_weight, beyond)
    )
    if in_place:
        sent = [
            widen([keep[1], parts[0][1]]).astype(BF16) for (_, keep), parts in zip(sides[0], got[0])
        ]
        sent, beyond, passed_near = lax.optimization_barrier((sent, beyond, passed_near))
        later = [[[swap(x, axis, 1)] for x, axis in zip(sent, ("outer", "inner"))]]
        passed_near = swap(passed_near, "tp", 1)
    else:
        later = [second_round(sides[0], got[0])]
    other_weight = swap(own_weight, "core", 1)
    got += [first_round(side) for side in sides[1:]]
    if in_place:
        value_proj, coefficient = weight_call(
            functools.partial(value_end_kernel, width),
            places[1],
            residual,
            other_weight,
            [in_hbm(total), cot, inv_rms],
            [
                jax.ShapeDtypeStruct((rows_here, features), BF16),
                jax.ShapeDtypeStruct((rows_here, 1), F32),
            ],
        )
    else:
        both = jnp.stack([own_weight, other_weight], axis=1)
        weight = jnp.where(core == 0, both, both[:, ::-1]).reshape(width, features)
        value_acc = jnp.dot(residual, weight, preferred_element_type=F32)
        value_proj = (inv_rms * value_acc).astype(BF16)
        share = jnp.sum(cot.astype(F32) * value_acc, axis=1, keepdims=True)
        coefficient = inv_rms * inv_rms * share * (1.0 / width)
    later[0], coefficient = lax.optimization_barrier((later[0], coefficient))
    if in_place:
        groups = [[keep] + parts + then for (_, keep), parts, then in zip(sides[0], got[0], later[0])]
        sent = sums_of(groups, 0)
        last = [swap(x, "tp", k) for x, k in zip(sent, pairs[0])]
        coefficient, beyond = lax.optimization_barrier((coefficient, beyond))
        crossed = swap(widen([kept[2:], beyond]).astype(BF16), "outer", 1)
        grad_shape = jax.ShapeDtypeStruct((rows_here, width), BF16)
        resid_grad = weight_call(
            grad_kernel, places[0], residual, in_hbm(own_weight), [cot, coefficient], grad_shape
        )
        crossed, passed_near, resid_grad = lax.optimization_barrier(
            (crossed, passed_near, resid_grad)
        )
        beside = swap(widen([kept[1], passed_near[1], crossed[1]]).astype(BF16), "inner", 1)
        resid_grad = weight_call(
            grad_kernel, places[1], residual, other_weight, [cot, coefficient], grad_shape, resid_grad
        )
        last, beside, resid_grad = lax.optimization_barrier((last, beside, resid_grad))
        grad_rows = widen([kept[0], passed_near[0], crossed[0], beside] + last)
    else:
        normed_grad = lax.dot_general(
            cot, weight, (((1,), (1,)), ((), ())), preferred_element_type=F32
        )
        resid_grad = (normed_grad - residual.astype(F32) * coefficient).astype(BF16)
        later += [second_round(side, parts) for side, parts in zip(sides[1:], got[1:])]
        sums = {}
        for pair, *rounds in zip(pairs, sides, got, later):
            sums.update(zip(pair, summed(*rounds)))
        last = [swap(sums[k].astype(BF16), "tp", k) for k in backward[:-1]]
        grad_rows = widen([sums[0]] + last)
    late_gain, late_weight, grad_rows = lax.optimization_barrier((norm_gain, value_weight, grad_rows))
    weight_grad = (late_gain.astype(F32)[None, :] * grad_rows).T
    gain_grad = jnp.sum(late_weight.astype(F32).T * grad_rows, axis=0)
    return (value_proj, resid_grad, weight_grad, gain_grad)


def solution(mesh):
    rep_count, tp_count = mesh.shape["rep"], mesh.shape["tp"]
    split = jax.sharding.Mesh(
        mesh.devices.reshape(OUTER, rep_count // (OUTER * CORES), CORES, tp_count),
        ("outer", "inner", "core", "tp"),
    )
    rep = ("outer", "inner", "core")
    rows = rep + ("tp",)
    return jax.shard_map(
        per_device,
        mesh=split,
        in_specs=(
            P(rows, None),
            P(rows),
            P(rows, None),
            P(rows, None),
            P(rows),
            P("tp", rep),
            P("tp", rep),
            P("tp", rep),
            P(rep),
            P(),
        ),
        out_specs=(P(rows, None), P(rows, None), P(rows, None), P(rows)),
        check_vma=False,
    )
```
